32 devices in a mesh: scene: 2 (over y), az: 8 (over z, x), rg: 2 (over core).
Axes of the slice: x: 2, y: 2, z: 4, core: 2. Of those that a mesh axis runs over, the one named last changes fastest.
Arguments:
- raw_re: float32 [64, 32768], P('rg', ('scene', 'az')), parts along dimension 1, may hold values from -6 to 6
- raw_im: float32 [64, 32768], P('rg', ('scene', 'az')), parts along dimension 1, may hold values from -6 to 6
- ref_blocks: float32 [16, 64, 64], P(('scene', 'az'), None, 'rg'), parts along dimension 0, may hold values from -3.140625 to 3.140625
- owners: int32 [4], P('scene'), parts along dimension 0, may hold values from 0 to 7, as said below
- offsets: int32 [4], P('rg'), may hold values from -8 to 8
- taps: float32 [64, 8], P('rg'), may hold values from -3 to 3
Outputs:
- image_re: float32 [64, 32768], P('rg', ('scene', 'az')), parts along dimension 1
- image_im: float32 [64, 32768], P('rg', ('scene', 'az')), parts along dimension 1
The draws below stay inside these ranges and needn't reach their ends.
There are 2 independent parts, one for each index of `scene`. The reference program is written for one: setup_inputs(seed, part) draws one part's arguments, and reference() takes and returns one part's arrays. A program takes and returns all parts, laid end to end along the dimension named above; an argument that names none is the same for every part. Nothing has to cross between parts.
Inputs may be any that keep to these rules, and one draw needn't show every extreme that they name: The two sub-apertures have different owners.
All inputs are finite; a program needn't handle non-finite values.
Results may differ from the reference program's by a relative error of at most 0.00014.
Values sent between devices are 32-bit elements; how exact they have to be, the bound alone decides.
No kernel may reach another device: no remote copies, remote signals or barrier semaphores. Data moves between devices by JAX's collectives and lax.ppermute only.
A program may use at most 64 MiB of HBM per device.

```python
import jax
import jax.numpy as jnp
from jax import lax

TAPS = 8
REACH = 8
BLOCK = 16
REF_ROWS = 64
NA = 16384
NR = 64
NBLK = 4
N_AZ = 8


def draw_owners(key, part):
    other_key = jax.random.fold_in(key, 11)
    slot_key = jax.random.fold_in(key, 23)
    other = jax.random.randint(other_key, (), 0, N_AZ - 1, dtype=jnp.int32)
    last = jnp.full((), N_AZ - 1, dtype=jnp.int32)
    which = jax.random.randint(slot_key, (), 0, 2, dtype=jnp.int32)
    first = jnp.where(which == 0, last, other)
    second = jnp.where(which == 0, other, last)
    return jnp.stack([first, second]).astype(jnp.int32)


def set_ends(array, key, least, largest):
    extent = array.shape
    index_at = [jax.random.randint(jax.random.fold_in(key, axis), (), 0, extent[axis]) for axis in range(len(extent))]
    array = array.at[tuple(index_at)].set(least)
    longest = extent.index(max(extent))
    index_at[longest] = (index_at[longest] + 1) % extent[longest]
    return array.at[tuple(index_at)].set(largest)


def levels(key, dims, split, least, largest):
    level, own = 1.0, jax.random.fold_in(key, 6)
    for axis_at, blocks in split:
        draws = jnp.exp(jax.random.uniform(jax.random.fold_in(own, axis_at), (blocks,), jnp.float32, least / len(split), largest / len(split)))
        level = level * jnp.repeat(draws, dims[axis_at] // blocks).reshape([-1 if axis == axis_at else 1 for axis in range(len(dims))])
    return level


def bell_draw(rng, extent, deviation, most, split=(), kind=jnp.bfloat16):
    array = jax.random.normal(rng, extent, jnp.float32) * deviation
    if len(split) > 0:
        array = levels(rng, extent, split, -0.22, 0.18) * array
    return jnp.clip(array, min=-most, max=most).astype(kind)


def setup_inputs(seed: int = 0, part: int = 0) -> dict:
    arg_keys = jax.random.split(jax.random.key(seed), 7)
    part_keys = jax.random.split(jax.random.fold_in(arg_keys[6], part), 7)
    raw_re = bell_draw(part_keys[0], (NR, NA), 1.0, 6.0, ((0, 2), (1, 8)), jnp.float32)
    raw_im = bell_draw(part_keys[1], (NR, NA), 1.0, 6.0, ((0, 2), (1, 8)), jnp.float32)
    ref_blocks = jnp.clip(jax.random.uniform(part_keys[2], (N_AZ, REF_ROWS, NR), jnp.float32, -3.140625, 3.140625), -3.140625, 3.140625)
    owners = draw_owners(jax.random.fold_in(jax.random.fold_in(arg_keys[6], part), 71), part)
    offsets = set_ends(jax.random.randint(arg_keys[4], (NBLK,), 0 - REACH, REACH + 1), jax.random.fold_in(arg_keys[4], 1), 0 - REACH, REACH).astype(jnp.int32)
    taps = bell_draw(arg_keys[5], (NR, TAPS), 0.5, 3.0, ((0, 2),), jnp.float32)
    return dict(raw_re=raw_re, raw_im=raw_im, ref_blocks=ref_blocks, owners=owners, offsets=offsets, taps=taps)


PHASE_GAIN = 50.0

def reference(raw_re, raw_im, ref_blocks, owners, offsets, taps):
    rg_total = raw_re.shape[0]
    az_total = raw_re.shape[1]
    spectrum = jnp.fft.fft(lax.complex(raw_re, raw_im), axis=1)
    frequency = jnp.arange(az_total, dtype=jnp.int32)
    signed = (frequency + az_total // 2) % az_total - az_total // 2
    az_freq = signed.astype(jnp.float32) / az_total
    rg_index = jnp.arange(rg_total, dtype=jnp.int32)
    rg_freq = (rg_index.astype(jnp.float32) + 0.5) / (2 * rg_total) - 0.25
    model_phase = PHASE_GAIN * jnp.sqrt((1.0 + rg_freq)[:, None] ** 2 - az_freq[None, :] ** 2)
    chosen = ref_blocks[owners]
    coarse = frequency * REF_ROWS // az_total
    picked = jnp.where((signed >= 0)[None, :], chosen[1][coarse].T, chosen[0][coarse].T)
    phase_all = model_phase + picked
    matched = spectrum * lax.complex(jnp.cos(phase_all), jnp.sin(phase_all))
    rim_width = REACH + TAPS // 2
    padded = jnp.pad(matched, ((rim_width, rim_width), (0, 0)))
    offset_cols = jnp.repeat(offsets, BLOCK)
    stolt = jnp.zeros_like(matched)
    for tap_num in range(TAPS):
        source = rg_index + rim_width + offset_cols + tap_num - TAPS // 2
        stolt = stolt + taps[:, tap_num][:, None] * padded[source, :]
    image = jnp.fft.ifft(stolt, axis=1)
    return (image.real, image.imag)
```

```python
import functools
import math

import jax
import jax.numpy as jnp
import numpy as np
from jax import lax
from jax.experimental import pallas as pl
from jax.experimental.pallas import tpu as pltpu
from jax.sharding import PartitionSpec as P

SPLIT = 4
TAPS = 8
REACH = 8
BLOCK = 16


PRECISE = lax.Precision.HIGHEST
PHASE_GAIN = 50.0


def partner_2(value, axis, stride):
    return lax.ppermute(value, axis, [(i, i ^ 1 << stride) for i in range(lax.axis_size(axis))])


def from_root(block, axis, source):
    block = jnp.where(lax.axis_index(axis) == source, block, jnp.zeros_like(block))
    return lax.psum(block, axis)


def padded_2(value, sides, width):
    for axis, dim in sides:
        size, length = (lax.axis_size(axis), value.shape[dim])
        up = [(i, (i + 1) % size) for i in range(size - 1)]
        down = [(j, i) for i, j in up]
        last = lax.slice_in_dim(value, length - width, length, axis=dim)
        initial = lax.slice_in_dim(value, 0, width, axis=dim)
        before = lax.ppermute(last, axis, up)
        after = lax.ppermute(initial, axis, down)
        value = jnp.concatenate([before, value, after], axis=dim)
    return value


def angles(numerator, denominator, sign_value):
    return sign_value * 2.0 * math.pi * numerator.astype(jnp.float32) / denominator


def rotate(signal, cosine, sine_part):
    real_part = signal[0] * cosine - signal[1] * sine_part
    imag_part = signal[0] * sine_part + signal[1] * cosine
    return jnp.stack([real_part, imag_part])


def dft_table(length_n, sign_value):
    counter = jnp.arange(length_n, dtype=jnp.int32)
    turn_count = counter[:, None] * counter[None, :] % length_n
    angle_set = angles(turn_count, length_n, sign_value)
    return (jnp.cos(angle_set), jnp.sin(angle_set))


def complex_apply(einsum_form, cosine, sine_part, signal):
    real_part = jnp.einsum(einsum_form, cosine, signal[0], precision=PRECISE) - jnp.einsum(
        einsum_form, sine_part, signal[1], precision=PRECISE
    )
    imag_part = jnp.einsum(einsum_form, cosine, signal[1], precision=PRECISE) + jnp.einsum(
        einsum_form, sine_part, signal[0], precision=PRECISE
    )
    return jnp.stack([real_part, imag_part])


def local_dft(signal, sign_value):
    rg_cols = signal.shape[1]
    az_rows = signal.shape[2]
    inner_len = az_rows // SPLIT
    shaped = signal.reshape(2, rg_cols, SPLIT, inner_len)
    first_cos, first_sin = dft_table(SPLIT, sign_value)
    first_pass = complex_apply("aj,cjk->cak", first_cos, first_sin, shaped)
    outer_idx = jnp.arange(SPLIT, dtype=jnp.int32)
    inner_idx = jnp.arange(inner_len, dtype=jnp.int32)
    twist = angles(outer_idx[:, None] * inner_idx[None, :] % az_rows, az_rows, sign_value)
    first_pass = rotate(first_pass, jnp.cos(twist)[None, :, :], jnp.sin(twist)[None, :, :])
    second_cos, second_sin = dft_table(inner_len, sign_value)
    second_pass = complex_apply("bk,cak->cba", second_cos, second_sin, first_pass)
    return second_pass.reshape(2, rg_cols, az_rows)


def butterfly_down(signal, az_place, bit_count):
    for bit_num in reversed(range(bit_count)):
        half_span = 1 << bit_num
        partner = partner_2(signal, "az", bit_num)
        is_upper = az_place >> bit_num & 1 == 1
        angle_set = angles(az_place % half_span, 2 * half_span, -1.0)
        difference = rotate(partner - signal, jnp.cos(angle_set), jnp.sin(angle_set))
        signal = jnp.where(is_upper, difference, signal + partner)
    return signal


def butterfly_up(signal, az_place, bit_count):
    for bit_num in range(bit_count):
        half_span = 1 << bit_num
        partner = partner_2(signal, "az", bit_num)
        is_upper = az_place >> bit_num & 1 == 1
        angle_set = angles(az_place % half_span, 2 * half_span, 1.0)
        cosine = jnp.cos(angle_set)
        sine_part = jnp.sin(angle_set)
        lower_new = (signal + rotate(partner, cosine, sine_part)) * 0.5
        upper_new = (partner - rotate(signal, cosine, sine_part)) * 0.5
        signal = jnp.where(is_upper, upper_new, lower_new)
    return signal


def butterfly_shards(raw_re, raw_im, ref_blocks, owners, offsets, taps):
    rg_cols = raw_re.shape[0]
    az_rows = raw_re.shape[1]
    az_count = lax.axis_size("az")
    az_place = lax.axis_index("az")
    bit_count = az_count.bit_length() - 1
    az_total = az_rows * az_count
    rg_total = rg_cols * lax.axis_size("rg")
    own_block = ref_blocks[0]
    lower_ref = from_root(own_block, "az", owners[0])
    upper_ref = from_root(own_block, "az", owners[1])
    signal = jnp.stack([raw_re, raw_im])
    signal = butterfly_down(signal, az_place, bit_count)
    column = jnp.zeros((), jnp.int32)
    for bit_num in range(bit_count):
        column = column + ((az_place >> bit_num & 1) << bit_count - 1 - bit_num)
    row_index = jnp.arange(az_rows, dtype=jnp.int32)
    twist = angles(row_index * column % az_total, az_total, -1.0)
    signal = rotate(signal, jnp.cos(twist)[None, :], jnp.sin(twist)[None, :])
    signal = local_dft(signal, -1.0)
    frequency = column + az_count * row_index
    signed = (frequency + az_total // 2) % az_total - az_total // 2
    az_freq = signed.astype(jnp.float32) / az_total
    rg_index = lax.axis_index("rg") * rg_cols + jnp.arange(rg_cols, dtype=jnp.int32)
    rg_freq = (rg_index.astype(jnp.float32) + 0.5) / (2 * rg_total) - 0.25
    model_phase = PHASE_GAIN * jnp.sqrt((1.0 + rg_freq)[:, None] ** 2 - az_freq[None, :] ** 2)
    ref_rows = own_block.shape[0]
    coarse = frequency * ref_rows // az_total
    slot_index = jnp.where(signed >= 0, ref_rows + coarse, coarse)
    one_hot = (jnp.arange(2 * ref_rows, dtype=jnp.int32)[:, None] == slot_index[None, :]).astype(
        jnp.float32
    )
    both_refs = jnp.concatenate([lower_ref, upper_ref], axis=0)
    picked = jnp.dot(both_refs.T, one_hot, precision=PRECISE)
    phase_all = model_phase + picked
    signal = rotate(signal, jnp.cos(phase_all), jnp.sin(phase_all))
    rim_width = REACH + TAPS // 2
    padded = padded_2(signal, (("rg", 1),), rim_width)
    offset_cols = jnp.repeat(offsets, BLOCK)
    local_cols = jnp.arange(rg_cols, dtype=jnp.int32)
    tap_index = jnp.arange(TAPS, dtype=jnp.int32)
    target = local_cols[:, None] + rim_width + offset_cols[:, None] + tap_index[None, :] - TAPS // 2
    padded_index = jnp.arange(rg_cols + 2 * rim_width, dtype=jnp.int32)
    hits = (padded_index[:, None, None] == target[None, :, :]).astype(jnp.float32)
    band_matrix = jnp.sum(hits * taps[None, :, :], axis=2)
    signal = jnp.einsum("zma,mi->zia", padded, band_matrix, precision=PRECISE)
    signal = local_dft(signal, 1.0) / az_rows
    twist_back = angles(row_index * column % az_total, az_total, 1.0)
    signal = rotate(signal, jnp.cos(twist_back)[None, :], jnp.sin(twist_back)[None, :])
    signal = butterfly_up(signal, az_place, bit_count)
    return (signal[0], signal[1])


FACTOR = 128
GROUP = 4
WINDOW = 4 * GROUP
EDGE = 16


def split_bf16(value):
    high = value.astype(jnp.bfloat16)
    low = (value - high.astype(jnp.float32)).astype(jnp.bfloat16)
    return high, low


def dot_split(left, right):
    left_high, left_low = left
    right_high, right_low = right
    dot = functools.partial(jnp.dot, preferred_element_type=jnp.float32)
    return dot(left_high, right_high) + (dot(left_high, right_low) + dot(left_low, right_high))


def dft_constants():
    counter = np.arange(FACTOR)
    turns = np.outer(counter, counter)
    angle = 2 * np.pi * (turns % FACTOR) / FACTOR
    cosine, sine = np.cos(angle), np.sin(angle)
    pair = []
    for matrix in (np.block([[cosine, sine], [-sine, cosine]]), np.block([[cosine, -sine], [sine, cosine]])):
        high = matrix.astype(jnp.bfloat16)
        low = (matrix - high.astype(np.float64)).astype(jnp.bfloat16)
        pair.append((high, low))
    twist = 2 * np.pi * turns / FACTOR**2
    return pair[0], pair[1], (np.cos(twist).astype(np.float32), np.sin(twist).astype(np.float32))


def cos_sin_quarters(quarters):
    whole = jnp.floor(quarters + 0.5)
    rest = (quarters - whole) * (math.pi / 2)
    square = rest * rest
    sine = rest + rest * square * (
        -1.6666654611e-1 + square * (8.3321608736e-3 + square * (-1.9515295891e-4))
    )
    cosine = 1.0 - 0.5 * square + square * square * (
        4.166664568298827e-2 + square * (-1.388731625493765e-3 + square * 2.443315711809948e-5)
    )
    number = whole.astype(jnp.int32)
    odd = (number & 1) == 1
    turned_cos = jnp.where(odd, sine, cosine)
    turned_sin = jnp.where(odd, cosine, sine)
    cos_sign = jnp.where(((number + 1) & 2) == 2, -1.0, 1.0)
    sin_sign = jnp.where((number & 2) == 2, -1.0, 1.0)
    return turned_cos * cos_sign, turned_sin * sin_sign


def window_start(chip, side, offsets_own, offsets_other):
    block = chip * 2 * GROUP // BLOCK
    blocks = offsets_own.shape[0]
    local = lax.rem(block, blocks)
    shift = jnp.where(lax.div(block, blocks) == side, offsets_own[local], offsets_other[local])
    return chip * 2 * GROUP + shift - TAPS // 2


def group_starts(side):
    return GROUP + GROUP * side, 3 * GROUP * side


def pack_kernel(re_own, im_own, re_other, im_other, ref_own, ref_other, off_own, off_other, *refs):
    messages, (re_all, im_all, ref_all) = refs[:-3], refs[-3:]
    bins, samples = re_own.shape
    part_rows = samples // FACTOR
    place, side = lax.axis_index("az"), lax.axis_index("rg")
    own_at, other_at = EDGE + side * bins, EDGE + (1 - side) * bins
    zeros = jnp.zeros((EDGE * part_rows, FACTOR), jnp.float32)
    for all_ref, own, other in ((re_all, re_own, re_other), (im_all, im_own, im_other)):
        all_ref[: EDGE * part_rows, :] = zeros
        all_ref[(EDGE + 2 * bins) * part_rows :, :] = zeros
        for base, ref in ((own_at, own), (other_at, other)):
            for tile in range(0, bins, 8):
                for row in range(part_rows):
                    all_ref[pl.ds((base + tile) * part_rows + row, 8, stride=part_rows), :] = ref[
                        tile : tile + 8, row * FACTOR : (row + 1) * FACTOR
                    ]
    ref_rows = ref_own.shape[0]
    row = lax.broadcasted_iota(jnp.int32, (ref_rows, FACTOR), 0)
    column = lax.broadcasted_iota(jnp.int32, (ref_rows, FACTOR), 1)
    spread = (column * ref_rows // FACTOR == row).astype(jnp.float32)
    ref_all[:EDGE, :] = jnp.zeros((EDGE, FACTOR), jnp.float32)
    ref_all[EDGE + 2 * bins :, :] = jnp.zeros((EDGE, FACTOR), jnp.float32)
    for at, ref in ((own_at, ref_own), (other_at, ref_other)):
        ref_all[pl.ds(pl.multiple_of(at, 16), bins), :] = lax.dot_general(
            ref[...], spread, (((0,), (0,)), ((), ())), precision=PRECISE, preferred_element_type=jnp.float32
        )
    body = GROUP * part_rows
    for step, message in enumerate(messages):
        chip = place ^ step
        start = window_start(chip, side, off_own, off_other) + EDGE
        for group, group_at in enumerate(group_starts(side)):
            rows = pl.ds(pl.multiple_of((start + group_at) * part_rows, 8), body)
            message[group, :body, :] = re_all[rows, :]
            message[group, body : 2 * body, :] = im_all[rows, :]
            for bin_num in range(GROUP):
                message[group, 2 * body + bin_num, :] = ref_all[start + group_at + bin_num, :]
            message[group, 2 * body + GROUP :, :] = jnp.zeros((8 - GROUP, FACTOR), jnp.float32)


def phase_kernel(bins_total, off_own, off_other, out):
    place, side = lax.axis_index("az"), lax.axis_index("rg")
    start = window_start(place, side, off_own, off_other)
    shape = (FACTOR, FACTOR)
    frequency = lax.broadcasted_iota(jnp.int32, shape, 0) + FACTOR * lax.broadcasted_iota(jnp.int32, shape, 1)
    total = FACTOR * FACTOR
    signed = jnp.where(frequency >= total // 2, frequency - total, frequency)
    az_freq = signed.astype(jnp.float32) / total
    az_square = az_freq * az_freq
    for group, group_at in enumerate(group_starts(side)):
        for bin_num in range(GROUP):
            rg_index = (start + group_at + bin_num).astype(jnp.float32)
            rg_freq = (rg_index + 0.5) / (2 * bins_total) - 0.25
            base = (1.0 + rg_freq) * (1.0 + rg_freq)
            root = jnp.sqrt(base - az_square)
            cosine, sine = cos_sin_quarters(root * (PHASE_GAIN * 2 / math.pi))
            out[group, bin_num, 0] = cosine
            out[group, bin_num, 1] = sine


def spectrum_body(places, *refs):
    chunks, refs = refs[:places], refs[places:]
    owners, phase, high1, low1, high2, low2, twist_cos, twist_sin, out, lines, picks = refs
    place = lax.axis_index("az")
    samples = FACTOR * FACTOR // places
    part_rows = samples // FACTOR
    for step, chunk in enumerate(chunks):
        source = place ^ step
        for line in range(2 * GROUP):
            at = pl.multiple_of(line * FACTOR + source * part_rows, 8)
            lines[pl.ds(at, part_rows), :] = chunk[0, line * part_rows : (line + 1) * part_rows, :]
        picks[source] = chunk[0, 2 * GROUP * part_rows :, :]
    lane = lax.broadcasted_iota(jnp.int32, (2 * GROUP, FACTOR), 1)
    ref_phase = jnp.where(lane < FACTOR // 2, picks[owners[1]], picks[owners[0]])
    ref_cos, ref_sin = cos_sin_quarters(ref_phase * (2 / math.pi))
    first, second = (high1[...], low1[...]), (high2[...], low2[...])
    for pair in range(GROUP // 2):
        bins = (2 * pair, 2 * pair + 1)
        columns = []
        for bin_num in bins:
            real = lines[bin_num * FACTOR : (bin_num + 1) * FACTOR, :]
            imag = lines[(GROUP + bin_num) * FACTOR : (GROUP + bin_num + 1) * FACTOR, :]
            columns.append(jnp.concatenate([real, imag], axis=0))
        passed = dot_split(first, split_bf16(jnp.concatenate(columns, axis=1)))
        rows = []
        for at in range(2):
            real = passed[:FACTOR, at * FACTOR : (at + 1) * FACTOR]
            imag = passed[FACTOR:, at * FACTOR : (at + 1) * FACTOR]
            turned_real = real * twist_cos[...] + imag * twist_sin[...]
            turned_imag = imag * twist_cos[...] - real * twist_sin[...]
            rows.append(jnp.concatenate([turned_real, turned_imag], axis=1))
        passed = dot_split(split_bf16(jnp.concatenate(rows, axis=0)), second)
        for at, bin_num in enumerate(bins):
            real = passed[at * FACTOR : (at + 1) * FACTOR, :FACTOR]
            imag = passed[at * FACTOR : (at + 1) * FACTOR, FACTOR:]
            model_cos, model_sin = phase[0, bin_num, 0], phase[0, bin_num, 1]
            row_cos, row_sin = ref_cos[bin_num : bin_num + 1, :], ref_sin[bin_num : bin_num + 1, :]
            cosine = model_cos * row_cos - model_sin * row_sin
            sine = model_sin * row_cos + model_cos * row_sin
            out[bin_num, 0] = real * cosine - imag * sine
            out[bin_num, 1] = real * sine + imag * cosine


def image_kernel(places, *refs):
    shared, kept, received, taps_own, taps_other, high1, low1, high2, low2, twist_cos, twist_sin = refs[:11]
    messages, (band, lines) = refs[11:-2], refs[-2:]
    place, side = lax.axis_index("az"), lax.axis_index("rg")
    samples = FACTOR * FACTOR // places
    part_rows = samples // FACTOR
    bins_held = taps_own.shape[0]
    first_bin = place * 2 * GROUP + side * GROUP
    held = lax.div(first_bin, bins_held) == side
    local = lax.rem(first_bin, bins_held)
    weights = [
        [jnp.where(held, taps_own[local + j, t], taps_other[local + j, t]) for t in range(TAPS)] for j in range(GROUP)
    ]
    is_first = side == 0
    strip = 16
    for part in range(2):
        for at in range(0, FACTOR, strip):
            rows = slice(at, at + strip)
            sums = [None] * GROUP
            for slot in range(3 * GROUP):
                if slot < GROUP:
                    value = jnp.where(is_first, kept[slot, part, rows], received[slot, part, rows])
                elif slot < 2 * GROUP:
                    value = shared[slot - GROUP, part, rows]
                else:
                    at_slot = slot - 2 * GROUP
                    value = jnp.where(is_first, received[at_slot, part, rows], kept[at_slot, part, rows])
                for j in range(GROUP):
                    if 0 <= slot - j < TAPS:
                        term = value * weights[j][slot - j]
                        sums[j] = term if sums[j] is None else sums[j] + term
            for j in range(GROUP):
                band[j * FACTOR + at : j * FACTOR + at + strip, part * FACTOR : (part + 1) * FACTOR] = sums[j]
    first, second = (high1[...], low1[...]), (high2[...], low2[...])
    scale = 1.0 / (FACTOR * FACTOR)
    cos_table, sin_table = twist_cos[...] * scale, twist_sin[...] * scale
    for pair in range(GROUP // 2):
        bins = (2 * pair, 2 * pair + 1)
        passed = dot_split(split_bf16(band[2 * pair * FACTOR : (2 * pair + 2) * FACTOR, :]), first)
        columns = []
        for at in range(2):
            real = passed[at * FACTOR : (at + 1) * FACTOR, :FACTOR]
            imag = passed[at * FACTOR : (at + 1) * FACTOR, FACTOR:]
            turned_real = real * cos_table - imag * sin_table
            turned_imag = imag * cos_table + real * sin_table
            columns.append(jnp.concatenate([turned_real, turned_imag], axis=0))
        passed = dot_split(second, split_bf16(jnp.concatenate(columns, axis=1)))
        for at, bin_num in enumerate(bins):
            for part in range(2):
                lines[(part * GROUP + bin_num) * FACTOR : (part * GROUP + bin_num + 1) * FACTOR, :] = passed[
                    part * FACTOR : (part + 1) * FACTOR, at * FACTOR : (at + 1) * FACTOR
                ]
    index = lax.rem(place, places // 2) * 2 + side
    for step, message in enumerate(messages):
        chip = index ^ step
        for line in range(2 * GROUP):
            at = pl.multiple_of(line * FACTOR + chip * part_rows, 8)
            message[line * part_rows : (line + 1) * part_rows, :] = lines[pl.ds(at, part_rows), :]


def place_kernel(*refs):
    messages, (out_re, out_im, re_all, im_all) = refs[:-4], refs[-4:]
    bins, samples = out_re.shape
    part_rows = samples // FACTOR
    body = GROUP * part_rows
    place = lax.axis_index("az")
    for step, message in enumerate(messages):
        at = pl.multiple_of((place ^ step) * body, 8)
        re_all[pl.ds(at, body), :] = message[:body, :]
        im_all[pl.ds(at, body), :] = message[body:, :]
    for out, all_ref in ((out_re, re_all), (out_im, im_all)):
        for tile in range(0, bins, 8):
            for row in range(part_rows):
                out[tile : tile + 8, row * FACTOR : (row + 1) * FACTOR] = all_ref[
                    pl.ds(tile * part_rows + row, 8, stride=part_rows), :
                ]


VMEM = pl.BlockSpec(memory_space=pltpu.VMEM)
SMEM = pl.BlockSpec(memory_space=pltpu.SMEM)
KERNEL = pltpu.CompilerParams(vmem_limit_bytes=32 * 1024 * 1024)


def cost(flops, count):
    return pl.CostEstimate(flops=flops, bytes_accessed=count, transcendentals=0)


def transposed_shards(raw_re, raw_im, ref_blocks, owners, offsets, taps):
    bins, samples = raw_re.shape
    places = lax.axis_size("az")
    f32 = jnp.float32
    tables = dft_constants()
    matrices = [jnp.asarray(part) for pair in tables[:2] for part in pair]
    twists = [jnp.asarray(part) for part in tables[2]]
    ref_own = ref_blocks[0]
    swap = functools.partial(lax.ppermute, axis_name="rg", perm=[(0, 1), (1, 0)])
    offsets_other = swap(offsets)
    ref_other, re_other, im_other, taps_other = swap(ref_own), swap(raw_re), swap(raw_im), swap(taps)

    part_rows = samples // FACTOR
    message = jax.ShapeDtypeStruct((2, 2 * GROUP * part_rows + 8, FACTOR), f32)
    messages = pl.pallas_call(
        pack_kernel,
        out_shape=[message] * places,
        in_specs=[VMEM] * 6 + [SMEM] * 2,
        out_specs=[VMEM] * places,
        scratch_shapes=[
            pltpu.VMEM(((2 * bins + 2 * EDGE) * part_rows, FACTOR), f32),
            pltpu.VMEM(((2 * bins + 2 * EDGE) * part_rows, FACTOR), f32),
            pltpu.VMEM((2 * bins + 2 * EDGE, FACTOR), f32),
        ],
        compiler_params=KERNEL,
        cost_estimate=cost(10**6, 4 * 10**6),
        name="pack",
    )(raw_re, raw_im, re_other, im_other, ref_own, ref_other, offsets, offsets_other)
    chunks = [messages[0]] + [
        lax.ppermute(messages[step], "az", [(i, i ^ step) for i in range(places)]) for step in range(1, places)
    ]

    phases = pl.pallas_call(
        functools.partial(phase_kernel, 2 * bins),
        out_shape=jax.ShapeDtypeStruct((2, GROUP, 2, FACTOR, FACTOR), f32),
        in_specs=[SMEM] * 2,
        out_specs=VMEM,
        compiler_params=KERNEL,
        cost_estimate=cost(10**7, 10**6),
        name="phase",
    )(offsets, offsets_other)

    def spectrum(group):
        return pl.pallas_call(
            functools.partial(spectrum_body, places),
            out_shape=jax.ShapeDtypeStruct((GROUP, 2, FACTOR, FACTOR), f32),
            grid=(1,),
            in_specs=[pl.BlockSpec((1,) + message.shape[1:], lambda i: (group, 0, 0))] * places
            + [SMEM, pl.BlockSpec((1, GROUP, 2, FACTOR, FACTOR), lambda i: (group, 0, 0, 0, 0))]
            + [VMEM] * 6,
            out_specs=VMEM,
            scratch_shapes=[
                pltpu.VMEM((2 * GROUP * FACTOR, FACTOR), f32),
                pltpu.VMEM((places, 2 * GROUP, FACTOR), f32),
            ],
            compiler_params=KERNEL,
            cost_estimate=cost(4 * 10**8, 2 * 10**6),
            name="spectrum",
        )(*chunks, owners, phases, *matrices, *twists)

    shared = spectrum(0)
    received = swap(shared)
    kept = spectrum(1)

    pieces = pl.pallas_call(
        functools.partial(image_kernel, places),
        out_shape=[jax.ShapeDtypeStruct((2 * GROUP * part_rows, FACTOR), f32)] * places,
        in_specs=[VMEM] * 3 + [SMEM] * 2 + [VMEM] * 6,
        out_specs=[VMEM] * places,
        scratch_shapes=[
            pltpu.VMEM((GROUP * FACTOR, 2 * FACTOR), f32),
            pltpu.VMEM((2 * GROUP * FACTOR, FACTOR), f32),
        ],
        compiler_params=KERNEL,
        cost_estimate=cost(4 * 10**8, 2 * 10**6),
        name="image",
    )(shared, kept, received, taps, taps_other, *matrices, *twists)

    half = places // 2
    routes = []
    for step in range(places):
        routes.append(
            [
                (p * 2 + core, (((p % half) * 2 + core) ^ step) * 2 + p // half)
                for p in range(places)
                for core in range(2)
            ]
        )
    pieces = [lax.ppermute(piece, ("az", "rg"), route) for piece, route in zip(pieces, routes)]
    return pl.pallas_call(
        place_kernel,
        out_shape=[jax.ShapeDtypeStruct((bins, samples), f32)] * 2,
        in_specs=[VMEM] * places,
        out_specs=[VMEM] * 2,
        scratch_shapes=[pltpu.VMEM((bins * part_rows, FACTOR), f32)] * 2,
        compiler_params=KERNEL,
        cost_estimate=cost(0, 10**6),
        name="place",
    )(*pieces)


def solution(mesh):
    sizes = mesh.shape

    def whole(raw_re, raw_im, ref_blocks, owners, offsets, taps):
        line = raw_re.shape[1] // sizes["scene"]
        fits = (
            sizes["rg"] == 2
            and raw_re.shape[0] == 2 * GROUP * sizes["az"]
            and line == FACTOR * FACTOR
            and line // sizes["az"] % (8 * FACTOR) == 0
            and ref_blocks.shape[1] <= FACTOR
            and FACTOR % ref_blocks.shape[1] == 0
        )
        return jax.shard_map(
            transposed_shards if fits else butterfly_shards,
            mesh=mesh,
            in_specs=(
                P("rg", ("scene", "az")),
                P("rg", ("scene", "az")),
                P(("scene", "az"), None, "rg"),
                P("scene"),
                P("rg"),
                P("rg", None),
            ),
            out_specs=(P("rg", ("scene", "az")), P("rg", ("scene", "az"))),
            check_vma=False,
        )(raw_re, raw_im, ref_blocks, owners, offsets, taps)

    return whole
```

```python
import functools
import math

import jax
import jax.numpy as jnp
import numpy as np
from jax import lax
from jax.experimental import pallas as pl
from jax.experimental.pallas import tpu as pltpu
from jax.sharding import PartitionSpec as P

SPLIT = 4
TAPS = 8
REACH = 8
BLOCK = 16


PRECISE = lax.Precision.HIGHEST
PHASE_GAIN = 50.0


def partner_2(value, axis, stride):
    return lax.ppermute(value, axis, [(i, i ^ 1 << stride) for i in range(lax.axis_size(axis))])


def from_root(block, axis, source):
    block = jnp.where(lax.axis_index(axis) == source, block, jnp.zeros_like(block))
    return lax.psum(block, axis)


def padded_2(value, sides, width):
    for axis, dim in sides:
        size, length = (lax.axis_size(axis), value.shape[dim])
        up = [(i, (i + 1) % size) for i in range(size - 1)]
        down = [(j, i) for i, j in up]
        last = lax.slice_in_dim(value, length - width, length, axis=dim)
        initial = lax.slice_in_dim(value, 0, width, axis=dim)
        before = lax.ppermute(last, axis, up)
        after = lax.ppermute(initial, axis, down)
        value = jnp.concatenate([before, value, after], axis=dim)
    return value


def angles(numerator, denominator, sign_value):
    return sign_value * 2.0 * math.pi * numerator.astype(jnp.float32) / denominator


def rotate(signal, cosine, sine_part):
    real_part = signal[0] * cosine - signal[1] * sine_part
    imag_part = signal[0] * sine_part + signal[1] * cosine
    return jnp.stack([real_part, imag_part])


def dft_table(length_n, sign_value):
    counter = jnp.arange(length_n, dtype=jnp.int32)
    turn_count = counter[:, None] * counter[None, :] % length_n
    angle_set = angles(turn_count, length_n, sign_value)
    return (jnp.cos(angle_set), jnp.sin(angle_set))


def complex_apply(einsum_form, cosine, sine_part, signal):
    real_part = jnp.einsum(einsum_form, cosine, signal[0], precision=PRECISE) - jnp.einsum(
        einsum_form, sine_part, signal[1], precision=PRECISE
    )
    imag_part = jnp.einsum(einsum_form, cosine, signal[1], precision=PRECISE) + jnp.einsum(
        einsum_form, sine_part, signal[0], precision=PRECISE
    )
    return jnp.stack([real_part, imag_part])


def local_dft(signal, sign_value):
    rg_cols = signal.shape[1]
    az_rows = signal.shape[2]
    inner_len = az_rows // SPLIT
    shaped = signal.reshape(2, rg_cols, SPLIT, inner_len)
    first_cos, first_sin = dft_table(SPLIT, sign_value)
    first_pass = complex_apply("aj,cjk->cak", first_cos, first_sin, shaped)
    outer_idx = jnp.arange(SPLIT, dtype=jnp.int32)
    inner_idx = jnp.arange(inner_len, dtype=jnp.int32)
    twist = angles(outer_idx[:, None] * inner_idx[None, :] % az_rows, az_rows, sign_value)
    first_pass = rotate(first_pass, jnp.cos(twist)[None, :, :], jnp.sin(twist)[None, :, :])
    second_cos, second_sin = dft_table(inner_len, sign_value)
    second_pass = complex_apply("bk,cak->cba", second_cos, second_sin, first_pass)
    return second_pass.reshape(2, rg_cols, az_rows)


def butterfly_down(signal, az_place, bit_count):
    for bit_num in reversed(range(bit_count)):
        half_span = 1 << bit_num
        partner = partner_2(signal, "az", bit_num)
        is_upper = az_place >> bit_num & 1 == 1
        angle_set = angles(az_place % half_span, 2 * half_span, -1.0)
        difference = rotate(partner - signal, jnp.cos(angle_set), jnp.sin(angle_set))
        signal = jnp.where(is_upper, difference, signal + partner)
    return signal


def butterfly_up(signal, az_place, bit_count):
    for bit_num in range(bit_count):
        half_span = 1 << bit_num
        partner = partner_2(signal, "az", bit_num)
        is_upper = az_place >> bit_num & 1 == 1
        angle_set = angles(az_place % half_span, 2 * half_span, 1.0)
        cosine = jnp.cos(angle_set)
        sine_part = jnp.sin(angle_set)
        lower_new = (signal + rotate(partner, cosine, sine_part)) * 0.5
        upper_new = (partner - rotate(signal, cosine, sine_part)) * 0.5
        signal = jnp.where(is_upper, upper_new, lower_new)
    return signal


def butterfly_shards(raw_re, raw_im, ref_blocks, owners, offsets, taps):
    rg_cols = raw_re.shape[0]
    az_rows = raw_re.shape[1]
    az_count = lax.axis_size("az")
    az_place = lax.axis_index("az")
    bit_count = az_count.bit_length() - 1
    az_total = az_rows * az_count
    rg_total = rg_cols * lax.axis_size("rg")
    own_block = ref_blocks[0]
    lower_ref = from_root(own_block, "az", owners[0])
    upper_ref = from_root(own_block, "az", owners[1])
    signal = jnp.stack([raw_re, raw_im])
    signal = butterfly_down(signal, az_place, bit_count)
    column = jnp.zeros((), jnp.int32)
    for bit_num in range(bit_count):
        column = column + ((az_place >> bit_num & 1) << bit_count - 1 - bit_num)
    row_index = jnp.arange(az_rows, dtype=jnp.int32)
    twist = angles(row_index * column % az_total, az_total, -1.0)
    signal = rotate(signal, jnp.cos(twist)[None, :], jnp.sin(twist)[None, :])
    signal = local_dft(signal, -1.0)
    frequency = column + az_count * row_index
    signed = (frequency + az_total // 2) % az_total - az_total // 2
    az_freq = signed.astype(jnp.float32) / az_total
    rg_index = lax.axis_index("rg") * rg_cols + jnp.arange(rg_cols, dtype=jnp.int32)
    rg_freq = (rg_index.astype(jnp.float32) + 0.5) / (2 * rg_total) - 0.25
    model_phase = PHASE_GAIN * jnp.sqrt((1.0 + rg_freq)[:, None] ** 2 - az_freq[None, :] ** 2)
    ref_rows = own_block.shape[0]
    coarse = frequency * ref_rows // az_total
    slot_index = jnp.where(signed >= 0, ref_rows + coarse, coarse)
    one_hot = (jnp.arange(2 * ref_rows, dtype=jnp.int32)[:, None] == slot_index[None, :]).astype(
        jnp.float32
    )
    both_refs = jnp.concatenate([lower_ref, upper_ref], axis=0)
    picked = jnp.dot(both_refs.T, one_hot, precision=PRECISE)
    phase_all = model_phase + picked
    signal = rotate(signal, jnp.cos(phase_all), jnp.sin(phase_all))
    rim_width = REACH + TAPS // 2
    padded = padded_2(signal, (("rg", 1),), rim_width)
    offset_cols = jnp.repeat(offsets, BLOCK)
    local_cols = jnp.arange(rg_cols, dtype=jnp.int32)
    tap_index = jnp.arange(TAPS, dtype=jnp.int32)
    target = local_cols[:, None] + rim_width + offset_cols[:, None] + tap_index[None, :] - TAPS // 2
    padded_index = jnp.arange(rg_cols + 2 * rim_width, dtype=jnp.int32)
    hits = (padded_index[:, None, None] == target[None, :, :]).astype(jnp.float32)
    band_matrix = jnp.sum(hits * taps[None, :, :], axis=2)
    signal = jnp.einsum("zma,mi->zia", padded, band_matrix, precision=PRECISE)
    signal = local_dft(signal, 1.0) / az_rows
    twist_back = angles(row_index * column % az_total, az_total, 1.0)
    signal = rotate(signal, jnp.cos(twist_back)[None, :], jnp.sin(twist_back)[None, :])
    signal = butterfly_up(signal, az_place, bit_count)
    return (signal[0], signal[1])


FACTOR = 128
GROUP = 4
WINDOW = 4 * GROUP
EDGE = 16


def split_bf16(value):
    high = value.astype(jnp.bfloat16)
    low = (value - high.astype(jnp.float32)).astype(jnp.bfloat16)
    return high, low


def dot_split(left, right):
    left_high, left_low = left
    right_high, right_low = right
    dot = functools.partial(jnp.dot, preferred_element_type=jnp.float32)
    return dot(left_high, right_high) + (dot(left_high, right_low) + dot(left_low, right_high))


def dft_constants():
    counter = np.arange(FACTOR)
    turns = np.outer(counter, counter)
    angle = 2 * np.pi * (turns % FACTOR) / FACTOR
    cosine, sine = np.cos(angle), np.sin(angle)
    pair = []
    for matrix in (np.block([[cosine, sine], [-sine, cosine]]), np.block([[cosine, -sine], [sine, cosine]])):
        high = matrix.astype(jnp.bfloat16)
        low = (matrix - high.astype(np.float64)).astype(jnp.bfloat16)
        pair.append((high, low))
    twist = 2 * np.pi * turns / FACTOR**2
    return pair[0], pair[1], (np.cos(twist).astype(np.float32), np.sin(twist).astype(np.float32))


def cos_sin_quarters(quarters):
    whole = jnp.floor(quarters + 0.5)
    rest = (quarters - whole) * (math.pi / 2)
    square = rest * rest
    sine = rest + rest * square * (
        -1.6666654611e-1 + square * (8.3321608736e-3 + square * (-1.9515295891e-4))
    )
    cosine = 1.0 - 0.5 * square + square * square * (
        4.166664568298827e-2 + square * (-1.388731625493765e-3 + square * 2.443315711809948e-5)
    )
    number = whole.astype(jnp.int32)
    odd = (number & 1) == 1
    turned_cos = jnp.where(odd, sine, cosine)
    turned_sin = jnp.where(odd, cosine, sine)
    cos_sign = jnp.where(((number + 1) & 2) == 2, -1.0, 1.0)
    sin_sign = jnp.where((number & 2) == 2, -1.0, 1.0)
    return turned_cos * cos_sign, turned_sin * sin_sign


def window_start(chip, side, offsets_own, offsets_other):
    block = chip * 2 * GROUP // BLOCK
    blocks = offsets_own.shape[0]
    local = lax.rem(block, blocks)
    shift = jnp.where(lax.div(block, blocks) == side, offsets_own[local], offsets_other[local])
    return chip * 2 * GROUP + shift - TAPS // 2


def group_starts(side):
    return GROUP + GROUP * side, 3 * GROUP * side


def pack_kernel(re_own, im_own, re_other, im_other, ref_own, ref_other, off_own, off_other, *refs):
    messages, re_all, im_all, ref_all = refs
    bins, samples = re_own.shape
    part_rows = samples // FACTOR
    side = lax.axis_index("rg")
    own_at, other_at = EDGE + side * bins, EDGE + (1 - side) * bins
    zeros = jnp.zeros((EDGE * part_rows, FACTOR), jnp.float32)
    for all_ref, own, other in ((re_all, re_own, re_other), (im_all, im_own, im_other)):
        all_ref[: EDGE * part_rows, :] = zeros
        all_ref[(EDGE + 2 * bins) * part_rows :, :] = zeros
        for base, ref in ((own_at, own), (other_at, other)):
            for tile in range(0, bins, 8):
                for row in range(part_rows):
                    all_ref[pl.ds((base + tile) * part_rows + row, 8, stride=part_rows), :] = ref[
                        tile : tile + 8, row * FACTOR : (row + 1) * FACTOR
                    ]
    ref_rows = ref_own.shape[0]
    row = lax.broadcasted_iota(jnp.int32, (ref_rows, FACTOR), 0)
    column = lax.broadcasted_iota(jnp.int32, (ref_rows, FACTOR), 1)
    spread = (column * ref_rows // FACTOR == row).astype(jnp.float32)
    ref_all[:EDGE, :] = jnp.zeros((EDGE, FACTOR), jnp.float32)
    ref_all[EDGE + 2 * bins :, :] = jnp.zeros((EDGE, FACTOR), jnp.float32)
    for at, ref in ((own_at, ref_own), (other_at, ref_other)):
        ref_all[pl.ds(pl.multiple_of(at, 16), bins), :] = lax.dot_general(
            ref[...], spread, (((0,), (0,)), ((), ())), precision=PRECISE, preferred_element_type=jnp.float32
        )
    body = GROUP * part_rows
    for chip in range(messages.shape[0]):
        message = messages.at[chip]
        start = window_start(chip, side, off_own, off_other) + EDGE
        for group, group_at in enumerate(group_starts(side)):
            rows = pl.ds(pl.multiple_of((start + group_at) * part_rows, 8), body)
            message[group, :body, :] = re_all[rows, :]
            message[group, body : 2 * body, :] = im_all[rows, :]
            for bin_num in range(GROUP):
                message[group, 2 * body + bin_num, :] = ref_all[start + group_at + bin_num, :]
            message[group, 2 * body + GROUP :, :] = jnp.zeros((8 - GROUP, FACTOR), jnp.float32)


def phase_kernel(bins_total, off_own, off_other, out):
    place, side = lax.axis_index("az"), lax.axis_index("rg")
    start = window_start(place, side, off_own, off_other)
    shape = (FACTOR, FACTOR)
    frequency = lax.broadcasted_iota(jnp.int32, shape, 0) + FACTOR * lax.broadcasted_iota(jnp.int32, shape, 1)
    total = FACTOR * FACTOR
    signed = jnp.where(frequency >= total // 2, frequency - total, frequency)
    az_freq = signed.astype(jnp.float32) / total
    az_square = az_freq * az_freq
    for group, group_at in enumerate(group_starts(side)):
        for bin_num in range(GROUP):
            rg_index = (start + group_at + bin_num).astype(jnp.float32)
            rg_freq = (rg_index + 0.5) / (2 * bins_total) - 0.25
            base = (1.0 + rg_freq) * (1.0 + rg_freq)
            root = jnp.sqrt(base - az_square)
            cosine, sine = cos_sin_quarters(root * (PHASE_GAIN * 2 / math.pi))
            out[group, bin_num, 0] = cosine
            out[group, bin_num, 1] = sine


def spectrum_body(places, *refs):
    chunks, owners, phase, high1, low1, high2, low2, twist_cos, twist_sin, out, lines, picks = refs
    samples = FACTOR * FACTOR // places
    part_rows = samples // FACTOR
    for source in range(places):
        chunk = chunks.at[source]
        for line in range(2 * GROUP):
            at = pl.multiple_of(line * FACTOR + source * part_rows, 8)
            lines[pl.ds(at, part_rows), :] = chunk[0, line * part_rows : (line + 1) * part_rows, :]
        picks[source] = chunk[0, 2 * GROUP * part_rows :, :]
    lane = lax.broadcasted_iota(jnp.int32, (2 * GROUP, FACTOR), 1)
    ref_phase = jnp.where(lane < FACTOR // 2, picks[owners[1]], picks[owners[0]])
    ref_cos, ref_sin = cos_sin_quarters(ref_phase * (2 / math.pi))
    first, second = (high1[...], low1[...]), (high2[...], low2[...])
    for pair in range(GROUP // 2):
        bins = (2 * pair, 2 * pair + 1)
        columns = []
        for bin_num in bins:
            real = lines[bin_num * FACTOR : (bin_num + 1) * FACTOR, :]
            imag = lines[(GROUP + bin_num) * FACTOR : (GROUP + bin_num + 1) * FACTOR, :]
            columns.append(jnp.concatenate([real, imag], axis=0))
        passed = dot_split(first, split_bf16(jnp.concatenate(columns, axis=1)))
        rows = []
        for at in range(2):
            real = passed[:FACTOR, at * FACTOR : (at + 1) * FACTOR]
            imag = passed[FACTOR:, at * FACTOR : (at + 1) * FACTOR]
            turned_real = real * twist_cos[...] + imag * twist_sin[...]
            turned_imag = imag * twist_cos[...] - real * twist_sin[...]
            rows.append(jnp.concatenate([turned_real, turned_imag], axis=1))
        passed = dot_split(split_bf16(jnp.concatenate(rows, axis=0)), second)
        for at, bin_num in enumerate(bins):
            real = passed[at * FACTOR : (at + 1) * FACTOR, :FACTOR]
            imag = passed[at * FACTOR : (at + 1) * FACTOR, FACTOR:]
            model_cos, model_sin = phase[0, bin_num, 0], phase[0, bin_num, 1]
            row_cos, row_sin = ref_cos[bin_num : bin_num + 1, :], ref_sin[bin_num : bin_num + 1, :]
            cosine = model_cos * row_cos - model_sin * row_sin
            sine = model_sin * row_cos + model_cos * row_sin
            out[bin_num, 0] = real * cosine - imag * sine
            out[bin_num, 1] = real * sine + imag * cosine


def image_kernel(places, *refs):
    shared, kept, received, taps_own, taps_other, high1, low1, high2, low2, twist_cos, twist_sin = refs[:11]
    messages, band, lines = refs[11:]
    place, side = lax.axis_index("az"), lax.axis_index("rg")
    samples = FACTOR * FACTOR // places
    part_rows = samples // FACTOR
    bins_held = taps_own.shape[0]
    first_bin = place * 2 * GROUP + side * GROUP
    held = lax.div(first_bin, bins_held) == side
    local = lax.rem(first_bin, bins_held)
    weights = [
        [jnp.where(held, taps_own[local + j, t], taps_other[local + j, t]) for t in range(TAPS)] for j in range(GROUP)
    ]
    is_first = side == 0
    strip = 16
    for part in range(2):
        for at in range(0, FACTOR, strip):
            rows = slice(at, at + strip)
            sums = [None] * GROUP
            for slot in range(3 * GROUP):
                if slot < GROUP:
                    value = jnp.where(is_first, kept[slot, part, rows], received[slot, part, rows])
                elif slot < 2 * GROUP:
                    value = shared[slot - GROUP, part, rows]
                else:
                    at_slot = slot - 2 * GROUP
                    value = jnp.where(is_first, received[at_slot, part, rows], kept[at_slot, part, rows])
                for j in range(GROUP):
                    if 0 <= slot - j < TAPS:
                        term = value * weights[j][slot - j]
                        sums[j] = term if sums[j] is None else sums[j] + term
            for j in range(GROUP):
                band[j * FACTOR + at : j * FACTOR + at + strip, part * FACTOR : (part + 1) * FACTOR] = sums[j]
    first, second = (high1[...], low1[...]), (high2[...], low2[...])
    scale = 1.0 / (FACTOR * FACTOR)
    cos_table, sin_table = twist_cos[...] * scale, twist_sin[...] * scale
    for pair in range(GROUP // 2):
        bins = (2 * pair, 2 * pair + 1)
        passed = dot_split(split_bf16(band[2 * pair * FACTOR : (2 * pair + 2) * FACTOR, :]), first)
        columns = []
        for at in range(2):
            real = passed[at * FACTOR : (at + 1) * FACTOR, :FACTOR]
            imag = passed[at * FACTOR : (at + 1) * FACTOR, FACTOR:]
            turned_real = real * cos_table - imag * sin_table
            turned_imag = imag * cos_table + real * sin_table
            columns.append(jnp.concatenate([turned_real, turned_imag], axis=0))
        passed = dot_split(second, split_bf16(jnp.concatenate(columns, axis=1)))
        for at, bin_num in enumerate(bins):
            for part in range(2):
                lines[(part * GROUP + bin_num) * FACTOR : (part * GROUP + bin_num + 1) * FACTOR, :] = passed[
                    part * FACTOR : (part + 1) * FACTOR, at * FACTOR : (at + 1) * FACTOR
                ]
    for chip in range(places):
        message = messages.at[chip]
        for line in range(2 * GROUP):
            at = line * FACTOR + chip * part_rows
            message[line * part_rows : (line + 1) * part_rows, :] = lines[pl.ds(at, part_rows), :]


def place_kernel(own, other, out_re, out_im, re_all, im_all):
    bins, samples = out_re.shape
    part_rows = samples // FACTOR
    body = GROUP * part_rows
    half = own.shape[0] // 2
    side = lax.axis_index("rg")
    for step in range(half):
        for ref, core in ((own, side), (other, 1 - side)):
            at = pl.multiple_of((2 * step + core) * body, 8)
            re_all[pl.ds(at, body), :] = ref[side * half + step, :body, :]
            im_all[pl.ds(at, body), :] = ref[side * half + step, body:, :]
    for out, all_ref in ((out_re, re_all), (out_im, im_all)):
        for tile in range(0, bins, 8):
            for row in range(part_rows):
                out[tile : tile + 8, row * FACTOR : (row + 1) * FACTOR] = all_ref[
                    pl.ds(tile * part_rows + row, 8, stride=part_rows), :
                ]


VMEM = pl.BlockSpec(memory_space=pltpu.VMEM)
SMEM = pl.BlockSpec(memory_space=pltpu.SMEM)
KERNEL = pltpu.CompilerParams(vmem_limit_bytes=32 * 1024 * 1024)


def cost(flops, count):
    return pl.CostEstimate(flops=flops, bytes_accessed=count, transcendentals=0)


def transposed_shards(raw_re, raw_im, ref_blocks, owners, offsets, taps):
    bins, samples = raw_re.shape
    places = lax.axis_size("az")
    f32 = jnp.float32
    tables = dft_constants()
    matrices = [jnp.asarray(part) for pair in tables[:2] for part in pair]
    twists = [jnp.asarray(part) for part in tables[2]]
    ref_own = ref_blocks[0]
    swap = functools.partial(lax.ppermute, axis_name="rg", perm=[(0, 1), (1, 0)])
    offsets_other = swap(offsets)
    ref_other, re_other, im_other, taps_other = swap(ref_own), swap(raw_re), swap(raw_im), swap(taps)

    part_rows = samples // FACTOR
    message = jax.ShapeDtypeStruct((2, 2 * GROUP * part_rows + 8, FACTOR), f32)
    messages = pl.pallas_call(
        pack_kernel,
        out_shape=jax.ShapeDtypeStruct((places,) + message.shape, f32),
        in_specs=[VMEM] * 6 + [SMEM] * 2,
        out_specs=VMEM,
        scratch_shapes=[
            pltpu.VMEM(((2 * bins + 2 * EDGE) * part_rows, FACTOR), f32),
            pltpu.VMEM(((2 * bins + 2 * EDGE) * part_rows, FACTOR), f32),
            pltpu.VMEM((2 * bins + 2 * EDGE, FACTOR), f32),
        ],
        compiler_params=KERNEL,
        cost_estimate=cost(10**6, 4 * 10**6),
        name="pack",
    )(raw_re, raw_im, re_other, im_other, ref_own, ref_other, offsets, offsets_other)
    chunks = lax.all_to_all(messages, "az", 0, 0, tiled=True)

    phases = pl.pallas_call(
        functools.partial(phase_kernel, 2 * bins),
        out_shape=jax.ShapeDtypeStruct((2, GROUP, 2, FACTOR, FACTOR), f32),
        in_specs=[SMEM] * 2,
        out_specs=VMEM,
        compiler_params=KERNEL,
        cost_estimate=cost(10**7, 10**6),
        name="phase",
    )(offsets, offsets_other)

    def spectrum(group):
        return pl.pallas_call(
            functools.partial(spectrum_body, places),
            out_shape=jax.ShapeDtypeStruct((GROUP, 2, FACTOR, FACTOR), f32),
            grid=(1,),
            in_specs=[
                pl.BlockSpec((places, 1) + message.shape[1:], lambda i: (0, group, 0, 0)),
                SMEM,
                pl.BlockSpec((1, GROUP, 2, FACTOR, FACTOR), lambda i: (group, 0, 0, 0, 0)),
            ]
            + [VMEM] * 6,
            out_specs=VMEM,
            scratch_shapes=[
                pltpu.VMEM((2 * GROUP * FACTOR, FACTOR), f32),
                pltpu.VMEM((places, 2 * GROUP, FACTOR), f32),
            ],
            compiler_params=KERNEL,
            cost_estimate=cost(4 * 10**8, 2 * 10**6),
            name="spectrum",
        )(chunks, owners, phases, *matrices, *twists)

    shared = spectrum(0)
    received = swap(shared)
    kept = spectrum(1)

    pieces = pl.pallas_call(
        functools.partial(image_kernel, places),
        out_shape=jax.ShapeDtypeStruct((places, 2 * GROUP * part_rows, FACTOR), f32),
        in_specs=[VMEM] * 3 + [SMEM] * 2 + [VMEM] * 6,
        out_specs=VMEM,
        scratch_shapes=[
            pltpu.VMEM((GROUP * FACTOR, 2 * FACTOR), f32),
            pltpu.VMEM((2 * GROUP * FACTOR, FACTOR), f32),
        ],
        compiler_params=KERNEL,
        cost_estimate=cost(4 * 10**8, 2 * 10**6),
        name="image",
    )(shared, kept, received, taps, taps_other, *matrices, *twists)

    pieces = lax.all_to_all(pieces, "az", 0, 0, tiled=True)
    pieces_other = swap(pieces)
    return pl.pallas_call(
        place_kernel,
        out_shape=[jax.ShapeDtypeStruct((bins, samples), f32)] * 2,
        in_specs=[VMEM] * 2,
        out_specs=[VMEM] * 2,
        scratch_shapes=[pltpu.VMEM((bins * part_rows, FACTOR), f32)] * 2,
        compiler_params=KERNEL,
        cost_estimate=cost(0, 10**6),
        name="place",
    )(pieces, pieces_other)


def solution(mesh):
    sizes = mesh.shape

    def whole(raw_re, raw_im, ref_blocks, owners, offsets, taps):
        line = raw_re.shape[1] // sizes["scene"]
        fits = (
            sizes["rg"] == 2
            and raw_re.shape[0] == 2 * GROUP * sizes["az"]
            and line == FACTOR * FACTOR
            and line // sizes["az"] % (8 * FACTOR) == 0
            and ref_blocks.shape[1] <= FACTOR
            and FACTOR % ref_blocks.shape[1] == 0
        )
        return jax.shard_map(
            transposed_shards if fits else butterfly_shards,
            mesh=mesh,
            in_specs=(
                P("rg", ("scene", "az")),
                P("rg", ("scene", "az")),
                P(("scene", "az"), None, "rg"),
                P("scene"),
                P("rg"),
                P("rg", None),
            ),
            out_specs=(P("rg", ("scene", "az")), P("rg", ("scene", "az"))),
            check_vma=False,
        )(raw_re, raw_im, ref_blocks, owners, offsets, taps)

    return whole
```

```python
import functools
import math

import jax
import jax.numpy as jnp
import numpy as np
from jax import lax
from jax.experimental import pallas as pl
from jax.experimental.pallas import tpu as pltpu
from jax.sharding import PartitionSpec as P

SPLIT = 4
TAPS = 8
REACH = 8
BLOCK = 16


PRECISE = lax.Precision.HIGHEST
PHASE_GAIN = 50.0


def partner_2(value, axis, stride):
    return lax.ppermute(value, axis, [(i, i ^ 1 << stride) for i in range(lax.axis_size(axis))])


def from_root(block, axis, source):
    block = jnp.where(lax.axis_index(axis) == source, block, jnp.zeros_like(block))
    return lax.psum(block, axis)


def padded_2(value, sides, width):
    for axis, dim in sides:
        size, length = (lax.axis_size(axis), value.shape[dim])
        up = [(i, (i + 1) % size) for i in range(size - 1)]
        down = [(j, i) for i, j in up]
        last = lax.slice_in_dim(value, length - width, length, axis=dim)
        initial = lax.slice_in_dim(value, 0, width, axis=dim)
        before = lax.ppermute(last, axis, up)
        after = lax.ppermute(initial, axis, down)
        value = jnp.concatenate([before, value, after], axis=dim)
    return value


def angles(numerator, denominator, sign_value):
    return sign_value * 2.0 * math.pi * numerator.astype(jnp.float32) / denominator


def rotate(signal, cosine, sine_part):
    real_part = signal[0] * cosine - signal[1] * sine_part
    imag_part = signal[0] * sine_part + signal[1] * cosine
    return jnp.stack([real_part, imag_part])


def dft_table(length_n, sign_value):
    counter = jnp.arange(length_n, dtype=jnp.int32)
    turn_count = counter[:, None] * counter[None, :] % length_n
    angle_set = angles(turn_count, length_n, sign_value)
    return (jnp.cos(angle_set), jnp.sin(angle_set))


def complex_apply(einsum_form, cosine, sine_part, signal):
    real_part = jnp.einsum(einsum_form, cosine, signal[0], precision=PRECISE) - jnp.einsum(
        einsum_form, sine_part, signal[1], precision=PRECISE
    )
    imag_part = jnp.einsum(einsum_form, cosine, signal[1], precision=PRECISE) + jnp.einsum(
        einsum_form, sine_part, signal[0], precision=PRECISE
    )
    return jnp.stack([real_part, imag_part])


def local_dft(signal, sign_value):
    rg_cols = signal.shape[1]
    az_rows = signal.shape[2]
    inner_len = az_rows // SPLIT
    shaped = signal.reshape(2, rg_cols, SPLIT, inner_len)
    first_cos, first_sin = dft_table(SPLIT, sign_value)
    first_pass = complex_apply("aj,cjk->cak", first_cos, first_sin, shaped)
    outer_idx = jnp.arange(SPLIT, dtype=jnp.int32)
    inner_idx = jnp.arange(inner_len, dtype=jnp.int32)
    twist = angles(outer_idx[:, None] * inner_idx[None, :] % az_rows, az_rows, sign_value)
    first_pass = rotate(first_pass, jnp.cos(twist)[None, :, :], jnp.sin(twist)[None, :, :])
    second_cos, second_sin = dft_table(inner_len, sign_value)
    second_pass = complex_apply("bk,cak->cba", second_cos, second_sin, first_pass)
    return second_pass.reshape(2, rg_cols, az_rows)


def butterfly_down(signal, az_place, bit_count):
    for bit_num in reversed(range(bit_count)):
        half_span = 1 << bit_num
        partner = partner_2(signal, "az", bit_num)
        is_upper = az_place >> bit_num & 1 == 1
        angle_set = angles(az_place % half_span, 2 * half_span, -1.0)
        difference = rotate(partner - signal, jnp.cos(angle_set), jnp.sin(angle_set))
        signal = jnp.where(is_upper, difference, signal + partner)
    return signal


def butterfly_up(signal, az_place, bit_count):
    for bit_num in range(bit_count):
        half_span = 1 << bit_num
        partner = partner_2(signal, "az", bit_num)
        is_upper = az_place >> bit_num & 1 == 1
        angle_set = angles(az_place % half_span, 2 * half_span, 1.0)
        cosine = jnp.cos(angle_set)
        sine_part = jnp.sin(angle_set)
        lower_new = (signal + rotate(partner, cosine, sine_part)) * 0.5
        upper_new = (partner - rotate(signal, cosine, sine_part)) * 0.5
        signal = jnp.where(is_upper, upper_new, lower_new)
    return signal


def butterfly_shards(raw_re, raw_im, ref_blocks, owners, offsets, taps):
    rg_cols = raw_re.shape[0]
    az_rows = raw_re.shape[1]
    az_count = lax.axis_size("az")
    az_place = lax.axis_index("az")
    bit_count = az_count.bit_length() - 1
    az_total = az_rows * az_count
    rg_total = rg_cols * lax.axis_size("rg")
    own_block = ref_blocks[0]
    lower_ref = from_root(own_block, "az", owners[0])
    upper_ref = from_root(own_block, "az", owners[1])
    signal = jnp.stack([raw_re, raw_im])
    signal = butterfly_down(signal, az_place, bit_count)
    column = jnp.zeros((), jnp.int32)
    for bit_num in range(bit_count):
        column = column + ((az_place >> bit_num & 1) << bit_count - 1 - bit_num)
    row_index = jnp.arange(az_rows, dtype=jnp.int32)
    twist = angles(row_index * column % az_total, az_total, -1.0)
    signal = rotate(signal, jnp.cos(twist)[None, :], jnp.sin(twist)[None, :])
    signal = local_dft(signal, -1.0)
    frequency = column + az_count * row_index
    signed = (frequency + az_total // 2) % az_total - az_total // 2
    az_freq = signed.astype(jnp.float32) / az_total
    rg_index = lax.axis_index("rg") * rg_cols + jnp.arange(rg_cols, dtype=jnp.int32)
    rg_freq = (rg_index.astype(jnp.float32) + 0.5) / (2 * rg_total) - 0.25
    model_phase = PHASE_GAIN * jnp.sqrt((1.0 + rg_freq)[:, None] ** 2 - az_freq[None, :] ** 2)
    ref_rows = own_block.shape[0]
    coarse = frequency * ref_rows // az_total
    slot_index = jnp.where(signed >= 0, ref_rows + coarse, coarse)
    one_hot = (jnp.arange(2 * ref_rows, dtype=jnp.int32)[:, None] == slot_index[None, :]).astype(
        jnp.float32
    )
    both_refs = jnp.concatenate([lower_ref, upper_ref], axis=0)
    picked = jnp.dot(both_refs.T, one_hot, precision=PRECISE)
    phase_all = model_phase + picked
    signal = rotate(signal, jnp.cos(phase_all), jnp.sin(phase_all))
    rim_width = REACH + TAPS // 2
    padded = padded_2(signal, (("rg", 1),), rim_width)
    offset_cols = jnp.repeat(offsets, BLOCK)
    local_cols = jnp.arange(rg_cols, dtype=jnp.int32)
    tap_index = jnp.arange(TAPS, dtype=jnp.int32)
    target = local_cols[:, None] + rim_width + offset_cols[:, None] + tap_index[None, :] - TAPS // 2
    padded_index = jnp.arange(rg_cols + 2 * rim_width, dtype=jnp.int32)
    hits = (padded_index[:, None, None] == target[None, :, :]).astype(jnp.float32)
    band_matrix = jnp.sum(hits * taps[None, :, :], axis=2)
    signal = jnp.einsum("zma,mi->zia", padded, band_matrix, precision=PRECISE)
    signal = local_dft(signal, 1.0) / az_rows
    twist_back = angles(row_index * column % az_total, az_total, 1.0)
    signal = rotate(signal, jnp.cos(twist_back)[None, :], jnp.sin(twist_back)[None, :])
    signal = butterfly_up(signal, az_place, bit_count)
    return (signal[0], signal[1])


FACTOR = 128
GROUP = 4
WINDOW = 4 * GROUP
EDGE = 16


def split_bf16(value):
    high = value.astype(jnp.bfloat16)
    low = (value - high.astype(jnp.float32)).astype(jnp.bfloat16)
    return high, low


def dot_split(left, right):
    left_high, left_low = left
    right_high, right_low = right
    dot = functools.partial(jnp.dot, preferred_element_type=jnp.float32)
    return dot(left_high, right_high) + (dot(left_high, right_low) + dot(left_low, right_high))


def dft_constants():
    counter = np.arange(FACTOR)
    turns = np.outer(counter, counter)
    angle = 2 * np.pi * (turns % FACTOR) / FACTOR
    cosine, sine = np.cos(angle), np.sin(angle)
    pair = []
    for matrix in (np.block([[cosine, sine], [-sine, cosine]]), np.block([[cosine, -sine], [sine, cosine]])):
        high = matrix.astype(jnp.bfloat16)
        low = (matrix - high.astype(np.float64)).astype(jnp.bfloat16)
        pair.append((high, low))
    twist = 2 * np.pi * turns / FACTOR**2
    return pair[0], pair[1], (np.cos(twist).astype(np.float32), np.sin(twist).astype(np.float32))


def cos_sin_quarters(quarters):
    whole = jnp.floor(quarters + 0.5)
    rest = (quarters - whole) * (math.pi / 2)
    square = rest * rest
    sine = rest + rest * square * (
        -1.6666654611e-1 + square * (8.3321608736e-3 + square * (-1.9515295891e-4))
    )
    cosine = 1.0 - 0.5 * square + square * square * (
        4.166664568298827e-2 + square * (-1.388731625493765e-3 + square * 2.443315711809948e-5)
    )
    number = whole.astype(jnp.int32)
    odd = (number & 1) == 1
    turned_cos = jnp.where(odd, sine, cosine)
    turned_sin = jnp.where(odd, cosine, sine)
    cos_sign = jnp.where(((number + 1) & 2) == 2, -1.0, 1.0)
    sin_sign = jnp.where((number & 2) == 2, -1.0, 1.0)
    return turned_cos * cos_sign, turned_sin * sin_sign


def window_start(chip, side, offsets_own, offsets_other):
    block = chip * 2 * GROUP // BLOCK
    blocks = offsets_own.shape[0]
    local = lax.rem(block, blocks)
    shift = jnp.where(lax.div(block, blocks) == side, offsets_own[local], offsets_other[local])
    return chip * 2 * GROUP + shift - TAPS // 2


def group_starts(side):
    return GROUP + GROUP * side, 3 * GROUP * side


def spread_lines(target, base, source):
    bins, samples = source.shape
    part_rows = samples // FACTOR
    for tile in range(0, bins, 8):
        for row in range(part_rows):
            target[pl.ds((base + tile) * part_rows + row, 8, stride=part_rows), :] = source[
                tile : tile + 8, row * FACTOR : (row + 1) * FACTOR
            ]


def spread_kernel(re_own, im_own, re_lines, im_lines):
    spread_lines(re_lines, 0, re_own)
    spread_lines(im_lines, 0, im_own)


def pack_kernel(re_lines, im_lines, re_other, im_other, ref_own, ref_other, off_own, off_other, *refs):
    messages, (re_all, im_all, ref_all) = refs[:-3], refs[-3:]
    bins, samples = re_other.shape
    part_rows = samples // FACTOR
    place, side = lax.axis_index("az"), lax.axis_index("rg")
    own_at, other_at = EDGE + side * bins, EDGE + (1 - side) * bins
    zeros = jnp.zeros((EDGE * part_rows, FACTOR), jnp.float32)
    for all_ref, own, other in ((re_all, re_lines, re_other), (im_all, im_lines, im_other)):
        all_ref[: EDGE * part_rows, :] = zeros
        all_ref[(EDGE + 2 * bins) * part_rows :, :] = zeros
        all_ref[pl.ds(pl.multiple_of(own_at * part_rows, 8), bins * part_rows), :] = own[...]
        spread_lines(all_ref, other_at, other)
    ref_rows = ref_own.shape[0]
    row = lax.broadcasted_iota(jnp.int32, (ref_rows, FACTOR), 0)
    column = lax.broadcasted_iota(jnp.int32, (ref_rows, FACTOR), 1)
    spread = (column * ref_rows // FACTOR == row).astype(jnp.float32)
    ref_all[:EDGE, :] = jnp.zeros((EDGE, FACTOR), jnp.float32)
    ref_all[EDGE + 2 * bins :, :] = jnp.zeros((EDGE, FACTOR), jnp.float32)
    for at, ref in ((own_at, ref_own), (other_at, ref_other)):
        ref_all[pl.ds(pl.multiple_of(at, 16), bins), :] = lax.dot_general(
            ref[...], spread, (((0,), (0,)), ((), ())), precision=PRECISE, preferred_element_type=jnp.float32
        )
    body = GROUP * part_rows
    for step, message in enumerate(messages):
        chip = place ^ step
        start = window_start(chip, side, off_own, off_other) + EDGE
        for group, group_at in enumerate(group_starts(side)):
            rows = pl.ds(pl.multiple_of((start + group_at) * part_rows, 8), body)
            message[group, :body, :] = re_all[rows, :]
            message[group, body : 2 * body, :] = im_all[rows, :]
            for bin_num in range(GROUP):
                message[group, 2 * body + bin_num, :] = ref_all[start + group_at + bin_num, :]
            message[group, 2 * body + GROUP :, :] = jnp.zeros((8 - GROUP, FACTOR), jnp.float32)


def phase_kernel(bins_total, off_own, off_other, out):
    place, side = lax.axis_index("az"), lax.axis_index("rg")
    start = window_start(place, side, off_own, off_other)
    shape = (FACTOR, FACTOR)
    frequency = lax.broadcasted_iota(jnp.int32, shape, 0) + FACTOR * lax.broadcasted_iota(jnp.int32, shape, 1)
    total = FACTOR * FACTOR
    signed = jnp.where(frequency >= total // 2, frequency - total, frequency)
    az_freq = signed.astype(jnp.float32) / total
    az_square = az_freq * az_freq
    for group, group_at in enumerate(group_starts(side)):
        for bin_num in range(GROUP):
            rg_index = (start + group_at + bin_num).astype(jnp.float32)
            rg_freq = (rg_index + 0.5) / (2 * bins_total) - 0.25
            base = (1.0 + rg_freq) * (1.0 + rg_freq)
            root = jnp.sqrt(base - az_square)
            cosine, sine = cos_sin_quarters(root * (PHASE_GAIN * 2 / math.pi))
            out[group, bin_num, 0] = cosine
            out[group, bin_num, 1] = sine


def spectrum_body(steps, group, *refs):
    places = len(steps)
    chunks, refs = refs[:places], refs[places:]
    owners, phase, high1, low1, high2, low2, twist_cos, twist_sin, out, lines, picks = refs
    place = lax.axis_index("az")
    samples = FACTOR * FACTOR // places
    part_rows = samples // FACTOR
    for step, chunk in zip(steps, chunks):
        source = place ^ step
        for line in range(2 * GROUP):
            at = pl.multiple_of(line * FACTOR + source * part_rows, 8)
            lines[pl.ds(at, part_rows), :] = chunk[group, line * part_rows : (line + 1) * part_rows, :]
        picks[source] = chunk[group, 2 * GROUP * part_rows :, :]
    lane = lax.broadcasted_iota(jnp.int32, (2 * GROUP, FACTOR), 1)
    ref_phase = jnp.where(lane < FACTOR // 2, picks[owners[1]], picks[owners[0]])
    ref_cos, ref_sin = cos_sin_quarters(ref_phase * (2 / math.pi))
    first, second = (high1[...], low1[...]), (high2[...], low2[...])
    for pair in range(GROUP // 2):
        bins = (2 * pair, 2 * pair + 1)
        columns = []
        for bin_num in bins:
            real = lines[bin_num * FACTOR : (bin_num + 1) * FACTOR, :]
            imag = lines[(GROUP + bin_num) * FACTOR : (GROUP + bin_num + 1) * FACTOR, :]
            columns.append(jnp.concatenate([real, imag], axis=0))
        passed = dot_split(first, split_bf16(jnp.concatenate(columns, axis=1)))
        rows = []
        for at in range(2):
            real = passed[:FACTOR, at * FACTOR : (at + 1) * FACTOR]
            imag = passed[FACTOR:, at * FACTOR : (at + 1) * FACTOR]
            turned_real = real * twist_cos[...] + imag * twist_sin[...]
            turned_imag = imag * twist_cos[...] - real * twist_sin[...]
            rows.append(jnp.concatenate([turned_real, turned_imag], axis=1))
        passed = dot_split(split_bf16(jnp.concatenate(rows, axis=0)), second)
        for at, bin_num in enumerate(bins):
            real = passed[at * FACTOR : (at + 1) * FACTOR, :FACTOR]
            imag = passed[at * FACTOR : (at + 1) * FACTOR, FACTOR:]
            model_cos, model_sin = phase[group, bin_num, 0], phase[group, bin_num, 1]
            row_cos, row_sin = ref_cos[bin_num : bin_num + 1, :], ref_sin[bin_num : bin_num + 1, :]
            cosine = model_cos * row_cos - model_sin * row_sin
            sine = model_sin * row_cos + model_cos * row_sin
            out[bin_num, 0] = real * cosine - imag * sine
            out[bin_num, 1] = real * sine + imag * cosine


def image_kernel(places, *refs):
    shared, kept, received, taps_own, taps_other, high1, low1, high2, low2, twist_cos, twist_sin = refs[:11]
    messages, (band, lines) = refs[11:-2], refs[-2:]
    place, side = lax.axis_index("az"), lax.axis_index("rg")
    samples = FACTOR * FACTOR // places
    part_rows = samples // FACTOR
    bins_held = taps_own.shape[0]
    first_bin = place * 2 * GROUP + side * GROUP
    held = lax.div(first_bin, bins_held) == side
    local = lax.rem(first_bin, bins_held)
    weights = [
        [jnp.where(held, taps_own[local + j, t], taps_other[local + j, t]) for t in range(TAPS)] for j in range(GROUP)
    ]
    is_first = side == 0
    strip = 16
    for part in range(2):
        for at in range(0, FACTOR, strip):
            rows = slice(at, at + strip)
            sums = [None] * GROUP
            for slot in range(3 * GROUP):
                if slot < GROUP:
                    value = jnp.where(is_first, kept[slot, part, rows], received[slot, part, rows])
                elif slot < 2 * GROUP:
                    value = shared[slot - GROUP, part, rows]
                else:
                    at_slot = slot - 2 * GROUP
                    value = jnp.where(is_first, received[at_slot, part, rows], kept[at_slot, part, rows])
                for j in range(GROUP):
                    if 0 <= slot - j < TAPS:
                        term = value * weights[j][slot - j]
                        sums[j] = term if sums[j] is None else sums[j] + term
            for j in range(GROUP):
                band[j * FACTOR + at : j * FACTOR + at + strip, part * FACTOR : (part + 1) * FACTOR] = sums[j]
    first, second = (high1[...], low1[...]), (high2[...], low2[...])
    scale = 1.0 / (FACTOR * FACTOR)
    cos_table, sin_table = twist_cos[...] * scale, twist_sin[...] * scale
    for pair in range(GROUP // 2):
        bins = (2 * pair, 2 * pair + 1)
        passed = dot_split(split_bf16(band[2 * pair * FACTOR : (2 * pair + 2) * FACTOR, :]), first)
        columns = []
        for at in range(2):
            real = passed[at * FACTOR : (at + 1) * FACTOR, :FACTOR]
            imag = passed[at * FACTOR : (at + 1) * FACTOR, FACTOR:]
            turned_real = real * cos_table - imag * sin_table
            turned_imag = imag * cos_table + real * sin_table
            columns.append(jnp.concatenate([turned_real, turned_imag], axis=0))
        passed = dot_split(second, split_bf16(jnp.concatenate(columns, axis=1)))
        for at, bin_num in enumerate(bins):
            for part in range(2):
                lines[(part * GROUP + bin_num) * FACTOR : (part * GROUP + bin_num + 1) * FACTOR, :] = passed[
                    part * FACTOR : (part + 1) * FACTOR, at * FACTOR : (at + 1) * FACTOR
                ]
    for step, message in enumerate(messages):
        chip = place ^ step ^ (side * (places // 2))
        for line in range(2 * GROUP):
            at = pl.multiple_of(line * FACTOR + chip * part_rows, 8)
            message[line * part_rows : (line + 1) * part_rows, :] = lines[pl.ds(at, part_rows), :]


def place_kernel(*refs):
    messages, (out_re, out_im, re_all, im_all) = refs[:-4], refs[-4:]
    bins, samples = out_re.shape
    part_rows = samples // FACTOR
    body = GROUP * part_rows
    half = len(messages) // 2
    place, side = lax.axis_index("az"), lax.axis_index("rg")
    for step, message in enumerate(messages):
        chip = place ^ step
        core = (lax.div(chip, half) != side).astype(jnp.int32)
        at = pl.multiple_of((lax.rem(chip, half) * 2 + core) * body, 8)
        re_all[pl.ds(at, body), :] = message[:body, :]
        im_all[pl.ds(at, body), :] = message[body:, :]
    for out, all_ref in ((out_re, re_all), (out_im, im_all)):
        for tile in range(0, bins, 8):
            for row in range(part_rows):
                out[tile : tile + 8, row * FACTOR : (row + 1) * FACTOR] = all_ref[
                    pl.ds(tile * part_rows + row, 8, stride=part_rows), :
                ]


VMEM = pl.BlockSpec(memory_space=pltpu.VMEM)
SMEM = pl.BlockSpec(memory_space=pltpu.SMEM)
KERNEL = pltpu.CompilerParams(vmem_limit_bytes=32 * 1024 * 1024)


def cost(flops, count):
    return pl.CostEstimate(flops=flops, bytes_accessed=count, transcendentals=0)


def transposed_shards(raw_re, raw_im, ref_blocks, owners, offsets, taps):
    bins, samples = raw_re.shape
    places = lax.axis_size("az")
    f32 = jnp.float32
    tables = dft_constants()
    matrices = [jnp.asarray(part) for pair in tables[:2] for part in pair]
    twists = [jnp.asarray(part) for part in tables[2]]
    ref_own = ref_blocks[0]
    swap = functools.partial(lax.ppermute, axis_name="rg", perm=[(0, 1), (1, 0)])
    offsets_other = swap(offsets)
    ref_other, re_other, im_other, taps_other = swap(ref_own), swap(raw_re), swap(raw_im), swap(taps)

    part_rows = samples // FACTOR
    message = jax.ShapeDtypeStruct((2, 2 * GROUP * part_rows + 8, FACTOR), f32)
    lines = pl.pallas_call(
        spread_kernel,
        out_shape=[jax.ShapeDtypeStruct((bins * part_rows, FACTOR), f32)] * 2,
        in_specs=[VMEM] * 2,
        out_specs=[VMEM] * 2,
        compiler_params=KERNEL,
        cost_estimate=cost(0, 2 * 10**6),
        name="spread",
    )(raw_re, raw_im)
    messages = pl.pallas_call(
        pack_kernel,
        out_shape=[message] * places,
        in_specs=[VMEM] * 6 + [SMEM] * 2,
        out_specs=[VMEM] * places,
        scratch_shapes=[
            pltpu.VMEM(((2 * bins + 2 * EDGE) * part_rows, FACTOR), f32),
            pltpu.VMEM(((2 * bins + 2 * EDGE) * part_rows, FACTOR), f32),
            pltpu.VMEM((2 * bins + 2 * EDGE, FACTOR), f32),
        ],
        compiler_params=KERNEL,
        cost_estimate=cost(10**6, 4 * 10**6),
        name="pack",
    )(*lines, re_other, im_other, ref_own, ref_other, offsets, offsets_other)
    steps = (0, 1, 2, 7, 6, 5, 4, 3)
    chunks = [
        lax.ppermute(messages[step], "az", [(i, i ^ step) for i in range(places)]) if step else messages[step]
        for step in steps
    ]

    phases = pl.pallas_call(
        functools.partial(phase_kernel, 2 * bins),
        out_shape=jax.ShapeDtypeStruct((2, GROUP, 2, FACTOR, FACTOR), f32),
        in_specs=[SMEM] * 2,
        out_specs=VMEM,
        compiler_params=KERNEL,
        cost_estimate=cost(10**7, 10**6),
        name="phase",
    )(offsets, offsets_other)

    def spectrum(group):
        return pl.pallas_call(
            functools.partial(spectrum_body, steps, group),
            out_shape=jax.ShapeDtypeStruct((GROUP, 2, FACTOR, FACTOR), f32),
            in_specs=[VMEM] * places + [SMEM] + [VMEM] * 7,
            out_specs=VMEM,
            scratch_shapes=[
                pltpu.VMEM((2 * GROUP * FACTOR, FACTOR), f32),
                pltpu.VMEM((places, 2 * GROUP, FACTOR), f32),
            ],
            compiler_params=KERNEL,
            cost_estimate=cost(4 * 10**8, 2 * 10**6),
            name="spectrum",
        )(*chunks, owners, phases, *matrices, *twists)

    shared = spectrum(0)
    received = swap(shared)
    kept = spectrum(1)

    pieces = pl.pallas_call(
        functools.partial(image_kernel, places),
        out_shape=[jax.ShapeDtypeStruct((2 * GROUP * part_rows, FACTOR), f32)] * places,
        in_specs=[VMEM] * 3 + [SMEM] * 2 + [VMEM] * 6,
        out_specs=[VMEM] * places,
        scratch_shapes=[
            pltpu.VMEM((GROUP * FACTOR, 2 * FACTOR), f32),
            pltpu.VMEM((2 * GROUP * FACTOR, FACTOR), f32),
        ],
        compiler_params=KERNEL,
        cost_estimate=cost(4 * 10**8, 2 * 10**6),
        name="image",
    )(shared, kept, received, taps, taps_other, *matrices, *twists)

    half = places // 2
    routes = [
        [
            (chip * 2 + core, (chip ^ step ^ (core * half)) * 2 + chip // half)
            for chip in range(places)
            for core in range(2)
        ]
        for step in range(places)
    ]
    pieces = [lax.ppermute(piece, ("az", "rg"), route) for piece, route in zip(pieces, routes)]
    return pl.pallas_call(
        place_kernel,
        out_shape=[jax.ShapeDtypeStruct((bins, samples), f32)] * 2,
        in_specs=[VMEM] * places,
        out_specs=[VMEM] * 2,
        scratch_shapes=[pltpu.VMEM((bins * part_rows, FACTOR), f32)] * 2,
        compiler_params=KERNEL,
        cost_estimate=cost(0, 10**6),
        name="place",
    )(*pieces)


def solution(mesh):
    sizes = mesh.shape

    def whole(raw_re, raw_im, ref_blocks, owners, offsets, taps):
        line = raw_re.shape[1] // sizes["scene"]
        fits = (
            sizes["rg"] == 2
            and raw_re.shape[0] == 2 * GROUP * sizes["az"]
            and line == FACTOR * FACTOR
            and line // sizes["az"] % (8 * FACTOR) == 0
            and ref_blocks.shape[1] <= FACTOR
            and FACTOR % ref_blocks.shape[1] == 0
        )
        return jax.shard_map(
            transposed_shards if fits else butterfly_shards,
            mesh=mesh,
            in_specs=(
                P("rg", ("scene", "az")),
                P("rg", ("scene", "az")),
                P(("scene", "az"), None, "rg"),
                P("scene"),
                P("rg"),
                P("rg", None),
            ),
            out_specs=(P("rg", ("scene", "az")), P("rg", ("scene", "az"))),
            check_vma=False,
        )(raw_re, raw_im, ref_blocks, owners, offsets, taps)

    return whole
```

```python
import functools
import math

import jax
import jax.numpy as jnp
import numpy as np
from jax import lax
from jax.experimental import pallas as pl
from jax.experimental.pallas import tpu as pltpu
from jax.sharding import PartitionSpec as P

SPLIT = 4
TAPS = 8
REACH = 8
BLOCK = 16


PRECISE = lax.Precision.HIGHEST
PHASE_GAIN = 50.0


def partner_2(value, axis, stride):
    return lax.ppermute(value, axis, [(i, i ^ 1 << stride) for i in range(lax.axis_size(axis))])


def from_root(block, axis, source):
    block = jnp.where(lax.axis_index(axis) == source, block, jnp.zeros_like(block))
    return lax.psum(block, axis)


def padded_2(value, sides, width):
    for axis, dim in sides:
        size, length = (lax.axis_size(axis), value.shape[dim])
        up = [(i, (i + 1) % size) for i in range(size - 1)]
        down = [(j, i) for i, j in up]
        last = lax.slice_in_dim(value, length - width, length, axis=dim)
        initial = lax.slice_in_dim(value, 0, width, axis=dim)
        before = lax.ppermute(last, axis, up)
        after = lax.ppermute(initial, axis, down)
        value = jnp.concatenate([before, value, after], axis=dim)
    return value


def angles(numerator, denominator, sign_value):
    return sign_value * 2.0 * math.pi * numerator.astype(jnp.float32) / denominator


def rotate(signal, cosine, sine_part):
    real_part = signal[0] * cosine - signal[1] * sine_part
    imag_part = signal[0] * sine_part + signal[1] * cosine
    return jnp.stack([real_part, imag_part])


def dft_table(length_n, sign_value):
    counter = jnp.arange(length_n, dtype=jnp.int32)
    turn_count = counter[:, None] * counter[None, :] % length_n
    angle_set = angles(turn_count, length_n, sign_value)
    return (jnp.cos(angle_set), jnp.sin(angle_set))


def complex_apply(einsum_form, cosine, sine_part, signal):
    real_part = jnp.einsum(einsum_form, cosine, signal[0], precision=PRECISE) - jnp.einsum(
        einsum_form, sine_part, signal[1], precision=PRECISE
    )
    imag_part = jnp.einsum(einsum_form, cosine, signal[1], precision=PRECISE) + jnp.einsum(
        einsum_form, sine_part, signal[0], precision=PRECISE
    )
    return jnp.stack([real_part, imag_part])


def local_dft(signal, sign_value):
    rg_cols = signal.shape[1]
    az_rows = signal.shape[2]
    inner_len = az_rows // SPLIT
    shaped = signal.reshape(2, rg_cols, SPLIT, inner_len)
    first_cos, first_sin = dft_table(SPLIT, sign_value)
    first_pass = complex_apply("aj,cjk->cak", first_cos, first_sin, shaped)
    outer_idx = jnp.arange(SPLIT, dtype=jnp.int32)
    inner_idx = jnp.arange(inner_len, dtype=jnp.int32)
    twist = angles(outer_idx[:, None] * inner_idx[None, :] % az_rows, az_rows, sign_value)
    first_pass = rotate(first_pass, jnp.cos(twist)[None, :, :], jnp.sin(twist)[None, :, :])
    second_cos, second_sin = dft_table(inner_len, sign_value)
    second_pass = complex_apply("bk,cak->cba", second_cos, second_sin, first_pass)
    return second_pass.reshape(2, rg_cols, az_rows)


def butterfly_down(signal, az_place, bit_count):
    for bit_num in reversed(range(bit_count)):
        half_span = 1 << bit_num
        partner = partner_2(signal, "az", bit_num)
        is_upper = az_place >> bit_num & 1 == 1
        angle_set = angles(az_place % half_span, 2 * half_span, -1.0)
        difference = rotate(partner - signal, jnp.cos(angle_set), jnp.sin(angle_set))
        signal = jnp.where(is_upper, difference, signal + partner)
    return signal


def butterfly_up(signal, az_place, bit_count):
    for bit_num in range(bit_count):
        half_span = 1 << bit_num
        partner = partner_2(signal, "az", bit_num)
        is_upper = az_place >> bit_num & 1 == 1
        angle_set = angles(az_place % half_span, 2 * half_span, 1.0)
        cosine = jnp.cos(angle_set)
        sine_part = jnp.sin(angle_set)
        lower_new = (signal + rotate(partner, cosine, sine_part)) * 0.5
        upper_new = (partner - rotate(signal, cosine, sine_part)) * 0.5
        signal = jnp.where(is_upper, upper_new, lower_new)
    return signal


def butterfly_shards(raw_re, raw_im, ref_blocks, owners, offsets, taps):
    rg_cols = raw_re.shape[0]
    az_rows = raw_re.shape[1]
    az_count = lax.axis_size("az")
    az_place = lax.axis_index("az")
    bit_count = az_count.bit_length() - 1
    az_total = az_rows * az_count
    rg_total = rg_cols * lax.axis_size("rg")
    own_block = ref_blocks[0]
    lower_ref = from_root(own_block, "az", owners[0])
    upper_ref = from_root(own_block, "az", owners[1])
    signal = jnp.stack([raw_re, raw_im])
    signal = butterfly_down(signal, az_place, bit_count)
    column = jnp.zeros((), jnp.int32)
    for bit_num in range(bit_count):
        column = column + ((az_place >> bit_num & 1) << bit_count - 1 - bit_num)
    row_index = jnp.arange(az_rows, dtype=jnp.int32)
    twist = angles(row_index * column % az_total, az_total, -1.0)
    signal = rotate(signal, jnp.cos(twist)[None, :], jnp.sin(twist)[None, :])
    signal = local_dft(signal, -1.0)
    frequency = column + az_count * row_index
    signed = (frequency + az_total // 2) % az_total - az_total // 2
    az_freq = signed.astype(jnp.float32) / az_total
    rg_index = lax.axis_index("rg") * rg_cols + jnp.arange(rg_cols, dtype=jnp.int32)
    rg_freq = (rg_index.astype(jnp.float32) + 0.5) / (2 * rg_total) - 0.25
    model_phase = PHASE_GAIN * jnp.sqrt((1.0 + rg_freq)[:, None] ** 2 - az_freq[None, :] ** 2)
    ref_rows = own_block.shape[0]
    coarse = frequency * ref_rows // az_total
    slot_index = jnp.where(signed >= 0, ref_rows + coarse, coarse)
    one_hot = (jnp.arange(2 * ref_rows, dtype=jnp.int32)[:, None] == slot_index[None, :]).astype(
        jnp.float32
    )
    both_refs = jnp.concatenate([lower_ref, upper_ref], axis=0)
    picked = jnp.dot(both_refs.T, one_hot, precision=PRECISE)
    phase_all = model_phase + picked
    signal = rotate(signal, jnp.cos(phase_all), jnp.sin(phase_all))
    rim_width = REACH + TAPS // 2
    padded = padded_2(signal, (("rg", 1),), rim_width)
    offset_cols = jnp.repeat(offsets, BLOCK)
    local_cols = jnp.arange(rg_cols, dtype=jnp.int32)
    tap_index = jnp.arange(TAPS, dtype=jnp.int32)
    target = local_cols[:, None] + rim_width + offset_cols[:, None] + tap_index[None, :] - TAPS // 2
    padded_index = jnp.arange(rg_cols + 2 * rim_width, dtype=jnp.int32)
    hits = (padded_index[:, None, None] == target[None, :, :]).astype(jnp.float32)
    band_matrix = jnp.sum(hits * taps[None, :, :], axis=2)
    signal = jnp.einsum("zma,mi->zia", padded, band_matrix, precision=PRECISE)
    signal = local_dft(signal, 1.0) / az_rows
    twist_back = angles(row_index * column % az_total, az_total, 1.0)
    signal = rotate(signal, jnp.cos(twist_back)[None, :], jnp.sin(twist_back)[None, :])
    signal = butterfly_up(signal, az_place, bit_count)
    return (signal[0], signal[1])


FACTOR = 128
GROUP = 4
WINDOW = 2 * GROUP + TAPS - 1
REF_LINES = 8
EDGE = 16


def split_bf16(value):
    high = value.astype(jnp.bfloat16)
    low = (value - high.astype(jnp.float32)).astype(jnp.bfloat16)
    return high, low


def dot_split(left, right):
    left_high, left_low = left
    right_high, right_low = right
    dot = functools.partial(jnp.dot, preferred_element_type=jnp.float32)
    return dot(left_high, right_high) + (dot(left_high, right_low) + dot(left_low, right_high))


def dft_constants():
    counter = np.arange(FACTOR)
    turns = np.outer(counter, counter)
    angle = 2 * np.pi * (turns % FACTOR) / FACTOR
    cosine, sine = np.cos(angle), np.sin(angle)
    pair = []
    for matrix in (np.block([[cosine, sine], [-sine, cosine]]), np.block([[cosine, -sine], [sine, cosine]])):
        high = matrix.astype(jnp.bfloat16)
        low = (matrix - high.astype(np.float64)).astype(jnp.bfloat16)
        pair.append((high, low))
    twist = 2 * np.pi * turns / FACTOR**2
    return pair[0], pair[1], (np.cos(twist).astype(np.float32), np.sin(twist).astype(np.float32))


def cos_sin_quarters(quarters):
    whole = jnp.floor(quarters + 0.5)
    rest = (quarters - whole) * (math.pi / 2)
    square = rest * rest
    sine = rest + rest * square * (
        -1.6666654611e-1 + square * (8.3321608736e-3 + square * (-1.9515295891e-4))
    )
    cosine = 1.0 - 0.5 * square + square * square * (
        4.166664568298827e-2 + square * (-1.388731625493765e-3 + square * 2.443315711809948e-5)
    )
    number = whole.astype(jnp.int32)
    odd = (number & 1) == 1
    turned_cos = jnp.where(odd, sine, cosine)
    turned_sin = jnp.where(odd, cosine, sine)
    cos_sign = jnp.where(((number + 1) & 2) == 2, -1.0, 1.0)
    sin_sign = jnp.where((number & 2) == 2, -1.0, 1.0)
    return turned_cos * cos_sign, turned_sin * sin_sign


def window_start(chip, side, offsets_own, offsets_other):
    block = chip * 2 * GROUP // BLOCK
    blocks = offsets_own.shape[0]
    local = lax.rem(block, blocks)
    shift = jnp.where(lax.div(block, blocks) == side, offsets_own[local], offsets_other[local])
    return chip * 2 * GROUP + shift - TAPS // 2


def group_starts(side):
    return GROUP + GROUP * side, 3 * GROUP * side


def spread_lines(target, base, source):
    bins, samples = source.shape
    part_rows = samples // FACTOR
    for tile in range(0, bins, 8):
        for row in range(part_rows):
            target[pl.ds((base + tile) * part_rows + row, 8, stride=part_rows), :] = source[
                tile : tile + 8, row * FACTOR : (row + 1) * FACTOR
            ]


def spread_kernel(re_own, im_own, re_lines, im_lines):
    spread_lines(re_lines, 0, re_own)
    spread_lines(im_lines, 0, im_own)


def pack_kernel(re_lines, im_lines, re_other, im_other, ref_own, ref_other, off_own, off_other, *refs):
    messages, (re_all, im_all, ref_all) = refs[:-3], refs[-3:]
    bins, samples = re_other.shape
    part_rows = samples // FACTOR
    place, side = lax.axis_index("az"), lax.axis_index("rg")
    own_at, other_at = EDGE + side * bins, EDGE + (1 - side) * bins
    zeros = jnp.zeros((EDGE * part_rows, FACTOR), jnp.float32)
    for all_ref, own, other in ((re_all, re_lines, re_other), (im_all, im_lines, im_other)):
        all_ref[: EDGE * part_rows, :] = zeros
        all_ref[(EDGE + 2 * bins) * part_rows :, :] = zeros
        all_ref[pl.ds(pl.multiple_of(own_at * part_rows, 8), bins * part_rows), :] = own[...]
        spread_lines(all_ref, other_at, other)
    ref_rows = ref_own.shape[0]
    row = lax.broadcasted_iota(jnp.int32, (ref_rows, FACTOR), 0)
    column = lax.broadcasted_iota(jnp.int32, (ref_rows, FACTOR), 1)
    twice = (lax.rem(column, ref_rows) == row).astype(jnp.float32)
    ref_all[:EDGE, :] = jnp.zeros((EDGE, FACTOR), jnp.float32)
    ref_all[EDGE + 2 * bins :, :] = jnp.zeros((EDGE, FACTOR), jnp.float32)
    for at, ref in ((own_at, ref_own), (other_at, ref_other)):
        ref_all[pl.ds(pl.multiple_of(at, 16), bins), :] = lax.dot_general(
            ref[...], twice, (((0,), (0,)), ((), ())), precision=PRECISE, preferred_element_type=jnp.float32
        )
    body = WINDOW * part_rows
    lane = lax.broadcasted_iota(jnp.int32, (1, FACTOR), 1)
    for step, message in enumerate(messages):
        start = window_start(((place >> 1) ^ step) * 2 + side, side, off_own, off_other) + EDGE
        rows = pl.ds(pl.multiple_of(start * part_rows, 8), body)
        message[:body, :] = re_all[rows, :]
        message[body : 2 * body, :] = im_all[rows, :]
        for bin_num in range(REF_LINES):
            low = ref_all[pl.ds(start + bin_num, 1), :]
            high = ref_all[pl.ds(start + REF_LINES + bin_num, 1), :]
            message[2 * body + bin_num : 2 * body + bin_num + 1, :] = jnp.where(lane < FACTOR // 2, low, high)


def phase_kernel(bins_total, off_own, off_other, out):
    place, side = lax.axis_index("az"), lax.axis_index("rg")
    start = window_start(place, side, off_own, off_other)
    shape = (FACTOR, FACTOR)
    frequency = lax.broadcasted_iota(jnp.int32, shape, 0) + FACTOR * lax.broadcasted_iota(jnp.int32, shape, 1)
    total = FACTOR * FACTOR
    signed = jnp.where(frequency >= total // 2, frequency - total, frequency)
    az_freq = signed.astype(jnp.float32) / total
    az_square = az_freq * az_freq
    for group, group_at in enumerate(group_starts(side)):
        for bin_num in range(GROUP):
            rg_index = (start + group_at + bin_num).astype(jnp.float32)
            rg_freq = (rg_index + 0.5) / (2 * bins_total) - 0.25
            base = (1.0 + rg_freq) * (1.0 + rg_freq)
            root = jnp.sqrt(base - az_square)
            cosine, sine = cos_sin_quarters(root * (PHASE_GAIN * 2 / math.pi))
            out[group, bin_num, 0] = cosine
            out[group, bin_num, 1] = sine


def spectrum_body(places, group, *refs):
    chunks, refs = refs[:places], refs[places:]
    owners, phase, high1, low1, high2, low2, twist_cos, twist_sin, out, lines, picks, picked = refs
    place, side = lax.axis_index("az"), lax.axis_index("rg")
    samples = FACTOR * FACTOR // places
    part_rows = samples // FACTOR
    body = WINDOW * part_rows
    start = group_starts(side)[group]
    for at, chunk in enumerate(chunks):
        source = ((place >> 1) ^ (at // 2)) * 2 + (side if at % 2 == 0 else 1 - side)
        for part in range(2):
            for bin_num in range(GROUP):
                row = jnp.minimum(start + bin_num, WINDOW - 1)
                read = pl.multiple_of(part * body + row * part_rows, 8)
                write = pl.multiple_of((part * GROUP + bin_num) * FACTOR + source * part_rows, 8)
                lines[pl.ds(write, part_rows), :] = chunk[pl.ds(read, part_rows), :]
        picks[source] = chunk[2 * body :, :]
    row = lax.broadcasted_iota(jnp.int32, (FACTOR, FACTOR), 0)
    column = lax.broadcasted_iota(jnp.int32, (FACTOR, FACTOR), 1)
    lane = lax.broadcasted_iota(jnp.int32, (REF_LINES, FACTOR), 1)
    for block in range(2):
        spread = (row == column // 2 + block * (FACTOR // 2)).astype(jnp.float32)
        wide = [
            jnp.dot(picks[owners[which]], spread, precision=PRECISE, preferred_element_type=jnp.float32)
            for which in range(2)
        ]
        ref_phase = jnp.where(lane < FACTOR // 2, wide[1], wide[0])
        ref_cos, ref_sin = cos_sin_quarters(ref_phase * (2 / math.pi))
        picked[0, block * REF_LINES : (block + 1) * REF_LINES, :] = ref_cos
        picked[1, block * REF_LINES : (block + 1) * REF_LINES, :] = ref_sin
    first, second = (high1[...], low1[...]), (high2[...], low2[...])
    for pair in range(GROUP // 2):
        bins = (2 * pair, 2 * pair + 1)
        columns = []
        for bin_num in bins:
            real = lines[bin_num * FACTOR : (bin_num + 1) * FACTOR, :]
            imag = lines[(GROUP + bin_num) * FACTOR : (GROUP + bin_num + 1) * FACTOR, :]
            columns.append(jnp.concatenate([real, imag], axis=0))
        passed = dot_split(first, split_bf16(jnp.concatenate(columns, axis=1)))
        rows = []
        for at in range(2):
            real = passed[:FACTOR, at * FACTOR : (at + 1) * FACTOR]
            imag = passed[FACTOR:, at * FACTOR : (at + 1) * FACTOR]
            turned_real = real * twist_cos[...] + imag * twist_sin[...]
            turned_imag = imag * twist_cos[...] - real * twist_sin[...]
            rows.append(jnp.concatenate([turned_real, turned_imag], axis=1))
        passed = dot_split(split_bf16(jnp.concatenate(rows, axis=0)), second)
        for at, bin_num in enumerate(bins):
            real = passed[at * FACTOR : (at + 1) * FACTOR, :FACTOR]
            imag = passed[at * FACTOR : (at + 1) * FACTOR, FACTOR:]
            model_cos, model_sin = phase[group, bin_num, 0], phase[group, bin_num, 1]
            row_cos, row_sin = picked[0, pl.ds(start + bin_num, 1), :], picked[1, pl.ds(start + bin_num, 1), :]
            cosine = model_cos * row_cos - model_sin * row_sin
            sine = model_sin * row_cos + model_cos * row_sin
            out[bin_num, 0] = real * cosine - imag * sine
            out[bin_num, 1] = real * sine + imag * cosine


def image_kernel(places, *refs):
    shared, kept, received, taps_own, taps_other, high1, low1, high2, low2, twist_cos, twist_sin = refs[:11]
    give, keep, band, lines = refs[11:]
    place, side = lax.axis_index("az"), lax.axis_index("rg")
    samples = FACTOR * FACTOR // places
    part_rows = samples // FACTOR
    bins_held = taps_own.shape[0]
    first_bin = place * 2 * GROUP + side * GROUP
    held = lax.div(first_bin, bins_held) == side
    local = lax.rem(first_bin, bins_held)
    weights = [
        [jnp.where(held, taps_own[local + j, t], taps_other[local + j, t]) for t in range(TAPS)] for j in range(GROUP)
    ]
    is_first = side == 0
    strip = 16
    for part in range(2):
        for at in range(0, FACTOR, strip):
            rows = slice(at, at + strip)
            sums = [None] * GROUP
            for slot in range(3 * GROUP):
                if slot < GROUP:
                    value = jnp.where(is_first, kept[slot, part, rows], received[slot, part, rows])
                elif slot < 2 * GROUP:
                    value = shared[slot - GROUP, part, rows]
                else:
                    at_slot = slot - 2 * GROUP
                    value = jnp.where(is_first, received[at_slot, part, rows], kept[at_slot, part, rows])
                for j in range(GROUP):
                    if 0 <= slot - j < TAPS:
                        term = value * weights[j][slot - j]
                        sums[j] = term if sums[j] is None else sums[j] + term
            for j in range(GROUP):
                band[j * FACTOR + at : j * FACTOR + at + strip, part * FACTOR : (part + 1) * FACTOR] = sums[j]
    first, second = (high1[...], low1[...]), (high2[...], low2[...])
    scale = 1.0 / (FACTOR * FACTOR)
    cos_table, sin_table = twist_cos[...] * scale, twist_sin[...] * scale
    for pair in range(GROUP // 2):
        bins = (2 * pair, 2 * pair + 1)
        passed = dot_split(split_bf16(band[2 * pair * FACTOR : (2 * pair + 2) * FACTOR, :]), first)
        columns = []
        for at in range(2):
            real = passed[at * FACTOR : (at + 1) * FACTOR, :FACTOR]
            imag = passed[at * FACTOR : (at + 1) * FACTOR, FACTOR:]
            turned_real = real * cos_table - imag * sin_table
            turned_imag = imag * cos_table + real * sin_table
            columns.append(jnp.concatenate([turned_real, turned_imag], axis=0))
        passed = dot_split(second, split_bf16(jnp.concatenate(columns, axis=1)))
        for at, bin_num in enumerate(bins):
            for part in range(2):
                lines[(part * GROUP + bin_num) * FACTOR : (part * GROUP + bin_num + 1) * FACTOR, :] = passed[
                    part * FACTOR : (part + 1) * FACTOR, at * FACTOR : (at + 1) * FACTOR
                ]
    for pair in range(places // 2):
        for piece, core in ((give, 1 - side), (keep, side)):
            for line in range(2 * GROUP):
                at = pl.multiple_of(line * FACTOR + (2 * pair + core) * part_rows, 8)
                piece[pair, line * part_rows : (line + 1) * part_rows, :] = lines[pl.ds(at, part_rows), :]


def merge_kernel(half, keep, got, *messages):
    quarter = lax.rem(lax.axis_index("az"), half)
    size = keep.shape[1]
    for step, message in enumerate(messages):
        message[:size, :] = keep[quarter ^ step]
        message[size:, :] = got[quarter ^ step]


def place_kernel(*refs):
    messages, (out_re, out_im, re_all, im_all) = refs[:-4], refs[-4:]
    bins, samples = out_re.shape
    part_rows = samples // FACTOR
    body = GROUP * part_rows
    place = lax.axis_index("az")
    core = place & 1
    for step, message in enumerate(messages):
        sender = (place >> 1) ^ step
        for which in range(2):
            at = pl.multiple_of((sender * 2 + (core if which == 0 else 1 - core)) * body, 8)
            re_all[pl.ds(at, body), :] = message[2 * which * body : (2 * which + 1) * body, :]
            im_all[pl.ds(at, body), :] = message[(2 * which + 1) * body : (2 * which + 2) * body, :]
    for out, all_ref in ((out_re, re_all), (out_im, im_all)):
        for tile in range(0, bins, 8):
            for row in range(part_rows):
                out[tile : tile + 8, row * FACTOR : (row + 1) * FACTOR] = all_ref[
                    pl.ds(tile * part_rows + row, 8, stride=part_rows), :
                ]


VMEM = pl.BlockSpec(memory_space=pltpu.VMEM)
SMEM = pl.BlockSpec(memory_space=pltpu.SMEM)
KERNEL = pltpu.CompilerParams(vmem_limit_bytes=32 * 1024 * 1024)


def cost(flops, count):
    return pl.CostEstimate(flops=flops, bytes_accessed=count, transcendentals=0)


def transposed_shards(raw_re, raw_im, ref_blocks, owners, offsets, taps):
    bins, samples = raw_re.shape
    places = lax.axis_size("az")
    f32 = jnp.float32
    tables = dft_constants()
    matrices = [jnp.asarray(part) for pair in tables[:2] for part in pair]
    twists = [jnp.asarray(part) for part in tables[2]]
    ref_own = ref_blocks[0]
    swap = functools.partial(lax.ppermute, axis_name="rg", perm=[(0, 1), (1, 0)])
    offsets_other = swap(offsets)
    ref_other, re_other, im_other, taps_other = swap(ref_own), swap(raw_re), swap(raw_im), swap(taps)

    part_rows = samples // FACTOR
    half = places // 2
    message = jax.ShapeDtypeStruct((2 * WINDOW * part_rows + REF_LINES, FACTOR), f32)
    lines = pl.pallas_call(
        spread_kernel,
        out_shape=[jax.ShapeDtypeStruct((bins * part_rows, FACTOR), f32)] * 2,
        in_specs=[VMEM] * 2,
        out_specs=[VMEM] * 2,
        compiler_params=KERNEL,
        cost_estimate=cost(0, 2 * 10**6),
        name="spread",
    )(raw_re, raw_im)
    messages = pl.pallas_call(
        pack_kernel,
        out_shape=[message] * half,
        in_specs=[VMEM] * 6 + [SMEM] * 2,
        out_specs=[VMEM] * half,
        scratch_shapes=[
            pltpu.VMEM(((2 * bins + 2 * EDGE) * part_rows, FACTOR), f32),
            pltpu.VMEM(((2 * bins + 2 * EDGE) * part_rows, FACTOR), f32),
            pltpu.VMEM((2 * bins + 2 * EDGE, FACTOR), f32),
        ],
        compiler_params=KERNEL,
        cost_estimate=cost(10**6, 4 * 10**6),
        name="pack",
    )(*lines, re_other, im_other, ref_own, ref_other, offsets, offsets_other)
    chunks = [None] * places
    for step in reversed(range(half)):
        route = [
            (chip * 2 + core, (((chip >> 1) ^ step) * 2 + core) * 2 + (chip & 1))
            for chip in range(places)
            for core in range(2)
        ]
        chunks[2 * step] = lax.ppermute(messages[step], ("az", "rg"), route)
        chunks[2 * step + 1] = swap(chunks[2 * step])

    phases = pl.pallas_call(
        functools.partial(phase_kernel, 2 * bins),
        out_shape=jax.ShapeDtypeStruct((2, GROUP, 2, FACTOR, FACTOR), f32),
        in_specs=[SMEM] * 2,
        out_specs=VMEM,
        compiler_params=KERNEL,
        cost_estimate=cost(10**7, 10**6),
        name="phase",
    )(offsets, offsets_other)

    def spectrum(group):
        return pl.pallas_call(
            functools.partial(spectrum_body, places, group),
            out_shape=jax.ShapeDtypeStruct((GROUP, 2, FACTOR, FACTOR), f32),
            in_specs=[VMEM] * places + [SMEM] + [VMEM] * 7,
            out_specs=VMEM,
            scratch_shapes=[
                pltpu.VMEM((2 * GROUP * FACTOR, FACTOR), f32),
                pltpu.VMEM((places, REF_LINES, FACTOR), f32),
                pltpu.VMEM((2, 2 * REF_LINES, FACTOR), f32),
            ],
            compiler_params=KERNEL,
            cost_estimate=cost(4 * 10**8, 2 * 10**6),
            name="spectrum",
        )(*chunks, owners, phases, *matrices, *twists)

    shared = spectrum(0)
    received = swap(shared)
    kept = spectrum(1)

    piece = jax.ShapeDtypeStruct((half, 2 * GROUP * part_rows, FACTOR), f32)
    give, keep = pl.pallas_call(
        functools.partial(image_kernel, places),
        out_shape=[piece] * 2,
        in_specs=[VMEM] * 3 + [SMEM] * 2 + [VMEM] * 6,
        out_specs=[VMEM] * 2,
        scratch_shapes=[
            pltpu.VMEM((GROUP * FACTOR, 2 * FACTOR), f32),
            pltpu.VMEM((2 * GROUP * FACTOR, FACTOR), f32),
        ],
        compiler_params=KERNEL,
        cost_estimate=cost(4 * 10**8, 2 * 10**6),
        name="image",
    )(shared, kept, received, taps, taps_other, *matrices, *twists)
    pieces = pl.pallas_call(
        functools.partial(merge_kernel, half),
        out_shape=[jax.ShapeDtypeStruct((4 * GROUP * part_rows, FACTOR), f32)] * half,
        in_specs=[VMEM] * 2,
        out_specs=[VMEM] * half,
        compiler_params=KERNEL,
        cost_estimate=cost(0, 10**6),
        name="merge",
    )(keep, swap(give))

    routes = [
        [
            (chip * 2 + core, (((chip % half) ^ step) * 2 + core) * 2 + chip // half)
            for chip in range(places)
            for core in range(2)
        ]
        for step in range(half)
    ]
    pieces = [lax.ppermute(piece, ("az", "rg"), route) for piece, route in zip(pieces, routes)]
    return pl.pallas_call(
        place_kernel,
        out_shape=[jax.ShapeDtypeStruct((bins, samples), f32)] * 2,
        in_specs=[VMEM] * half,
        out_specs=[VMEM] * 2,
        scratch_shapes=[pltpu.VMEM((bins * part_rows, FACTOR), f32)] * 2,
        compiler_params=KERNEL,
        cost_estimate=cost(0, 10**6),
        name="place",
    )(*pieces)


def solution(mesh):
    sizes = mesh.shape

    def whole(raw_re, raw_im, ref_blocks, owners, offsets, taps):
        line = raw_re.shape[1] // sizes["scene"]
        fits = (
            sizes["rg"] == 2
            and raw_re.shape[0] == 2 * GROUP * sizes["az"]
            and line == FACTOR * FACTOR
            and line // sizes["az"] % (8 * FACTOR) == 0
            and ref_blocks.shape[1] == FACTOR // 2
        )
        return jax.shard_map(
            transposed_shards if fits else butterfly_shards,
            mesh=mesh,
            in_specs=(
                P("rg", ("scene", "az")),
                P("rg", ("scene", "az")),
                P(("scene", "az"), None, "rg"),
                P("scene"),
                P("rg"),
                P("rg", None),
            ),
            out_specs=(P("rg", ("scene", "az")), P("rg", ("scene", "az"))),
            check_vma=False,
        )(raw_re, raw_im, ref_blocks, owners, offsets, taps)

    return whole
```

```python
import functools
import math

import jax
import jax.numpy as jnp
import numpy as np
from jax import lax
from jax.experimental import pallas as pl
from jax.experimental.pallas import tpu as pltpu
from jax.sharding import PartitionSpec as P

SPLIT = 4
TAPS = 8
REACH = 8
BLOCK = 16


PRECISE = lax.Precision.HIGHEST
PHASE_GAIN = 50.0


def partner_2(value, axis, stride):
    return lax.ppermute(value, axis, [(i, i ^ 1 << stride) for i in range(lax.axis_size(axis))])


def from_root(block, axis, source):
    block = jnp.where(lax.axis_index(axis) == source, block, jnp.zeros_like(block))
    return lax.psum(block, axis)


def padded_2(value, sides, width):
    for axis, dim in sides:
        size, length = (lax.axis_size(axis), value.shape[dim])
        up = [(i, (i + 1) % size) for i in range(size - 1)]
        down = [(j, i) for i, j in up]
        last = lax.slice_in_dim(value, length - width, length, axis=dim)
        initial = lax.slice_in_dim(value, 0, width, axis=dim)
        before = lax.ppermute(last, axis, up)
        after = lax.ppermute(initial, axis, down)
        value = jnp.concatenate([before, value, after], axis=dim)
    return value


def angles(numerator, denominator, sign_value):
    return sign_value * 2.0 * math.pi * numerator.astype(jnp.float32) / denominator


def rotate(signal, cosine, sine_part):
    real_part = signal[0] * cosine - signal[1] * sine_part
    imag_part = signal[0] * sine_part + signal[1] * cosine
    return jnp.stack([real_part, imag_part])


def dft_table(length_n, sign_value):
    counter = jnp.arange(length_n, dtype=jnp.int32)
    turn_count = counter[:, None] * counter[None, :] % length_n
    angle_set = angles(turn_count, length_n, sign_value)
    return (jnp.cos(angle_set), jnp.sin(angle_set))


def complex_apply(einsum_form, cosine, sine_part, signal):
    real_part = jnp.einsum(einsum_form, cosine, signal[0], precision=PRECISE) - jnp.einsum(
        einsum_form, sine_part, signal[1], precision=PRECISE
    )
    imag_part = jnp.einsum(einsum_form, cosine, signal[1], precision=PRECISE) + jnp.einsum(
        einsum_form, sine_part, signal[0], precision=PRECISE
    )
    return jnp.stack([real_part, imag_part])


def local_dft(signal, sign_value):
    rg_cols = signal.shape[1]
    az_rows = signal.shape[2]
    inner_len = az_rows // SPLIT
    shaped = signal.reshape(2, rg_cols, SPLIT, inner_len)
    first_cos, first_sin = dft_table(SPLIT, sign_value)
    first_pass = complex_apply("aj,cjk->cak", first_cos, first_sin, shaped)
    outer_idx = jnp.arange(SPLIT, dtype=jnp.int32)
    inner_idx = jnp.arange(inner_len, dtype=jnp.int32)
    twist = angles(outer_idx[:, None] * inner_idx[None, :] % az_rows, az_rows, sign_value)
    first_pass = rotate(first_pass, jnp.cos(twist)[None, :, :], jnp.sin(twist)[None, :, :])
    second_cos, second_sin = dft_table(inner_len, sign_value)
    second_pass = complex_apply("bk,cak->cba", second_cos, second_sin, first_pass)
    return second_pass.reshape(2, rg_cols, az_rows)


def butterfly_down(signal, az_place, bit_count):
    for bit_num in reversed(range(bit_count)):
        half_span = 1 << bit_num
        partner = partner_2(signal, "az", bit_num)
        is_upper = az_place >> bit_num & 1 == 1
        angle_set = angles(az_place % half_span, 2 * half_span, -1.0)
        difference = rotate(partner - signal, jnp.cos(angle_set), jnp.sin(angle_set))
        signal = jnp.where(is_upper, difference, signal + partner)
    return signal


def butterfly_up(signal, az_place, bit_count):
    for bit_num in range(bit_count):
        half_span = 1 << bit_num
        partner = partner_2(signal, "az", bit_num)
        is_upper = az_place >> bit_num & 1 == 1
        angle_set = angles(az_place % half_span, 2 * half_span, 1.0)
        cosine = jnp.cos(angle_set)
        sine_part = jnp.sin(angle_set)
        lower_new = (signal + rotate(partner, cosine, sine_part)) * 0.5
        upper_new = (partner - rotate(signal, cosine, sine_part)) * 0.5
        signal = jnp.where(is_upper, upper_new, lower_new)
    return signal


def butterfly_shards(raw_re, raw_im, ref_blocks, owners, offsets, taps):
    rg_cols = raw_re.shape[0]
    az_rows = raw_re.shape[1]
    az_count = lax.axis_size("az")
    az_place = lax.axis_index("az")
    bit_count = az_count.bit_length() - 1
    az_total = az_rows * az_count
    rg_total = rg_cols * lax.axis_size("rg")
    own_block = ref_blocks[0]
    lower_ref = from_root(own_block, "az", owners[0])
    upper_ref = from_root(own_block, "az", owners[1])
    signal = jnp.stack([raw_re, raw_im])
    signal = butterfly_down(signal, az_place, bit_count)
    column = jnp.zeros((), jnp.int32)
    for bit_num in range(bit_count):
        column = column + ((az_place >> bit_num & 1) << bit_count - 1 - bit_num)
    row_index = jnp.arange(az_rows, dtype=jnp.int32)
    twist = angles(row_index * column % az_total, az_total, -1.0)
    signal = rotate(signal, jnp.cos(twist)[None, :], jnp.sin(twist)[None, :])
    signal = local_dft(signal, -1.0)
    frequency = column + az_count * row_index
    signed = (frequency + az_total // 2) % az_total - az_total // 2
    az_freq = signed.astype(jnp.float32) / az_total
    rg_index = lax.axis_index("rg") * rg_cols + jnp.arange(rg_cols, dtype=jnp.int32)
    rg_freq = (rg_index.astype(jnp.float32) + 0.5) / (2 * rg_total) - 0.25
    model_phase = PHASE_GAIN * jnp.sqrt((1.0 + rg_freq)[:, None] ** 2 - az_freq[None, :] ** 2)
    ref_rows = own_block.shape[0]
    coarse = frequency * ref_rows // az_total
    slot_index = jnp.where(signed >= 0, ref_rows + coarse, coarse)
    one_hot = (jnp.arange(2 * ref_rows, dtype=jnp.int32)[:, None] == slot_index[None, :]).astype(
        jnp.float32
    )
    both_refs = jnp.concatenate([lower_ref, upper_ref], axis=0)
    picked = jnp.dot(both_refs.T, one_hot, precision=PRECISE)
    phase_all = model_phase + picked
    signal = rotate(signal, jnp.cos(phase_all), jnp.sin(phase_all))
    rim_width = REACH + TAPS // 2
    padded = padded_2(signal, (("rg", 1),), rim_width)
    offset_cols = jnp.repeat(offsets, BLOCK)
    local_cols = jnp.arange(rg_cols, dtype=jnp.int32)
    tap_index = jnp.arange(TAPS, dtype=jnp.int32)
    target = local_cols[:, None] + rim_width + offset_cols[:, None] + tap_index[None, :] - TAPS // 2
    padded_index = jnp.arange(rg_cols + 2 * rim_width, dtype=jnp.int32)
    hits = (padded_index[:, None, None] == target[None, :, :]).astype(jnp.float32)
    band_matrix = jnp.sum(hits * taps[None, :, :], axis=2)
    signal = jnp.einsum("zma,mi->zia", padded, band_matrix, precision=PRECISE)
    signal = local_dft(signal, 1.0) / az_rows
    twist_back = angles(row_index * column % az_total, az_total, 1.0)
    signal = rotate(signal, jnp.cos(twist_back)[None, :], jnp.sin(twist_back)[None, :])
    signal = butterfly_up(signal, az_place, bit_count)
    return (signal[0], signal[1])


FACTOR = 128
PLACES = 8
PART = FACTOR // PLACES
HALF = FACTOR // 2
OUT_BINS = 8
WINDOW = OUT_BINS + TAPS - 1
REF_LINES = 8
EDGE = 16
CHUNKS = (((0, WINDOW), (0, OUT_BINS)),)


def split_bf16(value):
    high = value.astype(jnp.bfloat16)
    low = (value - high.astype(jnp.float32)).astype(jnp.bfloat16)
    return high, low


def dot_split(left, right):
    left_high, left_low = left
    right_high, right_low = right
    dot = functools.partial(jnp.dot, preferred_element_type=jnp.float32)
    return dot(left_high, right_high) + (dot(left_high, right_low) + dot(left_low, right_high))


def both_bf16(matrix):
    high = matrix.astype(jnp.bfloat16)
    return high, (matrix - high.astype(np.float64)).astype(jnp.bfloat16)


def dft_constants():
    counter = np.arange(FACTOR)
    kappa = np.arange(HALF)
    first, last, twists = [], [], []
    for side in range(2):
        order = [(middle, low, line) for low in (side, 1 - side) for middle in range(2) for line in range(PART)]
        mine = np.array([(2 * middle + low) * PART + line for middle, low, line in order])
        angle = 2 * np.pi * (np.outer(2 * kappa + side, mine) % FACTOR) / FACTOR
        cosine, sine = np.cos(angle), np.sin(angle)
        first.append(np.block([[cosine, sine], [-sine, cosine]]))
        back_re, back_im = np.block([cosine.T, -sine.T]), np.block([sine.T, cosine.T])
        own, other = slice(0, HALF // 2), slice(HALF // 2, HALF)
        last.append(np.concatenate([back_re[own], back_im[own], back_re[other], back_im[other]]))
        twist = 2 * np.pi * np.outer(2 * kappa + side, counter) / FACTOR**2
        twists.append(np.stack([np.cos(twist), np.sin(twist)]))
    angle = 2 * np.pi * (np.outer(counter, counter) % FACTOR) / FACTOR
    cosine, sine = np.cos(angle), np.sin(angle)
    there = np.block([[cosine, -sine], [sine, cosine]])
    back = np.block([[cosine, sine], [-sine, cosine]])
    matrices = [both_bf16(matrix) for matrix in (np.stack(first), there, back, np.stack(last))]
    return [part for pair in matrices for part in pair], np.stack(twists).astype(np.float32)


def cos_sin_quarters(quarters):
    whole = jnp.floor(quarters + 0.5)
    rest = (quarters - whole) * (math.pi / 2)
    square = rest * rest
    sine = rest + rest * square * (
        -1.6666654611e-1 + square * (8.3321608736e-3 + square * (-1.9515295891e-4))
    )
    cosine = 1.0 - 0.5 * square + square * square * (
        4.166664568298827e-2 + square * (-1.388731625493765e-3 + square * 2.443315711809948e-5)
    )
    number = whole.astype(jnp.int32)
    odd = (number & 1) == 1
    turned_cos = jnp.where(odd, sine, cosine)
    turned_sin = jnp.where(odd, cosine, sine)
    cos_sign = jnp.where(((number + 1) & 2) == 2, -1.0, 1.0)
    sin_sign = jnp.where((number & 2) == 2, -1.0, 1.0)
    return turned_cos * cos_sign, turned_sin * sin_sign


def window_start(chip, side, offsets_own, offsets_other):
    block = chip * OUT_BINS // BLOCK
    blocks = offsets_own.shape[0]
    local = lax.rem(block, blocks)
    shift = jnp.where(lax.div(block, blocks) == side, offsets_own[local], offsets_other[local])
    return chip * OUT_BINS + shift - TAPS // 2


def spread_lines(target, base, source):
    bins, samples = source.shape
    part_rows = samples // FACTOR
    for tile in range(0, bins, 8):
        for row in range(part_rows):
            target[pl.ds((base + tile) * part_rows + row, 8, stride=part_rows), :] = source[
                tile : tile + 8, row * FACTOR : (row + 1) * FACTOR
            ]


def spread_kernel(re_own, im_own, re_lines, im_lines):
    spread_lines(re_lines, 0, re_own)
    spread_lines(im_lines, 0, im_own)


def pack_kernel(re_lines, im_lines, re_other, im_other, ref_own, ref_other, off_own, off_other, *refs):
    messages, (re_all, im_all, ref_all) = refs[:-3], refs[-3:]
    bins, samples = re_other.shape
    part_rows = samples // FACTOR
    place, side = lax.axis_index("az"), lax.axis_index("rg")
    own_at, other_at = EDGE + side * bins, EDGE + (1 - side) * bins
    zeros = jnp.zeros((EDGE * part_rows, FACTOR), jnp.float32)
    for all_ref, own, other in ((re_all, re_lines, re_other), (im_all, im_lines, im_other)):
        all_ref[: EDGE * part_rows, :] = zeros
        all_ref[(EDGE + 2 * bins) * part_rows :, :] = zeros
        all_ref[pl.ds(pl.multiple_of(own_at * part_rows, 8), bins * part_rows), :] = own[...]
        spread_lines(all_ref, other_at, other)
    ref_rows = ref_own.shape[0]
    row = lax.broadcasted_iota(jnp.int32, (ref_rows, FACTOR), 0)
    column = lax.broadcasted_iota(jnp.int32, (ref_rows, FACTOR), 1)
    twice = (lax.rem(column, ref_rows) == row).astype(jnp.float32)
    ref_all[:EDGE, :] = jnp.zeros((EDGE, FACTOR), jnp.float32)
    ref_all[EDGE + 2 * bins :, :] = jnp.zeros((EDGE, FACTOR), jnp.float32)
    for at, ref in ((own_at, ref_own), (other_at, ref_other)):
        ref_all[pl.ds(pl.multiple_of(at, 16), bins), :] = lax.dot_general(
            ref[...], twice, (((0,), (0,)), ((), ())), precision=PRECISE, preferred_element_type=jnp.float32
        )
    lane = lax.broadcasted_iota(jnp.int32, (1, FACTOR), 1)
    for at, message in enumerate(messages):
        step = at % (PLACES // 2)
        (first_bin, last_bin), _ = CHUNKS[at // (PLACES // 2)]
        body = (last_bin - first_bin) * part_rows
        start = window_start(((place >> 1) ^ step) * 2 + side, side, off_own, off_other) + EDGE
        rows = pl.ds(pl.multiple_of((start + first_bin) * part_rows, 8), body)
        message[:body, :] = re_all[rows, :]
        message[body : 2 * body, :] = im_all[rows, :]
        if first_bin == 0:
            for bin_num in range(REF_LINES):
                low = ref_all[pl.ds(start + bin_num, 1), :]
                high = ref_all[pl.ds(start + REF_LINES + bin_num, 1), :]
                message[2 * body + bin_num : 2 * body + bin_num + 1, :] = jnp.where(lane < HALF, low, high)


def phase_kernel(bins_total, off_own, off_other, out):
    place, side = lax.axis_index("az"), lax.axis_index("rg")
    start = window_start(place, side, off_own, off_other)
    shape = (HALF, FACTOR)
    kappa = lax.broadcasted_iota(jnp.int32, shape, 0)
    frequency = 2 * kappa + side + FACTOR * lax.broadcasted_iota(jnp.int32, shape, 1)
    total = FACTOR * FACTOR
    signed = jnp.where(frequency >= total // 2, frequency - total, frequency)
    az_freq = signed.astype(jnp.float32) / total
    az_square = az_freq * az_freq
    for bin_num in range(WINDOW):
        rg_index = (start + bin_num).astype(jnp.float32)
        rg_freq = (rg_index + 0.5) / (2 * bins_total) - 0.25
        base = (1.0 + rg_freq) * (1.0 + rg_freq)
        root = jnp.sqrt(base - az_square)
        cosine, sine = cos_sin_quarters(root * (PHASE_GAIN * 2 / math.pi))
        out[bin_num, 0] = cosine
        out[bin_num, 1] = sine


def parity_kernel(bins, has_ref, *refs):
    chunks, refs = refs[: PLACES // 2], refs[PLACES // 2 :]
    place, side = lax.axis_index("az"), lax.axis_index("rg")
    if has_ref:
        owners, keep, give, keep_ref = refs
    else:
        keep, give = refs
    sign = jnp.where(place >= PLACES // 2, -1.0, 1.0)
    even = side == 0
    keep_near, keep_far = jnp.where(even, 1.0, sign), jnp.where(even, 1.0, -sign)
    give_near, give_far = jnp.where(even, sign, 1.0), jnp.where(even, -sign, 1.0)
    middle = (place >> 1) & 1
    for step in range(2):
        near, far = chunks[step], chunks[step + 2]
        for line in range(2 * bins):
            read = slice(line * PART, (line + 1) * PART)
            write = pl.ds(pl.multiple_of(line * 2 * PART + (middle ^ step) * PART, 8), PART)
            near_value, far_value = near[read, :], far[read, :]
            keep[write, :] = near_value * keep_near + far_value * keep_far
            give[write, :] = near_value * give_near + far_value * give_far
    if has_ref:
        for which in range(2):
            step = (owners[which] >> 1) ^ (place >> 1)
            for other in range(PLACES // 2):

                @pl.when(step == other)
                def _():
                    value = chunks[other][2 * bins * PART :, :]
                    give[pl.ds(2 * bins * 2 * PART + which * REF_LINES, REF_LINES), :] = value
                    keep_ref[which] = value


def band_kernel(chunk, *refs):
    (first_bin, last_bin), (first_out, last_out) = CHUNKS[chunk]
    bins = last_bin - first_bin
    keep, got, keep_ref, got_ref, owners, phase, taps_own, taps_other = refs[:8]
    first_high, first_low, there_high, there_low, back_high, back_low, last_high, last_low, twists = refs[8:17]
    refs = refs[17:]
    if chunk:
        earlier, refs = refs[0], refs[1:]
    keep_out, give_out, spectra, band, picked = refs
    place, side = lax.axis_index("az"), lax.axis_index("rg")

    row = lax.broadcasted_iota(jnp.int32, (FACTOR, FACTOR), 0)
    column = lax.broadcasted_iota(jnp.int32, (FACTOR, FACTOR), 1)
    lane = lax.broadcasted_iota(jnp.int32, (REF_LINES, FACTOR), 1)
    ref_at = got_ref.shape[0] - 2 * REF_LINES
    lines = [
        jnp.where(
            (owners[which] & 1) == side,
            keep_ref[which],
            got_ref[ref_at + which * REF_LINES : ref_at + (which + 1) * REF_LINES, :],
        )
        for which in range(2)
    ]
    for block in range(2):
        spread = (row == column // 2 + block * HALF).astype(jnp.float32)
        wide = [
            jnp.dot(lines[which], spread, precision=PRECISE, preferred_element_type=jnp.float32) for which in range(2)
        ]
        ref_phase = jnp.where(lane < HALF, wide[1], wide[0])
        ref_cos, ref_sin = cos_sin_quarters(ref_phase * (2 / math.pi))
        picked[0, block * REF_LINES : (block + 1) * REF_LINES, :] = ref_cos
        picked[1, block * REF_LINES : (block + 1) * REF_LINES, :] = ref_sin

    first, last = (first_high[side], first_low[side]), (last_high[side], last_low[side])
    there, back = (there_high[...], there_low[...]), (back_high[...], back_low[...])
    twist_cos, twist_sin = twists[side, 0], twists[side, 1]
    width = 2 * PART
    for at in range(0, bins, 4):
        group = range(at, min(at + 4, bins))
        columns = [
            jnp.concatenate(
                [
                    ref[(part * bins + bin_num) * width : (part * bins + bin_num + 1) * width, :]
                    for part in range(2)
                    for ref in (keep, got)
                ],
                axis=0,
            )
            for bin_num in group
        ]
        passed = dot_split(first, split_bf16(jnp.concatenate(columns, axis=1)))
        rows = []
        for index in range(len(group)):
            real = passed[:HALF, index * FACTOR : (index + 1) * FACTOR]
            imag = passed[HALF:, index * FACTOR : (index + 1) * FACTOR]
            rows.append(
                jnp.concatenate([real * twist_cos + imag * twist_sin, imag * twist_cos - real * twist_sin], axis=1)
            )
        passed = dot_split(split_bf16(jnp.concatenate(rows, axis=0)), there)
        for index, bin_num in enumerate(group):
            real = passed[index * HALF : (index + 1) * HALF, :FACTOR]
            imag = passed[index * HALF : (index + 1) * HALF, FACTOR:]
            whole = first_bin + bin_num
            model_cos, model_sin = phase[whole, 0], phase[whole, 1]
            row_cos, row_sin = picked[0, whole : whole + 1, :], picked[1, whole : whole + 1, :]
            cosine = model_cos * row_cos - model_sin * row_sin
            sine = model_sin * row_cos + model_cos * row_sin
            spectra[bin_num, 0] = real * cosine - imag * sine
            spectra[bin_num, 1] = real * sine + imag * cosine

    bins_held = taps_own.shape[0]
    held = lax.div(place * OUT_BINS, bins_held) == side
    local = lax.rem(place * OUT_BINS, bins_held)
    outs = range(first_out, last_out)
    weights = {
        out: [jnp.where(held, taps_own[local + out, tap], taps_other[local + out, tap]) for tap in range(TAPS)]
        for out in outs
    }
    strip = 8
    for part in range(2):
        for at in range(0, HALF, strip):
            rows = slice(at, at + strip)
            sums = {}
            for bin_num in range(first_out, last_out + TAPS - 1):
                if bin_num < first_bin:
                    value = earlier[bin_num, part, rows]
                else:
                    value = spectra[bin_num - first_bin, part, rows]
                for out in outs:
                    if 0 <= bin_num - out < TAPS:
                        term = value * weights[out][bin_num - out]
                        sums[out] = sums[out] + term if out in sums else term
            for out in outs:
                line = (out - first_out) * HALF + at
                band[line : line + strip, part * FACTOR : (part + 1) * FACTOR] = sums[out]

    scale = 1.0 / (FACTOR * FACTOR)
    cos_table, sin_table = twist_cos * scale, twist_sin * scale
    for at in range(0, last_out - first_out, 4):
        passed = dot_split(split_bf16(band[at * HALF : (at + 4) * HALF, :]), back)
        columns = []
        for index in range(4):
            real = passed[index * HALF : (index + 1) * HALF, :FACTOR]
            imag = passed[index * HALF : (index + 1) * HALF, FACTOR:]
            columns.append(
                jnp.concatenate([real * cos_table - imag * sin_table, imag * cos_table + real * sin_table], axis=0)
            )
        passed = dot_split(last, split_bf16(jnp.concatenate(columns, axis=1)))
        for index in range(4):
            lines = slice((at + index) * HALF, (at + index + 1) * HALF)
            keep_out[lines, :] = passed[:HALF, index * FACTOR : (index + 1) * FACTOR]
            give_out[lines, :] = passed[HALF:, index * FACTOR : (index + 1) * FACTOR]


def join_kernel(outs, keep, got, *messages):
    place, side = lax.axis_index("az"), lax.axis_index("rg")
    quarter = lax.rem(place, PLACES // 2)
    sign = jnp.where(side == 0, 1.0, -1.0)
    for step, message in enumerate(messages):
        target = quarter ^ step
        top, middle = target >> 1, target & 1
        keep_factor, got_factor = jnp.where(top == 0, 1.0, sign), jnp.where(top == 0, 1.0, -sign)
        for line in range(2 * outs):
            read = pl.ds(pl.multiple_of(line * 2 * PART + middle * PART, 8), PART)
            message[line * PART : (line + 1) * PART, :] = keep[read, :] * keep_factor + got[read, :] * got_factor


def place_kernel(*refs):
    messages, (out_re, out_im, re_all, im_all) = refs[:-4], refs[-4:]
    bins, samples = out_re.shape
    place = lax.axis_index("az")
    for at, message in enumerate(messages):
        sender = (place >> 1) ^ (at % (PLACES // 2))
        _, (first_out, last_out) = CHUNKS[at // (PLACES // 2)]
        for out in range(last_out - first_out):
            line = pl.multiple_of((sender * OUT_BINS + first_out + out) * PART, 8)
            re_all[pl.ds(line, PART), :] = message[2 * out * PART : (2 * out + 1) * PART, :]
            im_all[pl.ds(line, PART), :] = message[(2 * out + 1) * PART : (2 * out + 2) * PART, :]
    for out, all_ref in ((out_re, re_all), (out_im, im_all)):
        for tile in range(0, bins, 8):
            for row in range(PART):
                out[tile : tile + 8, row * FACTOR : (row + 1) * FACTOR] = all_ref[
                    pl.ds(tile * PART + row, 8, stride=PART), :
                ]


VMEM = pl.BlockSpec(memory_space=pltpu.VMEM)
SMEM = pl.BlockSpec(memory_space=pltpu.SMEM)


def kernel_call(body, name, out_shape, operands, scratch=(), flops=0, count=10**6, limit=8):
    specs = [SMEM if operand.size <= 1024 else VMEM for operand in operands]
    return pl.pallas_call(
        body,
        out_shape=out_shape,
        in_specs=specs,
        out_specs=jax.tree.map(lambda _: VMEM, out_shape),
        scratch_shapes=[pltpu.VMEM(shape, jnp.float32) for shape in scratch],
        compiler_params=pltpu.CompilerParams(vmem_limit_bytes=limit * 1024 * 1024),
        cost_estimate=pl.CostEstimate(flops=flops, bytes_accessed=count, transcendentals=0),
        name=name,
    )(*operands)


def transposed_shards(raw_re, raw_im, ref_blocks, owners, offsets, taps):
    bins, samples = raw_re.shape

    def array(*shape):
        return jax.ShapeDtypeStruct(shape, jnp.float32)

    matrices, twists = dft_constants()
    tables = [jnp.asarray(part) for part in matrices] + [jnp.asarray(twists)]
    swap = functools.partial(lax.ppermute, axis_name="rg", perm=[(0, 1), (1, 0)])
    half = PLACES // 2
    ref_own = ref_blocks[0]
    offsets_other = swap(offsets)
    ref_other, re_other, im_other, taps_other = swap(ref_own), swap(raw_re), swap(raw_im), swap(taps)

    lines = kernel_call(spread_kernel, "spread", [array(bins * PART, FACTOR)] * 2, [raw_re, raw_im], count=2 * 10**6)
    shapes = []
    for (first_bin, last_bin), _ in CHUNKS:
        ref_lines = REF_LINES if first_bin == 0 else 0
        shapes += [array(2 * (last_bin - first_bin) * PART + ref_lines, FACTOR)] * half
    all_lines = (2 * bins + 2 * EDGE) * PART
    messages = kernel_call(
        pack_kernel,
        "pack",
        shapes,
        [*lines, re_other, im_other, ref_own, ref_other, offsets, offsets_other],
        scratch=[(all_lines, FACTOR), (all_lines, FACTOR), (2 * bins + 2 * EDGE, FACTOR)],
        count=4 * 10**6,
    )
    phases = kernel_call(
        functools.partial(phase_kernel, 2 * bins),
        "phase",
        array(WINDOW, 2, HALF, FACTOR),
        [offsets, offsets_other],
        flops=10**7,
    )

    routes = [
        [
            (chip * 2 + core, (((chip >> 1) ^ step) * 2 + core) * 2 + (chip & 1))
            for chip in range(PLACES)
            for core in range(2)
        ]
        for step in range(half)
    ]
    routes_back = [
        [
            (chip * 2 + core, (((chip % half) ^ step) * 2 + core) * 2 + chip // half)
            for chip in range(PLACES)
            for core in range(2)
        ]
        for step in range(half)
    ]
    arrived = [lax.ppermute(message, ("az", "rg"), routes[at % half]) for at, message in enumerate(messages)]

    results = []
    refs, earlier = None, []
    for chunk, ((first_bin, last_bin), (first_out, last_out)) in enumerate(CHUNKS):
        count, outs = last_bin - first_bin, last_out - first_out
        has_ref = chunk == 0
        size = 2 * count * 2 * PART
        shapes = [array(size, FACTOR), array(size + (2 * REF_LINES if has_ref else 0), FACTOR)]
        operands = arrived[chunk * half : (chunk + 1) * half]
        if has_ref:
            shapes.append(array(2, REF_LINES, FACTOR))
            operands = operands + [owners]
        parity = kernel_call(functools.partial(parity_kernel, count, has_ref), "parity", shapes, operands)
        keep, give = parity[:2]
        got = swap(give)
        if has_ref:
            refs = [parity[2], got]
        pieces = kernel_call(
            functools.partial(band_kernel, chunk),
            "band",
            [array(outs * HALF, FACTOR), array(outs * HALF, FACTOR), array(count, 2, HALF, FACTOR)],
            [keep, got, *refs, owners, phases, taps, taps_other, *tables, *earlier],
            scratch=[(outs * HALF, 2 * FACTOR), (2, 2 * REF_LINES, FACTOR)],
            flops=10**9,
            count=4 * 10**6,
            limit=16,
        )
        keep, give, spectra = pieces
        earlier = [spectra]
        sent = kernel_call(
            functools.partial(join_kernel, outs),
            "join",
            [array(2 * outs * PART, FACTOR)] * half,
            [keep, swap(give)],
        )
        results += [lax.ppermute(message, ("az", "rg"), route) for message, route in zip(sent, routes_back)]
    return kernel_call(
        place_kernel, "place", [array(bins, samples)] * 2, results, scratch=[(bins * PART, FACTOR)] * 2
    )


def solution(mesh):
    sizes = mesh.shape

    def whole(raw_re, raw_im, ref_blocks, owners, offsets, taps):
        line = raw_re.shape[1] // sizes["scene"]
        fits = (
            sizes["rg"] == 2
            and sizes["az"] == PLACES
            and raw_re.shape[0] == OUT_BINS * PLACES
            and line == FACTOR * FACTOR
            and ref_blocks.shape[1] == HALF
        )
        return jax.shard_map(
            transposed_shards if fits else butterfly_shards,
            mesh=mesh,
            in_specs=(
                P("rg", ("scene", "az")),
                P("rg", ("scene", "az")),
                P(("scene", "az"), None, "rg"),
                P("scene"),
                P("rg"),
                P("rg", None),
            ),
            out_specs=(P("rg", ("scene", "az")), P("rg", ("scene", "az"))),
            check_vma=False,
        )(raw_re, raw_im, ref_blocks, owners, offsets, taps)

    return whole
```

```python
import functools
import math

import jax
import jax.numpy as jnp
import numpy as np
from jax import lax
from jax.experimental import pallas as pl
from jax.experimental.pallas import tpu as pltpu
from jax.sharding import PartitionSpec as P

SPLIT = 4
TAPS = 8
REACH = 8
BLOCK = 16


PRECISE = lax.Precision.HIGHEST
PHASE_GAIN = 50.0


def partner_2(value, axis, stride):
    return lax.ppermute(value, axis, [(i, i ^ 1 << stride) for i in range(lax.axis_size(axis))])


def from_root(block, axis, source):
    block = jnp.where(lax.axis_index(axis) == source, block, jnp.zeros_like(block))
    return lax.psum(block, axis)


def padded_2(value, sides, width):
    for axis, dim in sides:
        size, length = (lax.axis_size(axis), value.shape[dim])
        up = [(i, (i + 1) % size) for i in range(size - 1)]
        down = [(j, i) for i, j in up]
        last = lax.slice_in_dim(value, length - width, length, axis=dim)
        initial = lax.slice_in_dim(value, 0, width, axis=dim)
        before = lax.ppermute(last, axis, up)
        after = lax.ppermute(initial, axis, down)
        value = jnp.concatenate([before, value, after], axis=dim)
    return value


def angles(numerator, denominator, sign_value):
    return sign_value * 2.0 * math.pi * numerator.astype(jnp.float32) / denominator


def rotate(signal, cosine, sine_part):
    real_part = signal[0] * cosine - signal[1] * sine_part
    imag_part = signal[0] * sine_part + signal[1] * cosine
    return jnp.stack([real_part, imag_part])


def dft_table(length_n, sign_value):
    counter = jnp.arange(length_n, dtype=jnp.int32)
    turn_count = counter[:, None] * counter[None, :] % length_n
    angle_set = angles(turn_count, length_n, sign_value)
    return (jnp.cos(angle_set), jnp.sin(angle_set))


def complex_apply(einsum_form, cosine, sine_part, signal):
    real_part = jnp.einsum(einsum_form, cosine, signal[0], precision=PRECISE) - jnp.einsum(
        einsum_form, sine_part, signal[1], precision=PRECISE
    )
    imag_part = jnp.einsum(einsum_form, cosine, signal[1], precision=PRECISE) + jnp.einsum(
        einsum_form, sine_part, signal[0], precision=PRECISE
    )
    return jnp.stack([real_part, imag_part])


def local_dft(signal, sign_value):
    rg_cols = signal.shape[1]
    az_rows = signal.shape[2]
    inner_len = az_rows // SPLIT
    shaped = signal.reshape(2, rg_cols, SPLIT, inner_len)
    first_cos, first_sin = dft_table(SPLIT, sign_value)
    first_pass = complex_apply("aj,cjk->cak", first_cos, first_sin, shaped)
    outer_idx = jnp.arange(SPLIT, dtype=jnp.int32)
    inner_idx = jnp.arange(inner_len, dtype=jnp.int32)
    twist = angles(outer_idx[:, None] * inner_idx[None, :] % az_rows, az_rows, sign_value)
    first_pass = rotate(first_pass, jnp.cos(twist)[None, :, :], jnp.sin(twist)[None, :, :])
    second_cos, second_sin = dft_table(inner_len, sign_value)
    second_pass = complex_apply("bk,cak->cba", second_cos, second_sin, first_pass)
    return second_pass.reshape(2, rg_cols, az_rows)


def butterfly_down(signal, az_place, bit_count):
    for bit_num in reversed(range(bit_count)):
        half_span = 1 << bit_num
        partner = partner_2(signal, "az", bit_num)
        is_upper = az_place >> bit_num & 1 == 1
        angle_set = angles(az_place % half_span, 2 * half_span, -1.0)
        difference = rotate(partner - signal, jnp.cos(angle_set), jnp.sin(angle_set))
        signal = jnp.where(is_upper, difference, signal + partner)
    return signal


def butterfly_up(signal, az_place, bit_count):
    for bit_num in range(bit_count):
        half_span = 1 << bit_num
        partner = partner_2(signal, "az", bit_num)
        is_upper = az_place >> bit_num & 1 == 1
        angle_set = angles(az_place % half_span, 2 * half_span, 1.0)
        cosine = jnp.cos(angle_set)
        sine_part = jnp.sin(angle_set)
        lower_new = (signal + rotate(partner, cosine, sine_part)) * 0.5
        upper_new = (partner - rotate(signal, cosine, sine_part)) * 0.5
        signal = jnp.where(is_upper, upper_new, lower_new)
    return signal


def butterfly_shards(raw_re, raw_im, ref_blocks, owners, offsets, taps):
    rg_cols = raw_re.shape[0]
    az_rows = raw_re.shape[1]
    az_count = lax.axis_size("az")
    az_place = lax.axis_index("az")
    bit_count = az_count.bit_length() - 1
    az_total = az_rows * az_count
    rg_total = rg_cols * lax.axis_size("rg")
    own_block = ref_blocks[0]
    lower_ref = from_root(own_block, "az", owners[0])
    upper_ref = from_root(own_block, "az", owners[1])
    signal = jnp.stack([raw_re, raw_im])
    signal = butterfly_down(signal, az_place, bit_count)
    column = jnp.zeros((), jnp.int32)
    for bit_num in range(bit_count):
        column = column + ((az_place >> bit_num & 1) << bit_count - 1 - bit_num)
    row_index = jnp.arange(az_rows, dtype=jnp.int32)
    twist = angles(row_index * column % az_total, az_total, -1.0)
    signal = rotate(signal, jnp.cos(twist)[None, :], jnp.sin(twist)[None, :])
    signal = local_dft(signal, -1.0)
    frequency = column + az_count * row_index
    signed = (frequency + az_total // 2) % az_total - az_total // 2
    az_freq = signed.astype(jnp.float32) / az_total
    rg_index = lax.axis_index("rg") * rg_cols + jnp.arange(rg_cols, dtype=jnp.int32)
    rg_freq = (rg_index.astype(jnp.float32) + 0.5) / (2 * rg_total) - 0.25
    model_phase = PHASE_GAIN * jnp.sqrt((1.0 + rg_freq)[:, None] ** 2 - az_freq[None, :] ** 2)
    ref_rows = own_block.shape[0]
    coarse = frequency * ref_rows // az_total
    slot_index = jnp.where(signed >= 0, ref_rows + coarse, coarse)
    one_hot = (jnp.arange(2 * ref_rows, dtype=jnp.int32)[:, None] == slot_index[None, :]).astype(
        jnp.float32
    )
    both_refs = jnp.concatenate([lower_ref, upper_ref], axis=0)
    picked = jnp.dot(both_refs.T, one_hot, precision=PRECISE)
    phase_all = model_phase + picked
    signal = rotate(signal, jnp.cos(phase_all), jnp.sin(phase_all))
    rim_width = REACH + TAPS // 2
    padded = padded_2(signal, (("rg", 1),), rim_width)
    offset_cols = jnp.repeat(offsets, BLOCK)
    local_cols = jnp.arange(rg_cols, dtype=jnp.int32)
    tap_index = jnp.arange(TAPS, dtype=jnp.int32)
    target = local_cols[:, None] + rim_width + offset_cols[:, None] + tap_index[None, :] - TAPS // 2
    padded_index = jnp.arange(rg_cols + 2 * rim_width, dtype=jnp.int32)
    hits = (padded_index[:, None, None] == target[None, :, :]).astype(jnp.float32)
    band_matrix = jnp.sum(hits * taps[None, :, :], axis=2)
    signal = jnp.einsum("zma,mi->zia", padded, band_matrix, precision=PRECISE)
    signal = local_dft(signal, 1.0) / az_rows
    twist_back = angles(row_index * column % az_total, az_total, 1.0)
    signal = rotate(signal, jnp.cos(twist_back)[None, :], jnp.sin(twist_back)[None, :])
    signal = butterfly_up(signal, az_place, bit_count)
    return (signal[0], signal[1])


FACTOR = 128
PLACES = 8
PART = FACTOR // PLACES
HALF = FACTOR // 2
OUT_BINS = 8
WINDOW = OUT_BINS + TAPS - 1
REF_LINES = 8
EDGE = 16
CHUNKS = (((0, WINDOW), (0, OUT_BINS)),)


def split_bf16(value):
    high = value.astype(jnp.bfloat16)
    low = (value - high.astype(jnp.float32)).astype(jnp.bfloat16)
    return high, low


def dot_split(left, right):
    left_high, left_low = left
    right_high, right_low = right
    dot = functools.partial(jnp.dot, preferred_element_type=jnp.float32)
    return dot(left_high, right_high) + (dot(left_high, right_low) + dot(left_low, right_high))


def both_bf16(matrix):
    high = matrix.astype(jnp.bfloat16)
    return high, (matrix - high.astype(np.float64)).astype(jnp.bfloat16)


def dft_constants():
    counter = np.arange(FACTOR)
    kappa = np.arange(HALF)
    first, last, twists = [], [], []
    for side in range(2):
        order = [(middle, low, line) for low in (side, 1 - side) for middle in range(2) for line in range(PART)]
        mine = np.array([(2 * middle + low) * PART + line for middle, low, line in order])
        angle = 2 * np.pi * (np.outer(2 * kappa + side, mine) % FACTOR) / FACTOR
        cosine, sine = np.cos(angle), np.sin(angle)
        first.append(np.block([[cosine, sine], [-sine, cosine]]))
        back_re, back_im = np.block([cosine.T, -sine.T]), np.block([sine.T, cosine.T])
        own, other = slice(0, HALF // 2), slice(HALF // 2, HALF)
        last.append(np.concatenate([back_re[own], back_im[own], back_re[other], back_im[other]]))
        twist = 2 * np.pi * np.outer(2 * kappa + side, counter) / FACTOR**2
        twists.append(np.stack([np.cos(twist), np.sin(twist)]))
    angle = 2 * np.pi * (np.outer(counter, counter) % FACTOR) / FACTOR
    cosine, sine = np.cos(angle), np.sin(angle)
    there = np.block([[cosine, -sine], [sine, cosine]])
    back = np.block([[cosine, sine], [-sine, cosine]])
    matrices = [both_bf16(matrix) for matrix in (np.stack(first), there, back, np.stack(last))]
    return [part for pair in matrices for part in pair], np.stack(twists).astype(np.float32)


def cos_sin_quarters(quarters):
    whole = jnp.floor(quarters + 0.5)
    rest = (quarters - whole) * (math.pi / 2)
    square = rest * rest
    sine = rest + rest * square * (
        -1.6666654611e-1 + square * (8.3321608736e-3 + square * (-1.9515295891e-4))
    )
    cosine = 1.0 - 0.5 * square + square * square * (
        4.166664568298827e-2 + square * (-1.388731625493765e-3 + square * 2.443315711809948e-5)
    )
    number = whole.astype(jnp.int32)
    odd = (number & 1) == 1
    turned_cos = jnp.where(odd, sine, cosine)
    turned_sin = jnp.where(odd, cosine, sine)
    cos_sign = jnp.where(((number + 1) & 2) == 2, -1.0, 1.0)
    sin_sign = jnp.where((number & 2) == 2, -1.0, 1.0)
    return turned_cos * cos_sign, turned_sin * sin_sign


def window_start(chip, side, offsets_own, offsets_other):
    block = chip * OUT_BINS // BLOCK
    blocks = offsets_own.shape[0]
    local = lax.rem(block, blocks)
    shift = jnp.where(lax.div(block, blocks) == side, offsets_own[local], offsets_other[local])
    return chip * OUT_BINS + shift - TAPS // 2


def spread_lines(target, base, source):
    bins, samples = source.shape
    part_rows = samples // FACTOR
    for tile in range(0, bins, 8):
        for row in range(part_rows):
            target[pl.ds((base + tile) * part_rows + row, 8, stride=part_rows), :] = source[
                tile : tile + 8, row * FACTOR : (row + 1) * FACTOR
            ]


def spread_kernel(re_raw, im_raw, ref_own, lines, halo, held, sems):
    bins = re_raw.shape[0]
    side = lax.axis_index("rg")
    copies = []
    for part, raw in enumerate((re_raw, im_raw)):
        for tile in range(bins // 8):
            at = part * (bins // 8) + tile
            copies.append(pltpu.make_async_copy(raw.at[pl.ds(tile * 8, 8)], held.at[at], sems.at[at]))
            copies[-1].start()
    ref_rows = ref_own.shape[0]
    row = lax.broadcasted_iota(jnp.int32, (ref_rows, FACTOR), 0)
    column = lax.broadcasted_iota(jnp.int32, (ref_rows, FACTOR), 1)
    twice = (lax.rem(column, ref_rows) == row).astype(jnp.float32)
    lines[2 * bins * PART :, :] = lax.dot_general(
        ref_own[...], twice, (((0,), (0,)), ((), ())), precision=PRECISE, preferred_element_type=jnp.float32
    )
    for at, copy in enumerate(copies):
        copy.wait()
        spread_lines(lines, at * 8, held.at[at])
    first = (1 - side) * (bins - EDGE)
    for part in range(2):
        rows = pl.ds(pl.multiple_of((part * bins + first) * PART, 8), EDGE * PART)
        halo[part * EDGE * PART : (part + 1) * EDGE * PART, :] = lines[rows, :]
    halo[2 * EDGE * PART :, :] = lines[pl.ds(pl.multiple_of(2 * bins * PART + first, 8), EDGE), :]


def pack_kernel(lines, halo, offsets, *refs):
    messages, (re_all, im_all, ref_all) = refs[:-3], refs[-3:]
    bins = re_all.shape[0] // PART - 2 * EDGE
    place, side = lax.axis_index("az"), lax.axis_index("rg")
    halo_at, empty_at = (1 - side) * (EDGE + bins), side * (EDGE + bins)
    for part, all_ref in enumerate((re_all, im_all, ref_all)):
        size = PART if part < 2 else 1
        edge = EDGE * size
        all_ref[edge : edge + bins * size, :] = lines[part * bins * PART : part * bins * PART + bins * size, :]
        halo_rows = slice(part * EDGE * PART, part * EDGE * PART + edge)
        all_ref[pl.ds(pl.multiple_of(halo_at * size, 8), edge), :] = halo[halo_rows, :]
        all_ref[pl.ds(pl.multiple_of(empty_at * size, 8), edge), :] = jnp.zeros((edge, FACTOR), jnp.float32)
    lane = lax.broadcasted_iota(jnp.int32, (1, FACTOR), 1)
    for at, message in enumerate(messages):
        step = at % (PLACES // 2)
        (first_bin, last_bin), _ = CHUNKS[at // (PLACES // 2)]
        body = (last_bin - first_bin) * PART
        chip = side * (PLACES // 2) + ((place >> 1) ^ step)
        start = window_start(chip, side, offsets, offsets) - side * bins + EDGE
        rows = pl.ds(pl.multiple_of((start + first_bin) * PART, 8), body)
        message[:body, :] = re_all[rows, :]
        message[body : 2 * body, :] = im_all[rows, :]
        if first_bin == 0:
            for bin_num in range(REF_LINES):
                low = ref_all[pl.ds(start + bin_num, 1), :]
                high = ref_all[pl.ds(start + REF_LINES + bin_num, 1), :]
                message[2 * body + bin_num : 2 * body + bin_num + 1, :] = jnp.where(lane < HALF, low, high)


def phase_kernel(bins_total, off_own, off_other, out):
    place, side = lax.axis_index("az"), lax.axis_index("rg")
    start = window_start(place, side, off_own, off_other)
    shape = (HALF, FACTOR)
    kappa = lax.broadcasted_iota(jnp.int32, shape, 0)
    frequency = 2 * kappa + side + FACTOR * lax.broadcasted_iota(jnp.int32, shape, 1)
    total = FACTOR * FACTOR
    signed = jnp.where(frequency >= total // 2, frequency - total, frequency)
    az_freq = signed.astype(jnp.float32) / total
    az_square = az_freq * az_freq
    for bin_num in range(WINDOW):
        rg_index = (start + bin_num).astype(jnp.float32)
        rg_freq = (rg_index + 0.5) / (2 * bins_total) - 0.25
        base = (1.0 + rg_freq) * (1.0 + rg_freq)
        root = jnp.sqrt(base - az_square)
        cosine, sine = cos_sin_quarters(root * (PHASE_GAIN * 2 / math.pi))
        out[bin_num, 0] = cosine
        out[bin_num, 1] = sine


def parity_kernel(bins, has_ref, *refs):
    chunks, refs = refs[: PLACES // 2], refs[PLACES // 2 :]
    place, side = lax.axis_index("az"), lax.axis_index("rg")
    if has_ref:
        owners, keep, give, keep_ref = refs
    else:
        keep, give = refs
    sign = jnp.where(((place >> 1) & 1) == 1, -1.0, 1.0)
    even = side == 0
    keep_near, keep_far = jnp.where(even, 1.0, sign), jnp.where(even, 1.0, -sign)
    give_near, give_far = jnp.where(even, sign, 1.0), jnp.where(even, -sign, 1.0)
    middle = place & 1
    for step in range(2):
        near, far = chunks[step], chunks[step + 2]
        for line in range(2 * bins):
            read = slice(line * PART, (line + 1) * PART)
            write = pl.ds(pl.multiple_of(line * 2 * PART + (middle ^ step) * PART, 8), PART)
            near_value, far_value = near[read, :], far[read, :]
            keep[write, :] = near_value * keep_near + far_value * keep_far
            give[write, :] = near_value * give_near + far_value * give_far
    if has_ref:
        for which in range(2):
            step = (owners[which] >> 1) ^ (place & (PLACES // 2 - 1))
            for other in range(PLACES // 2):

                @pl.when(step == other)
                def _():
                    value = chunks[other][2 * bins * PART :, :]
                    give[pl.ds(2 * bins * 2 * PART + which * REF_LINES, REF_LINES), :] = value
                    keep_ref[which] = value


def band_kernel(chunk, *refs):
    (first_bin, last_bin), (first_out, last_out) = CHUNKS[chunk]
    bins = last_bin - first_bin
    keep, got, keep_ref, got_ref, owners, phase, taps_own, taps_other = refs[:8]
    first_high, first_low, there_high, there_low, back_high, back_low, last_high, last_low, twists = refs[8:17]
    refs = refs[17:]
    if chunk:
        earlier, refs = refs[0], refs[1:]
    keep_out, give_out, spectra, band, picked = refs
    place, side = lax.axis_index("az"), lax.axis_index("rg")

    row = lax.broadcasted_iota(jnp.int32, (FACTOR, FACTOR), 0)
    column = lax.broadcasted_iota(jnp.int32, (FACTOR, FACTOR), 1)
    lane = lax.broadcasted_iota(jnp.int32, (REF_LINES, FACTOR), 1)
    ref_at = got_ref.shape[0] - 2 * REF_LINES
    lines = [
        jnp.where(
            (owners[which] & 1) == side,
            keep_ref[which],
            got_ref[ref_at + which * REF_LINES : ref_at + (which + 1) * REF_LINES, :],
        )
        for which in range(2)
    ]
    for block in range(2):
        spread = (row == column // 2 + block * HALF).astype(jnp.float32)
        wide = [
            jnp.dot(lines[which], spread, precision=PRECISE, preferred_element_type=jnp.float32) for which in range(2)
        ]
        ref_phase = jnp.where(lane < HALF, wide[1], wide[0])
        ref_cos, ref_sin = cos_sin_quarters(ref_phase * (2 / math.pi))
        picked[0, block * REF_LINES : (block + 1) * REF_LINES, :] = ref_cos
        picked[1, block * REF_LINES : (block + 1) * REF_LINES, :] = ref_sin

    first, last = (first_high[side], first_low[side]), (last_high[side], last_low[side])
    there, back = (there_high[...], there_low[...]), (back_high[...], back_low[...])
    twist_cos, twist_sin = twists[side, 0], twists[side, 1]
    width = 2 * PART
    for at in range(0, bins, 4):
        group = range(at, min(at + 4, bins))
        columns = [
            jnp.concatenate(
                [
                    ref[(part * bins + bin_num) * width : (part * bins + bin_num + 1) * width, :]
                    for part in range(2)
                    for ref in (keep, got)
                ],
                axis=0,
            )
            for bin_num in group
        ]
        passed = dot_split(first, split_bf16(jnp.concatenate(columns, axis=1)))
        rows = []
        for index in range(len(group)):
            real = passed[:HALF, index * FACTOR : (index + 1) * FACTOR]
            imag = passed[HALF:, index * FACTOR : (index + 1) * FACTOR]
            rows.append(
                jnp.concatenate([real * twist_cos + imag * twist_sin, imag * twist_cos - real * twist_sin], axis=1)
            )
        passed = dot_split(split_bf16(jnp.concatenate(rows, axis=0)), there)
        for index, bin_num in enumerate(group):
            real = passed[index * HALF : (index + 1) * HALF, :FACTOR]
            imag = passed[index * HALF : (index + 1) * HALF, FACTOR:]
            whole = first_bin + bin_num
            model_cos, model_sin = phase[whole, 0], phase[whole, 1]
            row_cos, row_sin = picked[0, whole : whole + 1, :], picked[1, whole : whole + 1, :]
            cosine = model_cos * row_cos - model_sin * row_sin
            sine = model_sin * row_cos + model_cos * row_sin
            spectra[bin_num, 0] = real * cosine - imag * sine
            spectra[bin_num, 1] = real * sine + imag * cosine

    bins_held = taps_own.shape[0]
    held = lax.div(place * OUT_BINS, bins_held) == side
    local = lax.rem(place * OUT_BINS, bins_held)
    outs = range(first_out, last_out)
    weights = {
        out: [jnp.where(held, taps_own[local + out, tap], taps_other[local + out, tap]) for tap in range(TAPS)]
        for out in outs
    }
    strip = 8
    for part in range(2):
        for at in range(0, HALF, strip):
            rows = slice(at, at + strip)
            sums = {}
            for bin_num in range(first_out, last_out + TAPS - 1):
                if bin_num < first_bin:
                    value = earlier[bin_num, part, rows]
                else:
                    value = spectra[bin_num - first_bin, part, rows]
                for out in outs:
                    if 0 <= bin_num - out < TAPS:
                        term = value * weights[out][bin_num - out]
                        sums[out] = sums[out] + term if out in sums else term
            for out in outs:
                line = (out - first_out) * HALF + at
                band[line : line + strip, part * FACTOR : (part + 1) * FACTOR] = sums[out]

    scale = 1.0 / (FACTOR * FACTOR)
    cos_table, sin_table = twist_cos * scale, twist_sin * scale
    for at in range(0, last_out - first_out, 4):
        passed = dot_split(split_bf16(band[at * HALF : (at + 4) * HALF, :]), back)
        columns = []
        for index in range(4):
            real = passed[index * HALF : (index + 1) * HALF, :FACTOR]
            imag = passed[index * HALF : (index + 1) * HALF, FACTOR:]
            columns.append(
                jnp.concatenate([real * cos_table - imag * sin_table, imag * cos_table + real * sin_table], axis=0)
            )
        passed = dot_split(last, split_bf16(jnp.concatenate(columns, axis=1)))
        for index in range(4):
            lines = slice((at + index) * HALF, (at + index + 1) * HALF)
            keep_out[lines, :] = passed[:HALF, index * FACTOR : (index + 1) * FACTOR]
            give_out[lines, :] = passed[HALF:, index * FACTOR : (index + 1) * FACTOR]


def join_kernel(outs, keep, got, *messages):
    place, side = lax.axis_index("az"), lax.axis_index("rg")
    quarter = lax.rem(place, PLACES // 2)
    sign = jnp.where(side == 0, 1.0, -1.0)
    for step, message in enumerate(messages):
        target = quarter ^ step
        top, middle = target >> 1, target & 1
        keep_factor, got_factor = jnp.where(top == 0, 1.0, sign), jnp.where(top == 0, 1.0, -sign)
        for line in range(2 * outs):
            read = pl.ds(pl.multiple_of(line * 2 * PART + middle * PART, 8), PART)
            message[line * PART : (line + 1) * PART, :] = keep[read, :] * keep_factor + got[read, :] * got_factor


def place_kernel(*refs):
    messages, (out_re, out_im, re_all, im_all) = refs[:-4], refs[-4:]
    bins, samples = out_re.shape
    place = lax.axis_index("az")
    for at, message in enumerate(messages):
        sender = (place >> 1) ^ (at % (PLACES // 2))
        _, (first_out, last_out) = CHUNKS[at // (PLACES // 2)]
        for out in range(last_out - first_out):
            line = pl.multiple_of((sender * OUT_BINS + first_out + out) * PART, 8)
            re_all[pl.ds(line, PART), :] = message[2 * out * PART : (2 * out + 1) * PART, :]
            im_all[pl.ds(line, PART), :] = message[(2 * out + 1) * PART : (2 * out + 2) * PART, :]
    for out, all_ref in ((out_re, re_all), (out_im, im_all)):
        for tile in range(0, bins, 8):
            for row in range(PART):
                out[tile : tile + 8, row * FACTOR : (row + 1) * FACTOR] = all_ref[
                    pl.ds(tile * PART + row, 8, stride=PART), :
                ]


VMEM = pl.BlockSpec(memory_space=pltpu.VMEM)
SMEM = pl.BlockSpec(memory_space=pltpu.SMEM)


def kernel_call(body, name, out_shape, operands, scratch=(), limit=8):
    specs = [SMEM if operand.size <= 1024 else VMEM for operand in operands]
    return pl.pallas_call(
        body,
        out_shape=out_shape,
        in_specs=specs,
        out_specs=jax.tree.map(lambda _: VMEM, out_shape),
        scratch_shapes=[pltpu.VMEM(shape, jnp.float32) for shape in scratch],
        compiler_params=pltpu.CompilerParams(vmem_limit_bytes=limit * 1024 * 1024),
        cost_estimate=pl.CostEstimate(flops=1, bytes_accessed=1, transcendentals=0),
        name=name,
    )(*operands)


def transposed_shards(raw_re, raw_im, ref_blocks, owners, offsets, taps):
    bins, samples = raw_re.shape

    def array(*shape):
        return jax.ShapeDtypeStruct(shape, jnp.float32)

    matrices, twists = dft_constants()
    tables = [jnp.asarray(part) for part in matrices] + [jnp.asarray(twists)]
    swap = functools.partial(lax.ppermute, axis_name="rg", perm=[(0, 1), (1, 0)])
    half = PLACES // 2
    lines, halo = pl.pallas_call(
        spread_kernel,
        out_shape=[array(2 * bins * PART + bins, FACTOR), array(2 * EDGE * PART + EDGE, FACTOR)],
        in_specs=[pl.BlockSpec(memory_space=pl.ANY)] * 2 + [VMEM],
        out_specs=[VMEM] * 2,
        scratch_shapes=[
            pltpu.VMEM((2 * bins // 8, 8, samples), jnp.float32),
            pltpu.SemaphoreType.DMA((2 * bins // 8,)),
        ],
        compiler_params=pltpu.CompilerParams(vmem_limit_bytes=8 * 1024 * 1024),
        cost_estimate=pl.CostEstimate(flops=1, bytes_accessed=1, transcendentals=0),
        name="spread",
    )(raw_re, raw_im, ref_blocks[0])
    halo = swap(halo)
    offsets_other, taps_other = swap(offsets), swap(taps)

    shapes = []
    for (first_bin, last_bin), _ in CHUNKS:
        ref_lines = REF_LINES if first_bin == 0 else 0
        shapes += [array(2 * (last_bin - first_bin) * PART + ref_lines, FACTOR)] * half
    all_bins = bins + 2 * EDGE
    messages = kernel_call(
        pack_kernel,
        "pack",
        shapes,
        [lines, halo, offsets],
        scratch=[(all_bins * PART, FACTOR), (all_bins * PART, FACTOR), (all_bins, FACTOR)],
    )
    phases = kernel_call(
        functools.partial(phase_kernel, 2 * bins),
        "phase",
        array(WINDOW, 2, HALF, FACTOR),
        [offsets, offsets_other],
    )

    routes = [
        [
            (chip * 2 + core, (core * half + ((chip >> 1) ^ step)) * 2 + (chip & 1))
            for chip in range(PLACES)
            for core in range(2)
        ]
        for step in range(half)
    ]
    routes_back = [
        [
            (chip * 2 + core, (((chip % half) ^ step) * 2 + core) * 2 + chip // half)
            for chip in range(PLACES)
            for core in range(2)
        ]
        for step in range(half)
    ]
    arrived = [lax.ppermute(message, ("az", "rg"), routes[at % half]) for at, message in enumerate(messages)]

    def send_back(sent):
        return [lax.ppermute(message, ("az", "rg"), route) for message, route in zip(sent, routes_back)]

    results = []
    refs, earlier = None, []
    for chunk, ((first_bin, last_bin), (first_out, last_out)) in enumerate(CHUNKS):
        count, outs = last_bin - first_bin, last_out - first_out
        has_ref = chunk == 0
        size = 2 * count * 2 * PART
        shapes = [array(size, FACTOR), array(size + (2 * REF_LINES if has_ref else 0), FACTOR)]
        operands = arrived[chunk * half : (chunk + 1) * half]
        if chunk == 0:
            *operands, phases = lax.optimization_barrier((*operands, phases))
        else:
            *operands, _ = lax.optimization_barrier((*operands, sent[0]))
            results += send_back(sent)
        if has_ref:
            shapes.append(array(2, REF_LINES, FACTOR))
            operands = operands + [owners]
        parity = kernel_call(functools.partial(parity_kernel, count, has_ref), "parity", shapes, operands)
        keep, give = parity[:2]
        got = swap(give)
        if has_ref:
            refs = [parity[2], got]
        pieces = kernel_call(
            functools.partial(band_kernel, chunk),
            "band",
            [array(outs * HALF, FACTOR), array(outs * HALF, FACTOR), array(count, 2, HALF, FACTOR)],
            [keep, got, *refs, owners, phases, taps, taps_other, *tables, *earlier],
            scratch=[(outs * HALF, 2 * FACTOR), (2, 2 * REF_LINES, FACTOR)],
                limit=16,
        )
        keep, give, spectra = pieces
        earlier = [spectra]
        sent = kernel_call(
            functools.partial(join_kernel, outs),
            "join",
            [array(2 * outs * PART, FACTOR)] * half,
            [keep, swap(give)],
        )
    results += send_back(sent)
    return kernel_call(
        place_kernel, "place", [array(bins, samples)] * 2, results, scratch=[(bins * PART, FACTOR)] * 2
    )


def solution(mesh):
    sizes = mesh.shape

    def whole(raw_re, raw_im, ref_blocks, owners, offsets, taps):
        line = raw_re.shape[1] // sizes["scene"]
        fits = (
            sizes["rg"] == 2
            and sizes["az"] == PLACES
            and raw_re.shape[0] == OUT_BINS * PLACES
            and line == FACTOR * FACTOR
            and ref_blocks.shape[1] == HALF
        )
        return jax.shard_map(
            transposed_shards if fits else butterfly_shards,
            mesh=mesh,
            in_specs=(
                P("rg", ("scene", "az")),
                P("rg", ("scene", "az")),
                P(("scene", "az"), None, "rg"),
                P("scene"),
                P("rg"),
                P("rg", None),
            ),
            out_specs=(P("rg", ("scene", "az")), P("rg", ("scene", "az"))),
            check_vma=False,
        )(raw_re, raw_im, ref_blocks, owners, offsets, taps)

    return whole
```

```python
import functools
import math

import jax
import jax.numpy as jnp
import numpy as np
from jax import lax
from jax.experimental import pallas as pl
from jax.experimental.pallas import tpu as pltpu
from jax.sharding import PartitionSpec as P

SPLIT = 4
TAPS = 8
REACH = 8
BLOCK = 16


PRECISE = lax.Precision.HIGHEST
PHASE_GAIN = 50.0


def partner_2(value, axis, stride):
    return lax.ppermute(value, axis, [(i, i ^ 1 << stride) for i in range(lax.axis_size(axis))])


def from_root(block, axis, source):
    block = jnp.where(lax.axis_index(axis) == source, block, jnp.zeros_like(block))
    return lax.psum(block, axis)


def padded_2(value, sides, width):
    for axis, dim in sides:
        size, length = (lax.axis_size(axis), value.shape[dim])
        up = [(i, (i + 1) % size) for i in range(size - 1)]
        down = [(j, i) for i, j in up]
        last = lax.slice_in_dim(value, length - width, length, axis=dim)
        initial = lax.slice_in_dim(value, 0, width, axis=dim)
        before = lax.ppermute(last, axis, up)
        after = lax.ppermute(initial, axis, down)
        value = jnp.concatenate([before, value, after], axis=dim)
    return value


def angles(numerator, denominator, sign_value):
    return sign_value * 2.0 * math.pi * numerator.astype(jnp.float32) / denominator


def rotate(signal, cosine, sine_part):
    real_part = signal[0] * cosine - signal[1] * sine_part
    imag_part = signal[0] * sine_part + signal[1] * cosine
    return jnp.stack([real_part, imag_part])


def dft_table(length_n, sign_value):
    counter = jnp.arange(length_n, dtype=jnp.int32)
    turn_count = counter[:, None] * counter[None, :] % length_n
    angle_set = angles(turn_count, length_n, sign_value)
    return (jnp.cos(angle_set), jnp.sin(angle_set))


def complex_apply(einsum_form, cosine, sine_part, signal):
    real_part = jnp.einsum(einsum_form, cosine, signal[0], precision=PRECISE) - jnp.einsum(
        einsum_form, sine_part, signal[1], precision=PRECISE
    )
    imag_part = jnp.einsum(einsum_form, cosine, signal[1], precision=PRECISE) + jnp.einsum(
        einsum_form, sine_part, signal[0], precision=PRECISE
    )
    return jnp.stack([real_part, imag_part])


def local_dft(signal, sign_value):
    rg_cols = signal.shape[1]
    az_rows = signal.shape[2]
    inner_len = az_rows // SPLIT
    shaped = signal.reshape(2, rg_cols, SPLIT, inner_len)
    first_cos, first_sin = dft_table(SPLIT, sign_value)
    first_pass = complex_apply("aj,cjk->cak", first_cos, first_sin, shaped)
    outer_idx = jnp.arange(SPLIT, dtype=jnp.int32)
    inner_idx = jnp.arange(inner_len, dtype=jnp.int32)
    twist = angles(outer_idx[:, None] * inner_idx[None, :] % az_rows, az_rows, sign_value)
    first_pass = rotate(first_pass, jnp.cos(twist)[None, :, :], jnp.sin(twist)[None, :, :])
    second_cos, second_sin = dft_table(inner_len, sign_value)
    second_pass = complex_apply("bk,cak->cba", second_cos, second_sin, first_pass)
    return second_pass.reshape(2, rg_cols, az_rows)


def butterfly_down(signal, az_place, bit_count):
    for bit_num in reversed(range(bit_count)):
        half_span = 1 << bit_num
        partner = partner_2(signal, "az", bit_num)
        is_upper = az_place >> bit_num & 1 == 1
        angle_set = angles(az_place % half_span, 2 * half_span, -1.0)
        difference = rotate(partner - signal, jnp.cos(angle_set), jnp.sin(angle_set))
        signal = jnp.where(is_upper, difference, signal + partner)
    return signal


def butterfly_up(signal, az_place, bit_count):
    for bit_num in range(bit_count):
        half_span = 1 << bit_num
        partner = partner_2(signal, "az", bit_num)
        is_upper = az_place >> bit_num & 1 == 1
        angle_set = angles(az_place % half_span, 2 * half_span, 1.0)
        cosine = jnp.cos(angle_set)
        sine_part = jnp.sin(angle_set)
        lower_new = (signal + rotate(partner, cosine, sine_part)) * 0.5
        upper_new = (partner - rotate(signal, cosine, sine_part)) * 0.5
        signal = jnp.where(is_upper, upper_new, lower_new)
    return signal


def butterfly_shards(raw_re, raw_im, ref_blocks, owners, offsets, taps):
    rg_cols = raw_re.shape[0]
    az_rows = raw_re.shape[1]
    az_count = lax.axis_size("az")
    az_place = lax.axis_index("az")
    bit_count = az_count.bit_length() - 1
    az_total = az_rows * az_count
    rg_total = rg_cols * lax.axis_size("rg")
    own_block = ref_blocks[0]
    lower_ref = from_root(own_block, "az", owners[0])
    upper_ref = from_root(own_block, "az", owners[1])
    signal = jnp.stack([raw_re, raw_im])
    signal = butterfly_down(signal, az_place, bit_count)
    column = jnp.zeros((), jnp.int32)
    for bit_num in range(bit_count):
        column = column + ((az_place >> bit_num & 1) << bit_count - 1 - bit_num)
    row_index = jnp.arange(az_rows, dtype=jnp.int32)
    twist = angles(row_index * column % az_total, az_total, -1.0)
    signal = rotate(signal, jnp.cos(twist)[None, :], jnp.sin(twist)[None, :])
    signal = local_dft(signal, -1.0)
    frequency = column + az_count * row_index
    signed = (frequency + az_total // 2) % az_total - az_total // 2
    az_freq = signed.astype(jnp.float32) / az_total
    rg_index = lax.axis_index("rg") * rg_cols + jnp.arange(rg_cols, dtype=jnp.int32)
    rg_freq = (rg_index.astype(jnp.float32) + 0.5) / (2 * rg_total) - 0.25
    model_phase = PHASE_GAIN * jnp.sqrt((1.0 + rg_freq)[:, None] ** 2 - az_freq[None, :] ** 2)
    ref_rows = own_block.shape[0]
    coarse = frequency * ref_rows // az_total
    slot_index = jnp.where(signed >= 0, ref_rows + coarse, coarse)
    one_hot = (jnp.arange(2 * ref_rows, dtype=jnp.int32)[:, None] == slot_index[None, :]).astype(
        jnp.float32
    )
    both_refs = jnp.concatenate([lower_ref, upper_ref], axis=0)
    picked = jnp.dot(both_refs.T, one_hot, precision=PRECISE)
    phase_all = model_phase + picked
    signal = rotate(signal, jnp.cos(phase_all), jnp.sin(phase_all))
    rim_width = REACH + TAPS // 2
    padded = padded_2(signal, (("rg", 1),), rim_width)
    offset_cols = jnp.repeat(offsets, BLOCK)
    local_cols = jnp.arange(rg_cols, dtype=jnp.int32)
    tap_index = jnp.arange(TAPS, dtype=jnp.int32)
    target = local_cols[:, None] + rim_width + offset_cols[:, None] + tap_index[None, :] - TAPS // 2
    padded_index = jnp.arange(rg_cols + 2 * rim_width, dtype=jnp.int32)
    hits = (padded_index[:, None, None] == target[None, :, :]).astype(jnp.float32)
    band_matrix = jnp.sum(hits * taps[None, :, :], axis=2)
    signal = jnp.einsum("zma,mi->zia", padded, band_matrix, precision=PRECISE)
    signal = local_dft(signal, 1.0) / az_rows
    twist_back = angles(row_index * column % az_total, az_total, 1.0)
    signal = rotate(signal, jnp.cos(twist_back)[None, :], jnp.sin(twist_back)[None, :])
    signal = butterfly_up(signal, az_place, bit_count)
    return (signal[0], signal[1])


FACTOR = 128
PLACES = 8
PART = FACTOR // PLACES
HALF = FACTOR // 2
OUT_BINS = 8
WINDOW = OUT_BINS + TAPS - 1
REF_LINES = 8
EDGE = 16
STEPS = (2, 3, 1, 0)
CHUNKS = (((0, WINDOW), (0, OUT_BINS)),)


def split_bf16(value):
    high = value.astype(jnp.bfloat16)
    low = (value - high.astype(jnp.float32)).astype(jnp.bfloat16)
    return high, low


def dot_split(left, right):
    left_high, left_low = left
    right_high, right_low = right
    dot = functools.partial(jnp.dot, preferred_element_type=jnp.float32)
    return dot(left_high, right_high) + (dot(left_high, right_low) + dot(left_low, right_high))


def both_bf16(matrix):
    high = matrix.astype(jnp.bfloat16)
    return high, (matrix - high.astype(np.float64)).astype(jnp.bfloat16)


def dft_constants():
    counter = np.arange(FACTOR)
    kappa = np.arange(HALF)
    first, last, twists = [], [], []
    for side in range(2):
        order = [(middle, low, line) for low in (side, 1 - side) for middle in range(2) for line in range(PART)]
        mine = np.array([(2 * middle + low) * PART + line for middle, low, line in order])
        angle = 2 * np.pi * (np.outer(2 * kappa + side, mine) % FACTOR) / FACTOR
        cosine, sine = np.cos(angle), np.sin(angle)
        first.append(np.block([[cosine, sine], [-sine, cosine]]))
        back_re, back_im = np.block([cosine.T, -sine.T]), np.block([sine.T, cosine.T])
        own, other = slice(0, HALF // 2), slice(HALF // 2, HALF)
        last.append(np.concatenate([back_re[own], back_im[own], back_re[other], back_im[other]]))
        twist = 2 * np.pi * np.outer(2 * kappa + side, counter) / FACTOR**2
        twists.append(np.stack([np.cos(twist), np.sin(twist)]))
    angle = 2 * np.pi * (np.outer(counter, counter) % FACTOR) / FACTOR
    cosine, sine = np.cos(angle), np.sin(angle)
    there = np.block([[cosine, -sine], [sine, cosine]])
    back = np.block([[cosine, sine], [-sine, cosine]])
    matrices = [both_bf16(matrix) for matrix in (np.stack(first), there, back, np.stack(last))]
    return [part for pair in matrices for part in pair], np.stack(twists).astype(np.float32)


def cos_sin_quarters(quarters):
    whole = jnp.floor(quarters + 0.5)
    rest = (quarters - whole) * (math.pi / 2)
    square = rest * rest
    sine = rest + rest * square * (
        -1.6666654611e-1 + square * (8.3321608736e-3 + square * (-1.9515295891e-4))
    )
    cosine = 1.0 - 0.5 * square + square * square * (
        4.166664568298827e-2 + square * (-1.388731625493765e-3 + square * 2.443315711809948e-5)
    )
    number = whole.astype(jnp.int32)
    odd = (number & 1) == 1
    turned_cos = jnp.where(odd, sine, cosine)
    turned_sin = jnp.where(odd, cosine, sine)
    cos_sign = jnp.where(((number + 1) & 2) == 2, -1.0, 1.0)
    sin_sign = jnp.where((number & 2) == 2, -1.0, 1.0)
    return turned_cos * cos_sign, turned_sin * sin_sign


def window_start(chip, side, offsets_own, offsets_other):
    block = chip * OUT_BINS // BLOCK
    blocks = offsets_own.shape[0]
    local = lax.rem(block, blocks)
    shift = jnp.where(lax.div(block, blocks) == side, offsets_own[local], offsets_other[local])
    return chip * OUT_BINS + shift - TAPS // 2


def spread_lines(target, base, source):
    bins, samples = source.shape
    part_rows = samples // FACTOR
    for tile in range(0, bins, 8):
        for row in range(part_rows):
            target[pl.ds((base + tile) * part_rows + row, 8, stride=part_rows), :] = source[
                tile : tile + 8, row * FACTOR : (row + 1) * FACTOR
            ]


def spread_kernel(re_own, im_own, re_lines, im_lines):
    at = pl.program_id(0) * 8
    for target, source in ((re_lines, re_own), (im_lines, im_own)):
        for row in range(PART):
            target[pl.ds(at * PART + row, 8, stride=PART), :] = source[:, row * FACTOR : (row + 1) * FACTOR]


def pack_kernel(re_lines, im_lines, re_other, im_other, ref_own, ref_other, off_own, off_other, *refs):
    messages, (re_all, im_all, ref_all) = refs[:-3], refs[-3:]
    bins, samples = re_other.shape
    part_rows = samples // FACTOR
    place, side = lax.axis_index("az"), lax.axis_index("rg")
    own_at, other_at = EDGE + side * bins, EDGE + (1 - side) * bins
    zeros = jnp.zeros((EDGE * part_rows, FACTOR), jnp.float32)
    for all_ref, own, other in ((re_all, re_lines, re_other), (im_all, im_lines, im_other)):
        all_ref[: EDGE * part_rows, :] = zeros
        all_ref[(EDGE + 2 * bins) * part_rows :, :] = zeros
        all_ref[pl.ds(pl.multiple_of(own_at * part_rows, 8), bins * part_rows), :] = own[...]
        spread_lines(all_ref, other_at, other)
    ref_rows = ref_own.shape[0]
    row = lax.broadcasted_iota(jnp.int32, (ref_rows, FACTOR), 0)
    column = lax.broadcasted_iota(jnp.int32, (ref_rows, FACTOR), 1)
    twice = (lax.rem(column, ref_rows) == row).astype(jnp.float32)
    ref_all[:EDGE, :] = jnp.zeros((EDGE, FACTOR), jnp.float32)
    ref_all[EDGE + 2 * bins :, :] = jnp.zeros((EDGE, FACTOR), jnp.float32)
    for at, ref in ((own_at, ref_own), (other_at, ref_other)):
        ref_all[pl.ds(pl.multiple_of(at, 16), bins), :] = lax.dot_general(
            ref[...], twice, (((0,), (0,)), ((), ())), precision=PRECISE, preferred_element_type=jnp.float32
        )
    lane = lax.broadcasted_iota(jnp.int32, (1, FACTOR), 1)
    for at, message in enumerate(messages):
        step = at % (PLACES // 2)
        (first_bin, last_bin), _ = CHUNKS[at // (PLACES // 2)]
        body = (last_bin - first_bin) * part_rows
        start = window_start(((place >> 1) ^ step) * 2 + side, side, off_own, off_other) + EDGE
        rows = pl.ds(pl.multiple_of((start + first_bin) * part_rows, 8), body)
        message[:body, :] = re_all[rows, :]
        message[body : 2 * body, :] = im_all[rows, :]
        if first_bin == 0:
            for bin_num in range(REF_LINES):
                low = ref_all[pl.ds(start + bin_num, 1), :]
                high = ref_all[pl.ds(start + REF_LINES + bin_num, 1), :]
                message[2 * body + bin_num : 2 * body + bin_num + 1, :] = jnp.where(lane < HALF, low, high)


def phase_kernel(bins_total, off_own, off_other, out):
    place, side = lax.axis_index("az"), lax.axis_index("rg")
    start = window_start(place, side, off_own, off_other)
    shape = (HALF, FACTOR)
    kappa = lax.broadcasted_iota(jnp.int32, shape, 0)
    frequency = 2 * kappa + side + FACTOR * lax.broadcasted_iota(jnp.int32, shape, 1)
    total = FACTOR * FACTOR
    signed = jnp.where(frequency >= total // 2, frequency - total, frequency)
    az_freq = signed.astype(jnp.float32) / total
    az_square = az_freq * az_freq
    for bin_num in range(WINDOW):
        rg_index = (start + bin_num).astype(jnp.float32)
        rg_freq = (rg_index + 0.5) / (2 * bins_total) - 0.25
        base = (1.0 + rg_freq) * (1.0 + rg_freq)
        root = jnp.sqrt(base - az_square)
        cosine, sine = cos_sin_quarters(root * (PHASE_GAIN * 2 / math.pi))
        out[bin_num, 0] = cosine
        out[bin_num, 1] = sine


def parity_kernel(bins, has_ref, *refs):
    chunks = dict(zip(STEPS, refs))
    refs = refs[PLACES // 2 :]
    place, side = lax.axis_index("az"), lax.axis_index("rg")
    if has_ref:
        owners, keep, give, keep_ref = refs
    else:
        keep, give = refs
    sign = jnp.where(place >= PLACES // 2, -1.0, 1.0)
    even = side == 0
    keep_near, keep_far = jnp.where(even, 1.0, sign), jnp.where(even, 1.0, -sign)
    give_near, give_far = jnp.where(even, sign, 1.0), jnp.where(even, -sign, 1.0)
    middle = (place >> 1) & 1
    for step in range(2):
        near, far = chunks[step], chunks[step + 2]
        for line in range(2 * bins):
            read = slice(line * PART, (line + 1) * PART)
            write = pl.ds(pl.multiple_of(line * 2 * PART + (middle ^ step) * PART, 8), PART)
            near_value, far_value = near[read, :], far[read, :]
            keep[write, :] = near_value * keep_near + far_value * keep_far
            give[write, :] = near_value * give_near + far_value * give_far
    if has_ref:
        for which in range(2):
            step = (owners[which] >> 1) ^ (place >> 1)
            for other in range(PLACES // 2):

                @pl.when(step == other)
                def _():
                    value = chunks[other][2 * bins * PART :, :]
                    give[pl.ds(2 * bins * 2 * PART + which * REF_LINES, REF_LINES), :] = value
                    keep_ref[which] = value


def band_kernel(chunk, *refs):
    (first_bin, last_bin), (first_out, last_out) = CHUNKS[chunk]
    bins = last_bin - first_bin
    keep, got, keep_ref, got_ref, owners, phase, taps_own, taps_other = refs[:8]
    first_high, first_low, there_high, there_low, back_high, back_low, last_high, last_low, twists = refs[8:17]
    refs = refs[17:]
    if chunk:
        earlier, refs = refs[0], refs[1:]
    keep_out, give_out, spectra, band, picked = refs
    place, side = lax.axis_index("az"), lax.axis_index("rg")

    row = lax.broadcasted_iota(jnp.int32, (FACTOR, FACTOR), 0)
    column = lax.broadcasted_iota(jnp.int32, (FACTOR, FACTOR), 1)
    lane = lax.broadcasted_iota(jnp.int32, (REF_LINES, FACTOR), 1)
    ref_at = got_ref.shape[0] - 2 * REF_LINES
    lines = [
        jnp.where(
            (owners[which] & 1) == side,
            keep_ref[which],
            got_ref[ref_at + which * REF_LINES : ref_at + (which + 1) * REF_LINES, :],
        )
        for which in range(2)
    ]
    for block in range(2):
        spread = (row == column // 2 + block * HALF).astype(jnp.float32)
        wide = [
            jnp.dot(lines[which], spread, precision=PRECISE, preferred_element_type=jnp.float32) for which in range(2)
        ]
        ref_phase = jnp.where(lane < HALF, wide[1], wide[0])
        ref_cos, ref_sin = cos_sin_quarters(ref_phase * (2 / math.pi))
        picked[0, block * REF_LINES : (block + 1) * REF_LINES, :] = ref_cos
        picked[1, block * REF_LINES : (block + 1) * REF_LINES, :] = ref_sin

    first, last = (first_high[side], first_low[side]), (last_high[side], last_low[side])
    there, back = (there_high[...], there_low[...]), (back_high[...], back_low[...])
    twist_cos, twist_sin = twists[side, 0], twists[side, 1]
    width = 2 * PART
    for at in range(0, bins, 4):
        group = range(at, min(at + 4, bins))
        columns = [
            jnp.concatenate(
                [
                    ref[(part * bins + bin_num) * width : (part * bins + bin_num + 1) * width, :]
                    for part in range(2)
                    for ref in (keep, got)
                ],
                axis=0,
            )
            for bin_num in group
        ]
        passed = dot_split(first, split_bf16(jnp.concatenate(columns, axis=1)))
        rows = []
        for index in range(len(group)):
            real = passed[:HALF, index * FACTOR : (index + 1) * FACTOR]
            imag = passed[HALF:, index * FACTOR : (index + 1) * FACTOR]
            rows.append(
                jnp.concatenate([real * twist_cos + imag * twist_sin, imag * twist_cos - real * twist_sin], axis=1)
            )
        passed = dot_split(split_bf16(jnp.concatenate(rows, axis=0)), there)
        for index, bin_num in enumerate(group):
            real = passed[index * HALF : (index + 1) * HALF, :FACTOR]
            imag = passed[index * HALF : (index + 1) * HALF, FACTOR:]
            whole = first_bin + bin_num
            model_cos, model_sin = phase[whole, 0], phase[whole, 1]
            row_cos, row_sin = picked[0, whole : whole + 1, :], picked[1, whole : whole + 1, :]
            cosine = model_cos * row_cos - model_sin * row_sin
            sine = model_sin * row_cos + model_cos * row_sin
            spectra[bin_num, 0] = real * cosine - imag * sine
            spectra[bin_num, 1] = real * sine + imag * cosine

    bins_held = taps_own.shape[0]
    held = lax.div(place * OUT_BINS, bins_held) == side
    local = lax.rem(place * OUT_BINS, bins_held)
    outs = range(first_out, last_out)
    weights = {
        out: [jnp.where(held, taps_own[local + out, tap], taps_other[local + out, tap]) for tap in range(TAPS)]
        for out in outs
    }
    strip = 8
    for part in range(2):
        for at in range(0, HALF, strip):
            rows = slice(at, at + strip)
            sums = {}
            for bin_num in range(first_out, last_out + TAPS - 1):
                if bin_num < first_bin:
                    value = earlier[bin_num, part, rows]
                else:
                    value = spectra[bin_num - first_bin, part, rows]
                for out in outs:
                    if 0 <= bin_num - out < TAPS:
                        term = value * weights[out][bin_num - out]
                        sums[out] = sums[out] + term if out in sums else term
            for out in outs:
                line = (out - first_out) * HALF + at
                band[line : line + strip, part * FACTOR : (part + 1) * FACTOR] = sums[out]

    scale = 1.0 / (FACTOR * FACTOR)
    cos_table, sin_table = twist_cos * scale, twist_sin * scale
    for at in range(0, last_out - first_out, 4):
        passed = dot_split(split_bf16(band[at * HALF : (at + 4) * HALF, :]), back)
        columns = []
        for index in range(4):
            real = passed[index * HALF : (index + 1) * HALF, :FACTOR]
            imag = passed[index * HALF : (index + 1) * HALF, FACTOR:]
            columns.append(
                jnp.concatenate([real * cos_table - imag * sin_table, imag * cos_table + real * sin_table], axis=0)
            )
        passed = dot_split(last, split_bf16(jnp.concatenate(columns, axis=1)))
        for index in range(4):
            lines = slice((at + index) * HALF, (at + index + 1) * HALF)
            keep_out[lines, :] = passed[:HALF, index * FACTOR : (index + 1) * FACTOR]
            give_out[lines, :] = passed[HALF:, index * FACTOR : (index + 1) * FACTOR]


def join_kernel(outs, keep, got, *messages):
    place, side = lax.axis_index("az"), lax.axis_index("rg")
    quarter = lax.rem(place, PLACES // 2)
    sign = jnp.where(side == 0, 1.0, -1.0)
    for step, message in enumerate(messages):
        target = quarter ^ step
        top, middle = target >> 1, target & 1
        keep_factor, got_factor = jnp.where(top == 0, 1.0, sign), jnp.where(top == 0, 1.0, -sign)
        for line in range(2 * outs):
            read = pl.ds(pl.multiple_of(line * 2 * PART + middle * PART, 8), PART)
            message[line * PART : (line + 1) * PART, :] = keep[read, :] * keep_factor + got[read, :] * got_factor


def place_kernel(*refs):
    messages, (out_re, out_im, re_all, im_all) = refs[:-4], refs[-4:]
    bins, samples = out_re.shape
    place = lax.axis_index("az")
    for at, message in enumerate(messages):
        sender = (place >> 1) ^ (at % (PLACES // 2))
        _, (first_out, last_out) = CHUNKS[at // (PLACES // 2)]
        for out in range(last_out - first_out):
            line = pl.multiple_of((sender * OUT_BINS + first_out + out) * PART, 8)
            re_all[pl.ds(line, PART), :] = message[2 * out * PART : (2 * out + 1) * PART, :]
            im_all[pl.ds(line, PART), :] = message[(2 * out + 1) * PART : (2 * out + 2) * PART, :]
    for out, all_ref in ((out_re, re_all), (out_im, im_all)):
        for tile in range(0, bins, 8):
            for row in range(PART):
                out[tile : tile + 8, row * FACTOR : (row + 1) * FACTOR] = all_ref[
                    pl.ds(tile * PART + row, 8, stride=PART), :
                ]


VMEM = pl.BlockSpec(memory_space=pltpu.VMEM)
SMEM = pl.BlockSpec(memory_space=pltpu.SMEM)


def kernel_call(body, name, out_shape, operands, scratch=(), flops=0, count=10**6, limit=8):
    specs = [SMEM if operand.size <= 1024 else VMEM for operand in operands]
    return pl.pallas_call(
        body,
        out_shape=out_shape,
        in_specs=specs,
        out_specs=jax.tree.map(lambda _: VMEM, out_shape),
        scratch_shapes=[pltpu.VMEM(shape, jnp.float32) for shape in scratch],
        compiler_params=pltpu.CompilerParams(vmem_limit_bytes=limit * 1024 * 1024),
        cost_estimate=pl.CostEstimate(flops=flops, bytes_accessed=count, transcendentals=0),
        name=name,
    )(*operands)


def transposed_shards(raw_re, raw_im, ref_blocks, owners, offsets, taps):
    bins, samples = raw_re.shape

    def array(*shape):
        return jax.ShapeDtypeStruct(shape, jnp.float32)

    matrices, twists = dft_constants()
    tables = [jnp.asarray(part) for part in matrices] + [jnp.asarray(twists)]
    swap = functools.partial(lax.ppermute, axis_name="rg", perm=[(0, 1), (1, 0)])
    half = PLACES // 2
    ref_own = ref_blocks[0]
    offsets_other = swap(offsets)
    ref_other, re_other, im_other, taps_other = swap(ref_own), swap(raw_re), swap(raw_im), swap(taps)

    lines = pl.pallas_call(
        spread_kernel,
        out_shape=[array(bins * PART, FACTOR)] * 2,
        grid=(bins // 8,),
        in_specs=[pl.BlockSpec((8, samples), lambda i: (i, 0))] * 2,
        out_specs=[pl.BlockSpec((bins * PART, FACTOR), lambda i: (0, 0))] * 2,
        cost_estimate=pl.CostEstimate(flops=1, bytes_accessed=2 * 10**6, transcendentals=0),
        name="spread",
    )(raw_re, raw_im)
    shapes = []
    for (first_bin, last_bin), _ in CHUNKS:
        ref_lines = REF_LINES if first_bin == 0 else 0
        shapes += [array(2 * (last_bin - first_bin) * PART + ref_lines, FACTOR)] * half
    all_lines = (2 * bins + 2 * EDGE) * PART
    messages = kernel_call(
        pack_kernel,
        "pack",
        shapes,
        [*lines, re_other, im_other, ref_own, ref_other, offsets, offsets_other],
        scratch=[(all_lines, FACTOR), (all_lines, FACTOR), (2 * bins + 2 * EDGE, FACTOR)],
        count=4 * 10**6,
    )
    phases = kernel_call(
        functools.partial(phase_kernel, 2 * bins),
        "phase",
        array(WINDOW, 2, HALF, FACTOR),
        [offsets, offsets_other],
        flops=10**7,
    )

    routes = [
        [
            (chip * 2 + core, (((chip >> 1) ^ step) * 2 + core) * 2 + (chip & 1))
            for chip in range(PLACES)
            for core in range(2)
        ]
        for step in range(half)
    ]
    routes_back = [
        [
            (chip * 2 + core, (((chip % half) ^ step) * 2 + core) * 2 + chip // half)
            for chip in range(PLACES)
            for core in range(2)
        ]
        for step in range(half)
    ]
    arrived = [
        lax.ppermute(messages[chunk * half + step], ("az", "rg"), routes[step])
        for chunk in range(len(CHUNKS))
        for step in STEPS
    ]

    results = []
    refs, earlier = None, []
    for chunk, ((first_bin, last_bin), (first_out, last_out)) in enumerate(CHUNKS):
        count, outs = last_bin - first_bin, last_out - first_out
        has_ref = chunk == 0
        size = 2 * count * 2 * PART
        shapes = [array(size, FACTOR), array(size + (2 * REF_LINES if has_ref else 0), FACTOR)]
        operands = arrived[chunk * half : (chunk + 1) * half]
        if chunk == 0:
            *operands, phases, taps_other = lax.optimization_barrier((*operands, phases, taps_other))
        if has_ref:
            shapes.append(array(2, REF_LINES, FACTOR))
            operands = operands + [owners]
        parity = kernel_call(functools.partial(parity_kernel, count, has_ref), "parity", shapes, operands)
        keep, give = parity[:2]
        got = swap(give)
        if has_ref:
            refs = [parity[2], got]
        pieces = kernel_call(
            functools.partial(band_kernel, chunk),
            "band",
            [array(outs * HALF, FACTOR), array(outs * HALF, FACTOR), array(count, 2, HALF, FACTOR)],
            [keep, got, *refs, owners, phases, taps, taps_other, *tables, *earlier],
            scratch=[(outs * HALF, 2 * FACTOR), (2, 2 * REF_LINES, FACTOR)],
            flops=10**9,
            count=4 * 10**6,
            limit=16,
        )
        keep, give, spectra = pieces
        earlier = [spectra]
        sent = kernel_call(
            functools.partial(join_kernel, outs),
            "join",
            [array(2 * outs * PART, FACTOR)] * half,
            [keep, swap(give)],
        )
        results += [lax.ppermute(message, ("az", "rg"), route) for message, route in zip(sent, routes_back)]
    return kernel_call(
        place_kernel, "place", [array(bins, samples)] * 2, results, scratch=[(bins * PART, FACTOR)] * 2
    )


def solution(mesh):
    sizes = mesh.shape

    def whole(raw_re, raw_im, ref_blocks, owners, offsets, taps):
        line = raw_re.shape[1] // sizes["scene"]
        fits = (
            sizes["rg"] == 2
            and sizes["az"] == PLACES
            and raw_re.shape[0] == OUT_BINS * PLACES
            and line == FACTOR * FACTOR
            and ref_blocks.shape[1] == HALF
        )
        return jax.shard_map(
            transposed_shards if fits else butterfly_shards,
            mesh=mesh,
            in_specs=(
                P("rg", ("scene", "az")),
                P("rg", ("scene", "az")),
                P(("scene", "az"), None, "rg"),
                P("scene"),
                P("rg"),
                P("rg", None),
            ),
            out_specs=(P("rg", ("scene", "az")), P("rg", ("scene", "az"))),
            check_vma=False,
        )(raw_re, raw_im, ref_blocks, owners, offsets, taps)

    return whole
```

```python
import functools
import math

import jax
import jax.numpy as jnp
import numpy as np
from jax import lax
from jax.experimental import pallas as pl
from jax.experimental.pallas import tpu as pltpu
from jax.sharding import PartitionSpec as P

SPLIT = 4
TAPS = 8
REACH = 8
BLOCK = 16


PRECISE = lax.Precision.HIGHEST
PHASE_GAIN = 50.0


def partner_2(value, axis, stride):
    return lax.ppermute(value, axis, [(i, i ^ 1 << stride) for i in range(lax.axis_size(axis))])


def from_root(block, axis, source):
    block = jnp.where(lax.axis_index(axis) == source, block, jnp.zeros_like(block))
    return lax.psum(block, axis)


def padded_2(value, sides, width):
    for axis, dim in sides:
        size, length = (lax.axis_size(axis), value.shape[dim])
        up = [(i, (i + 1) % size) for i in range(size - 1)]
        down = [(j, i) for i, j in up]
        last = lax.slice_in_dim(value, length - width, length, axis=dim)
        initial = lax.slice_in_dim(value, 0, width, axis=dim)
        before = lax.ppermute(last, axis, up)
        after = lax.ppermute(initial, axis, down)
        value = jnp.concatenate([before, value, after], axis=dim)
    return value


def angles(numerator, denominator, sign_value):
    return sign_value * 2.0 * math.pi * numerator.astype(jnp.float32) / denominator


def rotate(signal, cosine, sine_part):
    real_part = signal[0] * cosine - signal[1] * sine_part
    imag_part = signal[0] * sine_part + signal[1] * cosine
    return jnp.stack([real_part, imag_part])


def dft_table(length_n, sign_value):
    counter = jnp.arange(length_n, dtype=jnp.int32)
    turn_count = counter[:, None] * counter[None, :] % length_n
    angle_set = angles(turn_count, length_n, sign_value)
    return (jnp.cos(angle_set), jnp.sin(angle_set))


def complex_apply(einsum_form, cosine, sine_part, signal):
    real_part = jnp.einsum(einsum_form, cosine, signal[0], precision=PRECISE) - jnp.einsum(
        einsum_form, sine_part, signal[1], precision=PRECISE
    )
    imag_part = jnp.einsum(einsum_form, cosine, signal[1], precision=PRECISE) + jnp.einsum(
        einsum_form, sine_part, signal[0], precision=PRECISE
    )
    return jnp.stack([real_part, imag_part])


def local_dft(signal, sign_value):
    rg_cols = signal.shape[1]
    az_rows = signal.shape[2]
    inner_len = az_rows // SPLIT
    shaped = signal.reshape(2, rg_cols, SPLIT, inner_len)
    first_cos, first_sin = dft_table(SPLIT, sign_value)
    first_pass = complex_apply("aj,cjk->cak", first_cos, first_sin, shaped)
    outer_idx = jnp.arange(SPLIT, dtype=jnp.int32)
    inner_idx = jnp.arange(inner_len, dtype=jnp.int32)
    twist = angles(outer_idx[:, None] * inner_idx[None, :] % az_rows, az_rows, sign_value)
    first_pass = rotate(first_pass, jnp.cos(twist)[None, :, :], jnp.sin(twist)[None, :, :])
    second_cos, second_sin = dft_table(inner_len, sign_value)
    second_pass = complex_apply("bk,cak->cba", second_cos, second_sin, first_pass)
    return second_pass.reshape(2, rg_cols, az_rows)


def butterfly_down(signal, az_place, bit_count):
    for bit_num in reversed(range(bit_count)):
        half_span = 1 << bit_num
        partner = partner_2(signal, "az", bit_num)
        is_upper = az_place >> bit_num & 1 == 1
        angle_set = angles(az_place % half_span, 2 * half_span, -1.0)
        difference = rotate(partner - signal, jnp.cos(angle_set), jnp.sin(angle_set))
        signal = jnp.where(is_upper, difference, signal + partner)
    return signal


def butterfly_up(signal, az_place, bit_count):
    for bit_num in range(bit_count):
        half_span = 1 << bit_num
        partner = partner_2(signal, "az", bit_num)
        is_upper = az_place >> bit_num & 1 == 1
        angle_set = angles(az_place % half_span, 2 * half_span, 1.0)
        cosine = jnp.cos(angle_set)
        sine_part = jnp.sin(angle_set)
        lower_new = (signal + rotate(partner, cosine, sine_part)) * 0.5
        upper_new = (partner - rotate(signal, cosine, sine_part)) * 0.5
        signal = jnp.where(is_upper, upper_new, lower_new)
    return signal


def butterfly_shards(raw_re, raw_im, ref_blocks, owners, offsets, taps):
    rg_cols = raw_re.shape[0]
    az_rows = raw_re.shape[1]
    az_count = lax.axis_size("az")
    az_place = lax.axis_index("az")
    bit_count = az_count.bit_length() - 1
    az_total = az_rows * az_count
    rg_total = rg_cols * lax.axis_size("rg")
    own_block = ref_blocks[0]
    lower_ref = from_root(own_block, "az", owners[0])
    upper_ref = from_root(own_block, "az", owners[1])
    signal = jnp.stack([raw_re, raw_im])
    signal = butterfly_down(signal, az_place, bit_count)
    column = jnp.zeros((), jnp.int32)
    for bit_num in range(bit_count):
        column = column + ((az_place >> bit_num & 1) << bit_count - 1 - bit_num)
    row_index = jnp.arange(az_rows, dtype=jnp.int32)
    twist = angles(row_index * column % az_total, az_total, -1.0)
    signal = rotate(signal, jnp.cos(twist)[None, :], jnp.sin(twist)[None, :])
    signal = local_dft(signal, -1.0)
    frequency = column + az_count * row_index
    signed = (frequency + az_total // 2) % az_total - az_total // 2
    az_freq = signed.astype(jnp.float32) / az_total
    rg_index = lax.axis_index("rg") * rg_cols + jnp.arange(rg_cols, dtype=jnp.int32)
    rg_freq = (rg_index.astype(jnp.float32) + 0.5) / (2 * rg_total) - 0.25
    model_phase = PHASE_GAIN * jnp.sqrt((1.0 + rg_freq)[:, None] ** 2 - az_freq[None, :] ** 2)
    ref_rows = own_block.shape[0]
    coarse = frequency * ref_rows // az_total
    slot_index = jnp.where(signed >= 0, ref_rows + coarse, coarse)
    one_hot = (jnp.arange(2 * ref_rows, dtype=jnp.int32)[:, None] == slot_index[None, :]).astype(
        jnp.float32
    )
    both_refs = jnp.concatenate([lower_ref, upper_ref], axis=0)
    picked = jnp.dot(both_refs.T, one_hot, precision=PRECISE)
    phase_all = model_phase + picked
    signal = rotate(signal, jnp.cos(phase_all), jnp.sin(phase_all))
    rim_width = REACH + TAPS // 2
    padded = padded_2(signal, (("rg", 1),), rim_width)
    offset_cols = jnp.repeat(offsets, BLOCK)
    local_cols = jnp.arange(rg_cols, dtype=jnp.int32)
    tap_index = jnp.arange(TAPS, dtype=jnp.int32)
    target = local_cols[:, None] + rim_width + offset_cols[:, None] + tap_index[None, :] - TAPS // 2
    padded_index = jnp.arange(rg_cols + 2 * rim_width, dtype=jnp.int32)
    hits = (padded_index[:, None, None] == target[None, :, :]).astype(jnp.float32)
    band_matrix = jnp.sum(hits * taps[None, :, :], axis=2)
    signal = jnp.einsum("zma,mi->zia", padded, band_matrix, precision=PRECISE)
    signal = local_dft(signal, 1.0) / az_rows
    twist_back = angles(row_index * column % az_total, az_total, 1.0)
    signal = rotate(signal, jnp.cos(twist_back)[None, :], jnp.sin(twist_back)[None, :])
    signal = butterfly_up(signal, az_place, bit_count)
    return (signal[0], signal[1])


FACTOR = 128
PLACES = 8
PART = FACTOR // PLACES
HALF = FACTOR // 2
OUT_BINS = 8
WINDOW = OUT_BINS + TAPS - 1
REF_LINES = 8
EDGE = 16
STEPS = (2, 3, 1, 0)
CHUNKS = (((0, WINDOW), (0, OUT_BINS)),)


def split_bf16(value, axis):
    high = value.astype(jnp.bfloat16)
    low = (value - high.astype(jnp.float32)).astype(jnp.bfloat16)
    return jnp.concatenate([high, low, high], axis=axis)


def dot(left, right):
    return jnp.dot(left, right, preferred_element_type=jnp.float32)


def both_bf16(matrix, axis):
    high = matrix.astype(jnp.bfloat16)
    low = (matrix - high.astype(np.float64)).astype(jnp.bfloat16)
    return np.concatenate([high, high, low], axis=axis)


def dft_constants():
    counter = np.arange(FACTOR)
    kappa = np.arange(HALF)
    near, far, last, twists = [], [], [], []
    for side in range(2):
        order = [(middle, low, line) for low in (side, 1 - side) for middle in range(2) for line in range(PART)]
        mine = np.array([(2 * middle + low) * PART + line for middle, low, line in order])
        angle = 2 * np.pi * (np.outer(2 * kappa + side, mine) % FACTOR) / FACTOR
        cosine, sine = np.cos(angle), np.sin(angle)
        whole = np.block([[cosine, sine], [-sine, cosine]])
        quarters = np.split(whole, 4, axis=1)
        near.append(np.concatenate(quarters[0::2], axis=1))
        far.append(np.concatenate(quarters[1::2], axis=1))
        back_re, back_im = np.block([cosine.T, -sine.T]), np.block([sine.T, cosine.T])
        own, other = slice(0, HALF // 2), slice(HALF // 2, HALF)
        last.append(np.concatenate([back_re[own], back_im[own], back_re[other], back_im[other]]))
        twist = 2 * np.pi * np.outer(2 * kappa + side, counter) / FACTOR**2
        twists.append(np.stack([np.cos(twist), np.sin(twist)]))
    angle = 2 * np.pi * (np.outer(counter, counter) % FACTOR) / FACTOR
    cosine, sine = np.cos(angle), np.sin(angle)
    there = np.block([[cosine, -sine], [sine, cosine]])
    back = np.block([[cosine, sine], [-sine, cosine]])
    matrices = [
        both_bf16(np.stack(near), 2),
        both_bf16(np.stack(far), 2),
        both_bf16(there, 0),
        both_bf16(back, 0),
        both_bf16(np.stack(last), 2),
    ]
    return matrices, np.stack(twists).astype(np.float32)


def cos_sin_quarters(quarters):
    whole = jnp.floor(quarters + 0.5)
    rest = (quarters - whole) * (math.pi / 2)
    square = rest * rest
    sine = rest + rest * square * (
        -1.6666654611e-1 + square * (8.3321608736e-3 + square * (-1.9515295891e-4))
    )
    cosine = 1.0 - 0.5 * square + square * square * (
        4.166664568298827e-2 + square * (-1.388731625493765e-3 + square * 2.443315711809948e-5)
    )
    number = whole.astype(jnp.int32)
    odd = (number & 1) == 1
    turned_cos = jnp.where(odd, sine, cosine)
    turned_sin = jnp.where(odd, cosine, sine)
    cos_sign = jnp.where(((number + 1) & 2) == 2, -1.0, 1.0)
    sin_sign = jnp.where((number & 2) == 2, -1.0, 1.0)
    return turned_cos * cos_sign, turned_sin * sin_sign


def window_start(chip, side, offsets_own, offsets_other):
    block = chip * OUT_BINS // BLOCK
    blocks = offsets_own.shape[0]
    local = lax.rem(block, blocks)
    shift = jnp.where(lax.div(block, blocks) == side, offsets_own[local], offsets_other[local])
    return chip * OUT_BINS + shift - TAPS // 2


def spread_lines(target, base, source):
    bins, samples = source.shape
    part_rows = samples // FACTOR
    for tile in range(0, bins, 8):
        for row in range(part_rows):
            target[pl.ds((base + tile) * part_rows + row, 8, stride=part_rows), :] = source[
                tile : tile + 8, row * FACTOR : (row + 1) * FACTOR
            ]


def pack_kernel(re_lines, im_lines, re_other, im_other, ref_own, ref_other, off_own, off_other, *refs):
    messages, (re_all, im_all, ref_all) = refs[:-3], refs[-3:]
    bins, samples = re_other.shape
    part_rows = samples // FACTOR
    place, side = lax.axis_index("az"), lax.axis_index("rg")
    own_at, other_at = EDGE + side * bins, EDGE + (1 - side) * bins
    zeros = jnp.zeros((EDGE * part_rows, FACTOR), jnp.float32)
    for all_ref, own, other in ((re_all, re_lines, re_other), (im_all, im_lines, im_other)):
        all_ref[: EDGE * part_rows, :] = zeros
        all_ref[(EDGE + 2 * bins) * part_rows :, :] = zeros
        all_ref[pl.ds(pl.multiple_of(own_at * part_rows, 8), bins * part_rows), :] = own[...]
        spread_lines(all_ref, other_at, other)
    ref_all[:EDGE, :] = jnp.zeros((EDGE, FACTOR), jnp.float32)
    ref_all[EDGE + 2 * bins :, :] = jnp.zeros((EDGE, FACTOR), jnp.float32)
    for at, ref in ((own_at, ref_own), (other_at, ref_other)):
        ref_all[pl.ds(pl.multiple_of(at, 16), bins), :] = jnp.concatenate([ref[...], ref[...]], axis=1)
    lane = lax.broadcasted_iota(jnp.int32, (1, FACTOR), 1)
    for at, message in enumerate(messages):
        step = at % (PLACES // 2)
        (first_bin, last_bin), _ = CHUNKS[at // (PLACES // 2)]
        body = (last_bin - first_bin) * part_rows
        start = window_start(((place >> 1) ^ step) * 2 + side, side, off_own, off_other) + EDGE
        rows = pl.ds(pl.multiple_of((start + first_bin) * part_rows, 8), body)
        message[:body, :] = re_all[rows, :]
        message[body : 2 * body, :] = im_all[rows, :]
        if first_bin == 0:
            for bin_num in range(REF_LINES):
                low = ref_all[pl.ds(start + bin_num, 1), :]
                high = ref_all[pl.ds(start + REF_LINES + bin_num, 1), :]
                message[2 * body + bin_num : 2 * body + bin_num + 1, :] = jnp.where(lane < HALF, low, high)


def phase_kernel(bins_total, off_own, off_other, out):
    place, side = lax.axis_index("az"), lax.axis_index("rg")
    start = window_start(place, side, off_own, off_other)
    shape = (HALF, FACTOR)
    kappa = lax.broadcasted_iota(jnp.int32, shape, 0)
    frequency = 2 * kappa + side + FACTOR * lax.broadcasted_iota(jnp.int32, shape, 1)
    total = FACTOR * FACTOR
    signed = jnp.where(frequency >= total // 2, frequency - total, frequency)
    az_freq = signed.astype(jnp.float32) / total
    az_square = az_freq * az_freq
    for bin_num in range(WINDOW):
        rg_index = (start + bin_num).astype(jnp.float32)
        rg_freq = (rg_index + 0.5) / (2 * bins_total) - 0.25
        base = (1.0 + rg_freq) * (1.0 + rg_freq)
        root = jnp.sqrt(base - az_square)
        cosine, sine = cos_sin_quarters(root * (PHASE_GAIN * 2 / math.pi))
        out[bin_num, 0] = cosine
        out[bin_num, 1] = sine


def parity_kernel(bins, has_ref, *refs):
    chunks = dict(zip(STEPS, refs))
    refs = refs[PLACES // 2 :]
    place, side = lax.axis_index("az"), lax.axis_index("rg")
    if has_ref:
        owners, keep, give, keep_ref = refs
    else:
        keep, give = refs
    sign = jnp.where(place >= PLACES // 2, -1.0, 1.0)
    even = side == 0
    keep_near, keep_far = jnp.where(even, 1.0, sign), jnp.where(even, 1.0, -sign)
    give_near, give_far = jnp.where(even, sign, 1.0), jnp.where(even, -sign, 1.0)
    middle = (place >> 1) & 1
    for step in range(2):
        near, far = chunks[step], chunks[step + 2]
        for line in range(2 * bins):
            read = slice(line * PART, (line + 1) * PART)
            write = pl.ds(pl.multiple_of(line * 2 * PART + (middle ^ step) * PART, 8), PART)
            near_value, far_value = near[read, :], far[read, :]
            keep[write, :] = near_value * keep_near + far_value * keep_far
            give[write, :] = near_value * give_near + far_value * give_far
    if has_ref:
        for which in range(2):
            step = (owners[which] >> 1) ^ (place >> 1)
            for other in range(PLACES // 2):

                @pl.when(step == other)
                def _():
                    value = chunks[other][2 * bins * PART :, :]
                    give[pl.ds(2 * bins * 2 * PART + which * REF_LINES, REF_LINES), :] = value
                    keep_ref[which] = value


def gather_lines(ref, bins, group):
    width = 2 * PART
    columns = [
        jnp.concatenate(
            [ref[(part * bins + bin_num) * width : (part * bins + bin_num + 1) * width, :] for part in range(2)], axis=0
        )
        for bin_num in group
    ]
    return jnp.concatenate(columns, axis=1)


def bin_groups(bins):
    return [range(at, min(at + 4, bins)) for at in range(0, bins, 4)]


def near_kernel(bins, keep, near, out):
    matrix = near[lax.axis_index("rg")]
    for index, group in enumerate(bin_groups(bins)):
        out[index, :, : len(group) * FACTOR] = dot(matrix, split_bf16(gather_lines(keep, bins, group), 0))


def band_kernel(chunk, *refs):
    (first_bin, last_bin), (first_out, last_out) = CHUNKS[chunk]
    bins = last_bin - first_bin
    partial, got, keep_ref, got_ref, owners, phase, taps_own, taps_other = refs[:8]
    far, there, back, last, twists = refs[8:13]
    refs = refs[13:]
    if chunk:
        earlier, refs = refs[0], refs[1:]
    keep_out, give_out, spectra, band, picked = refs
    place, side = lax.axis_index("az"), lax.axis_index("rg")

    row = lax.broadcasted_iota(jnp.int32, (FACTOR, FACTOR), 0)
    column = lax.broadcasted_iota(jnp.int32, (FACTOR, FACTOR), 1)
    lane = lax.broadcasted_iota(jnp.int32, (REF_LINES, FACTOR), 1)
    ref_at = got_ref.shape[0] - 2 * REF_LINES
    lines = [
        jnp.where(
            (owners[which] & 1) == side,
            keep_ref[which],
            got_ref[ref_at + which * REF_LINES : ref_at + (which + 1) * REF_LINES, :],
        )
        for which in range(2)
    ]
    for block in range(2):
        spread = (row == column // 2 + block * HALF).astype(jnp.float32)
        wide = [
            jnp.dot(lines[which], spread, precision=PRECISE, preferred_element_type=jnp.float32) for which in range(2)
        ]
        ref_phase = jnp.where(lane < HALF, wide[1], wide[0])
        ref_cos, ref_sin = cos_sin_quarters(ref_phase * (2 / math.pi))
        picked[0, block * REF_LINES : (block + 1) * REF_LINES, :] = ref_cos
        picked[1, block * REF_LINES : (block + 1) * REF_LINES, :] = ref_sin

    far, last, there, back = far[side], last[side], there[...], back[...]
    twist_cos, twist_sin = twists[side, 0], twists[side, 1]
    for number, group in enumerate(bin_groups(bins)):
        passed = partial[number, :, : len(group) * FACTOR] + dot(far, split_bf16(gather_lines(got, bins, group), 0))
        rows = []
        for index in range(len(group)):
            real = passed[:HALF, index * FACTOR : (index + 1) * FACTOR]
            imag = passed[HALF:, index * FACTOR : (index + 1) * FACTOR]
            rows.append(
                jnp.concatenate([real * twist_cos + imag * twist_sin, imag * twist_cos - real * twist_sin], axis=1)
            )
        passed = dot(split_bf16(jnp.concatenate(rows, axis=0), 1), there)
        for index, bin_num in enumerate(group):
            real = passed[index * HALF : (index + 1) * HALF, :FACTOR]
            imag = passed[index * HALF : (index + 1) * HALF, FACTOR:]
            whole = first_bin + bin_num
            model_cos, model_sin = phase[whole, 0], phase[whole, 1]
            row_cos, row_sin = picked[0, whole : whole + 1, :], picked[1, whole : whole + 1, :]
            cosine = model_cos * row_cos - model_sin * row_sin
            sine = model_sin * row_cos + model_cos * row_sin
            spectra[bin_num, 0] = real * cosine - imag * sine
            spectra[bin_num, 1] = real * sine + imag * cosine

    bins_held = taps_own.shape[0]
    held = lax.div(place * OUT_BINS, bins_held) == side
    local = lax.rem(place * OUT_BINS, bins_held)
    outs = range(first_out, last_out)
    weights = {
        out: [jnp.where(held, taps_own[local + out, tap], taps_other[local + out, tap]) for tap in range(TAPS)]
        for out in outs
    }
    strip = 8
    for part in range(2):
        for at in range(0, HALF, strip):
            rows = slice(at, at + strip)
            sums = {}
            for bin_num in range(first_out, last_out + TAPS - 1):
                if bin_num < first_bin:
                    value = earlier[bin_num, part, rows]
                else:
                    value = spectra[bin_num - first_bin, part, rows]
                for out in outs:
                    if 0 <= bin_num - out < TAPS:
                        term = value * weights[out][bin_num - out]
                        sums[out] = sums[out] + term if out in sums else term
            for out in outs:
                line = (out - first_out) * HALF + at
                band[line : line + strip, part * FACTOR : (part + 1) * FACTOR] = sums[out]

    scale = 1.0 / (FACTOR * FACTOR)
    cos_table, sin_table = twist_cos * scale, twist_sin * scale
    for at in range(0, last_out - first_out, 4):
        passed = dot(split_bf16(band[at * HALF : (at + 4) * HALF, :], 1), back)
        columns = []
        for index in range(4):
            real = passed[index * HALF : (index + 1) * HALF, :FACTOR]
            imag = passed[index * HALF : (index + 1) * HALF, FACTOR:]
            columns.append(
                jnp.concatenate([real * cos_table - imag * sin_table, imag * cos_table + real * sin_table], axis=0)
            )
        passed = dot(last, split_bf16(jnp.concatenate(columns, axis=1), 0))
        for index in range(4):
            lines = slice((at + index) * HALF, (at + index + 1) * HALF)
            keep_out[lines, :] = passed[:HALF, index * FACTOR : (index + 1) * FACTOR]
            give_out[lines, :] = passed[HALF:, index * FACTOR : (index + 1) * FACTOR]


def join_kernel(outs, keep, got, *messages):
    place, side = lax.axis_index("az"), lax.axis_index("rg")
    quarter = lax.rem(place, PLACES // 2)
    sign = jnp.where(side == 0, 1.0, -1.0)
    for step, message in enumerate(messages):
        target = quarter ^ step
        top, middle = target >> 1, target & 1
        keep_factor, got_factor = jnp.where(top == 0, 1.0, sign), jnp.where(top == 0, 1.0, -sign)
        for line in range(2 * outs):
            read = pl.ds(pl.multiple_of(line * 2 * PART + middle * PART, 8), PART)
            message[line * PART : (line + 1) * PART, :] = keep[read, :] * keep_factor + got[read, :] * got_factor


def place_kernel(*refs):
    messages, (out_re, out_im, re_all, im_all) = refs[:-4], refs[-4:]
    bins, samples = out_re.shape
    place = lax.axis_index("az")
    for at, message in enumerate(messages):
        sender = (place >> 1) ^ (at % (PLACES // 2))
        _, (first_out, last_out) = CHUNKS[at // (PLACES // 2)]
        for out in range(last_out - first_out):
            line = pl.multiple_of((sender * OUT_BINS + first_out + out) * PART, 8)
            re_all[pl.ds(line, PART), :] = message[2 * out * PART : (2 * out + 1) * PART, :]
            im_all[pl.ds(line, PART), :] = message[(2 * out + 1) * PART : (2 * out + 2) * PART, :]
    for out, all_ref in ((out_re, re_all), (out_im, im_all)):
        for tile in range(0, bins, 8):
            for row in range(PART):
                out[tile : tile + 8, row * FACTOR : (row + 1) * FACTOR] = all_ref[
                    pl.ds(tile * PART + row, 8, stride=PART), :
                ]


VMEM = pl.BlockSpec(memory_space=pltpu.VMEM)
SMEM = pl.BlockSpec(memory_space=pltpu.SMEM)


def kernel_call(body, name, out_shape, operands, scratch=(), flops=0, count=10**6, limit=8):
    specs = [SMEM if operand.size <= 1024 else VMEM for operand in operands]
    return pl.pallas_call(
        body,
        out_shape=out_shape,
        in_specs=specs,
        out_specs=jax.tree.map(lambda _: VMEM, out_shape),
        scratch_shapes=[pltpu.VMEM(shape, jnp.float32) for shape in scratch],
        compiler_params=pltpu.CompilerParams(vmem_limit_bytes=limit * 1024 * 1024),
        cost_estimate=pl.CostEstimate(flops=flops, bytes_accessed=count, transcendentals=0),
        name=name,
    )(*operands)


def transposed_shards(raw_re, raw_im, ref_blocks, owners, offsets, taps):
    bins, samples = raw_re.shape

    def array(*shape):
        return jax.ShapeDtypeStruct(shape, jnp.float32)

    matrices, twists = dft_constants()
    near_table, *tables = [jnp.asarray(table) for table in (*matrices, twists)]
    swap = functools.partial(lax.ppermute, axis_name="rg", perm=[(0, 1), (1, 0)])
    half = PLACES // 2
    ref_own = ref_blocks[0].T
    offsets_other = swap(offsets)
    ref_other, re_other, im_other, taps_other = swap(ref_own), swap(raw_re), swap(raw_im), swap(taps)

    lines = [raw_re.reshape(bins * PART, FACTOR), raw_im.reshape(bins * PART, FACTOR)]
    shapes = []
    for (first_bin, last_bin), _ in CHUNKS:
        ref_lines = REF_LINES if first_bin == 0 else 0
        shapes += [array(2 * (last_bin - first_bin) * PART + ref_lines, FACTOR)] * half
    all_lines = (2 * bins + 2 * EDGE) * PART
    messages = kernel_call(
        pack_kernel,
        "pack",
        shapes,
        [*lines, re_other, im_other, ref_own, ref_other, offsets, offsets_other],
        scratch=[(all_lines, FACTOR), (all_lines, FACTOR), (2 * bins + 2 * EDGE, FACTOR)],
        count=4 * 10**6,
    )
    phases = kernel_call(
        functools.partial(phase_kernel, 2 * bins),
        "phase",
        array(WINDOW, 2, HALF, FACTOR),
        [offsets, offsets_other],
        flops=10**7,
    )

    routes = [
        [
            (chip * 2 + core, (((chip >> 1) ^ step) * 2 + core) * 2 + (chip & 1))
            for chip in range(PLACES)
            for core in range(2)
        ]
        for step in range(half)
    ]
    routes_back = [
        [
            (chip * 2 + core, (((chip % half) ^ step) * 2 + core) * 2 + chip // half)
            for chip in range(PLACES)
            for core in range(2)
        ]
        for step in range(half)
    ]
    arrived = [
        lax.ppermute(messages[chunk * half + step], ("az", "rg"), routes[step])
        for chunk in range(len(CHUNKS))
        for step in STEPS
    ]

    results = []
    refs, earlier = None, []
    for chunk, ((first_bin, last_bin), (first_out, last_out)) in enumerate(CHUNKS):
        count, outs = last_bin - first_bin, last_out - first_out
        has_ref = chunk == 0
        size = 2 * count * 2 * PART
        shapes = [array(size, FACTOR), array(size + (2 * REF_LINES if has_ref else 0), FACTOR)]
        operands = arrived[chunk * half : (chunk + 1) * half]
        if chunk == 0:
            *operands, phases, taps_other = lax.optimization_barrier((*operands, phases, taps_other))
        if has_ref:
            shapes.append(array(2, REF_LINES, FACTOR))
            operands = operands + [owners]
        parity = kernel_call(functools.partial(parity_kernel, count, has_ref), "parity", shapes, operands)
        keep, give = parity[:2]
        got = swap(give)
        groups = len(bin_groups(count))
        partial = kernel_call(
            functools.partial(near_kernel, count), "near", array(groups, FACTOR, 4 * FACTOR), [keep, near_table]
        )
        if has_ref:
            refs = [parity[2], got]
        pieces = kernel_call(
            functools.partial(band_kernel, chunk),
            "band",
            [array(outs * HALF, FACTOR), array(outs * HALF, FACTOR), array(count, 2, HALF, FACTOR)],
            [partial, got, *refs, owners, phases, taps, taps_other, *tables, *earlier],
            scratch=[(outs * HALF, 2 * FACTOR), (2, 2 * REF_LINES, FACTOR)],
            flops=10**9,
            count=4 * 10**6,
            limit=16,
        )
        keep, give, spectra = pieces
        earlier = [spectra]
        sent = kernel_call(
            functools.partial(join_kernel, outs),
            "join",
            [array(2 * outs * PART, FACTOR)] * half,
            [keep, swap(give)],
        )
        results += [lax.ppermute(message, ("az", "rg"), route) for message, route in zip(sent, routes_back)]
    return kernel_call(
        place_kernel, "place", [array(bins, samples)] * 2, results, scratch=[(bins * PART, FACTOR)] * 2
    )


def solution(mesh):
    sizes = mesh.shape

    def whole(raw_re, raw_im, ref_blocks, owners, offsets, taps):
        line = raw_re.shape[1] // sizes["scene"]
        fits = (
            sizes["rg"] == 2
            and sizes["az"] == PLACES
            and raw_re.shape[0] == OUT_BINS * PLACES
            and line == FACTOR * FACTOR
            and ref_blocks.shape[1] == HALF
        )
        return jax.shard_map(
            transposed_shards if fits else butterfly_shards,
            mesh=mesh,
            in_specs=(
                P("rg", ("scene", "az")),
                P("rg", ("scene", "az")),
                P(("scene", "az"), None, "rg"),
                P("scene"),
                P("rg"),
                P("rg", None),
            ),
            out_specs=(P("rg", ("scene", "az")), P("rg", ("scene", "az"))),
            check_vma=False,
        )(raw_re, raw_im, ref_blocks, owners, offsets, taps)

    return whole
```

```python
import functools
import math

import jax
import jax.numpy as jnp
import numpy as np
from jax import lax
from jax.experimental import pallas as pl
from jax.experimental.pallas import tpu as pltpu
from jax.sharding import PartitionSpec as P

SPLIT = 4
TAPS = 8
REACH = 8
BLOCK = 16


PRECISE = lax.Precision.HIGHEST
PHASE_GAIN = 50.0


def partner_2(value, axis, stride):
    return lax.ppermute(value, axis, [(i, i ^ 1 << stride) for i in range(lax.axis_size(axis))])


def from_root(block, axis, source):
    block = jnp.where(lax.axis_index(axis) == source, block, jnp.zeros_like(block))
    return lax.psum(block, axis)


def padded_2(value, sides, width):
    for axis, dim in sides:
        size, length = (lax.axis_size(axis), value.shape[dim])
        up = [(i, (i + 1) % size) for i in range(size - 1)]
        down = [(j, i) for i, j in up]
        last = lax.slice_in_dim(value, length - width, length, axis=dim)
        initial = lax.slice_in_dim(value, 0, width, axis=dim)
        before = lax.ppermute(last, axis, up)
        after = lax.ppermute(initial, axis, down)
        value = jnp.concatenate([before, value, after], axis=dim)
    return value


def angles(numerator, denominator, sign_value):
    return sign_value * 2.0 * math.pi * numerator.astype(jnp.float32) / denominator


def rotate(signal, cosine, sine_part):
    real_part = signal[0] * cosine - signal[1] * sine_part
    imag_part = signal[0] * sine_part + signal[1] * cosine
    return jnp.stack([real_part, imag_part])


def dft_table(length_n, sign_value):
    counter = jnp.arange(length_n, dtype=jnp.int32)
    turn_count = counter[:, None] * counter[None, :] % length_n
    angle_set = angles(turn_count, length_n, sign_value)
    return (jnp.cos(angle_set), jnp.sin(angle_set))


def complex_apply(einsum_form, cosine, sine_part, signal):
    real_part = jnp.einsum(einsum_form, cosine, signal[0], precision=PRECISE) - jnp.einsum(
        einsum_form, sine_part, signal[1], precision=PRECISE
    )
    imag_part = jnp.einsum(einsum_form, cosine, signal[1], precision=PRECISE) + jnp.einsum(
        einsum_form, sine_part, signal[0], precision=PRECISE
    )
    return jnp.stack([real_part, imag_part])


def local_dft(signal, sign_value):
    rg_cols = signal.shape[1]
    az_rows = signal.shape[2]
    inner_len = az_rows // SPLIT
    shaped = signal.reshape(2, rg_cols, SPLIT, inner_len)
    first_cos, first_sin = dft_table(SPLIT, sign_value)
    first_pass = complex_apply("aj,cjk->cak", first_cos, first_sin, shaped)
    outer_idx = jnp.arange(SPLIT, dtype=jnp.int32)
    inner_idx = jnp.arange(inner_len, dtype=jnp.int32)
    twist = angles(outer_idx[:, None] * inner_idx[None, :] % az_rows, az_rows, sign_value)
    first_pass = rotate(first_pass, jnp.cos(twist)[None, :, :], jnp.sin(twist)[None, :, :])
    second_cos, second_sin = dft_table(inner_len, sign_value)
    second_pass = complex_apply("bk,cak->cba", second_cos, second_sin, first_pass)
    return second_pass.reshape(2, rg_cols, az_rows)


def butterfly_down(signal, az_place, bit_count):
    for bit_num in reversed(range(bit_count)):
        half_span = 1 << bit_num
        partner = partner_2(signal, "az", bit_num)
        is_upper = az_place >> bit_num & 1 == 1
        angle_set = angles(az_place % half_span, 2 * half_span, -1.0)
        difference = rotate(partner - signal, jnp.cos(angle_set), jnp.sin(angle_set))
        signal = jnp.where(is_upper, difference, signal + partner)
    return signal


def butterfly_up(signal, az_place, bit_count):
    for bit_num in range(bit_count):
        half_span = 1 << bit_num
        partner = partner_2(signal, "az", bit_num)
        is_upper = az_place >> bit_num & 1 == 1
        angle_set = angles(az_place % half_span, 2 * half_span, 1.0)
        cosine = jnp.cos(angle_set)
        sine_part = jnp.sin(angle_set)
        lower_new = (signal + rotate(partner, cosine, sine_part)) * 0.5
        upper_new = (partner - rotate(signal, cosine, sine_part)) * 0.5
        signal = jnp.where(is_upper, upper_new, lower_new)
    return signal


def butterfly_shards(raw_re, raw_im, ref_blocks, owners, offsets, taps):
    rg_cols = raw_re.shape[0]
    az_rows = raw_re.shape[1]
    az_count = lax.axis_size("az")
    az_place = lax.axis_index("az")
    bit_count = az_count.bit_length() - 1
    az_total = az_rows * az_count
    rg_total = rg_cols * lax.axis_size("rg")
    own_block = ref_blocks[0]
    lower_ref = from_root(own_block, "az", owners[0])
    upper_ref = from_root(own_block, "az", owners[1])
    signal = jnp.stack([raw_re, raw_im])
    signal = butterfly_down(signal, az_place, bit_count)
    column = jnp.zeros((), jnp.int32)
    for bit_num in range(bit_count):
        column = column + ((az_place >> bit_num & 1) << bit_count - 1 - bit_num)
    row_index = jnp.arange(az_rows, dtype=jnp.int32)
    twist = angles(row_index * column % az_total, az_total, -1.0)
    signal = rotate(signal, jnp.cos(twist)[None, :], jnp.sin(twist)[None, :])
    signal = local_dft(signal, -1.0)
    frequency = column + az_count * row_index
    signed = (frequency + az_total // 2) % az_total - az_total // 2
    az_freq = signed.astype(jnp.float32) / az_total
    rg_index = lax.axis_index("rg") * rg_cols + jnp.arange(rg_cols, dtype=jnp.int32)
    rg_freq = (rg_index.astype(jnp.float32) + 0.5) / (2 * rg_total) - 0.25
    model_phase = PHASE_GAIN * jnp.sqrt((1.0 + rg_freq)[:, None] ** 2 - az_freq[None, :] ** 2)
    ref_rows = own_block.shape[0]
    coarse = frequency * ref_rows // az_total
    slot_index = jnp.where(signed >= 0, ref_rows + coarse, coarse)
    one_hot = (jnp.arange(2 * ref_rows, dtype=jnp.int32)[:, None] == slot_index[None, :]).astype(
        jnp.float32
    )
    both_refs = jnp.concatenate([lower_ref, upper_ref], axis=0)
    picked = jnp.dot(both_refs.T, one_hot, precision=PRECISE)
    phase_all = model_phase + picked
    signal = rotate(signal, jnp.cos(phase_all), jnp.sin(phase_all))
    rim_width = REACH + TAPS // 2
    padded = padded_2(signal, (("rg", 1),), rim_width)
    offset_cols = jnp.repeat(offsets, BLOCK)
    local_cols = jnp.arange(rg_cols, dtype=jnp.int32)
    tap_index = jnp.arange(TAPS, dtype=jnp.int32)
    target = local_cols[:, None] + rim_width + offset_cols[:, None] + tap_index[None, :] - TAPS // 2
    padded_index = jnp.arange(rg_cols + 2 * rim_width, dtype=jnp.int32)
    hits = (padded_index[:, None, None] == target[None, :, :]).astype(jnp.float32)
    band_matrix = jnp.sum(hits * taps[None, :, :], axis=2)
    signal = jnp.einsum("zma,mi->zia", padded, band_matrix, precision=PRECISE)
    signal = local_dft(signal, 1.0) / az_rows
    twist_back = angles(row_index * column % az_total, az_total, 1.0)
    signal = rotate(signal, jnp.cos(twist_back)[None, :], jnp.sin(twist_back)[None, :])
    signal = butterfly_up(signal, az_place, bit_count)
    return (signal[0], signal[1])


FACTOR = 128
PLACES = 8
PART = FACTOR // PLACES
HALF = FACTOR // 2
OUT_BINS = 8
WINDOW = OUT_BINS + TAPS - 1
REF_LINES = 8
EDGE = 16
STEPS = (2, 3, 1, 0)
CHUNKS = (((0, WINDOW), (0, OUT_BINS)),)


def split_bf16(value):
    high = value.astype(jnp.bfloat16)
    low = (value - high.astype(jnp.float32)).astype(jnp.bfloat16)
    return high, low


def dot_split(left, right):
    dot = functools.partial(jnp.dot, preferred_element_type=jnp.float32)
    return dot(left[0], right[0]) + (dot(left[0], right[1]) + dot(left[1], right[0]))


def both_bf16(matrix):
    high = matrix.astype(jnp.bfloat16)
    return np.stack([high, (matrix - high.astype(np.float64)).astype(jnp.bfloat16)])


def dft_constants():
    counter = np.arange(FACTOR)
    kappa = np.arange(HALF)
    near, far, last, twists = [], [], [], []
    for side in range(2):
        order = [(middle, low, line) for low in (side, 1 - side) for middle in range(2) for line in range(PART)]
        mine = np.array([(2 * middle + low) * PART + line for middle, low, line in order])
        angle = 2 * np.pi * (np.outer(2 * kappa + side, mine) % FACTOR) / FACTOR
        cosine, sine = np.cos(angle), np.sin(angle)
        whole = np.block([[cosine, sine], [-sine, cosine]])
        quarters = np.split(whole, 4, axis=1)
        near.append(np.concatenate(quarters[0::2], axis=1))
        far.append(np.concatenate(quarters[1::2], axis=1))
        back_re, back_im = np.block([cosine.T, -sine.T]), np.block([sine.T, cosine.T])
        own, other = slice(0, HALF // 2), slice(HALF // 2, HALF)
        last.append(np.concatenate([back_re[own], back_im[own], back_re[other], back_im[other]]))
        twist = 2 * np.pi * np.outer(2 * kappa + side, counter) / FACTOR**2
        twists.append(np.stack([np.cos(twist), np.sin(twist)]))
    angle = 2 * np.pi * (np.outer(counter, counter) % FACTOR) / FACTOR
    cosine, sine = np.cos(angle), np.sin(angle)
    there = np.block([[cosine, -sine], [sine, cosine]])
    back = np.block([[cosine, sine], [-sine, cosine]])
    matrices = [
        both_bf16(np.stack(near)),
        both_bf16(np.stack(far)),
        both_bf16(there),
        both_bf16(back),
        both_bf16(np.stack(last)),
    ]
    return matrices, np.stack(twists).astype(np.float32)


def cos_sin_quarters(quarters):
    whole = jnp.floor(quarters + 0.5)
    rest = (quarters - whole) * (math.pi / 2)
    square = rest * rest
    sine = rest + rest * square * (
        -1.6666654611e-1 + square * (8.3321608736e-3 + square * (-1.9515295891e-4))
    )
    cosine = 1.0 - 0.5 * square + square * square * (
        4.166664568298827e-2 + square * (-1.388731625493765e-3 + square * 2.443315711809948e-5)
    )
    number = whole.astype(jnp.int32)
    odd = (number & 1) == 1
    turned_cos = jnp.where(odd, sine, cosine)
    turned_sin = jnp.where(odd, cosine, sine)
    cos_sign = jnp.where(((number + 1) & 2) == 2, -1.0, 1.0)
    sin_sign = jnp.where((number & 2) == 2, -1.0, 1.0)
    return turned_cos * cos_sign, turned_sin * sin_sign


def window_start(chip, side, offsets_own, offsets_other):
    block = chip * OUT_BINS // BLOCK
    blocks = offsets_own.shape[0]
    local = lax.rem(block, blocks)
    shift = jnp.where(lax.div(block, blocks) == side, offsets_own[local], offsets_other[local])
    return chip * OUT_BINS + shift - TAPS // 2


def spread_lines(target, base, source):
    bins, samples = source.shape
    part_rows = samples // FACTOR
    for tile in range(0, bins, 8):
        for row in range(part_rows):
            target[pl.ds((base + tile) * part_rows + row, 8, stride=part_rows), :] = source[
                tile : tile + 8, row * FACTOR : (row + 1) * FACTOR
            ]


def pack_kernel(re_lines, im_lines, re_other, im_other, ref_own, ref_other, off_own, off_other, *refs):
    messages, (re_all, im_all, ref_all) = refs[:-3], refs[-3:]
    bins, samples = re_other.shape
    part_rows = samples // FACTOR
    place, side = lax.axis_index("az"), lax.axis_index("rg")
    own_at, other_at = EDGE + side * bins, EDGE + (1 - side) * bins
    zeros = jnp.zeros((EDGE * part_rows, FACTOR), jnp.float32)
    for all_ref, own, other in ((re_all, re_lines, re_other), (im_all, im_lines, im_other)):
        all_ref[: EDGE * part_rows, :] = zeros
        all_ref[(EDGE + 2 * bins) * part_rows :, :] = zeros
        all_ref[pl.ds(pl.multiple_of(own_at * part_rows, 8), bins * part_rows), :] = own[...]
        spread_lines(all_ref, other_at, other)
    ref_all[:EDGE, :] = jnp.zeros((EDGE, FACTOR), jnp.float32)
    ref_all[EDGE + 2 * bins :, :] = jnp.zeros((EDGE, FACTOR), jnp.float32)
    for at, ref in ((own_at, ref_own), (other_at, ref_other)):
        ref_all[pl.ds(pl.multiple_of(at, 16), bins), :] = jnp.concatenate([ref[...], ref[...]], axis=1)
    lane = lax.broadcasted_iota(jnp.int32, (1, FACTOR), 1)
    for at, message in enumerate(messages):
        step = at % (PLACES // 2)
        (first_bin, last_bin), _ = CHUNKS[at // (PLACES // 2)]
        body = (last_bin - first_bin) * part_rows
        start = window_start(((place >> 1) ^ step) * 2 + side, side, off_own, off_other) + EDGE
        rows = pl.ds(pl.multiple_of((start + first_bin) * part_rows, 8), body)
        message[:body, :] = re_all[rows, :]
        message[body : 2 * body, :] = im_all[rows, :]
        if first_bin == 0:
            for bin_num in range(REF_LINES):
                low = ref_all[pl.ds(start + bin_num, 1), :]
                high = ref_all[pl.ds(start + REF_LINES + bin_num, 1), :]
                message[2 * body + bin_num : 2 * body + bin_num + 1, :] = jnp.where(lane < HALF, low, high)


def phase_kernel(bins_total, off_own, off_other, out):
    place, side = lax.axis_index("az"), lax.axis_index("rg")
    start = window_start(place, side, off_own, off_other)
    shape = (HALF, FACTOR)
    kappa = lax.broadcasted_iota(jnp.int32, shape, 0)
    frequency = 2 * kappa + side + FACTOR * lax.broadcasted_iota(jnp.int32, shape, 1)
    total = FACTOR * FACTOR
    signed = jnp.where(frequency >= total // 2, frequency - total, frequency)
    az_freq = signed.astype(jnp.float32) / total
    az_square = az_freq * az_freq
    for bin_num in range(WINDOW):
        rg_index = (start + bin_num).astype(jnp.float32)
        rg_freq = (rg_index + 0.5) / (2 * bins_total) - 0.25
        base = (1.0 + rg_freq) * (1.0 + rg_freq)
        root = jnp.sqrt(base - az_square)
        cosine, sine = cos_sin_quarters(root * (PHASE_GAIN * 2 / math.pi))
        out[bin_num, 0] = cosine
        out[bin_num, 1] = sine


def parity_kernel(bins, has_ref, *refs):
    chunks = dict(zip(STEPS, refs))
    refs = refs[PLACES // 2 :]
    place, side = lax.axis_index("az"), lax.axis_index("rg")
    if has_ref:
        owners, keep, give, keep_ref = refs
    else:
        keep, give = refs
    sign = jnp.where(place >= PLACES // 2, -1.0, 1.0)
    even = side == 0
    keep_near, keep_far = jnp.where(even, 1.0, sign), jnp.where(even, 1.0, -sign)
    give_near, give_far = jnp.where(even, sign, 1.0), jnp.where(even, -sign, 1.0)
    middle = (place >> 1) & 1
    for step in range(2):
        near, far = chunks[step], chunks[step + 2]
        for line in range(2 * bins):
            read = slice(line * PART, (line + 1) * PART)
            write = pl.ds(pl.multiple_of(line * 2 * PART + (middle ^ step) * PART, 8), PART)
            near_value, far_value = near[read, :], far[read, :]
            keep[write, :] = near_value * keep_near + far_value * keep_far
            give[write, :] = near_value * give_near + far_value * give_far
    if has_ref:
        for which in range(2):
            step = (owners[which] >> 1) ^ (place >> 1)
            value = chunks[0][2 * bins * PART :, :]
            for other in range(1, PLACES // 2):
                value = jnp.where(step == other, chunks[other][2 * bins * PART :, :], value)
            give[2 * bins * 2 * PART + which * REF_LINES : 2 * bins * 2 * PART + (which + 1) * REF_LINES, :] = value
            keep_ref[which] = value


def gather_lines(ref, bins, group):
    width = 2 * PART
    columns = [
        jnp.concatenate(
            [ref[(part * bins + bin_num) * width : (part * bins + bin_num + 1) * width, :] for part in range(2)], axis=0
        )
        for bin_num in group
    ]
    return jnp.concatenate(columns, axis=1)


def bin_groups(bins):
    return [range(at, min(at + 4, bins)) for at in range(0, bins, 4)]


def near_kernel(bins, keep, near, out):
    side = lax.axis_index("rg")
    matrix = (near[0, side], near[1, side])
    for index, group in enumerate(bin_groups(bins)):
        out[index, :, : len(group) * FACTOR] = dot_split(matrix, split_bf16(gather_lines(keep, bins, group)))


def band_kernel(chunk, *refs):
    (first_bin, last_bin), (first_out, last_out) = CHUNKS[chunk]
    bins = last_bin - first_bin
    partial, got, keep_ref, got_ref, owners, phase, taps_own, taps_other = refs[:8]
    far, there, back, last, twists = refs[8:13]
    refs = refs[13:]
    if chunk:
        earlier, refs = refs[0], refs[1:]
    keep_out, give_out, spectra, band, picked = refs
    place, side = lax.axis_index("az"), lax.axis_index("rg")

    lane = lax.broadcasted_iota(jnp.int32, (REF_LINES, FACTOR), 1)
    ref_at = got_ref.shape[0] - 2 * REF_LINES
    lines = [
        jnp.where(
            (owners[which] & 1) == side,
            keep_ref[which],
            got_ref[ref_at + which * REF_LINES : ref_at + (which + 1) * REF_LINES, :],
        )
        for which in range(2)
    ]
    for block in range(2):
        coarse = (lane >> 1) + block * HALF
        wide = [jnp.take_along_axis(lines[which], coarse, axis=1) for which in range(2)]
        ref_phase = jnp.where(lane < HALF, wide[1], wide[0])
        ref_cos, ref_sin = cos_sin_quarters(ref_phase * (2 / math.pi))
        picked[0, block * REF_LINES : (block + 1) * REF_LINES, :] = ref_cos
        picked[1, block * REF_LINES : (block + 1) * REF_LINES, :] = ref_sin

    far, last = (far[0, side], far[1, side]), (last[0, side], last[1, side])
    there, back = (there[0], there[1]), (back[0], back[1])
    twist_cos, twist_sin = twists[side, 0], twists[side, 1]
    for number, group in enumerate(bin_groups(bins)):
        passed = partial[number, :, : len(group) * FACTOR] + dot_split(far, split_bf16(gather_lines(got, bins, group)))
        rows = []
        for index in range(len(group)):
            real = passed[:HALF, index * FACTOR : (index + 1) * FACTOR]
            imag = passed[HALF:, index * FACTOR : (index + 1) * FACTOR]
            rows.append(
                jnp.concatenate([real * twist_cos + imag * twist_sin, imag * twist_cos - real * twist_sin], axis=1)
            )
        passed = dot_split(split_bf16(jnp.concatenate(rows, axis=0)), there)
        for index, bin_num in enumerate(group):
            real = passed[index * HALF : (index + 1) * HALF, :FACTOR]
            imag = passed[index * HALF : (index + 1) * HALF, FACTOR:]
            whole = first_bin + bin_num
            model_cos, model_sin = phase[whole, 0], phase[whole, 1]
            row_cos, row_sin = picked[0, whole : whole + 1, :], picked[1, whole : whole + 1, :]
            cosine = model_cos * row_cos - model_sin * row_sin
            sine = model_sin * row_cos + model_cos * row_sin
            spectra[bin_num, 0] = real * cosine - imag * sine
            spectra[bin_num, 1] = real * sine + imag * cosine

    bins_held = taps_own.shape[0]
    held = lax.div(place * OUT_BINS, bins_held) == side
    local = lax.rem(place * OUT_BINS, bins_held)
    outs = range(first_out, last_out)
    weights = {
        out: [jnp.where(held, taps_own[local + out, tap], taps_other[local + out, tap]) for tap in range(TAPS)]
        for out in outs
    }
    strip = 8
    for part in range(2):
        for at in range(0, HALF, strip):
            rows = slice(at, at + strip)
            sums = {}
            for bin_num in range(first_out, last_out + TAPS - 1):
                if bin_num < first_bin:
                    value = earlier[bin_num, part, rows]
                else:
                    value = spectra[bin_num - first_bin, part, rows]
                for out in outs:
                    if 0 <= bin_num - out < TAPS:
                        term = value * weights[out][bin_num - out]
                        sums[out] = sums[out] + term if out in sums else term
            for out in outs:
                line = (out - first_out) * HALF + at
                band[line : line + strip, part * FACTOR : (part + 1) * FACTOR] = sums[out]

    scale = 1.0 / (FACTOR * FACTOR)
    cos_table, sin_table = twist_cos * scale, twist_sin * scale
    for at in range(0, last_out - first_out, 4):
        passed = dot_split(split_bf16(band[at * HALF : (at + 4) * HALF, :]), back)
        columns = []
        for index in range(4):
            real = passed[index * HALF : (index + 1) * HALF, :FACTOR]
            imag = passed[index * HALF : (index + 1) * HALF, FACTOR:]
            columns.append(
                jnp.concatenate([real * cos_table - imag * sin_table, imag * cos_table + real * sin_table], axis=0)
            )
        passed = dot_split(last, split_bf16(jnp.concatenate(columns, axis=1)))
        for index in range(4):
            lines = slice((at + index) * HALF, (at + index + 1) * HALF)
            keep_out[lines, :] = passed[:HALF, index * FACTOR : (index + 1) * FACTOR]
            give_out[lines, :] = passed[HALF:, index * FACTOR : (index + 1) * FACTOR]


def join_kernel(outs, keep, got, *messages):
    place, side = lax.axis_index("az"), lax.axis_index("rg")
    quarter = lax.rem(place, PLACES // 2)
    sign = jnp.where(side == 0, 1.0, -1.0)
    for step, message in enumerate(messages):
        target = quarter ^ step
        top, middle = target >> 1, target & 1
        keep_factor, got_factor = jnp.where(top == 0, 1.0, sign), jnp.where(top == 0, 1.0, -sign)
        for line in range(2 * outs):
            read = pl.ds(pl.multiple_of(line * 2 * PART + middle * PART, 8), PART)
            message[line * PART : (line + 1) * PART, :] = keep[read, :] * keep_factor + got[read, :] * got_factor


def place_kernel(*refs):
    messages, (out_re, out_im, re_all, im_all) = refs[:-4], refs[-4:]
    bins, samples = out_re.shape
    place = lax.axis_index("az")
    for at, message in enumerate(messages):
        sender = (place >> 1) ^ (at % (PLACES // 2))
        _, (first_out, last_out) = CHUNKS[at // (PLACES // 2)]
        for out in range(last_out - first_out):
            line = pl.multiple_of((sender * OUT_BINS + first_out + out) * PART, 8)
            re_all[pl.ds(line, PART), :] = message[2 * out * PART : (2 * out + 1) * PART, :]
            im_all[pl.ds(line, PART), :] = message[(2 * out + 1) * PART : (2 * out + 2) * PART, :]
    for out, all_ref in ((out_re, re_all), (out_im, im_all)):
        for tile in range(0, bins, 8):
            for row in range(PART):
                out[tile : tile + 8, row * FACTOR : (row + 1) * FACTOR] = all_ref[
                    pl.ds(tile * PART + row, 8, stride=PART), :
                ]


VMEM = pl.BlockSpec(memory_space=pltpu.VMEM)
SMEM = pl.BlockSpec(memory_space=pltpu.SMEM)


def kernel_call(body, name, out_shape, operands, scratch=(), flops=0, count=10**6, limit=8):
    specs = [SMEM if operand.size <= 1024 else VMEM for operand in operands]
    return pl.pallas_call(
        body,
        out_shape=out_shape,
        in_specs=specs,
        out_specs=jax.tree.map(lambda _: VMEM, out_shape),
        scratch_shapes=[pltpu.VMEM(shape, jnp.float32) for shape in scratch],
        compiler_params=pltpu.CompilerParams(vmem_limit_bytes=limit * 1024 * 1024),
        cost_estimate=pl.CostEstimate(flops=flops, bytes_accessed=count, transcendentals=0),
        name=name,
    )(*operands)


def transposed_shards(raw_re, raw_im, ref_blocks, owners, offsets, taps):
    bins, samples = raw_re.shape

    def array(*shape):
        return jax.ShapeDtypeStruct(shape, jnp.float32)

    matrices, twists = dft_constants()
    near_table, *tables = [jnp.asarray(table) for table in (*matrices, twists)]
    swap = functools.partial(lax.ppermute, axis_name="rg", perm=[(0, 1), (1, 0)])
    half = PLACES // 2
    ref_own = ref_blocks[0].T
    offsets_other = swap(offsets)
    ref_other, re_other, im_other, taps_other = swap(ref_own), swap(raw_re), swap(raw_im), swap(taps)

    lines = [raw_re.reshape(bins * PART, FACTOR), raw_im.reshape(bins * PART, FACTOR)]
    shapes = []
    for (first_bin, last_bin), _ in CHUNKS:
        ref_lines = REF_LINES if first_bin == 0 else 0
        shapes += [array(2 * (last_bin - first_bin) * PART + ref_lines, FACTOR)] * half
    all_lines = (2 * bins + 2 * EDGE) * PART
    messages = kernel_call(
        pack_kernel,
        "pack",
        shapes,
        [*lines, re_other, im_other, ref_own, ref_other, offsets, offsets_other],
        scratch=[(all_lines, FACTOR), (all_lines, FACTOR), (2 * bins + 2 * EDGE, FACTOR)],
        count=4 * 10**6,
    )
    phases = kernel_call(
        functools.partial(phase_kernel, 2 * bins),
        "phase",
        array(WINDOW, 2, HALF, FACTOR),
        [offsets, offsets_other],
        flops=10**7,
    )

    routes = [
        [
            (chip * 2 + core, (((chip >> 1) ^ step) * 2 + core) * 2 + (chip & 1))
            for chip in range(PLACES)
            for core in range(2)
        ]
        for step in range(half)
    ]
    routes_back = [
        [
            (chip * 2 + core, (((chip % half) ^ step) * 2 + core) * 2 + chip // half)
            for chip in range(PLACES)
            for core in range(2)
        ]
        for step in range(half)
    ]
    arrived = [
        lax.ppermute(messages[chunk * half + step], ("az", "rg"), routes[step])
        for chunk in range(len(CHUNKS))
        for step in STEPS
    ]

    results = []
    refs, earlier = None, []
    for chunk, ((first_bin, last_bin), (first_out, last_out)) in enumerate(CHUNKS):
        count, outs = last_bin - first_bin, last_out - first_out
        has_ref = chunk == 0
        size = 2 * count * 2 * PART
        shapes = [array(size, FACTOR), array(size + (2 * REF_LINES if has_ref else 0), FACTOR)]
        operands = arrived[chunk * half : (chunk + 1) * half]
        if chunk == 0:
            *operands, phases, taps_other = lax.optimization_barrier((*operands, phases, taps_other))
        if has_ref:
            shapes.append(array(2, REF_LINES, FACTOR))
            operands = operands + [owners]
        parity = kernel_call(functools.partial(parity_kernel, count, has_ref), "parity", shapes, operands)
        keep, give = parity[:2]
        got = swap(give)
        groups = len(bin_groups(count))
        partial = kernel_call(
            functools.partial(near_kernel, count), "near", array(groups, FACTOR, 4 * FACTOR), [keep, near_table]
        )
        if has_ref:
            refs = [parity[2], got]
        pieces = kernel_call(
            functools.partial(band_kernel, chunk),
            "band",
            [array(outs * HALF, FACTOR), array(outs * HALF, FACTOR), array(count, 2, HALF, FACTOR)],
            [partial, got, *refs, owners, phases, taps, taps_other, *tables, *earlier],
            scratch=[(outs * HALF, 2 * FACTOR), (2, 2 * REF_LINES, FACTOR)],
            flops=10**9,
            count=4 * 10**6,
            limit=16,
        )
        keep, give, spectra = pieces
        earlier = [spectra]
        sent = kernel_call(
            functools.partial(join_kernel, outs),
            "join",
            [array(2 * outs * PART, FACTOR)] * half,
            [keep, swap(give)],
        )
        results += [lax.ppermute(message, ("az", "rg"), route) for message, route in zip(sent, routes_back)]
    return kernel_call(
        place_kernel, "place", [array(bins, samples)] * 2, results, scratch=[(bins * PART, FACTOR)] * 2
    )


def solution(mesh):
    sizes = mesh.shape

    def whole(raw_re, raw_im, ref_blocks, owners, offsets, taps):
        line = raw_re.shape[1] // sizes["scene"]
        fits = (
            sizes["rg"] == 2
            and sizes["az"] == PLACES
            and raw_re.shape[0] == OUT_BINS * PLACES
            and line == FACTOR * FACTOR
            and ref_blocks.shape[1] == HALF
        )
        return jax.shard_map(
            transposed_shards if fits else butterfly_shards,
            mesh=mesh,
            in_specs=(
                P("rg", ("scene", "az")),
                P("rg", ("scene", "az")),
                P(("scene", "az"), None, "rg"),
                P("scene"),
                P("rg"),
                P("rg", None),
            ),
            out_specs=(P("rg", ("scene", "az")), P("rg", ("scene", "az"))),
            check_vma=False,
        )(raw_re, raw_im, ref_blocks, owners, offsets, taps)

    return whole
```

```python
import functools
import math

import jax
import jax.numpy as jnp
import numpy as np
from jax import lax
from jax.experimental import pallas as pl
from jax.experimental.pallas import tpu as pltpu
from jax.sharding import PartitionSpec as P

SPLIT = 4
TAPS = 8
REACH = 8
BLOCK = 16


PRECISE = lax.Precision.HIGHEST
PHASE_GAIN = 50.0


def partner_2(value, axis, stride):
    return lax.ppermute(value, axis, [(i, i ^ 1 << stride) for i in range(lax.axis_size(axis))])


def from_root(block, axis, source):
    block = jnp.where(lax.axis_index(axis) == source, block, jnp.zeros_like(block))
    return lax.psum(block, axis)


def padded_2(value, sides, width):
    for axis, dim in sides:
        size, length = (lax.axis_size(axis), value.shape[dim])
        up = [(i, (i + 1) % size) for i in range(size - 1)]
        down = [(j, i) for i, j in up]
        last = lax.slice_in_dim(value, length - width, length, axis=dim)
        initial = lax.slice_in_dim(value, 0, width, axis=dim)
        before = lax.ppermute(last, axis, up)
        after = lax.ppermute(initial, axis, down)
        value = jnp.concatenate([before, value, after], axis=dim)
    return value


def angles(numerator, denominator, sign_value):
    return sign_value * 2.0 * math.pi * numerator.astype(jnp.float32) / denominator


def rotate(signal, cosine, sine_part):
    real_part = signal[0] * cosine - signal[1] * sine_part
    imag_part = signal[0] * sine_part + signal[1] * cosine
    return jnp.stack([real_part, imag_part])


def dft_table(length_n, sign_value):
    counter = jnp.arange(length_n, dtype=jnp.int32)
    turn_count = counter[:, None] * counter[None, :] % length_n
    angle_set = angles(turn_count, length_n, sign_value)
    return (jnp.cos(angle_set), jnp.sin(angle_set))


def complex_apply(einsum_form, cosine, sine_part, signal):
    real_part = jnp.einsum(einsum_form, cosine, signal[0], precision=PRECISE) - jnp.einsum(
        einsum_form, sine_part, signal[1], precision=PRECISE
    )
    imag_part = jnp.einsum(einsum_form, cosine, signal[1], precision=PRECISE) + jnp.einsum(
        einsum_form, sine_part, signal[0], precision=PRECISE
    )
    return jnp.stack([real_part, imag_part])


def local_dft(signal, sign_value):
    rg_cols = signal.shape[1]
    az_rows = signal.shape[2]
    inner_len = az_rows // SPLIT
    shaped = signal.reshape(2, rg_cols, SPLIT, inner_len)
    first_cos, first_sin = dft_table(SPLIT, sign_value)
    first_pass = complex_apply("aj,cjk->cak", first_cos, first_sin, shaped)
    outer_idx = jnp.arange(SPLIT, dtype=jnp.int32)
    inner_idx = jnp.arange(inner_len, dtype=jnp.int32)
    twist = angles(outer_idx[:, None] * inner_idx[None, :] % az_rows, az_rows, sign_value)
    first_pass = rotate(first_pass, jnp.cos(twist)[None, :, :], jnp.sin(twist)[None, :, :])
    second_cos, second_sin = dft_table(inner_len, sign_value)
    second_pass = complex_apply("bk,cak->cba", second_cos, second_sin, first_pass)
    return second_pass.reshape(2, rg_cols, az_rows)


def butterfly_down(signal, az_place, bit_count):
    for bit_num in reversed(range(bit_count)):
        half_span = 1 << bit_num
        partner = partner_2(signal, "az", bit_num)
        is_upper = az_place >> bit_num & 1 == 1
        angle_set = angles(az_place % half_span, 2 * half_span, -1.0)
        difference = rotate(partner - signal, jnp.cos(angle_set), jnp.sin(angle_set))
        signal = jnp.where(is_upper, difference, signal + partner)
    return signal


def butterfly_up(signal, az_place, bit_count):
    for bit_num in range(bit_count):
        half_span = 1 << bit_num
        partner = partner_2(signal, "az", bit_num)
        is_upper = az_place >> bit_num & 1 == 1
        angle_set = angles(az_place % half_span, 2 * half_span, 1.0)
        cosine = jnp.cos(angle_set)
        sine_part = jnp.sin(angle_set)
        lower_new = (signal + rotate(partner, cosine, sine_part)) * 0.5
        upper_new = (partner - rotate(signal, cosine, sine_part)) * 0.5
        signal = jnp.where(is_upper, upper_new, lower_new)
    return signal


def butterfly_shards(raw_re, raw_im, ref_blocks, owners, offsets, taps):
    rg_cols = raw_re.shape[0]
    az_rows = raw_re.shape[1]
    az_count = lax.axis_size("az")
    az_place = lax.axis_index("az")
    bit_count = az_count.bit_length() - 1
    az_total = az_rows * az_count
    rg_total = rg_cols * lax.axis_size("rg")
    own_block = ref_blocks[0]
    lower_ref = from_root(own_block, "az", owners[0])
    upper_ref = from_root(own_block, "az", owners[1])
    signal = jnp.stack([raw_re, raw_im])
    signal = butterfly_down(signal, az_place, bit_count)
    column = jnp.zeros((), jnp.int32)
    for bit_num in range(bit_count):
        column = column + ((az_place >> bit_num & 1) << bit_count - 1 - bit_num)
    row_index = jnp.arange(az_rows, dtype=jnp.int32)
    twist = angles(row_index * column % az_total, az_total, -1.0)
    signal = rotate(signal, jnp.cos(twist)[None, :], jnp.sin(twist)[None, :])
    signal = local_dft(signal, -1.0)
    frequency = column + az_count * row_index
    signed = (frequency + az_total // 2) % az_total - az_total // 2
    az_freq = signed.astype(jnp.float32) / az_total
    rg_index = lax.axis_index("rg") * rg_cols + jnp.arange(rg_cols, dtype=jnp.int32)
    rg_freq = (rg_index.astype(jnp.float32) + 0.5) / (2 * rg_total) - 0.25
    model_phase = PHASE_GAIN * jnp.sqrt((1.0 + rg_freq)[:, None] ** 2 - az_freq[None, :] ** 2)
    ref_rows = own_block.shape[0]
    coarse = frequency * ref_rows // az_total
    slot_index = jnp.where(signed >= 0, ref_rows + coarse, coarse)
    one_hot = (jnp.arange(2 * ref_rows, dtype=jnp.int32)[:, None] == slot_index[None, :]).astype(
        jnp.float32
    )
    both_refs = jnp.concatenate([lower_ref, upper_ref], axis=0)
    picked = jnp.dot(both_refs.T, one_hot, precision=PRECISE)
    phase_all = model_phase + picked
    signal = rotate(signal, jnp.cos(phase_all), jnp.sin(phase_all))
    rim_width = REACH + TAPS // 2
    padded = padded_2(signal, (("rg", 1),), rim_width)
    offset_cols = jnp.repeat(offsets, BLOCK)
    local_cols = jnp.arange(rg_cols, dtype=jnp.int32)
    tap_index = jnp.arange(TAPS, dtype=jnp.int32)
    target = local_cols[:, None] + rim_width + offset_cols[:, None] + tap_index[None, :] - TAPS // 2
    padded_index = jnp.arange(rg_cols + 2 * rim_width, dtype=jnp.int32)
    hits = (padded_index[:, None, None] == target[None, :, :]).astype(jnp.float32)
    band_matrix = jnp.sum(hits * taps[None, :, :], axis=2)
    signal = jnp.einsum("zma,mi->zia", padded, band_matrix, precision=PRECISE)
    signal = local_dft(signal, 1.0) / az_rows
    twist_back = angles(row_index * column % az_total, az_total, 1.0)
    signal = rotate(signal, jnp.cos(twist_back)[None, :], jnp.sin(twist_back)[None, :])
    signal = butterfly_up(signal, az_place, bit_count)
    return (signal[0], signal[1])


FACTOR = 128
PLACES = 8
PART = FACTOR // PLACES
HALF = FACTOR // 2
OUT_BINS = 8
WINDOW = OUT_BINS + TAPS - 1
REF_LINES = 8
EDGE = 16
STEPS = (2, 3, 1, 0)
CHUNKS = (((0, WINDOW), (0, OUT_BINS)),)


def split_bf16(value):
    high = value.astype(jnp.bfloat16)
    low = (value - high.astype(jnp.float32)).astype(jnp.bfloat16)
    return high, low


def dot(left, right):
    return jnp.dot(left, right, preferred_element_type=jnp.float32)


def dot_split(left, right):
    return dot(left[0], right[0]) + (dot(left[0], right[1]) + dot(left[1], right[0]))


def both_bf16(matrix):
    high = matrix.astype(jnp.bfloat16)
    return np.stack([high, (matrix - high.astype(np.float64)).astype(jnp.bfloat16)])


def long_bf16(matrix):
    high, low = both_bf16(matrix)
    return np.concatenate([high, high, low], axis=-1)


def long_rows(value):
    high, low = split_bf16(value)
    return jnp.concatenate([high, low, high], axis=0)


def dft_constants():
    counter = np.arange(FACTOR)
    kappa = np.arange(HALF)
    near, far, last, twists = [], [], [], []
    for side in range(2):
        order = [(middle, low, line) for low in (side, 1 - side) for middle in range(2) for line in range(PART)]
        mine = np.array([(2 * middle + low) * PART + line for middle, low, line in order])
        angle = 2 * np.pi * (np.outer(2 * kappa + side, mine) % FACTOR) / FACTOR
        cosine, sine = np.cos(angle), np.sin(angle)
        whole = np.block([[cosine, sine], [-sine, cosine]])
        quarters = np.split(whole, 4, axis=1)
        near.append(np.concatenate(quarters[0::2], axis=1))
        far.append(np.concatenate(quarters[1::2], axis=1))
        back_re, back_im = np.block([cosine.T, -sine.T]), np.block([sine.T, cosine.T])
        own, other = slice(0, HALF // 2), slice(HALF // 2, HALF)
        last.append(np.concatenate([back_re[own], back_im[own], back_re[other], back_im[other]]))
        twist = 2 * np.pi * np.outer(2 * kappa + side, counter) / FACTOR**2
        twists.append(np.stack([np.cos(twist), np.sin(twist)]))
    angle = 2 * np.pi * (np.outer(counter, counter) % FACTOR) / FACTOR
    cosine, sine = np.cos(angle), np.sin(angle)
    there = np.block([[cosine, -sine], [sine, cosine]])
    back = np.block([[cosine, sine], [-sine, cosine]])
    matrices = [
        long_bf16(np.stack(near)),
        long_bf16(np.stack(far)),
        both_bf16(there),
        both_bf16(back),
        long_bf16(np.stack(last)),
    ]
    return matrices, np.stack(twists).astype(np.float32)


def cos_sin_quarters(quarters):
    whole = jnp.floor(quarters + 0.5)
    rest = (quarters - whole) * (math.pi / 2)
    square = rest * rest
    sine = rest + rest * square * (
        -1.6666654611e-1 + square * (8.3321608736e-3 + square * (-1.9515295891e-4))
    )
    cosine = 1.0 - 0.5 * square + square * square * (
        4.166664568298827e-2 + square * (-1.388731625493765e-3 + square * 2.443315711809948e-5)
    )
    number = whole.astype(jnp.int32)
    odd = (number & 1) == 1
    turned_cos = jnp.where(odd, sine, cosine)
    turned_sin = jnp.where(odd, cosine, sine)
    cos_sign = jnp.where(((number + 1) & 2) == 2, -1.0, 1.0)
    sin_sign = jnp.where((number & 2) == 2, -1.0, 1.0)
    return turned_cos * cos_sign, turned_sin * sin_sign


def window_start(chip, side, offsets_own, offsets_other):
    block = chip * OUT_BINS // BLOCK
    blocks = offsets_own.shape[0]
    local = lax.rem(block, blocks)
    shift = jnp.where(lax.div(block, blocks) == side, offsets_own[local], offsets_other[local])
    return chip * OUT_BINS + shift - TAPS // 2


def spread_lines(target, base, source):
    bins, samples = source.shape
    part_rows = samples // FACTOR
    for tile in range(0, bins, 8):
        for row in range(part_rows):
            target[pl.ds((base + tile) * part_rows + row, 8, stride=part_rows), :] = source[
                tile : tile + 8, row * FACTOR : (row + 1) * FACTOR
            ]


def pack_kernel(re_lines, im_lines, re_other, im_other, ref_own, ref_other, off_own, off_other, *refs):
    messages, (re_all, im_all, ref_all) = refs[:-3], refs[-3:]
    bins, samples = re_other.shape
    part_rows = samples // FACTOR
    place, side = lax.axis_index("az"), lax.axis_index("rg")
    own_at, other_at = EDGE + side * bins, EDGE + (1 - side) * bins
    zeros = jnp.zeros((EDGE * part_rows, FACTOR), jnp.float32)
    for all_ref, own, other in ((re_all, re_lines, re_other), (im_all, im_lines, im_other)):
        all_ref[: EDGE * part_rows, :] = zeros
        all_ref[(EDGE + 2 * bins) * part_rows :, :] = zeros
        all_ref[pl.ds(pl.multiple_of(own_at * part_rows, 8), bins * part_rows), :] = own[...]
        spread_lines(all_ref, other_at, other)
    ref_all[:EDGE, :] = jnp.zeros((EDGE, FACTOR), jnp.float32)
    ref_all[EDGE + 2 * bins :, :] = jnp.zeros((EDGE, FACTOR), jnp.float32)
    for at, ref in ((own_at, ref_own), (other_at, ref_other)):
        ref_all[pl.ds(pl.multiple_of(at, 16), bins), :] = jnp.concatenate([ref[...], ref[...]], axis=1)
    lane = lax.broadcasted_iota(jnp.int32, (1, FACTOR), 1)
    for at, message in enumerate(messages):
        step = at % (PLACES // 2)
        (first_bin, last_bin), _ = CHUNKS[at // (PLACES // 2)]
        body = (last_bin - first_bin) * part_rows
        start = window_start(((place >> 1) ^ step) * 2 + side, side, off_own, off_other) + EDGE
        rows = pl.ds(pl.multiple_of((start + first_bin) * part_rows, 8), body)
        message[:body, :] = re_all[rows, :]
        message[body : 2 * body, :] = im_all[rows, :]
        if first_bin == 0:
            for bin_num in range(REF_LINES):
                low = ref_all[pl.ds(start + bin_num, 1), :]
                high = ref_all[pl.ds(start + REF_LINES + bin_num, 1), :]
                message[2 * body + bin_num : 2 * body + bin_num + 1, :] = jnp.where(lane < HALF, low, high)


def phase_kernel(bins_total, off_own, off_other, out):
    place, side = lax.axis_index("az"), lax.axis_index("rg")
    start = window_start(place, side, off_own, off_other)
    shape = (HALF, FACTOR)
    kappa = lax.broadcasted_iota(jnp.int32, shape, 0)
    frequency = 2 * kappa + side + FACTOR * lax.broadcasted_iota(jnp.int32, shape, 1)
    total = FACTOR * FACTOR
    signed = jnp.where(frequency >= total // 2, frequency - total, frequency)
    az_freq = signed.astype(jnp.float32) / total
    az_square = az_freq * az_freq
    for bin_num in range(WINDOW):
        rg_index = (start + bin_num).astype(jnp.float32)
        rg_freq = (rg_index + 0.5) / (2 * bins_total) - 0.25
        base = (1.0 + rg_freq) * (1.0 + rg_freq)
        root = jnp.sqrt(base - az_square)
        cosine, sine = cos_sin_quarters(root * (PHASE_GAIN * 2 / math.pi))
        out[bin_num, 0] = cosine
        out[bin_num, 1] = sine


def parity_kernel(bins, has_ref, *refs):
    chunks = dict(zip(STEPS, refs))
    refs = refs[PLACES // 2 :]
    place, side = lax.axis_index("az"), lax.axis_index("rg")
    if has_ref:
        owners, keep, give, keep_ref = refs
    else:
        keep, give = refs
    sign = jnp.where(place >= PLACES // 2, -1.0, 1.0)
    even = side == 0
    keep_near, keep_far = jnp.where(even, 1.0, sign), jnp.where(even, 1.0, -sign)
    give_near, give_far = jnp.where(even, sign, 1.0), jnp.where(even, -sign, 1.0)
    plain = ((place >> 1) & 1) == 0
    for line in range(2 * bins):
        read = slice(line * PART, (line + 1) * PART)
        write = line * 2 * PART
        values = [chunks[step][read, :] for step in range(4)]
        for target, near_factor, far_factor in ((keep, keep_near, keep_far), (give, give_near, give_far)):
            pair = [values[step] * near_factor + values[step + 2] * far_factor for step in range(2)]
            target[write : write + PART, :] = jnp.where(plain, pair[0], pair[1])
            target[write + PART : write + 2 * PART, :] = jnp.where(plain, pair[1], pair[0])
    if has_ref:
        for which in range(2):
            step = (owners[which] >> 1) ^ (place >> 1)
            value = chunks[0][2 * bins * PART :, :]
            for other in range(1, PLACES // 2):
                value = jnp.where(step == other, chunks[other][2 * bins * PART :, :], value)
            give[2 * bins * 2 * PART + which * REF_LINES : 2 * bins * 2 * PART + (which + 1) * REF_LINES, :] = value
            keep_ref[which] = value


def gather_lines(ref, bins, group):
    width = 2 * PART
    columns = [
        jnp.concatenate(
            [ref[(part * bins + bin_num) * width : (part * bins + bin_num + 1) * width, :] for part in range(2)], axis=0
        )
        for bin_num in group
    ]
    return jnp.concatenate(columns, axis=1)


def bin_groups(bins):
    return [range(at, min(at + 4, bins)) for at in range(0, bins, 4)]


def near_kernel(bins, keep, near, out):
    matrix = near[lax.axis_index("rg")]
    for index, group in enumerate(bin_groups(bins)):
        out[index, :, : len(group) * FACTOR] = dot(matrix, long_rows(gather_lines(keep, bins, group)))


def band_kernel(chunk, *refs):
    (first_bin, last_bin), (first_out, last_out) = CHUNKS[chunk]
    bins = last_bin - first_bin
    partial, got, keep_ref, got_ref, owners, phase, taps_own, taps_other = refs[:8]
    far, there, back, last, twists = refs[8:13]
    refs = refs[13:]
    if chunk:
        earlier, refs = refs[0], refs[1:]
    keep_out, give_out, spectra, band, picked = refs
    place, side = lax.axis_index("az"), lax.axis_index("rg")

    lane = lax.broadcasted_iota(jnp.int32, (REF_LINES, FACTOR), 1)
    ref_at = got_ref.shape[0] - 2 * REF_LINES
    lines = [
        jnp.where(
            (owners[which] & 1) == side,
            keep_ref[which],
            got_ref[ref_at + which * REF_LINES : ref_at + (which + 1) * REF_LINES, :],
        )
        for which in range(2)
    ]
    for block in range(2):
        coarse = (lane >> 1) + block * HALF
        wide = [jnp.take_along_axis(lines[which], coarse, axis=1) for which in range(2)]
        ref_phase = jnp.where(lane < HALF, wide[1], wide[0])
        ref_cos, ref_sin = cos_sin_quarters(ref_phase * (2 / math.pi))
        picked[0, block * REF_LINES : (block + 1) * REF_LINES, :] = ref_cos
        picked[1, block * REF_LINES : (block + 1) * REF_LINES, :] = ref_sin

    far, last = far[side], last[side]
    there, back = (there[0], there[1]), (back[0], back[1])
    twist_cos, twist_sin = twists[side, 0], twists[side, 1]
    for number, group in enumerate(bin_groups(bins)):
        passed = partial[number, :, : len(group) * FACTOR] + dot(far, long_rows(gather_lines(got, bins, group)))
        rows = []
        for index in range(len(group)):
            real = passed[:HALF, index * FACTOR : (index + 1) * FACTOR]
            imag = passed[HALF:, index * FACTOR : (index + 1) * FACTOR]
            rows.append(
                jnp.concatenate([real * twist_cos + imag * twist_sin, imag * twist_cos - real * twist_sin], axis=1)
            )
        passed = dot_split(split_bf16(jnp.concatenate(rows, axis=0)), there)
        for index, bin_num in enumerate(group):
            real = passed[index * HALF : (index + 1) * HALF, :FACTOR]
            imag = passed[index * HALF : (index + 1) * HALF, FACTOR:]
            whole = first_bin + bin_num
            model_cos, model_sin = phase[whole, 0], phase[whole, 1]
            row_cos, row_sin = picked[0, whole : whole + 1, :], picked[1, whole : whole + 1, :]
            cosine = model_cos * row_cos - model_sin * row_sin
            sine = model_sin * row_cos + model_cos * row_sin
            spectra[bin_num, 0] = real * cosine - imag * sine
            spectra[bin_num, 1] = real * sine + imag * cosine

    bins_held = taps_own.shape[0]
    held = lax.div(place * OUT_BINS, bins_held) == side
    local = lax.rem(place * OUT_BINS, bins_held)
    outs = range(first_out, last_out)
    weights = {
        out: [jnp.where(held, taps_own[local + out, tap], taps_other[local + out, tap]) for tap in range(TAPS)]
        for out in outs
    }
    strip = 8
    for part in range(2):
        for at in range(0, HALF, strip):
            rows = slice(at, at + strip)
            sums = {}
            for bin_num in range(first_out, last_out + TAPS - 1):
                if bin_num < first_bin:
                    value = earlier[bin_num, part, rows]
                else:
                    value = spectra[bin_num - first_bin, part, rows]
                for out in outs:
                    if 0 <= bin_num - out < TAPS:
                        term = value * weights[out][bin_num - out]
                        sums[out] = sums[out] + term if out in sums else term
            for out in outs:
                line = (out - first_out) * HALF + at
                band[line : line + strip, part * FACTOR : (part + 1) * FACTOR] = sums[out]

    scale = 1.0 / (FACTOR * FACTOR)
    cos_table, sin_table = twist_cos * scale, twist_sin * scale
    for at in range(0, last_out - first_out, 4):
        passed = dot_split(split_bf16(band[at * HALF : (at + 4) * HALF, :]), back)
        columns = []
        for index in range(4):
            real = passed[index * HALF : (index + 1) * HALF, :FACTOR]
            imag = passed[index * HALF : (index + 1) * HALF, FACTOR:]
            columns.append(
                jnp.concatenate([real * cos_table - imag * sin_table, imag * cos_table + real * sin_table], axis=0)
            )
        passed = dot(last, long_rows(jnp.concatenate(columns, axis=1)))
        for index in range(4):
            lines = slice((at + index) * HALF, (at + index + 1) * HALF)
            keep_out[lines, :] = passed[:HALF, index * FACTOR : (index + 1) * FACTOR]
            give_out[lines, :] = passed[HALF:, index * FACTOR : (index + 1) * FACTOR]


def crossed(quarter):
    return ((quarter & 1) << 1) | (quarter >> 1)


def join_kernel(outs, keep, got, *messages):
    place, side = lax.axis_index("az"), lax.axis_index("rg")
    quarter = lax.rem(place, PLACES // 2)
    sign = jnp.where(side == 0, 1.0, -1.0)
    for step, message in enumerate(messages):
        target = crossed(quarter) ^ step
        top, middle = target >> 1, target & 1
        keep_factor, got_factor = jnp.where(top == 0, 1.0, sign), jnp.where(top == 0, 1.0, -sign)
        for line in range(2 * outs):
            read = pl.ds(pl.multiple_of(line * 2 * PART + middle * PART, 8), PART)
            message[line * PART : (line + 1) * PART, :] = keep[read, :] * keep_factor + got[read, :] * got_factor


def place_kernel(*refs):
    messages, (out_re, out_im, re_all, im_all) = refs[:-4], refs[-4:]
    bins, samples = out_re.shape
    place = lax.axis_index("az")
    for at, message in enumerate(messages):
        sender = crossed((place >> 1) ^ (at % (PLACES // 2)))
        _, (first_out, last_out) = CHUNKS[at // (PLACES // 2)]
        for out in range(last_out - first_out):
            line = pl.multiple_of((sender * OUT_BINS + first_out + out) * PART, 8)
            re_all[pl.ds(line, PART), :] = message[2 * out * PART : (2 * out + 1) * PART, :]
            im_all[pl.ds(line, PART), :] = message[(2 * out + 1) * PART : (2 * out + 2) * PART, :]
    for out, all_ref in ((out_re, re_all), (out_im, im_all)):
        for tile in range(0, bins, 8):
            for row in range(PART):
                out[tile : tile + 8, row * FACTOR : (row + 1) * FACTOR] = all_ref[
                    pl.ds(tile * PART + row, 8, stride=PART), :
                ]


VMEM = pl.BlockSpec(memory_space=pltpu.VMEM)
SMEM = pl.BlockSpec(memory_space=pltpu.SMEM)


def kernel_call(body, name, out_shape, operands, scratch=(), flops=0, count=10**6, limit=8):
    specs = [SMEM if operand.size <= 1024 else VMEM for operand in operands]
    return pl.pallas_call(
        body,
        out_shape=out_shape,
        in_specs=specs,
        out_specs=jax.tree.map(lambda _: VMEM, out_shape),
        scratch_shapes=[pltpu.VMEM(shape, jnp.float32) for shape in scratch],
        compiler_params=pltpu.CompilerParams(vmem_limit_bytes=limit * 1024 * 1024),
        cost_estimate=pl.CostEstimate(flops=flops, bytes_accessed=count, transcendentals=0),
        name=name,
    )(*operands)


def transposed_shards(raw_re, raw_im, ref_blocks, owners, offsets, taps):
    bins, samples = raw_re.shape

    def array(*shape):
        return jax.ShapeDtypeStruct(shape, jnp.float32)

    matrices, twists = dft_constants()
    near_table, *tables = [jnp.asarray(table) for table in (*matrices, twists)]
    swap = functools.partial(lax.ppermute, axis_name="rg", perm=[(0, 1), (1, 0)])
    half = PLACES // 2
    ref_own = ref_blocks[0].T
    offsets_other = swap(offsets)
    ref_other, re_other, im_other, taps_other = swap(ref_own), swap(raw_re), swap(raw_im), swap(taps)

    lines = [raw_re.reshape(bins * PART, FACTOR), raw_im.reshape(bins * PART, FACTOR)]
    shapes = []
    for (first_bin, last_bin), _ in CHUNKS:
        ref_lines = REF_LINES if first_bin == 0 else 0
        shapes += [array(2 * (last_bin - first_bin) * PART + ref_lines, FACTOR)] * half
    all_lines = (2 * bins + 2 * EDGE) * PART
    messages = kernel_call(
        pack_kernel,
        "pack",
        shapes,
        [*lines, re_other, im_other, ref_own, ref_other, offsets, offsets_other],
        scratch=[(all_lines, FACTOR), (all_lines, FACTOR), (2 * bins + 2 * EDGE, FACTOR)],
        count=4 * 10**6,
    )
    phases = kernel_call(
        functools.partial(phase_kernel, 2 * bins),
        "phase",
        array(WINDOW, 2, HALF, FACTOR),
        [offsets, offsets_other],
        flops=10**7,
    )

    routes = [
        [
            (chip * 2 + core, (((chip >> 1) ^ step) * 2 + core) * 2 + (chip & 1))
            for chip in range(PLACES)
            for core in range(2)
        ]
        for step in range(half)
    ]
    routes_back = [
        [
            (chip * 2 + core, ((crossed(chip % half) ^ step) * 2 + core) * 2 + chip // half)
            for chip in range(PLACES)
            for core in range(2)
        ]
        for step in range(half)
    ]
    arrived = [
        lax.ppermute(messages[chunk * half + step], ("az", "rg"), routes[step])
        for chunk in range(len(CHUNKS))
        for step in STEPS
    ]

    results = []
    refs, earlier = None, []
    for chunk, ((first_bin, last_bin), (first_out, last_out)) in enumerate(CHUNKS):
        count, outs = last_bin - first_bin, last_out - first_out
        has_ref = chunk == 0
        size = 2 * count * 2 * PART
        shapes = [array(size, FACTOR), array(size + (2 * REF_LINES if has_ref else 0), FACTOR)]
        operands = arrived[chunk * half : (chunk + 1) * half]
        if chunk == 0:
            *operands, phases, taps_other = lax.optimization_barrier((*operands, phases, taps_other))
        if has_ref:
            shapes.append(array(2, REF_LINES, FACTOR))
            operands = operands + [owners]
        parity = kernel_call(functools.partial(parity_kernel, count, has_ref), "parity", shapes, operands)
        keep, give = parity[:2]
        got = swap(give)
        groups = len(bin_groups(count))
        partial = kernel_call(
            functools.partial(near_kernel, count), "near", array(groups, FACTOR, 4 * FACTOR), [keep, near_table]
        )
        if has_ref:
            refs = [parity[2], got]
        pieces = kernel_call(
            functools.partial(band_kernel, chunk),
            "band",
            [array(outs * HALF, FACTOR), array(outs * HALF, FACTOR), array(count, 2, HALF, FACTOR)],
            [partial, got, *refs, owners, phases, taps, taps_other, *tables, *earlier],
            scratch=[(outs * HALF, 2 * FACTOR), (2, 2 * REF_LINES, FACTOR)],
            flops=10**9,
            count=4 * 10**6,
            limit=16,
        )
        keep, give, spectra = pieces
        earlier = [spectra]
        sent = kernel_call(
            functools.partial(join_kernel, outs),
            "join",
            [array(2 * outs * PART, FACTOR)] * half,
            [keep, swap(give)],
        )
        results += [lax.ppermute(message, ("az", "rg"), route) for message, route in zip(sent, routes_back)]
    return kernel_call(
        place_kernel, "place", [array(bins, samples)] * 2, results, scratch=[(bins * PART, FACTOR)] * 2
    )


def solution(mesh):
    sizes = mesh.shape

    def whole(raw_re, raw_im, ref_blocks, owners, offsets, taps):
        line = raw_re.shape[1] // sizes["scene"]
        fits = (
            sizes["rg"] == 2
            and sizes["az"] == PLACES
            and raw_re.shape[0] == OUT_BINS * PLACES
            and line == FACTOR * FACTOR
            and ref_blocks.shape[1] == HALF
        )
        return jax.shard_map(
            transposed_shards if fits else butterfly_shards,
            mesh=mesh,
            in_specs=(
                P("rg", ("scene", "az")),
                P("rg", ("scene", "az")),
                P(("scene", "az"), None, "rg"),
                P("scene"),
                P("rg"),
                P("rg", None),
            ),
            out_specs=(P("rg", ("scene", "az")), P("rg", ("scene", "az"))),
            check_vma=False,
        )(raw_re, raw_im, ref_blocks, owners, offsets, taps)

    return whole
```

```python
import functools
import math

import jax
import jax.numpy as jnp
import numpy as np
from jax import lax
from jax.experimental import pallas as pl
from jax.experimental.pallas import tpu as pltpu
from jax.sharding import PartitionSpec as P

SPLIT = 4
TAPS = 8
REACH = 8
BLOCK = 16


PRECISE = lax.Precision.HIGHEST
PHASE_GAIN = 50.0


def partner_2(value, axis, stride):
    return lax.ppermute(value, axis, [(i, i ^ 1 << stride) for i in range(lax.axis_size(axis))])


def from_root(block, axis, source):
    block = jnp.where(lax.axis_index(axis) == source, block, jnp.zeros_like(block))
    return lax.psum(block, axis)


def padded_2(value, sides, width):
    for axis, dim in sides:
        size, length = (lax.axis_size(axis), value.shape[dim])
        up = [(i, (i + 1) % size) for i in range(size - 1)]
        down = [(j, i) for i, j in up]
        last = lax.slice_in_dim(value, length - width, length, axis=dim)
        initial = lax.slice_in_dim(value, 0, width, axis=dim)
        before = lax.ppermute(last, axis, up)
        after = lax.ppermute(initial, axis, down)
        value = jnp.concatenate([before, value, after], axis=dim)
    return value


def angles(numerator, denominator, sign_value):
    return sign_value * 2.0 * math.pi * numerator.astype(jnp.float32) / denominator


def rotate(signal, cosine, sine_part):
    real_part = signal[0] * cosine - signal[1] * sine_part
    imag_part = signal[0] * sine_part + signal[1] * cosine
    return jnp.stack([real_part, imag_part])


def dft_table(length_n, sign_value):
    counter = jnp.arange(length_n, dtype=jnp.int32)
    turn_count = counter[:, None] * counter[None, :] % length_n
    angle_set = angles(turn_count, length_n, sign_value)
    return (jnp.cos(angle_set), jnp.sin(angle_set))


def complex_apply(einsum_form, cosine, sine_part, signal):
    real_part = jnp.einsum(einsum_form, cosine, signal[0], precision=PRECISE) - jnp.einsum(
        einsum_form, sine_part, signal[1], precision=PRECISE
    )
    imag_part = jnp.einsum(einsum_form, cosine, signal[1], precision=PRECISE) + jnp.einsum(
        einsum_form, sine_part, signal[0], precision=PRECISE
    )
    return jnp.stack([real_part, imag_part])


def local_dft(signal, sign_value):
    rg_cols = signal.shape[1]
    az_rows = signal.shape[2]
    inner_len = az_rows // SPLIT
    shaped = signal.reshape(2, rg_cols, SPLIT, inner_len)
    first_cos, first_sin = dft_table(SPLIT, sign_value)
    first_pass = complex_apply("aj,cjk->cak", first_cos, first_sin, shaped)
    outer_idx = jnp.arange(SPLIT, dtype=jnp.int32)
    inner_idx = jnp.arange(inner_len, dtype=jnp.int32)
    twist = angles(outer_idx[:, None] * inner_idx[None, :] % az_rows, az_rows, sign_value)
    first_pass = rotate(first_pass, jnp.cos(twist)[None, :, :], jnp.sin(twist)[None, :, :])
    second_cos, second_sin = dft_table(inner_len, sign_value)
    second_pass = complex_apply("bk,cak->cba", second_cos, second_sin, first_pass)
    return second_pass.reshape(2, rg_cols, az_rows)


def butterfly_down(signal, az_place, bit_count):
    for bit_num in reversed(range(bit_count)):
        half_span = 1 << bit_num
        partner = partner_2(signal, "az", bit_num)
        is_upper = az_place >> bit_num & 1 == 1
        angle_set = angles(az_place % half_span, 2 * half_span, -1.0)
        difference = rotate(partner - signal, jnp.cos(angle_set), jnp.sin(angle_set))
        signal = jnp.where(is_upper, difference, signal + partner)
    return signal


def butterfly_up(signal, az_place, bit_count):
    for bit_num in range(bit_count):
        half_span = 1 << bit_num
        partner = partner_2(signal, "az", bit_num)
        is_upper = az_place >> bit_num & 1 == 1
        angle_set = angles(az_place % half_span, 2 * half_span, 1.0)
        cosine = jnp.cos(angle_set)
        sine_part = jnp.sin(angle_set)
        lower_new = (signal + rotate(partner, cosine, sine_part)) * 0.5
        upper_new = (partner - rotate(signal, cosine, sine_part)) * 0.5
        signal = jnp.where(is_upper, upper_new, lower_new)
    return signal


def butterfly_shards(raw_re, raw_im, ref_blocks, owners, offsets, taps):
    rg_cols = raw_re.shape[0]
    az_rows = raw_re.shape[1]
    az_count = lax.axis_size("az")
    az_place = lax.axis_index("az")
    bit_count = az_count.bit_length() - 1
    az_total = az_rows * az_count
    rg_total = rg_cols * lax.axis_size("rg")
    own_block = ref_blocks[0]
    lower_ref = from_root(own_block, "az", owners[0])
    upper_ref = from_root(own_block, "az", owners[1])
    signal = jnp.stack([raw_re, raw_im])
    signal = butterfly_down(signal, az_place, bit_count)
    column = jnp.zeros((), jnp.int32)
    for bit_num in range(bit_count):
        column = column + ((az_place >> bit_num & 1) << bit_count - 1 - bit_num)
    row_index = jnp.arange(az_rows, dtype=jnp.int32)
    twist = angles(row_index * column % az_total, az_total, -1.0)
    signal = rotate(signal, jnp.cos(twist)[None, :], jnp.sin(twist)[None, :])
    signal = local_dft(signal, -1.0)
    frequency = column + az_count * row_index
    signed = (frequency + az_total // 2) % az_total - az_total // 2
    az_freq = signed.astype(jnp.float32) / az_total
    rg_index = lax.axis_index("rg") * rg_cols + jnp.arange(rg_cols, dtype=jnp.int32)
    rg_freq = (rg_index.astype(jnp.float32) + 0.5) / (2 * rg_total) - 0.25
    model_phase = PHASE_GAIN * jnp.sqrt((1.0 + rg_freq)[:, None] ** 2 - az_freq[None, :] ** 2)
    ref_rows = own_block.shape[0]
    coarse = frequency * ref_rows // az_total
    slot_index = jnp.where(signed >= 0, ref_rows + coarse, coarse)
    one_hot = (jnp.arange(2 * ref_rows, dtype=jnp.int32)[:, None] == slot_index[None, :]).astype(
        jnp.float32
    )
    both_refs = jnp.concatenate([lower_ref, upper_ref], axis=0)
    picked = jnp.dot(both_refs.T, one_hot, precision=PRECISE)
    phase_all = model_phase + picked
    signal = rotate(signal, jnp.cos(phase_all), jnp.sin(phase_all))
    rim_width = REACH + TAPS // 2
    padded = padded_2(signal, (("rg", 1),), rim_width)
    offset_cols = jnp.repeat(offsets, BLOCK)
    local_cols = jnp.arange(rg_cols, dtype=jnp.int32)
    tap_index = jnp.arange(TAPS, dtype=jnp.int32)
    target = local_cols[:, None] + rim_width + offset_cols[:, None] + tap_index[None, :] - TAPS // 2
    padded_index = jnp.arange(rg_cols + 2 * rim_width, dtype=jnp.int32)
    hits = (padded_index[:, None, None] == target[None, :, :]).astype(jnp.float32)
    band_matrix = jnp.sum(hits * taps[None, :, :], axis=2)
    signal = jnp.einsum("zma,mi->zia", padded, band_matrix, precision=PRECISE)
    signal = local_dft(signal, 1.0) / az_rows
    twist_back = angles(row_index * column % az_total, az_total, 1.0)
    signal = rotate(signal, jnp.cos(twist_back)[None, :], jnp.sin(twist_back)[None, :])
    signal = butterfly_up(signal, az_place, bit_count)
    return (signal[0], signal[1])


FACTOR = 128
PLACES = 8
PART = FACTOR // PLACES
HALF = FACTOR // 2
OUT_BINS = 8
WINDOW = OUT_BINS + TAPS - 1
REF_LINES = 8
EDGE = 16
STEPS = (2, 3, 1, 0)


def split_bf16(value):
    high = value.astype(jnp.bfloat16)
    low = (value - high.astype(jnp.float32)).astype(jnp.bfloat16)
    return high, low


def dot(left, right):
    return jnp.dot(left, right, preferred_element_type=jnp.float32)


def dot_split(left, right):
    return dot(left[0], right[0]) + (dot(left[0], right[1]) + dot(left[1], right[0]))


def both_bf16(matrix):
    high = matrix.astype(jnp.bfloat16)
    return np.stack([high, (matrix - high.astype(np.float64)).astype(jnp.bfloat16)])


def long_bf16(matrix):
    high, low = both_bf16(matrix)
    return np.concatenate([high, high, low], axis=-1)


def long_rows(value):
    high, low = split_bf16(value)
    return jnp.concatenate([high, low, high], axis=0)


def dft_constants():
    counter = np.arange(FACTOR)
    kappa = np.arange(HALF)
    near, far, last, twists = [], [], [], []
    for side in range(2):
        order = [(middle, low, line) for low in (side, 1 - side) for middle in range(2) for line in range(PART)]
        mine = np.array([(2 * middle + low) * PART + line for middle, low, line in order])
        angle = 2 * np.pi * (np.outer(2 * kappa + side, mine) % FACTOR) / FACTOR
        cosine, sine = np.cos(angle), np.sin(angle)
        whole = np.block([[cosine, sine], [-sine, cosine]])
        quarters = np.split(whole, 4, axis=1)
        near.append(np.concatenate(quarters[0::2], axis=1))
        far.append(np.concatenate(quarters[1::2], axis=1))
        back_re, back_im = np.block([cosine.T, -sine.T]), np.block([sine.T, cosine.T])
        own, other = slice(0, HALF // 2), slice(HALF // 2, HALF)
        last.append(np.concatenate([back_re[own], back_im[own], back_re[other], back_im[other]]))
        twist = 2 * np.pi * np.outer(2 * kappa + side, counter) / FACTOR**2
        twists.append(np.stack([np.cos(twist), np.sin(twist)]))
    angle = 2 * np.pi * (np.outer(counter, counter) % FACTOR) / FACTOR
    cosine, sine = np.cos(angle), np.sin(angle)
    there = np.block([[cosine, -sine], [sine, cosine]])
    back = np.block([[cosine, sine], [-sine, cosine]])
    matrices = [
        long_bf16(np.stack(near)),
        long_bf16(np.stack(far)),
        both_bf16(there),
        both_bf16(back),
        both_bf16(np.stack(last)),
    ]
    return matrices, np.stack(twists).astype(np.float32)


def cos_sin_quarters(quarters):
    whole = jnp.floor(quarters + 0.5)
    rest = (quarters - whole) * (math.pi / 2)
    square = rest * rest
    sine = rest + rest * square * (
        -1.6666654611e-1 + square * (8.3321608736e-3 + square * (-1.9515295891e-4))
    )
    cosine = 1.0 - 0.5 * square + square * square * (
        4.166664568298827e-2 + square * (-1.388731625493765e-3 + square * 2.443315711809948e-5)
    )
    number = whole.astype(jnp.int32)
    odd = (number & 1) == 1
    turned_cos = jnp.where(odd, sine, cosine)
    turned_sin = jnp.where(odd, cosine, sine)
    cos_sign = jnp.where(((number + 1) & 2) == 2, -1.0, 1.0)
    sin_sign = jnp.where((number & 2) == 2, -1.0, 1.0)
    return turned_cos * cos_sign, turned_sin * sin_sign


def window_start(chip, side, offsets_own, offsets_other):
    block = chip * OUT_BINS // BLOCK
    blocks = offsets_own.shape[0]
    local = lax.rem(block, blocks)
    shift = jnp.where(lax.div(block, blocks) == side, offsets_own[local], offsets_other[local])
    return chip * OUT_BINS + shift - TAPS // 2


def spread_lines(target, base, source):
    bins, samples = source.shape
    part_rows = samples // FACTOR
    for tile in range(0, bins, 8):
        for row in range(part_rows):
            target[pl.ds((base + tile) * part_rows + row, 8, stride=part_rows), :] = source[
                tile : tile + 8, row * FACTOR : (row + 1) * FACTOR
            ]


def pack_kernel(re_lines, im_lines, re_other, im_other, ref_own, ref_other, off_own, off_other, *refs):
    messages, (re_all, im_all, ref_all) = refs[:-3], refs[-3:]
    bins, samples = re_other.shape
    part_rows = samples // FACTOR
    place, side = lax.axis_index("az"), lax.axis_index("rg")
    own_at, other_at = EDGE + side * bins, EDGE + (1 - side) * bins
    zeros = jnp.zeros((EDGE * part_rows, FACTOR), jnp.float32)
    for all_ref, own, other in ((re_all, re_lines, re_other), (im_all, im_lines, im_other)):
        all_ref[: EDGE * part_rows, :] = zeros
        all_ref[(EDGE + 2 * bins) * part_rows :, :] = zeros
        all_ref[pl.ds(pl.multiple_of(own_at * part_rows, 8), bins * part_rows), :] = own[...]
        spread_lines(all_ref, other_at, other)
    ref_all[:EDGE, :] = jnp.zeros((EDGE, FACTOR), jnp.float32)
    ref_all[EDGE + 2 * bins :, :] = jnp.zeros((EDGE, FACTOR), jnp.float32)
    for at, ref in ((own_at, ref_own), (other_at, ref_other)):
        ref_all[pl.ds(pl.multiple_of(at, 16), bins), :] = jnp.concatenate([ref[...], ref[...]], axis=1)
    lane = lax.broadcasted_iota(jnp.int32, (1, FACTOR), 1)
    for at, message in enumerate(messages):
        body = WINDOW * part_rows
        start = window_start(((place >> 1) ^ at) * 2 + side, side, off_own, off_other) + EDGE
        rows = pl.ds(pl.multiple_of(start * part_rows, 8), body)
        message[:body, :] = re_all[rows, :]
        message[body : 2 * body, :] = im_all[rows, :]
        for bin_num in range(REF_LINES):
            low = ref_all[pl.ds(start + bin_num, 1), :]
            high = ref_all[pl.ds(start + REF_LINES + bin_num, 1), :]
            message[2 * body + bin_num : 2 * body + bin_num + 1, :] = jnp.where(lane < HALF, low, high)


def phase_kernel(bins_total, off_own, off_other, owners, taps_own, taps_other, out, weights, choice):
    place, side = lax.axis_index("az"), lax.axis_index("rg")
    bins_held = taps_own.shape[0]
    held = lax.div(place * OUT_BINS, bins_held) == side
    local = lax.rem(place * OUT_BINS, bins_held)
    for bin_num in range(OUT_BINS):
        for tap in range(TAPS):
            weight = jnp.where(held, taps_own[local + bin_num, tap], taps_other[local + bin_num, tap])
            line = bin_num * TAPS + tap
            weights[line : line + 1, :] = jnp.full((1, FACTOR), weight, jnp.float32)
    line = lax.broadcasted_iota(jnp.int32, (2 * len(STEPS), FACTOR), 0)
    for which in range(2):
        owner = owners[which]
        step = (owner >> 1) ^ (place >> 1)
        wanted = jnp.where((owner & 1) == side, step, step + len(STEPS))
        choice[which] = jnp.where(line == wanted, 1.0, 0.0)
    start = window_start(place, side, off_own, off_other)
    shape = (HALF, FACTOR)
    kappa = lax.broadcasted_iota(jnp.int32, shape, 0)
    frequency = 2 * kappa + side + FACTOR * lax.broadcasted_iota(jnp.int32, shape, 1)
    total = FACTOR * FACTOR
    signed = jnp.where(frequency >= total // 2, frequency - total, frequency)
    az_freq = signed.astype(jnp.float32) / total
    az_square = az_freq * az_freq
    for bin_num in range(WINDOW):
        rg_index = (start + bin_num).astype(jnp.float32)
        rg_freq = (rg_index + 0.5) / (2 * bins_total) - 0.25
        base = (1.0 + rg_freq) * (1.0 + rg_freq)
        root = jnp.sqrt(base - az_square)
        cosine, sine = cos_sin_quarters(root * (PHASE_GAIN * 2 / math.pi))
        out[bin_num, 0] = cosine
        out[bin_num, 1] = sine


def parity_kernel(*refs):
    chunks = dict(zip(STEPS, refs))
    keep, give = refs[len(STEPS) :]
    place, side = lax.axis_index("az"), lax.axis_index("rg")
    sign = jnp.where(place >= PLACES // 2, -1.0, 1.0)
    even = side == 0
    keep_near, keep_far = jnp.where(even, 1.0, sign), jnp.where(even, 1.0, -sign)
    give_near, give_far = jnp.where(even, sign, 1.0), jnp.where(even, -sign, 1.0)
    plain = ((place >> 1) & 1) == 0
    for line in range(2 * WINDOW):
        read = slice(line * PART, (line + 1) * PART)
        write = line * 2 * PART
        values = [chunks[step][read, :] for step in range(4)]
        for target, near_factor, far_factor in ((keep, keep_near, keep_far), (give, give_near, give_far)):
            pair = [values[step] * near_factor + values[step + 2] * far_factor for step in range(2)]
            target[write : write + PART, :] = jnp.where(plain, pair[0], pair[1])
            target[write + PART : write + 2 * PART, :] = jnp.where(plain, pair[1], pair[0])
    for step in range(len(STEPS)):
        value = chunks[step][2 * WINDOW * PART :, :]
        at = 2 * WINDOW * 2 * PART + step * REF_LINES
        keep[at : at + REF_LINES, :] = value
        give[at : at + REF_LINES, :] = value


def gather_lines(ref, bins, group):
    width = 2 * PART
    columns = [
        jnp.concatenate(
            [ref[(part * bins + bin_num) * width : (part * bins + bin_num + 1) * width, :] for part in range(2)], axis=0
        )
        for bin_num in group
    ]
    return jnp.concatenate(columns, axis=1)


def bin_groups(bins):
    return [range(at, min(at + 4, bins)) for at in range(0, bins, 4)]


def near_kernel(keep, near, out):
    matrix = near[lax.axis_index("rg")]
    for index, group in enumerate(bin_groups(WINDOW)):
        out[index, :, : len(group) * FACTOR] = dot(matrix, long_rows(gather_lines(keep, WINDOW, group)))


def band_kernel(
    partial, keep, got, phase, weights, choice, far, there, back, last, twists, keep_out, give_out, spectra, band, picked
):
    side = lax.axis_index("rg")
    bins = WINDOW

    lane = lax.broadcasted_iota(jnp.int32, (REF_LINES, FACTOR), 1)
    lines = []
    for which in range(2):
        value = jnp.zeros((REF_LINES, FACTOR), jnp.float32)
        for option in range(2 * len(STEPS)):
            at = 2 * bins * 2 * PART + option % len(STEPS) * REF_LINES
            candidate = (keep if option < len(STEPS) else got)[at : at + REF_LINES, :]
            value = jnp.where(choice[which, option : option + 1, :] > 0.5, candidate, value)
        lines.append(value)
    for block in range(2):
        coarse = (lane >> 1) + block * HALF
        wide = [jnp.take_along_axis(lines[which], coarse, axis=1) for which in range(2)]
        ref_phase = jnp.where(lane < HALF, wide[1], wide[0])
        ref_cos, ref_sin = cos_sin_quarters(ref_phase * (2 / math.pi))
        picked[0, block * REF_LINES : (block + 1) * REF_LINES, :] = ref_cos
        picked[1, block * REF_LINES : (block + 1) * REF_LINES, :] = ref_sin

    far, last = far[side], (last[0, side], last[1, side])
    there, back = (there[0], there[1]), (back[0], back[1])
    twist_cos, twist_sin = twists[side, 0], twists[side, 1]
    for number, group in enumerate(bin_groups(bins)):
        passed = partial[number, :, : len(group) * FACTOR] + dot(far, long_rows(gather_lines(got, bins, group)))
        rows = []
        for index in range(len(group)):
            real = passed[:HALF, index * FACTOR : (index + 1) * FACTOR]
            imag = passed[HALF:, index * FACTOR : (index + 1) * FACTOR]
            rows.append(
                jnp.concatenate([real * twist_cos + imag * twist_sin, imag * twist_cos - real * twist_sin], axis=1)
            )
        passed = dot_split(split_bf16(jnp.concatenate(rows, axis=0)), there)
        for index, bin_num in enumerate(group):
            real = passed[index * HALF : (index + 1) * HALF, :FACTOR]
            imag = passed[index * HALF : (index + 1) * HALF, FACTOR:]
            model_cos, model_sin = phase[bin_num, 0], phase[bin_num, 1]
            row_cos, row_sin = picked[0, bin_num : bin_num + 1, :], picked[1, bin_num : bin_num + 1, :]
            cosine = model_cos * row_cos - model_sin * row_sin
            sine = model_sin * row_cos + model_cos * row_sin
            spectra[bin_num, 0] = real * cosine - imag * sine
            spectra[bin_num, 1] = real * sine + imag * cosine

    strip = 8
    for part in range(2):
        for at in range(0, HALF, strip):
            rows = slice(at, at + strip)
            sums = {}
            for bin_num in range(bins):
                value = spectra[bin_num, part, rows]
                for out in range(max(0, bin_num - TAPS + 1), min(OUT_BINS, bin_num + 1)):
                    weight = out * TAPS + bin_num - out
                    term = value * weights[weight : weight + 1, :]
                    sums[out] = sums[out] + term if out in sums else term
            for out in range(OUT_BINS):
                line = out * HALF + at
                band[line : line + strip, part * FACTOR : (part + 1) * FACTOR] = sums[out]

    scale = 1.0 / (FACTOR * FACTOR)
    cos_table, sin_table = twist_cos * scale, twist_sin * scale
    for at in range(0, OUT_BINS, 4):
        passed = dot_split(split_bf16(band[at * HALF : (at + 4) * HALF, :]), back)
        columns = []
        for index in range(4):
            real = passed[index * HALF : (index + 1) * HALF, :FACTOR]
            imag = passed[index * HALF : (index + 1) * HALF, FACTOR:]
            columns.append(
                jnp.concatenate([real * cos_table - imag * sin_table, imag * cos_table + real * sin_table], axis=0)
            )
        passed = dot_split(last, split_bf16(jnp.concatenate(columns, axis=1)))
        for index in range(4):
            lines = slice((at + index) * HALF, (at + index + 1) * HALF)
            keep_out[lines, :] = passed[:HALF, index * FACTOR : (index + 1) * FACTOR]
            give_out[lines, :] = passed[HALF:, index * FACTOR : (index + 1) * FACTOR]


def crossed(quarter):
    return ((quarter & 1) << 1) | (quarter >> 1)


def join_kernel(keep, got, *messages):
    place, side = lax.axis_index("az"), lax.axis_index("rg")
    quarter = lax.rem(place, PLACES // 2)
    sign = jnp.where(side == 0, 1.0, -1.0)
    for step, message in enumerate(messages):
        target = crossed(quarter) ^ step
        top, middle = target >> 1, target & 1
        keep_factor, got_factor = jnp.where(top == 0, 1.0, sign), jnp.where(top == 0, 1.0, -sign)
        for line in range(2 * OUT_BINS):
            read = pl.ds(pl.multiple_of(line * 2 * PART + middle * PART, 8), PART)
            message[line * PART : (line + 1) * PART, :] = keep[read, :] * keep_factor + got[read, :] * got_factor


def place_kernel(*refs):
    messages, (out_re, out_im, re_all, im_all) = refs[:-4], refs[-4:]
    bins, samples = out_re.shape
    place = lax.axis_index("az")
    for at, message in enumerate(messages):
        sender = crossed((place >> 1) ^ at)
        for out in range(OUT_BINS):
            line = pl.multiple_of((sender * OUT_BINS + out) * PART, 8)
            re_all[pl.ds(line, PART), :] = message[2 * out * PART : (2 * out + 1) * PART, :]
            im_all[pl.ds(line, PART), :] = message[(2 * out + 1) * PART : (2 * out + 2) * PART, :]
    for out, all_ref in ((out_re, re_all), (out_im, im_all)):
        for tile in range(0, bins, 8):
            for row in range(PART):
                out[tile : tile + 8, row * FACTOR : (row + 1) * FACTOR] = all_ref[
                    pl.ds(tile * PART + row, 8, stride=PART), :
                ]


VMEM = pl.BlockSpec(memory_space=pltpu.VMEM)
SMEM = pl.BlockSpec(memory_space=pltpu.SMEM)


def kernel_call(body, name, out_shape, operands, scratch=(), flops=0, count=10**6, limit=8):
    specs = [SMEM if operand.size <= 256 else VMEM for operand in operands]
    return pl.pallas_call(
        body,
        out_shape=out_shape,
        in_specs=specs,
        out_specs=jax.tree.map(lambda _: VMEM, out_shape),
        scratch_shapes=[pltpu.VMEM(shape, jnp.float32) for shape in scratch],
        compiler_params=pltpu.CompilerParams(vmem_limit_bytes=limit * 1024 * 1024),
        cost_estimate=pl.CostEstimate(flops=flops, bytes_accessed=count, transcendentals=0),
        name=name,
    )(*operands)


def transposed_shards(raw_re, raw_im, ref_blocks, owners, offsets, taps):
    bins, samples = raw_re.shape

    def array(*shape):
        return jax.ShapeDtypeStruct(shape, jnp.float32)

    matrices, twists = dft_constants()
    near_table, *tables = [jnp.asarray(table) for table in (*matrices, twists)]
    swap = functools.partial(lax.ppermute, axis_name="rg", perm=[(0, 1), (1, 0)])
    half = PLACES // 2
    ref_own = ref_blocks[0].T
    offsets_other = swap(offsets)
    ref_other, re_other, im_other, taps_other = swap(ref_own), swap(raw_re), swap(raw_im), swap(taps)

    lines = [raw_re.reshape(bins * PART, FACTOR), raw_im.reshape(bins * PART, FACTOR)]
    all_bins = 2 * bins + 2 * EDGE
    messages = kernel_call(
        pack_kernel,
        "pack",
        [array(2 * WINDOW * PART + REF_LINES, FACTOR)] * half,
        [*lines, re_other, im_other, ref_own, ref_other, offsets, offsets_other],
        scratch=[(all_bins * PART, FACTOR), (all_bins * PART, FACTOR), (all_bins, FACTOR)],
        count=4 * 10**6,
    )
    prepared = kernel_call(
        functools.partial(phase_kernel, 2 * bins),
        "phase",
        [array(WINDOW, 2, HALF, FACTOR), array(OUT_BINS * TAPS, FACTOR), array(2, 2 * half, FACTOR)],
        [offsets, offsets_other, owners, taps, taps_other],
    )

    routes = [
        [
            (chip * 2 + core, (((chip >> 1) ^ step) * 2 + core) * 2 + (chip & 1))
            for chip in range(PLACES)
            for core in range(2)
        ]
        for step in range(half)
    ]
    routes_back = [
        [
            (chip * 2 + core, ((crossed(chip % half) ^ step) * 2 + core) * 2 + chip // half)
            for chip in range(PLACES)
            for core in range(2)
        ]
        for step in range(half)
    ]
    arrived = [lax.ppermute(messages[step], ("az", "rg"), routes[step]) for step in STEPS]
    *arrived, phases, weights, choice = lax.optimization_barrier((*arrived, *prepared))

    size = 2 * WINDOW * 2 * PART + half * REF_LINES
    keep, give = kernel_call(parity_kernel, "parity", [array(size, FACTOR)] * 2, arrived)
    got = swap(give)
    partial = kernel_call(
        near_kernel, "near", array(len(bin_groups(WINDOW)), FACTOR, 4 * FACTOR), [keep, near_table]
    )
    keep, give = kernel_call(
        band_kernel,
        "band",
        [array(OUT_BINS * HALF, FACTOR)] * 2,
        [partial, keep, got, phases, weights, choice, *tables],
        scratch=[(WINDOW, 2, HALF, FACTOR), (OUT_BINS * HALF, 2 * FACTOR), (2, 2 * REF_LINES, FACTOR)],
        limit=16,
    )
    sent = kernel_call(join_kernel, "join", [array(2 * OUT_BINS * PART, FACTOR)] * half, [keep, swap(give)])
    results = [lax.ppermute(message, ("az", "rg"), route) for message, route in zip(sent, routes_back)]
    return kernel_call(
        place_kernel, "place", [array(bins, samples)] * 2, results, scratch=[(bins * PART, FACTOR)] * 2
    )


def solution(mesh):
    sizes = mesh.shape

    def whole(raw_re, raw_im, ref_blocks, owners, offsets, taps):
        line = raw_re.shape[1] // sizes["scene"]
        fits = (
            sizes["rg"] == 2
            and sizes["az"] == PLACES
            and raw_re.shape[0] == OUT_BINS * PLACES
            and line == FACTOR * FACTOR
            and ref_blocks.shape[1] == HALF
        )
        return jax.shard_map(
            transposed_shards if fits else butterfly_shards,
            mesh=mesh,
            in_specs=(
                P("rg", ("scene", "az")),
                P("rg", ("scene", "az")),
                P(("scene", "az"), None, "rg"),
                P("scene"),
                P("rg"),
                P("rg", None),
            ),
            out_specs=(P("rg", ("scene", "az")), P("rg", ("scene", "az"))),
            check_vma=False,
        )(raw_re, raw_im, ref_blocks, owners, offsets, taps)

    return whole
```

```python
import functools
import math

import jax
import jax.numpy as jnp
import numpy as np
from jax import lax
from jax.experimental import pallas as pl
from jax.experimental.pallas import tpu as pltpu
from jax.sharding import PartitionSpec as P

SPLIT = 4
TAPS = 8
REACH = 8
BLOCK = 16


PRECISE = lax.Precision.HIGHEST
PHASE_GAIN = 50.0


def partner_2(value, axis, stride):
    return lax.ppermute(value, axis, [(i, i ^ 1 << stride) for i in range(lax.axis_size(axis))])


def from_root(block, axis, source):
    block = jnp.where(lax.axis_index(axis) == source, block, jnp.zeros_like(block))
    return lax.psum(block, axis)


def padded_2(value, sides, width):
    for axis, dim in sides:
        size, length = (lax.axis_size(axis), value.shape[dim])
        up = [(i, (i + 1) % size) for i in range(size - 1)]
        down = [(j, i) for i, j in up]
        last = lax.slice_in_dim(value, length - width, length, axis=dim)
        initial = lax.slice_in_dim(value, 0, width, axis=dim)
        before = lax.ppermute(last, axis, up)
        after = lax.ppermute(initial, axis, down)
        value = jnp.concatenate([before, value, after], axis=dim)
    return value


def angles(numerator, denominator, sign_value):
    return sign_value * 2.0 * math.pi * numerator.astype(jnp.float32) / denominator


def rotate(signal, cosine, sine_part):
    real_part = signal[0] * cosine - signal[1] * sine_part
    imag_part = signal[0] * sine_part + signal[1] * cosine
    return jnp.stack([real_part, imag_part])


def dft_table(length_n, sign_value):
    counter = jnp.arange(length_n, dtype=jnp.int32)
    turn_count = counter[:, None] * counter[None, :] % length_n
    angle_set = angles(turn_count, length_n, sign_value)
    return (jnp.cos(angle_set), jnp.sin(angle_set))


def complex_apply(einsum_form, cosine, sine_part, signal):
    real_part = jnp.einsum(einsum_form, cosine, signal[0], precision=PRECISE) - jnp.einsum(
        einsum_form, sine_part, signal[1], precision=PRECISE
    )
    imag_part = jnp.einsum(einsum_form, cosine, signal[1], precision=PRECISE) + jnp.einsum(
        einsum_form, sine_part, signal[0], precision=PRECISE
    )
    return jnp.stack([real_part, imag_part])


def local_dft(signal, sign_value):
    rg_cols = signal.shape[1]
    az_rows = signal.shape[2]
    inner_len = az_rows // SPLIT
    shaped = signal.reshape(2, rg_cols, SPLIT, inner_len)
    first_cos, first_sin = dft_table(SPLIT, sign_value)
    first_pass = complex_apply("aj,cjk->cak", first_cos, first_sin, shaped)
    outer_idx = jnp.arange(SPLIT, dtype=jnp.int32)
    inner_idx = jnp.arange(inner_len, dtype=jnp.int32)
    twist = angles(outer_idx[:, None] * inner_idx[None, :] % az_rows, az_rows, sign_value)
    first_pass = rotate(first_pass, jnp.cos(twist)[None, :, :], jnp.sin(twist)[None, :, :])
    second_cos, second_sin = dft_table(inner_len, sign_value)
    second_pass = complex_apply("bk,cak->cba", second_cos, second_sin, first_pass)
    return second_pass.reshape(2, rg_cols, az_rows)


def butterfly_down(signal, az_place, bit_count):
    for bit_num in reversed(range(bit_count)):
        half_span = 1 << bit_num
        partner = partner_2(signal, "az", bit_num)
        is_upper = az_place >> bit_num & 1 == 1
        angle_set = angles(az_place % half_span, 2 * half_span, -1.0)
        difference = rotate(partner - signal, jnp.cos(angle_set), jnp.sin(angle_set))
        signal = jnp.where(is_upper, difference, signal + partner)
    return signal


def butterfly_up(signal, az_place, bit_count):
    for bit_num in range(bit_count):
        half_span = 1 << bit_num
        partner = partner_2(signal, "az", bit_num)
        is_upper = az_place >> bit_num & 1 == 1
        angle_set = angles(az_place % half_span, 2 * half_span, 1.0)
        cosine = jnp.cos(angle_set)
        sine_part = jnp.sin(angle_set)
        lower_new = (signal + rotate(partner, cosine, sine_part)) * 0.5
        upper_new = (partner - rotate(signal, cosine, sine_part)) * 0.5
        signal = jnp.where(is_upper, upper_new, lower_new)
    return signal


def butterfly_shards(raw_re, raw_im, ref_blocks, owners, offsets, taps):
    rg_cols = raw_re.shape[0]
    az_rows = raw_re.shape[1]
    az_count = lax.axis_size("az")
    az_place = lax.axis_index("az")
    bit_count = az_count.bit_length() - 1
    az_total = az_rows * az_count
    rg_total = rg_cols * lax.axis_size("rg")
    own_block = ref_blocks[0]
    lower_ref = from_root(own_block, "az", owners[0])
    upper_ref = from_root(own_block, "az", owners[1])
    signal = jnp.stack([raw_re, raw_im])
    signal = butterfly_down(signal, az_place, bit_count)
    column = jnp.zeros((), jnp.int32)
    for bit_num in range(bit_count):
        column = column + ((az_place >> bit_num & 1) << bit_count - 1 - bit_num)
    row_index = jnp.arange(az_rows, dtype=jnp.int32)
    twist = angles(row_index * column % az_total, az_total, -1.0)
    signal = rotate(signal, jnp.cos(twist)[None, :], jnp.sin(twist)[None, :])
    signal = local_dft(signal, -1.0)
    frequency = column + az_count * row_index
    signed = (frequency + az_total // 2) % az_total - az_total // 2
    az_freq = signed.astype(jnp.float32) / az_total
    rg_index = lax.axis_index("rg") * rg_cols + jnp.arange(rg_cols, dtype=jnp.int32)
    rg_freq = (rg_index.astype(jnp.float32) + 0.5) / (2 * rg_total) - 0.25
    model_phase = PHASE_GAIN * jnp.sqrt((1.0 + rg_freq)[:, None] ** 2 - az_freq[None, :] ** 2)
    ref_rows = own_block.shape[0]
    coarse = frequency * ref_rows // az_total
    slot_index = jnp.where(signed >= 0, ref_rows + coarse, coarse)
    one_hot = (jnp.arange(2 * ref_rows, dtype=jnp.int32)[:, None] == slot_index[None, :]).astype(
        jnp.float32
    )
    both_refs = jnp.concatenate([lower_ref, upper_ref], axis=0)
    picked = jnp.dot(both_refs.T, one_hot, precision=PRECISE)
    phase_all = model_phase + picked
    signal = rotate(signal, jnp.cos(phase_all), jnp.sin(phase_all))
    rim_width = REACH + TAPS // 2
    padded = padded_2(signal, (("rg", 1),), rim_width)
    offset_cols = jnp.repeat(offsets, BLOCK)
    local_cols = jnp.arange(rg_cols, dtype=jnp.int32)
    tap_index = jnp.arange(TAPS, dtype=jnp.int32)
    target = local_cols[:, None] + rim_width + offset_cols[:, None] + tap_index[None, :] - TAPS // 2
    padded_index = jnp.arange(rg_cols + 2 * rim_width, dtype=jnp.int32)
    hits = (padded_index[:, None, None] == target[None, :, :]).astype(jnp.float32)
    band_matrix = jnp.sum(hits * taps[None, :, :], axis=2)
    signal = jnp.einsum("zma,mi->zia", padded, band_matrix, precision=PRECISE)
    signal = local_dft(signal, 1.0) / az_rows
    twist_back = angles(row_index * column % az_total, az_total, 1.0)
    signal = rotate(signal, jnp.cos(twist_back)[None, :], jnp.sin(twist_back)[None, :])
    signal = butterfly_up(signal, az_place, bit_count)
    return (signal[0], signal[1])


FACTOR = 128
PLACES = 8
PART = FACTOR // PLACES
HALF = FACTOR // 2
OUT_BINS = 8
WINDOW = OUT_BINS + TAPS - 1
REF_LINES = 8
EDGE = 16
STEPS = (0, 1, 2, 3)


def split_bf16(value):
    high = value.astype(jnp.bfloat16)
    low = (value - high.astype(jnp.float32)).astype(jnp.bfloat16)
    return high, low


def dot(left, right):
    return jnp.dot(left, right, preferred_element_type=jnp.float32)


def dot_split(left, right):
    return dot(left[0], right[0]) + (dot(left[0], right[1]) + dot(left[1], right[0]))


def both_bf16(matrix):
    high = matrix.astype(jnp.bfloat16)
    return np.stack([high, (matrix - high.astype(np.float64)).astype(jnp.bfloat16)])


def long_bf16(matrix):
    high, low = both_bf16(matrix)
    return np.concatenate([high, high, low], axis=-1)


def long_rows(value):
    high, low = split_bf16(value)
    return jnp.concatenate([high, low, high], axis=0)


def dft_constants():
    counter = np.arange(FACTOR)
    kappa = np.arange(HALF)
    near, far, last, twists = [], [], [], []
    for side in range(2):
        order = [(middle, low, line) for low in (side, 1 - side) for middle in range(2) for line in range(PART)]
        mine = np.array([(2 * middle + low) * PART + line for middle, low, line in order])
        angle = 2 * np.pi * (np.outer(2 * kappa + side, mine) % FACTOR) / FACTOR
        cosine, sine = np.cos(angle), np.sin(angle)
        whole = np.block([[cosine, sine], [-sine, cosine]])
        quarters = np.split(whole, 4, axis=1)
        near.append(np.concatenate(quarters[0::2], axis=1))
        far.append(np.concatenate(quarters[1::2], axis=1))
        back_re, back_im = np.block([cosine.T, -sine.T]), np.block([sine.T, cosine.T])
        own, other = slice(0, HALF // 2), slice(HALF // 2, HALF)
        last.append(np.concatenate([back_re[own], back_im[own], back_re[other], back_im[other]]))
        twist = 2 * np.pi * np.outer(2 * kappa + side, counter) / FACTOR**2
        twists.append(np.stack([np.cos(twist), np.sin(twist)]))
    angle = 2 * np.pi * (np.outer(counter, counter) % FACTOR) / FACTOR
    cosine, sine = np.cos(angle), np.sin(angle)
    there = np.block([[cosine, -sine], [sine, cosine]])
    back = np.block([[cosine, sine], [-sine, cosine]])
    matrices = [
        long_bf16(np.stack(near)),
        long_bf16(np.stack(far)),
        both_bf16(there),
        both_bf16(back),
        both_bf16(np.stack(last)),
    ]
    return matrices, np.stack(twists).astype(np.float32)


def cos_sin_quarters(quarters):
    whole = jnp.floor(quarters + 0.5)
    rest = (quarters - whole) * (math.pi / 2)
    square = rest * rest
    sine = rest + rest * square * (
        -1.6666654611e-1 + square * (8.3321608736e-3 + square * (-1.9515295891e-4))
    )
    cosine = 1.0 - 0.5 * square + square * square * (
        4.166664568298827e-2 + square * (-1.388731625493765e-3 + square * 2.443315711809948e-5)
    )
    number = whole.astype(jnp.int32)
    odd = (number & 1) == 1
    turned_cos = jnp.where(odd, sine, cosine)
    turned_sin = jnp.where(odd, cosine, sine)
    cos_sign = jnp.where(((number + 1) & 2) == 2, -1.0, 1.0)
    sin_sign = jnp.where((number & 2) == 2, -1.0, 1.0)
    return turned_cos * cos_sign, turned_sin * sin_sign


def window_start(chip, side, offsets_own, offsets_other):
    block = chip * OUT_BINS // BLOCK
    blocks = offsets_own.shape[0]
    local = lax.rem(block, blocks)
    shift = jnp.where(lax.div(block, blocks) == side, offsets_own[local], offsets_other[local])
    return chip * OUT_BINS + shift - TAPS // 2


def spread_lines(target, base, source):
    bins, samples = source.shape
    part_rows = samples // FACTOR
    for tile in range(0, bins, 8):
        for row in range(part_rows):
            target[pl.ds((base + tile) * part_rows + row, 8, stride=part_rows), :] = source[
                tile : tile + 8, row * FACTOR : (row + 1) * FACTOR
            ]


def met(place, step, low):
    return (place >> 1) ^ step ^ (2 * low)


def pack_kernel(re_lines, im_lines, re_other, im_other, ref_own, ref_other, own_offsets, other_offsets, *refs):
    messages, (re_all, im_all, ref_all, off_own, off_other, sems) = refs[:-6], refs[-6:]
    copies = [
        pltpu.make_async_copy(source, target, sems.at[at])
        for at, (source, target) in enumerate(((own_offsets, off_own), (other_offsets, off_other)))
    ]
    for copy in copies:
        copy.start()
    bins, samples = re_other.shape
    part_rows = samples // FACTOR
    place, side = lax.axis_index("az"), lax.axis_index("rg")
    own_at, other_at = EDGE + side * bins, EDGE + (1 - side) * bins
    zeros = jnp.zeros((EDGE * part_rows, FACTOR), jnp.float32)
    for all_ref, own, other in ((re_all, re_lines, re_other), (im_all, im_lines, im_other)):
        all_ref[: EDGE * part_rows, :] = zeros
        all_ref[(EDGE + 2 * bins) * part_rows :, :] = zeros
        all_ref[pl.ds(pl.multiple_of(own_at * part_rows, 8), bins * part_rows), :] = own[...]
        spread_lines(all_ref, other_at, other)
    ref_all[:EDGE, :] = jnp.zeros((EDGE, FACTOR), jnp.float32)
    ref_all[EDGE + 2 * bins :, :] = jnp.zeros((EDGE, FACTOR), jnp.float32)
    for at, ref in ((own_at, ref_own), (other_at, ref_other)):
        ref_all[pl.ds(pl.multiple_of(at, 16), bins), :] = jnp.concatenate([ref[...], ref[...]], axis=1)
    for copy in copies:
        copy.wait()
    lane = lax.broadcasted_iota(jnp.int32, (1, FACTOR), 1)
    for at, message in enumerate(messages):
        body = WINDOW * part_rows
        start = window_start(met(place, at, place & 1) * 2 + side, side, off_own, off_other) + EDGE
        rows = pl.ds(pl.multiple_of(start * part_rows, 8), body)
        message[:body, :] = re_all[rows, :]
        message[body : 2 * body, :] = im_all[rows, :]
        for bin_num in range(REF_LINES):
            low = ref_all[pl.ds(start + bin_num, 1), :]
            high = ref_all[pl.ds(start + REF_LINES + bin_num, 1), :]
            message[2 * body + bin_num : 2 * body + bin_num + 1, :] = jnp.where(lane < HALF, low, high)


def phase_kernel(bins_total, off_own, off_other, owners, taps_own, taps_other, out, weights, choice):
    place, side = lax.axis_index("az"), lax.axis_index("rg")
    bins_held = taps_own.shape[0]
    held = lax.div(place * OUT_BINS, bins_held) == side
    local = lax.rem(place * OUT_BINS, bins_held)
    for bin_num in range(OUT_BINS):
        for tap in range(TAPS):
            weight = jnp.where(held, taps_own[local + bin_num, tap], taps_other[local + bin_num, tap])
            line = bin_num * TAPS + tap
            weights[line : line + 1, :] = jnp.full((1, FACTOR), weight, jnp.float32)
    line = lax.broadcasted_iota(jnp.int32, (2 * len(STEPS), FACTOR), 0)
    for which in range(2):
        owner = owners[which]
        step = met(place, owner >> 1, owner & 1)
        wanted = jnp.where((owner & 1) == side, step, step + len(STEPS))
        choice[which] = jnp.where(line == wanted, 1.0, 0.0)
    start = window_start(place, side, off_own, off_other)
    shape = (HALF, FACTOR)
    kappa = lax.broadcasted_iota(jnp.int32, shape, 0)
    frequency = 2 * kappa + side + FACTOR * lax.broadcasted_iota(jnp.int32, shape, 1)
    total = FACTOR * FACTOR
    signed = jnp.where(frequency >= total // 2, frequency - total, frequency)
    az_freq = signed.astype(jnp.float32) / total
    az_square = az_freq * az_freq
    for bin_num in range(WINDOW):
        rg_index = (start + bin_num).astype(jnp.float32)
        rg_freq = (rg_index + 0.5) / (2 * bins_total) - 0.25
        base = (1.0 + rg_freq) * (1.0 + rg_freq)
        root = jnp.sqrt(base - az_square)
        cosine, sine = cos_sin_quarters(root * (PHASE_GAIN * 2 / math.pi))
        out[bin_num, 0] = cosine
        out[bin_num, 1] = sine


def parity_kernel(*refs):
    chunks = dict(zip(STEPS, refs))
    keep, give = refs[len(STEPS) :]
    place, side = lax.axis_index("az"), lax.axis_index("rg")
    sign = jnp.where((place >> 2) ^ side == 1, -1.0, 1.0)
    even = side == 0
    keep_near, keep_far = jnp.where(even, 1.0, sign), jnp.where(even, 1.0, -sign)
    give_near, give_far = jnp.where(even, sign, 1.0), jnp.where(even, -sign, 1.0)
    plain = ((place >> 1) & 1) == 0
    for line in range(2 * WINDOW):
        read = slice(line * PART, (line + 1) * PART)
        write = line * 2 * PART
        values = [chunks[step][read, :] for step in range(4)]
        for target, near_factor, far_factor in ((keep, keep_near, keep_far), (give, give_near, give_far)):
            pair = [values[step] * near_factor + values[step + 2] * far_factor for step in range(2)]
            target[write : write + PART, :] = jnp.where(plain, pair[0], pair[1])
            target[write + PART : write + 2 * PART, :] = jnp.where(plain, pair[1], pair[0])
    for step in range(len(STEPS)):
        value = chunks[step][2 * WINDOW * PART :, :]
        at = 2 * WINDOW * 2 * PART + step * REF_LINES
        keep[at : at + REF_LINES, :] = value
        give[at : at + REF_LINES, :] = value


def gather_lines(ref, bins, group):
    width = 2 * PART
    columns = [
        jnp.concatenate(
            [ref[(part * bins + bin_num) * width : (part * bins + bin_num + 1) * width, :] for part in range(2)], axis=0
        )
        for bin_num in group
    ]
    return jnp.concatenate(columns, axis=1)


def bin_groups(bins):
    return [range(at, min(at + 4, bins)) for at in range(0, bins, 4)]


def near_kernel(keep, near, out):
    matrix = near[lax.axis_index("rg")]
    for index, group in enumerate(bin_groups(WINDOW)):
        out[index, :, : len(group) * FACTOR] = dot(matrix, long_rows(gather_lines(keep, WINDOW, group)))


def band_kernel(
    partial, keep, got, phase, weights, choice, far, there, back, last, twists, keep_out, give_out, spectra, band, picked
):
    side = lax.axis_index("rg")
    bins = WINDOW

    lane = lax.broadcasted_iota(jnp.int32, (REF_LINES, FACTOR), 1)
    lines = []
    for which in range(2):
        value = jnp.zeros((REF_LINES, FACTOR), jnp.float32)
        for option in range(2 * len(STEPS)):
            at = 2 * bins * 2 * PART + option % len(STEPS) * REF_LINES
            candidate = (keep if option < len(STEPS) else got)[at : at + REF_LINES, :]
            value = jnp.where(choice[which, option : option + 1, :] > 0.5, candidate, value)
        lines.append(value)
    for block in range(2):
        coarse = (lane >> 1) + block * HALF
        wide = [jnp.take_along_axis(lines[which], coarse, axis=1) for which in range(2)]
        ref_phase = jnp.where(lane < HALF, wide[1], wide[0])
        ref_cos, ref_sin = cos_sin_quarters(ref_phase * (2 / math.pi))
        picked[0, block * REF_LINES : (block + 1) * REF_LINES, :] = ref_cos
        picked[1, block * REF_LINES : (block + 1) * REF_LINES, :] = ref_sin

    far, last = far[side], (last[0, side], last[1, side])
    there, back = (there[0], there[1]), (back[0], back[1])
    twist_cos, twist_sin = twists[side, 0], twists[side, 1]
    for number, group in enumerate(bin_groups(bins)):
        passed = partial[number, :, : len(group) * FACTOR] + dot(far, long_rows(gather_lines(got, bins, group)))
        rows = []
        for index in range(len(group)):
            real = passed[:HALF, index * FACTOR : (index + 1) * FACTOR]
            imag = passed[HALF:, index * FACTOR : (index + 1) * FACTOR]
            rows.append(
                jnp.concatenate([real * twist_cos + imag * twist_sin, imag * twist_cos - real * twist_sin], axis=1)
            )
        passed = dot_split(split_bf16(jnp.concatenate(rows, axis=0)), there)
        for index, bin_num in enumerate(group):
            real = passed[index * HALF : (index + 1) * HALF, :FACTOR]
            imag = passed[index * HALF : (index + 1) * HALF, FACTOR:]
            model_cos, model_sin = phase[bin_num, 0], phase[bin_num, 1]
            row_cos, row_sin = picked[0, bin_num : bin_num + 1, :], picked[1, bin_num : bin_num + 1, :]
            cosine = model_cos * row_cos - model_sin * row_sin
            sine = model_sin * row_cos + model_cos * row_sin
            spectra[bin_num, 0] = real * cosine - imag * sine
            spectra[bin_num, 1] = real * sine + imag * cosine

    strip = 8
    for part in range(2):
        for at in range(0, HALF, strip):
            rows = slice(at, at + strip)
            sums = {}
            for bin_num in range(bins):
                value = spectra[bin_num, part, rows]
                for out in range(max(0, bin_num - TAPS + 1), min(OUT_BINS, bin_num + 1)):
                    weight = out * TAPS + bin_num - out
                    term = value * weights[weight : weight + 1, :]
                    sums[out] = sums[out] + term if out in sums else term
            for out in range(OUT_BINS):
                line = out * HALF + at
                band[line : line + strip, part * FACTOR : (part + 1) * FACTOR] = sums[out]

    scale = 1.0 / (FACTOR * FACTOR)
    cos_table, sin_table = twist_cos * scale, twist_sin * scale
    for at in range(0, OUT_BINS, 4):
        passed = dot_split(split_bf16(band[at * HALF : (at + 4) * HALF, :]), back)
        columns = []
        for index in range(4):
            real = passed[index * HALF : (index + 1) * HALF, :FACTOR]
            imag = passed[index * HALF : (index + 1) * HALF, FACTOR:]
            columns.append(
                jnp.concatenate([real * cos_table - imag * sin_table, imag * cos_table + real * sin_table], axis=0)
            )
        passed = dot_split(last, split_bf16(jnp.concatenate(columns, axis=1)))
        for index in range(4):
            lines = slice((at + index) * HALF, (at + index + 1) * HALF)
            keep_out[lines, :] = passed[:HALF, index * FACTOR : (index + 1) * FACTOR]
            give_out[lines, :] = passed[HALF:, index * FACTOR : (index + 1) * FACTOR]


def crossed(quarter):
    return ((quarter & 1) << 1) | (quarter >> 1)


def join_kernel(keep, got, *messages):
    place, side = lax.axis_index("az"), lax.axis_index("rg")
    quarter = lax.rem(place, PLACES // 2)
    sign = jnp.where(side == 0, 1.0, -1.0)
    for step, message in enumerate(messages):
        target = crossed(quarter) ^ step
        top, middle = target >> 1, target & 1
        keep_factor, got_factor = jnp.where(top == 0, 1.0, sign), jnp.where(top == 0, 1.0, -sign)
        for line in range(2 * OUT_BINS):
            read = pl.ds(pl.multiple_of(line * 2 * PART + middle * PART, 8), PART)
            message[line * PART : (line + 1) * PART, :] = keep[read, :] * keep_factor + got[read, :] * got_factor


def place_kernel(*refs):
    messages, (out_re, out_im, re_all, im_all, tiles, sems) = refs[:-6], refs[-6:]
    bins, samples = out_re.shape
    place = lax.axis_index("az")
    for at, message in enumerate(messages):
        sender = crossed((place >> 1) ^ at)
        for out in range(OUT_BINS):
            line = pl.multiple_of((sender * OUT_BINS + out) * PART, 8)
            re_all[pl.ds(line, PART), :] = message[2 * out * PART : (2 * out + 1) * PART, :]
            im_all[pl.ds(line, PART), :] = message[(2 * out + 1) * PART : (2 * out + 2) * PART, :]
    copies = []
    for out, all_ref in ((out_re, re_all), (out_im, im_all)):
        for tile in range(0, bins, 8):
            at = len(copies)
            for row in range(PART):
                tiles[at, :, row * FACTOR : (row + 1) * FACTOR] = all_ref[pl.ds(tile * PART + row, 8, stride=PART), :]
            copies.append(pltpu.make_async_copy(tiles.at[at], out.at[pl.ds(tile, 8)], sems.at[at]))
            copies[-1].start()
    for copy in copies:
        copy.wait()


VMEM = pl.BlockSpec(memory_space=pltpu.VMEM)
SMEM = pl.BlockSpec(memory_space=pltpu.SMEM)


def kernel_call(body, name, out_shape, operands, scratch=(), flops=0, count=10**6, limit=8):
    specs = [SMEM if operand.size <= 256 else VMEM for operand in operands]
    return pl.pallas_call(
        body,
        out_shape=out_shape,
        in_specs=specs,
        out_specs=jax.tree.map(lambda _: VMEM, out_shape),
        scratch_shapes=[pltpu.VMEM(shape, jnp.float32) for shape in scratch],
        compiler_params=pltpu.CompilerParams(vmem_limit_bytes=limit * 1024 * 1024),
        cost_estimate=pl.CostEstimate(flops=flops, bytes_accessed=count, transcendentals=0),
        name=name,
    )(*operands)


def transposed_shards(raw_re, raw_im, ref_blocks, owners, offsets, taps):
    bins, samples = raw_re.shape

    def array(*shape):
        return jax.ShapeDtypeStruct(shape, jnp.float32)

    matrices, twists = dft_constants()
    near_table, *tables = [jnp.asarray(table) for table in (*matrices, twists)]
    swap = functools.partial(lax.ppermute, axis_name="rg", perm=[(0, 1), (1, 0)])
    half = PLACES // 2
    ref_own = ref_blocks[0].T
    offsets_other = swap(offsets)
    ref_other, re_other, im_other, taps_other = swap(ref_own), swap(raw_re), swap(raw_im), swap(taps)

    lines = [raw_re.reshape(bins * PART, FACTOR), raw_im.reshape(bins * PART, FACTOR)]
    all_bins = 2 * bins + 2 * EDGE
    anywhere = pl.BlockSpec(memory_space=pl.ANY)
    messages = pl.pallas_call(
        pack_kernel,
        out_shape=[array(2 * WINDOW * PART + REF_LINES, FACTOR)] * half,
        in_specs=[VMEM] * 6 + [anywhere] * 2,
        out_specs=[VMEM] * half,
        scratch_shapes=[
            pltpu.VMEM((all_bins * PART, FACTOR), jnp.float32),
            pltpu.VMEM((all_bins * PART, FACTOR), jnp.float32),
            pltpu.VMEM((all_bins, FACTOR), jnp.float32),
            pltpu.SMEM(offsets.shape, jnp.int32),
            pltpu.SMEM(offsets.shape, jnp.int32),
            pltpu.SemaphoreType.DMA((2,)),
        ],
        compiler_params=pltpu.CompilerParams(vmem_limit_bytes=8 * 1024 * 1024),
        cost_estimate=pl.CostEstimate(flops=1, bytes_accessed=1, transcendentals=0),
        name="pack",
    )(*lines, re_other, im_other, ref_own, ref_other, offsets, offsets_other)
    prepared = kernel_call(
        functools.partial(phase_kernel, 2 * bins),
        "phase",
        [array(WINDOW, 2, HALF, FACTOR), array(OUT_BINS * TAPS, FACTOR), array(2, 2 * half, FACTOR)],
        [offsets, offsets_other, owners, taps, taps_other],
    )

    routes = [
        [
            (chip * 2 + core, (met(chip, step, chip & 1) * 2 + core) * 2 + (chip & 1))
            for chip in range(PLACES)
            for core in range(2)
        ]
        for step in range(half)
    ]
    routes_back = [
        [
            (chip * 2 + core, ((crossed(chip % half) ^ step) * 2 + core) * 2 + chip // half)
            for chip in range(PLACES)
            for core in range(2)
        ]
        for step in range(half)
    ]
    arrived = [lax.ppermute(messages[step], ("az", "rg"), routes[step]) for step in STEPS]
    *arrived, phases, weights, choice = lax.optimization_barrier((*arrived, *prepared))

    size = 2 * WINDOW * 2 * PART + half * REF_LINES
    keep, give = kernel_call(parity_kernel, "parity", [array(size, FACTOR)] * 2, arrived)
    got = swap(give)
    partial = kernel_call(
        near_kernel, "near", array(len(bin_groups(WINDOW)), FACTOR, 4 * FACTOR), [keep, near_table]
    )
    keep, give = kernel_call(
        band_kernel,
        "band",
        [array(OUT_BINS * HALF, FACTOR)] * 2,
        [partial, keep, got, phases, weights, choice, *tables],
        scratch=[(WINDOW, 2, HALF, FACTOR), (OUT_BINS * HALF, 2 * FACTOR), (2, 2 * REF_LINES, FACTOR)],
        limit=16,
    )
    sent = kernel_call(join_kernel, "join", [array(2 * OUT_BINS * PART, FACTOR)] * half, [keep, swap(give)])
    results = [lax.ppermute(message, ("az", "rg"), route) for message, route in zip(sent, routes_back)]
    tiles = 2 * bins // 8
    return pl.pallas_call(
        place_kernel,
        out_shape=[array(bins, samples)] * 2,
        in_specs=[VMEM] * half,
        out_specs=[anywhere] * 2,
        scratch_shapes=[
            pltpu.VMEM((bins * PART, FACTOR), jnp.float32),
            pltpu.VMEM((bins * PART, FACTOR), jnp.float32),
            pltpu.VMEM((tiles, 8, samples), jnp.float32),
            pltpu.SemaphoreType.DMA((tiles,)),
        ],
        compiler_params=pltpu.CompilerParams(vmem_limit_bytes=8 * 1024 * 1024),
        cost_estimate=pl.CostEstimate(flops=1, bytes_accessed=1, transcendentals=0),
        name="place",
    )(*results)


def solution(mesh):
    sizes = mesh.shape

    def whole(raw_re, raw_im, ref_blocks, owners, offsets, taps):
        line = raw_re.shape[1] // sizes["scene"]
        fits = (
            sizes["rg"] == 2
            and sizes["az"] == PLACES
            and raw_re.shape[0] == OUT_BINS * PLACES
            and line == FACTOR * FACTOR
            and ref_blocks.shape[1] == HALF
        )
        return jax.shard_map(
            transposed_shards if fits else butterfly_shards,
            mesh=mesh,
            in_specs=(
                P("rg", ("scene", "az")),
                P("rg", ("scene", "az")),
                P(("scene", "az"), None, "rg"),
                P("scene"),
                P("rg"),
                P("rg", None),
            ),
            out_specs=(P("rg", ("scene", "az")), P("rg", ("scene", "az"))),
            check_vma=False,
        )(raw_re, raw_im, ref_blocks, owners, offsets, taps)

    return whole
```

```python
import functools
import math

import jax
import jax.numpy as jnp
import numpy as np
from jax import lax
from jax.experimental import pallas as pl
from jax.experimental.pallas import tpu as pltpu
from jax.sharding import PartitionSpec as P

SPLIT = 4
TAPS = 8
REACH = 8
BLOCK = 16


PRECISE = lax.Precision.HIGHEST
PHASE_GAIN = 50.0


def partner_2(value, axis, stride):
    return lax.ppermute(value, axis, [(i, i ^ 1 << stride) for i in range(lax.axis_size(axis))])


def from_root(block, axis, source):
    block = jnp.where(lax.axis_index(axis) == source, block, jnp.zeros_like(block))
    return lax.psum(block, axis)


def padded_2(value, sides, width):
    for axis, dim in sides:
        size, length = (lax.axis_size(axis), value.shape[dim])
        up = [(i, (i + 1) % size) for i in range(size - 1)]
        down = [(j, i) for i, j in up]
        last = lax.slice_in_dim(value, length - width, length, axis=dim)
        initial = lax.slice_in_dim(value, 0, width, axis=dim)
        before = lax.ppermute(last, axis, up)
        after = lax.ppermute(initial, axis, down)
        value = jnp.concatenate([before, value, after], axis=dim)
    return value


def angles(numerator, denominator, sign_value):
    return sign_value * 2.0 * math.pi * numerator.astype(jnp.float32) / denominator


def rotate(signal, cosine, sine_part):
    real_part = signal[0] * cosine - signal[1] * sine_part
    imag_part = signal[0] * sine_part + signal[1] * cosine
    return jnp.stack([real_part, imag_part])


def dft_table(length_n, sign_value):
    counter = jnp.arange(length_n, dtype=jnp.int32)
    turn_count = counter[:, None] * counter[None, :] % length_n
    angle_set = angles(turn_count, length_n, sign_value)
    return (jnp.cos(angle_set), jnp.sin(angle_set))


def complex_apply(einsum_form, cosine, sine_part, signal):
    real_part = jnp.einsum(einsum_form, cosine, signal[0], precision=PRECISE) - jnp.einsum(
        einsum_form, sine_part, signal[1], precision=PRECISE
    )
    imag_part = jnp.einsum(einsum_form, cosine, signal[1], precision=PRECISE) + jnp.einsum(
        einsum_form, sine_part, signal[0], precision=PRECISE
    )
    return jnp.stack([real_part, imag_part])


def local_dft(signal, sign_value):
    rg_cols = signal.shape[1]
    az_rows = signal.shape[2]
    inner_len = az_rows // SPLIT
    shaped = signal.reshape(2, rg_cols, SPLIT, inner_len)
    first_cos, first_sin = dft_table(SPLIT, sign_value)
    first_pass = complex_apply("aj,cjk->cak", first_cos, first_sin, shaped)
    outer_idx = jnp.arange(SPLIT, dtype=jnp.int32)
    inner_idx = jnp.arange(inner_len, dtype=jnp.int32)
    twist = angles(outer_idx[:, None] * inner_idx[None, :] % az_rows, az_rows, sign_value)
    first_pass = rotate(first_pass, jnp.cos(twist)[None, :, :], jnp.sin(twist)[None, :, :])
    second_cos, second_sin = dft_table(inner_len, sign_value)
    second_pass = complex_apply("bk,cak->cba", second_cos, second_sin, first_pass)
    return second_pass.reshape(2, rg_cols, az_rows)


def butterfly_down(signal, az_place, bit_count):
    for bit_num in reversed(range(bit_count)):
        half_span = 1 << bit_num
        partner = partner_2(signal, "az", bit_num)
        is_upper = az_place >> bit_num & 1 == 1
        angle_set = angles(az_place % half_span, 2 * half_span, -1.0)
        difference = rotate(partner - signal, jnp.cos(angle_set), jnp.sin(angle_set))
        signal = jnp.where(is_upper, difference, signal + partner)
    return signal


def butterfly_up(signal, az_place, bit_count):
    for bit_num in range(bit_count):
        half_span = 1 << bit_num
        partner = partner_2(signal, "az", bit_num)
        is_upper = az_place >> bit_num & 1 == 1
        angle_set = angles(az_place % half_span, 2 * half_span, 1.0)
        cosine = jnp.cos(angle_set)
        sine_part = jnp.sin(angle_set)
        lower_new = (signal + rotate(partner, cosine, sine_part)) * 0.5
        upper_new = (partner - rotate(signal, cosine, sine_part)) * 0.5
        signal = jnp.where(is_upper, upper_new, lower_new)
    return signal


def butterfly_shards(raw_re, raw_im, ref_blocks, owners, offsets, taps):
    rg_cols = raw_re.shape[0]
    az_rows = raw_re.shape[1]
    az_count = lax.axis_size("az")
    az_place = lax.axis_index("az")
    bit_count = az_count.bit_length() - 1
    az_total = az_rows * az_count
    rg_total = rg_cols * lax.axis_size("rg")
    own_block = ref_blocks[0]
    lower_ref = from_root(own_block, "az", owners[0])
    upper_ref = from_root(own_block, "az", owners[1])
    signal = jnp.stack([raw_re, raw_im])
    signal = butterfly_down(signal, az_place, bit_count)
    column = jnp.zeros((), jnp.int32)
    for bit_num in range(bit_count):
        column = column + ((az_place >> bit_num & 1) << bit_count - 1 - bit_num)
    row_index = jnp.arange(az_rows, dtype=jnp.int32)
    twist = angles(row_index * column % az_total, az_total, -1.0)
    signal = rotate(signal, jnp.cos(twist)[None, :], jnp.sin(twist)[None, :])
    signal = local_dft(signal, -1.0)
    frequency = column + az_count * row_index
    signed = (frequency + az_total // 2) % az_total - az_total // 2
    az_freq = signed.astype(jnp.float32) / az_total
    rg_index = lax.axis_index("rg") * rg_cols + jnp.arange(rg_cols, dtype=jnp.int32)
    rg_freq = (rg_index.astype(jnp.float32) + 0.5) / (2 * rg_total) - 0.25
    model_phase = PHASE_GAIN * jnp.sqrt((1.0 + rg_freq)[:, None] ** 2 - az_freq[None, :] ** 2)
    ref_rows = own_block.shape[0]
    coarse = frequency * ref_rows // az_total
    slot_index = jnp.where(signed >= 0, ref_rows + coarse, coarse)
    one_hot = (jnp.arange(2 * ref_rows, dtype=jnp.int32)[:, None] == slot_index[None, :]).astype(
        jnp.float32
    )
    both_refs = jnp.concatenate([lower_ref, upper_ref], axis=0)
    picked = jnp.dot(both_refs.T, one_hot, precision=PRECISE)
    phase_all = model_phase + picked
    signal = rotate(signal, jnp.cos(phase_all), jnp.sin(phase_all))
    rim_width = REACH + TAPS // 2
    padded = padded_2(signal, (("rg", 1),), rim_width)
    offset_cols = jnp.repeat(offsets, BLOCK)
    local_cols = jnp.arange(rg_cols, dtype=jnp.int32)
    tap_index = jnp.arange(TAPS, dtype=jnp.int32)
    target = local_cols[:, None] + rim_width + offset_cols[:, None] + tap_index[None, :] - TAPS // 2
    padded_index = jnp.arange(rg_cols + 2 * rim_width, dtype=jnp.int32)
    hits = (padded_index[:, None, None] == target[None, :, :]).astype(jnp.float32)
    band_matrix = jnp.sum(hits * taps[None, :, :], axis=2)
    signal = jnp.einsum("zma,mi->zia", padded, band_matrix, precision=PRECISE)
    signal = local_dft(signal, 1.0) / az_rows
    twist_back = angles(row_index * column % az_total, az_total, 1.0)
    signal = rotate(signal, jnp.cos(twist_back)[None, :], jnp.sin(twist_back)[None, :])
    signal = butterfly_up(signal, az_place, bit_count)
    return (signal[0], signal[1])


FACTOR = 128
PLACES = 8
PART = FACTOR // PLACES
HALF = FACTOR // 2
OUT_BINS = 8
WINDOW = OUT_BINS + TAPS - 1
REF_LINES = 8
EDGE = 16
STEPS = (2, 3, 1, 0)


def split_bf16(value):
    high = value.astype(jnp.bfloat16)
    low = (value - high.astype(jnp.float32)).astype(jnp.bfloat16)
    return high, low


def dot(left, right):
    return jnp.dot(left, right, preferred_element_type=jnp.float32)


def dot_split(left, right):
    return dot(left[0], right[0]) + (dot(left[0], right[1]) + dot(left[1], right[0]))


def both_bf16(matrix):
    high = matrix.astype(jnp.bfloat16)
    return np.stack([high, (matrix - high.astype(np.float64)).astype(jnp.bfloat16)])


def long_bf16(matrix):
    high, low = both_bf16(matrix)
    return np.concatenate([high, high, low], axis=-1)


def long_rows(value):
    high, low = split_bf16(value)
    return jnp.concatenate([high, low, high], axis=0)


def dft_constants():
    counter = np.arange(FACTOR)
    kappa = np.arange(HALF)
    near, far, last, twists = [], [], [], []
    for side in range(2):
        order = [(middle, low, line) for low in (side, 1 - side) for middle in range(2) for line in range(PART)]
        mine = np.array([(2 * middle + low) * PART + line for middle, low, line in order])
        angle = 2 * np.pi * (np.outer(2 * kappa + side, mine) % FACTOR) / FACTOR
        cosine, sine = np.cos(angle), np.sin(angle)
        whole = np.block([[cosine, sine], [-sine, cosine]])
        quarters = np.split(whole, 4, axis=1)
        near.append(np.concatenate(quarters[0::2], axis=1))
        far.append(np.concatenate(quarters[1::2], axis=1))
        back_re, back_im = np.block([cosine.T, -sine.T]), np.block([sine.T, cosine.T])
        own, other = slice(0, HALF // 2), slice(HALF // 2, HALF)
        last.append(np.concatenate([back_re[own], back_im[own], back_re[other], back_im[other]]))
        twist = 2 * np.pi * np.outer(2 * kappa + side, counter) / FACTOR**2
        twists.append(np.stack([np.cos(twist), np.sin(twist)]))
    angle = 2 * np.pi * (np.outer(counter, counter) % FACTOR) / FACTOR
    cosine, sine = np.cos(angle), np.sin(angle)
    there = np.block([[cosine, -sine], [sine, cosine]])
    back = np.block([[cosine, sine], [-sine, cosine]])
    matrices = [
        long_bf16(np.stack(near)),
        long_bf16(np.stack(far)),
        both_bf16(there),
        both_bf16(back),
        both_bf16(np.stack(last)),
    ]
    return matrices, np.stack(twists).astype(np.float32)


def cos_sin_quarters(quarters):
    whole = jnp.floor(quarters + 0.5)
    rest = (quarters - whole) * (math.pi / 2)
    square = rest * rest
    sine = rest + rest * square * (
        -1.6666654611e-1 + square * (8.3321608736e-3 + square * (-1.9515295891e-4))
    )
    cosine = 1.0 - 0.5 * square + square * square * (
        4.166664568298827e-2 + square * (-1.388731625493765e-3 + square * 2.443315711809948e-5)
    )
    number = whole.astype(jnp.int32)
    odd = (number & 1) == 1
    turned_cos = jnp.where(odd, sine, cosine)
    turned_sin = jnp.where(odd, cosine, sine)
    cos_sign = jnp.where(((number + 1) & 2) == 2, -1.0, 1.0)
    sin_sign = jnp.where((number & 2) == 2, -1.0, 1.0)
    return turned_cos * cos_sign, turned_sin * sin_sign


def window_start(chip, side, offsets_own, offsets_other):
    block = chip * OUT_BINS // BLOCK
    blocks = offsets_own.shape[0]
    local = lax.rem(block, blocks)
    shift = jnp.where(lax.div(block, blocks) == side, offsets_own[local], offsets_other[local])
    return chip * OUT_BINS + shift - TAPS // 2


def spread_lines(target, base, source):
    bins, samples = source.shape
    part_rows = samples // FACTOR
    for tile in range(0, bins, 8):
        for row in range(part_rows):
            target[pl.ds((base + tile) * part_rows + row, 8, stride=part_rows), :] = source[
                tile : tile + 8, row * FACTOR : (row + 1) * FACTOR
            ]


def pack_kernel(re_lines, im_lines, re_other, im_other, ref_own, ref_other, own_offsets, other_offsets, *refs):
    messages, (re_all, im_all, ref_all, off_own, off_other, sems) = refs[:-6], refs[-6:]
    copies = [
        pltpu.make_async_copy(source, target, sems.at[at])
        for at, (source, target) in enumerate(((own_offsets, off_own), (other_offsets, off_other)))
    ]
    for copy in copies:
        copy.start()
    bins, samples = re_other.shape
    part_rows = samples // FACTOR
    place, side = lax.axis_index("az"), lax.axis_index("rg")
    own_at, other_at = EDGE + side * bins, EDGE + (1 - side) * bins
    zeros = jnp.zeros((EDGE * part_rows, FACTOR), jnp.float32)
    for all_ref, own, other in ((re_all, re_lines, re_other), (im_all, im_lines, im_other)):
        all_ref[: EDGE * part_rows, :] = zeros
        all_ref[(EDGE + 2 * bins) * part_rows :, :] = zeros
        all_ref[pl.ds(pl.multiple_of(own_at * part_rows, 8), bins * part_rows), :] = own[...]
        spread_lines(all_ref, other_at, other)
    ref_all[:EDGE, :] = jnp.zeros((EDGE, FACTOR), jnp.float32)
    ref_all[EDGE + 2 * bins :, :] = jnp.zeros((EDGE, FACTOR), jnp.float32)
    for at, ref in ((own_at, ref_own), (other_at, ref_other)):
        ref_all[pl.ds(pl.multiple_of(at, 16), bins), :] = jnp.concatenate([ref[...], ref[...]], axis=1)
    for copy in copies:
        copy.wait()
    lane = lax.broadcasted_iota(jnp.int32, (1, FACTOR), 1)
    for at, message in enumerate(messages):
        body = WINDOW * part_rows
        start = window_start(((place >> 1) ^ at) * 2 + side, side, off_own, off_other) + EDGE
        rows = pl.ds(pl.multiple_of(start * part_rows, 8), body)
        message[:body, :] = re_all[rows, :]
        message[body : 2 * body, :] = im_all[rows, :]
        for bin_num in range(REF_LINES):
            low = ref_all[pl.ds(start + bin_num, 1), :]
            high = ref_all[pl.ds(start + REF_LINES + bin_num, 1), :]
            message[2 * body + bin_num : 2 * body + bin_num + 1, :] = jnp.where(lane < HALF, low, high)


def phase_kernel(bins_total, off_own, off_other, owners, taps_own, taps_other, out, weights, choice):
    place, side = lax.axis_index("az"), lax.axis_index("rg")
    bins_held = taps_own.shape[0]
    held = lax.div(place * OUT_BINS, bins_held) == side
    local = lax.rem(place * OUT_BINS, bins_held)
    for bin_num in range(OUT_BINS):
        for tap in range(TAPS):
            weight = jnp.where(held, taps_own[local + bin_num, tap], taps_other[local + bin_num, tap])
            line = bin_num * TAPS + tap
            weights[line : line + 1, :] = jnp.full((1, FACTOR), weight, jnp.float32)
    line = lax.broadcasted_iota(jnp.int32, (2 * len(STEPS), FACTOR), 0)
    for which in range(2):
        owner = owners[which]
        step = (owner >> 1) ^ (place >> 1)
        wanted = jnp.where((owner & 1) == side, step, step + len(STEPS))
        choice[which] = jnp.where(line == wanted, 1.0, 0.0)
    start = window_start(place, side, off_own, off_other)
    shape = (HALF, FACTOR)
    kappa = lax.broadcasted_iota(jnp.int32, shape, 0)
    frequency = 2 * kappa + side + FACTOR * lax.broadcasted_iota(jnp.int32, shape, 1)
    total = FACTOR * FACTOR
    signed = jnp.where(frequency >= total // 2, frequency - total, frequency)
    az_freq = signed.astype(jnp.float32) / total
    az_square = az_freq * az_freq
    for bin_num in range(WINDOW):
        rg_index = (start + bin_num).astype(jnp.float32)
        rg_freq = (rg_index + 0.5) / (2 * bins_total) - 0.25
        base = (1.0 + rg_freq) * (1.0 + rg_freq)
        root = jnp.sqrt(base - az_square)
        cosine, sine = cos_sin_quarters(root * (PHASE_GAIN * 2 / math.pi))
        out[bin_num, 0] = cosine
        out[bin_num, 1] = sine


def parity_kernel(*refs):
    chunks = dict(zip(STEPS, refs))
    keep, give = refs[len(STEPS) :]
    place, side = lax.axis_index("az"), lax.axis_index("rg")
    sign = jnp.where(place >= PLACES // 2, -1.0, 1.0)
    even = side == 0
    keep_near, keep_far = jnp.where(even, 1.0, sign), jnp.where(even, 1.0, -sign)
    give_near, give_far = jnp.where(even, sign, 1.0), jnp.where(even, -sign, 1.0)
    plain = ((place >> 1) & 1) == 0
    for line in range(2 * WINDOW):
        read = slice(line * PART, (line + 1) * PART)
        write = line * 2 * PART
        values = [chunks[step][read, :] for step in range(4)]
        for target, near_factor, far_factor in ((keep, keep_near, keep_far), (give, give_near, give_far)):
            pair = [values[step] * near_factor + values[step + 2] * far_factor for step in range(2)]
            target[write : write + PART, :] = jnp.where(plain, pair[0], pair[1])
            target[write + PART : write + 2 * PART, :] = jnp.where(plain, pair[1], pair[0])
    for step in range(len(STEPS)):
        value = chunks[step][2 * WINDOW * PART :, :]
        at = 2 * WINDOW * 2 * PART + step * REF_LINES
        keep[at : at + REF_LINES, :] = value
        give[at : at + REF_LINES, :] = value


def gather_lines(ref, bins, group):
    width = 2 * PART
    columns = [
        jnp.concatenate(
            [ref[(part * bins + bin_num) * width : (part * bins + bin_num + 1) * width, :] for part in range(2)], axis=0
        )
        for bin_num in group
    ]
    return jnp.concatenate(columns, axis=1)


def bin_groups(bins):
    return [range(at, min(at + 4, bins)) for at in range(0, bins, 4)]


def near_kernel(keep, near, out):
    matrix = near[lax.axis_index("rg")]
    for index, group in enumerate(bin_groups(WINDOW)):
        out[index, :, : len(group) * FACTOR] = dot(matrix, long_rows(gather_lines(keep, WINDOW, group)))


def band_kernel(
    partial, keep, got, phase, weights, choice, far, there, back, last, twists, keep_out, give_out, spectra, band, picked
):
    side = lax.axis_index("rg")
    bins = WINDOW

    lane = lax.broadcasted_iota(jnp.int32, (REF_LINES, FACTOR), 1)
    lines = []
    for which in range(2):
        value = jnp.zeros((REF_LINES, FACTOR), jnp.float32)
        for option in range(2 * len(STEPS)):
            at = 2 * bins * 2 * PART + option % len(STEPS) * REF_LINES
            candidate = (keep if option < len(STEPS) else got)[at : at + REF_LINES, :]
            value = jnp.where(choice[which, option : option + 1, :] > 0.5, candidate, value)
        lines.append(value)
    for block in range(2):
        coarse = (lane >> 1) + block * HALF
        wide = [jnp.take_along_axis(lines[which], coarse, axis=1) for which in range(2)]
        ref_phase = jnp.where(lane < HALF, wide[1], wide[0])
        ref_cos, ref_sin = cos_sin_quarters(ref_phase * (2 / math.pi))
        picked[0, block * REF_LINES : (block + 1) * REF_LINES, :] = ref_cos
        picked[1, block * REF_LINES : (block + 1) * REF_LINES, :] = ref_sin

    far, last = far[side], (last[0, side], last[1, side])
    there, back = (there[0], there[1]), (back[0], back[1])
    twist_cos, twist_sin = twists[side, 0], twists[side, 1]
    for number, group in enumerate(bin_groups(bins)):
        passed = partial[number, :, : len(group) * FACTOR] + dot(far, long_rows(gather_lines(got, bins, group)))
        rows = []
        for index in range(len(group)):
            real = passed[:HALF, index * FACTOR : (index + 1) * FACTOR]
            imag = passed[HALF:, index * FACTOR : (index + 1) * FACTOR]
            rows.append(
                jnp.concatenate([real * twist_cos + imag * twist_sin, imag * twist_cos - real * twist_sin], axis=1)
            )
        passed = dot_split(split_bf16(jnp.concatenate(rows, axis=0)), there)
        for index, bin_num in enumerate(group):
            real = passed[index * HALF : (index + 1) * HALF, :FACTOR]
            imag = passed[index * HALF : (index + 1) * HALF, FACTOR:]
            model_cos, model_sin = phase[bin_num, 0], phase[bin_num, 1]
            row_cos, row_sin = picked[0, bin_num : bin_num + 1, :], picked[1, bin_num : bin_num + 1, :]
            cosine = model_cos * row_cos - model_sin * row_sin
            sine = model_sin * row_cos + model_cos * row_sin
            spectra[bin_num, 0] = real * cosine - imag * sine
            spectra[bin_num, 1] = real * sine + imag * cosine

    strip = 8
    for part in range(2):
        for at in range(0, HALF, strip):
            rows = slice(at, at + strip)
            sums = {}
            for bin_num in range(bins):
                value = spectra[bin_num, part, rows]
                for out in range(max(0, bin_num - TAPS + 1), min(OUT_BINS, bin_num + 1)):
                    weight = out * TAPS + bin_num - out
                    term = value * weights[weight : weight + 1, :]
                    sums[out] = sums[out] + term if out in sums else term
            for out in range(OUT_BINS):
                line = out * HALF + at
                band[line : line + strip, part * FACTOR : (part + 1) * FACTOR] = sums[out]

    scale = 1.0 / (FACTOR * FACTOR)
    cos_table, sin_table = twist_cos * scale, twist_sin * scale
    for at in range(0, OUT_BINS, 4):
        passed = dot_split(split_bf16(band[at * HALF : (at + 4) * HALF, :]), back)
        columns = []
        for index in range(4):
            real = passed[index * HALF : (index + 1) * HALF, :FACTOR]
            imag = passed[index * HALF : (index + 1) * HALF, FACTOR:]
            columns.append(
                jnp.concatenate([real * cos_table - imag * sin_table, imag * cos_table + real * sin_table], axis=0)
            )
        passed = dot_split(last, split_bf16(jnp.concatenate(columns, axis=1)))
        for index in range(4):
            lines = slice((at + index) * HALF, (at + index + 1) * HALF)
            keep_out[lines, :] = passed[:HALF, index * FACTOR : (index + 1) * FACTOR]
            give_out[lines, :] = passed[HALF:, index * FACTOR : (index + 1) * FACTOR]


def crossed(quarter):
    return ((quarter & 1) << 1) | (quarter >> 1)


def join_kernel(keep, got, *messages):
    place, side = lax.axis_index("az"), lax.axis_index("rg")
    quarter = lax.rem(place, PLACES // 2)
    sign = jnp.where(side == 0, 1.0, -1.0)
    for step, message in enumerate(messages):
        target = crossed(quarter) ^ step
        top, middle = target >> 1, target & 1
        keep_factor, got_factor = jnp.where(top == 0, 1.0, sign), jnp.where(top == 0, 1.0, -sign)
        for line in range(2 * OUT_BINS):
            read = pl.ds(pl.multiple_of(line * 2 * PART + middle * PART, 8), PART)
            message[line * PART : (line + 1) * PART, :] = keep[read, :] * keep_factor + got[read, :] * got_factor


def tile_kernel(message, re_tile, im_tile):
    for part, tile in enumerate((re_tile, im_tile)):
        for row in range(PART):
            tile[:, row * FACTOR : (row + 1) * FACTOR] = message[pl.ds(part * PART + row, OUT_BINS, stride=2 * PART), :]


def place_kernel(*refs):
    tiles, (out_re, out_im, sems) = refs[:-3], refs[-3:]
    place = lax.axis_index("az")
    copies = []
    for at, tile in enumerate(tiles):
        sender = crossed((place >> 1) ^ (at // 2))
        rows = pl.ds(pl.multiple_of(sender * OUT_BINS, 8), OUT_BINS)
        copies.append(pltpu.make_async_copy(tile, (out_re, out_im)[at % 2].at[rows], sems.at[at]))
        copies[-1].start()
    for copy in copies:
        copy.wait()


VMEM = pl.BlockSpec(memory_space=pltpu.VMEM)
SMEM = pl.BlockSpec(memory_space=pltpu.SMEM)


def kernel_call(body, name, out_shape, operands, scratch=(), flops=0, count=10**6, limit=8):
    specs = [SMEM if operand.size <= 256 else VMEM for operand in operands]
    return pl.pallas_call(
        body,
        out_shape=out_shape,
        in_specs=specs,
        out_specs=jax.tree.map(lambda _: VMEM, out_shape),
        scratch_shapes=[pltpu.VMEM(shape, jnp.float32) for shape in scratch],
        compiler_params=pltpu.CompilerParams(vmem_limit_bytes=limit * 1024 * 1024),
        cost_estimate=pl.CostEstimate(flops=flops, bytes_accessed=count, transcendentals=0),
        name=name,
    )(*operands)


def transposed_shards(raw_re, raw_im, ref_blocks, owners, offsets, taps):
    bins, samples = raw_re.shape

    def array(*shape):
        return jax.ShapeDtypeStruct(shape, jnp.float32)

    matrices, twists = dft_constants()
    near_table, *tables = [jnp.asarray(table) for table in (*matrices, twists)]
    swap = functools.partial(lax.ppermute, axis_name="rg", perm=[(0, 1), (1, 0)])
    half = PLACES // 2
    ref_own = ref_blocks[0].T
    offsets_other = swap(offsets)
    ref_other, re_other, im_other, taps_other = swap(ref_own), swap(raw_re), swap(raw_im), swap(taps)

    lines = [raw_re.reshape(bins * PART, FACTOR), raw_im.reshape(bins * PART, FACTOR)]
    all_bins = 2 * bins + 2 * EDGE
    anywhere = pl.BlockSpec(memory_space=pl.ANY)
    messages = pl.pallas_call(
        pack_kernel,
        out_shape=[array(2 * WINDOW * PART + REF_LINES, FACTOR)] * half,
        in_specs=[VMEM] * 6 + [anywhere] * 2,
        out_specs=[VMEM] * half,
        scratch_shapes=[
            pltpu.VMEM((all_bins * PART, FACTOR), jnp.float32),
            pltpu.VMEM((all_bins * PART, FACTOR), jnp.float32),
            pltpu.VMEM((all_bins, FACTOR), jnp.float32),
            pltpu.SMEM(offsets.shape, jnp.int32),
            pltpu.SMEM(offsets.shape, jnp.int32),
            pltpu.SemaphoreType.DMA((2,)),
        ],
        compiler_params=pltpu.CompilerParams(vmem_limit_bytes=8 * 1024 * 1024),
        cost_estimate=pl.CostEstimate(flops=1, bytes_accessed=1, transcendentals=0),
        name="pack",
    )(*lines, re_other, im_other, ref_own, ref_other, offsets, offsets_other)
    prepared = kernel_call(
        functools.partial(phase_kernel, 2 * bins),
        "phase",
        [array(WINDOW, 2, HALF, FACTOR), array(OUT_BINS * TAPS, FACTOR), array(2, 2 * half, FACTOR)],
        [offsets, offsets_other, owners, taps, taps_other],
    )

    routes = [
        [
            (chip * 2 + core, (((chip >> 1) ^ step) * 2 + core) * 2 + (chip & 1))
            for chip in range(PLACES)
            for core in range(2)
        ]
        for step in range(half)
    ]
    routes_back = [
        [
            (chip * 2 + core, ((crossed(chip % half) ^ step) * 2 + core) * 2 + chip // half)
            for chip in range(PLACES)
            for core in range(2)
        ]
        for step in range(half)
    ]
    arrived = [lax.ppermute(messages[step], ("az", "rg"), routes[step]) for step in STEPS]
    *arrived, phases, weights, choice = lax.optimization_barrier((*arrived, *prepared))

    size = 2 * WINDOW * 2 * PART + half * REF_LINES
    keep, give = kernel_call(parity_kernel, "parity", [array(size, FACTOR)] * 2, arrived)
    got = swap(give)
    partial = kernel_call(
        near_kernel, "near", array(len(bin_groups(WINDOW)), FACTOR, 4 * FACTOR), [keep, near_table]
    )
    keep, give = kernel_call(
        band_kernel,
        "band",
        [array(OUT_BINS * HALF, FACTOR)] * 2,
        [partial, keep, got, phases, weights, choice, *tables],
        scratch=[(WINDOW, 2, HALF, FACTOR), (OUT_BINS * HALF, 2 * FACTOR), (2, 2 * REF_LINES, FACTOR)],
        limit=16,
    )
    sent = kernel_call(join_kernel, "join", [array(2 * OUT_BINS * PART, FACTOR)] * half, [keep, swap(give)])
    results = [lax.ppermute(message, ("az", "rg"), route) for message, route in zip(sent, routes_back)]
    tiles = []
    for message in results:
        tiles += kernel_call(tile_kernel, "tile", [array(OUT_BINS, samples)] * 2, [message])
    return pl.pallas_call(
        place_kernel,
        out_shape=[array(bins, samples)] * 2,
        in_specs=[VMEM] * len(tiles),
        out_specs=[anywhere] * 2,
        scratch_shapes=[pltpu.SemaphoreType.DMA((len(tiles),))],
        compiler_params=pltpu.CompilerParams(vmem_limit_bytes=8 * 1024 * 1024),
        cost_estimate=pl.CostEstimate(flops=1, bytes_accessed=1, transcendentals=0),
        name="place",
    )(*tiles)


def solution(mesh):
    sizes = mesh.shape

    def whole(raw_re, raw_im, ref_blocks, owners, offsets, taps):
        line = raw_re.shape[1] // sizes["scene"]
        fits = (
            sizes["rg"] == 2
            and sizes["az"] == PLACES
            and raw_re.shape[0] == OUT_BINS * PLACES
            and line == FACTOR * FACTOR
            and ref_blocks.shape[1] == HALF
        )
        return jax.shard_map(
            transposed_shards if fits else butterfly_shards,
            mesh=mesh,
            in_specs=(
                P("rg", ("scene", "az")),
                P("rg", ("scene", "az")),
                P(("scene", "az"), None, "rg"),
                P("scene"),
                P("rg"),
                P("rg", None),
            ),
            out_specs=(P("rg", ("scene", "az")), P("rg", ("scene", "az"))),
            check_vma=False,
        )(raw_re, raw_im, ref_blocks, owners, offsets, taps)

    return whole
```

```python
import functools
import math

import jax
import jax.numpy as jnp
import numpy as np
from jax import lax
from jax.experimental import pallas as pl
from jax.experimental.pallas import tpu as pltpu
from jax.sharding import PartitionSpec as P

SPLIT = 4
TAPS = 8
REACH = 8
BLOCK = 16


PRECISE = lax.Precision.HIGHEST
PHASE_GAIN = 50.0


def partner_2(value, axis, stride):
    return lax.ppermute(value, axis, [(i, i ^ 1 << stride) for i in range(lax.axis_size(axis))])


def from_root(block, axis, source):
    block = jnp.where(lax.axis_index(axis) == source, block, jnp.zeros_like(block))
    return lax.psum(block, axis)


def padded_2(value, sides, width):
    for axis, dim in sides:
        size, length = (lax.axis_size(axis), value.shape[dim])
        up = [(i, (i + 1) % size) for i in range(size - 1)]
        down = [(j, i) for i, j in up]
        last = lax.slice_in_dim(value, length - width, length, axis=dim)
        initial = lax.slice_in_dim(value, 0, width, axis=dim)
        before = lax.ppermute(last, axis, up)
        after = lax.ppermute(initial, axis, down)
        value = jnp.concatenate([before, value, after], axis=dim)
    return value


def angles(numerator, denominator, sign_value):
    return sign_value * 2.0 * math.pi * numerator.astype(jnp.float32) / denominator


def rotate(signal, cosine, sine_part):
    real_part = signal[0] * cosine - signal[1] * sine_part
    imag_part = signal[0] * sine_part + signal[1] * cosine
    return jnp.stack([real_part, imag_part])


def dft_table(length_n, sign_value):
    counter = jnp.arange(length_n, dtype=jnp.int32)
    turn_count = counter[:, None] * counter[None, :] % length_n
    angle_set = angles(turn_count, length_n, sign_value)
    return (jnp.cos(angle_set), jnp.sin(angle_set))


def complex_apply(einsum_form, cosine, sine_part, signal):
    real_part = jnp.einsum(einsum_form, cosine, signal[0], precision=PRECISE) - jnp.einsum(
        einsum_form, sine_part, signal[1], precision=PRECISE
    )
    imag_part = jnp.einsum(einsum_form, cosine, signal[1], precision=PRECISE) + jnp.einsum(
        einsum_form, sine_part, signal[0], precision=PRECISE
    )
    return jnp.stack([real_part, imag_part])


def local_dft(signal, sign_value):
    rg_cols = signal.shape[1]
    az_rows = signal.shape[2]
    inner_len = az_rows // SPLIT
    shaped = signal.reshape(2, rg_cols, SPLIT, inner_len)
    first_cos, first_sin = dft_table(SPLIT, sign_value)
    first_pass = complex_apply("aj,cjk->cak", first_cos, first_sin, shaped)
    outer_idx = jnp.arange(SPLIT, dtype=jnp.int32)
    inner_idx = jnp.arange(inner_len, dtype=jnp.int32)
    twist = angles(outer_idx[:, None] * inner_idx[None, :] % az_rows, az_rows, sign_value)
    first_pass = rotate(first_pass, jnp.cos(twist)[None, :, :], jnp.sin(twist)[None, :, :])
    second_cos, second_sin = dft_table(inner_len, sign_value)
    second_pass = complex_apply("bk,cak->cba", second_cos, second_sin, first_pass)
    return second_pass.reshape(2, rg_cols, az_rows)


def butterfly_down(signal, az_place, bit_count):
    for bit_num in reversed(range(bit_count)):
        half_span = 1 << bit_num
        partner = partner_2(signal, "az", bit_num)
        is_upper = az_place >> bit_num & 1 == 1
        angle_set = angles(az_place % half_span, 2 * half_span, -1.0)
        difference = rotate(partner - signal, jnp.cos(angle_set), jnp.sin(angle_set))
        signal = jnp.where(is_upper, difference, signal + partner)
    return signal


def butterfly_up(signal, az_place, bit_count):
    for bit_num in range(bit_count):
        half_span = 1 << bit_num
        partner = partner_2(signal, "az", bit_num)
        is_upper = az_place >> bit_num & 1 == 1
        angle_set = angles(az_place % half_span, 2 * half_span, 1.0)
        cosine = jnp.cos(angle_set)
        sine_part = jnp.sin(angle_set)
        lower_new = (signal + rotate(partner, cosine, sine_part)) * 0.5
        upper_new = (partner - rotate(signal, cosine, sine_part)) * 0.5
        signal = jnp.where(is_upper, upper_new, lower_new)
    return signal


def butterfly_shards(raw_re, raw_im, ref_blocks, owners, offsets, taps):
    rg_cols = raw_re.shape[0]
    az_rows = raw_re.shape[1]
    az_count = lax.axis_size("az")
    az_place = lax.axis_index("az")
    bit_count = az_count.bit_length() - 1
    az_total = az_rows * az_count
    rg_total = rg_cols * lax.axis_size("rg")
    own_block = ref_blocks[0]
    lower_ref = from_root(own_block, "az", owners[0])
    upper_ref = from_root(own_block, "az", owners[1])
    signal = jnp.stack([raw_re, raw_im])
    signal = butterfly_down(signal, az_place, bit_count)
    column = jnp.zeros((), jnp.int32)
    for bit_num in range(bit_count):
        column = column + ((az_place >> bit_num & 1) << bit_count - 1 - bit_num)
    row_index = jnp.arange(az_rows, dtype=jnp.int32)
    twist = angles(row_index * column % az_total, az_total, -1.0)
    signal = rotate(signal, jnp.cos(twist)[None, :], jnp.sin(twist)[None, :])
    signal = local_dft(signal, -1.0)
    frequency = column + az_count * row_index
    signed = (frequency + az_total // 2) % az_total - az_total // 2
    az_freq = signed.astype(jnp.float32) / az_total
    rg_index = lax.axis_index("rg") * rg_cols + jnp.arange(rg_cols, dtype=jnp.int32)
    rg_freq = (rg_index.astype(jnp.float32) + 0.5) / (2 * rg_total) - 0.25
    model_phase = PHASE_GAIN * jnp.sqrt((1.0 + rg_freq)[:, None] ** 2 - az_freq[None, :] ** 2)
    ref_rows = own_block.shape[0]
    coarse = frequency * ref_rows // az_total
    slot_index = jnp.where(signed >= 0, ref_rows + coarse, coarse)
    one_hot = (jnp.arange(2 * ref_rows, dtype=jnp.int32)[:, None] == slot_index[None, :]).astype(
        jnp.float32
    )
    both_refs = jnp.concatenate([lower_ref, upper_ref], axis=0)
    picked = jnp.dot(both_refs.T, one_hot, precision=PRECISE)
    phase_all = model_phase + picked
    signal = rotate(signal, jnp.cos(phase_all), jnp.sin(phase_all))
    rim_width = REACH + TAPS // 2
    padded = padded_2(signal, (("rg", 1),), rim_width)
    offset_cols = jnp.repeat(offsets, BLOCK)
    local_cols = jnp.arange(rg_cols, dtype=jnp.int32)
    tap_index = jnp.arange(TAPS, dtype=jnp.int32)
    target = local_cols[:, None] + rim_width + offset_cols[:, None] + tap_index[None, :] - TAPS // 2
    padded_index = jnp.arange(rg_cols + 2 * rim_width, dtype=jnp.int32)
    hits = (padded_index[:, None, None] == target[None, :, :]).astype(jnp.float32)
    band_matrix = jnp.sum(hits * taps[None, :, :], axis=2)
    signal = jnp.einsum("zma,mi->zia", padded, band_matrix, precision=PRECISE)
    signal = local_dft(signal, 1.0) / az_rows
    twist_back = angles(row_index * column % az_total, az_total, 1.0)
    signal = rotate(signal, jnp.cos(twist_back)[None, :], jnp.sin(twist_back)[None, :])
    signal = butterfly_up(signal, az_place, bit_count)
    return (signal[0], signal[1])


FACTOR = 128
PLACES = 8
PART = FACTOR // PLACES
HALF = FACTOR // 2
OUT_BINS = 8
WINDOW = OUT_BINS + TAPS - 1
REF_LINES = 8
EDGE = 16
STEPS = (2, 3, 1, 0)


def split_bf16(value):
    high = value.astype(jnp.bfloat16)
    low = (value - high.astype(jnp.float32)).astype(jnp.bfloat16)
    return high, low


def dot(left, right):
    return jnp.dot(left, right, preferred_element_type=jnp.float32)


def dot_split(left, right):
    return dot(left[0], right[0]) + (dot(left[0], right[1]) + dot(left[1], right[0]))


def both_bf16(matrix):
    high = matrix.astype(jnp.bfloat16)
    return np.stack([high, (matrix - high.astype(np.float64)).astype(jnp.bfloat16)])


def long_bf16(matrix):
    high, low = both_bf16(matrix)
    return np.concatenate([high, high, low], axis=-1)


def long_rows(value):
    high, low = split_bf16(value)
    return jnp.concatenate([high, low, high], axis=0)


def dft_constants():
    counter = np.arange(FACTOR)
    kappa = np.arange(HALF)
    near, far, last, twists = [], [], [], []
    for side in range(2):
        order = [(middle, low, line) for low in (side, 1 - side) for middle in range(2) for line in range(PART)]
        mine = np.array([(2 * middle + low) * PART + line for middle, low, line in order])
        angle = 2 * np.pi * (np.outer(2 * kappa + side, mine) % FACTOR) / FACTOR
        cosine, sine = np.cos(angle), np.sin(angle)
        whole = np.block([[cosine, sine], [-sine, cosine]])
        quarters = np.split(whole, 4, axis=1)
        near.append(np.concatenate(quarters[0::2], axis=1))
        far.append(np.concatenate(quarters[1::2], axis=1))
        back_re, back_im = np.block([cosine.T, -sine.T]), np.block([sine.T, cosine.T])
        own, other = slice(0, HALF // 2), slice(HALF // 2, HALF)
        last.append(np.concatenate([back_re[own], back_im[own], back_re[other], back_im[other]]))
        twist = 2 * np.pi * np.outer(2 * kappa + side, counter) / FACTOR**2
        twists.append(np.stack([np.cos(twist), np.sin(twist)]))
    angle = 2 * np.pi * (np.outer(counter, counter) % FACTOR) / FACTOR
    cosine, sine = np.cos(angle), np.sin(angle)
    there = np.block([[cosine, -sine], [sine, cosine]])
    back = np.block([[cosine, sine], [-sine, cosine]])
    matrices = [
        long_bf16(np.stack(near)),
        long_bf16(np.stack(far)),
        both_bf16(there),
        both_bf16(back),
        both_bf16(np.stack(last)),
    ]
    return matrices, np.stack(twists).astype(np.float32)


def cos_sin_quarters(quarters):
    whole = jnp.floor(quarters + 0.5)
    rest = (quarters - whole) * (math.pi / 2)
    square = rest * rest
    sine = rest + rest * square * (
        -1.6666654611e-1 + square * (8.3321608736e-3 + square * (-1.9515295891e-4))
    )
    cosine = 1.0 - 0.5 * square + square * square * (
        4.166664568298827e-2 + square * (-1.388731625493765e-3 + square * 2.443315711809948e-5)
    )
    number = whole.astype(jnp.int32)
    odd = (number & 1) == 1
    turned_cos = jnp.where(odd, sine, cosine)
    turned_sin = jnp.where(odd, cosine, sine)
    cos_sign = jnp.where(((number + 1) & 2) == 2, -1.0, 1.0)
    sin_sign = jnp.where((number & 2) == 2, -1.0, 1.0)
    return turned_cos * cos_sign, turned_sin * sin_sign


def window_start(chip, side, offsets_own, offsets_other):
    block = chip * OUT_BINS // BLOCK
    blocks = offsets_own.shape[0]
    local = lax.rem(block, blocks)
    shift = jnp.where(lax.div(block, blocks) == side, offsets_own[local], offsets_other[local])
    return chip * OUT_BINS + shift - TAPS // 2


def spread_lines(target, base, source):
    bins, samples = source.shape
    part_rows = samples // FACTOR
    for tile in range(0, bins, 8):
        for row in range(part_rows):
            target[pl.ds((base + tile) * part_rows + row, 8, stride=part_rows), :] = source[
                tile : tile + 8, row * FACTOR : (row + 1) * FACTOR
            ]


def pack_kernel(re_lines, im_lines, re_other, im_other, ref_own, ref_other, own_offsets, other_offsets, *refs):
    messages, (re_all, im_all, ref_all, off_own, off_other, sems) = refs[:-6], refs[-6:]
    copies = [
        pltpu.make_async_copy(source, target, sems.at[at])
        for at, (source, target) in enumerate(((own_offsets, off_own), (other_offsets, off_other)))
    ]
    for copy in copies:
        copy.start()
    bins, samples = re_other.shape
    part_rows = samples // FACTOR
    place, side = lax.axis_index("az"), lax.axis_index("rg")
    own_at, other_at = EDGE + side * bins, EDGE + (1 - side) * bins
    zeros = jnp.zeros((EDGE * part_rows, FACTOR), jnp.float32)
    for all_ref, own, other in ((re_all, re_lines, re_other), (im_all, im_lines, im_other)):
        all_ref[: EDGE * part_rows, :] = zeros
        all_ref[(EDGE + 2 * bins) * part_rows :, :] = zeros
        all_ref[pl.ds(pl.multiple_of(own_at * part_rows, 8), bins * part_rows), :] = own[...]
        spread_lines(all_ref, other_at, other)
    ref_all[:EDGE, :] = jnp.zeros((EDGE, FACTOR), jnp.float32)
    ref_all[EDGE + 2 * bins :, :] = jnp.zeros((EDGE, FACTOR), jnp.float32)
    for at, ref in ((own_at, ref_own), (other_at, ref_other)):
        ref_all[pl.ds(pl.multiple_of(at, 16), bins), :] = jnp.concatenate([ref[...], ref[...]], axis=1)
    for copy in copies:
        copy.wait()
    lane = lax.broadcasted_iota(jnp.int32, (1, FACTOR), 1)
    for at, message in enumerate(messages):
        body = WINDOW * part_rows
        start = window_start(((place >> 1) ^ at) * 2 + side, side, off_own, off_other) + EDGE
        rows = pl.ds(pl.multiple_of(start * part_rows, 8), body)
        message[:body, :] = re_all[rows, :]
        message[body : 2 * body, :] = im_all[rows, :]
        for bin_num in range(REF_LINES):
            low = ref_all[pl.ds(start + bin_num, 1), :]
            high = ref_all[pl.ds(start + REF_LINES + bin_num, 1), :]
            message[2 * body + bin_num : 2 * body + bin_num + 1, :] = jnp.where(lane < HALF, low, high)


def phase_kernel(bins_total, off_own, off_other, owners, taps_own, taps_other, out, weights, choice):
    place, side = lax.axis_index("az"), lax.axis_index("rg")
    bins_held = taps_own.shape[0]
    held = lax.div(place * OUT_BINS, bins_held) == side
    local = lax.rem(place * OUT_BINS, bins_held)
    for bin_num in range(OUT_BINS):
        for tap in range(TAPS):
            weight = jnp.where(held, taps_own[local + bin_num, tap], taps_other[local + bin_num, tap])
            line = bin_num * TAPS + tap
            weights[line : line + 1, :] = jnp.full((1, FACTOR), weight, jnp.float32)
    line = lax.broadcasted_iota(jnp.int32, (2 * len(STEPS), FACTOR), 0)
    for which in range(2):
        owner = owners[which]
        step = (owner >> 1) ^ (place >> 1)
        wanted = jnp.where((owner & 1) == side, step, step + len(STEPS))
        choice[which] = jnp.where(line == wanted, 1.0, 0.0)
    start = window_start(place, side, off_own, off_other)
    shape = (HALF, FACTOR)
    kappa = lax.broadcasted_iota(jnp.int32, shape, 0)
    frequency = 2 * kappa + side + FACTOR * lax.broadcasted_iota(jnp.int32, shape, 1)
    total = FACTOR * FACTOR
    signed = jnp.where(frequency >= total // 2, frequency - total, frequency)
    az_freq = signed.astype(jnp.float32) / total
    az_square = az_freq * az_freq
    for bin_num in range(WINDOW):
        rg_index = (start + bin_num).astype(jnp.float32)
        rg_freq = (rg_index + 0.5) / (2 * bins_total) - 0.25
        base = (1.0 + rg_freq) * (1.0 + rg_freq)
        root = jnp.sqrt(base - az_square)
        cosine, sine = cos_sin_quarters(root * (PHASE_GAIN * 2 / math.pi))
        out[bin_num, 0] = cosine
        out[bin_num, 1] = sine


def parity_kernel(*refs):
    chunks = dict(zip(STEPS, refs))
    keep, give = refs[len(STEPS) :]
    place, side = lax.axis_index("az"), lax.axis_index("rg")
    sign = jnp.where(place >= PLACES // 2, -1.0, 1.0)
    even = side == 0
    keep_near, keep_far = jnp.where(even, 1.0, sign), jnp.where(even, 1.0, -sign)
    give_near, give_far = jnp.where(even, sign, 1.0), jnp.where(even, -sign, 1.0)
    plain = ((place >> 1) & 1) == 0
    for line in range(2 * WINDOW):
        read = slice(line * PART, (line + 1) * PART)
        write = line * 2 * PART
        values = [chunks[step][read, :] for step in range(4)]
        for target, near_factor, far_factor in ((keep, keep_near, keep_far), (give, give_near, give_far)):
            pair = [values[step] * near_factor + values[step + 2] * far_factor for step in range(2)]
            target[write : write + PART, :] = jnp.where(plain, pair[0], pair[1])
            target[write + PART : write + 2 * PART, :] = jnp.where(plain, pair[1], pair[0])
    for step in range(len(STEPS)):
        value = chunks[step][2 * WINDOW * PART :, :]
        at = 2 * WINDOW * 2 * PART + step * REF_LINES
        keep[at : at + REF_LINES, :] = value
        give[at : at + REF_LINES, :] = value


def gather_lines(ref, bins, group):
    width = 2 * PART
    columns = [
        jnp.concatenate(
            [ref[(part * bins + bin_num) * width : (part * bins + bin_num + 1) * width, :] for part in range(2)], axis=0
        )
        for bin_num in group
    ]
    return jnp.concatenate(columns, axis=1)


def bin_groups(bins):
    return [range(at, min(at + 4, bins)) for at in range(0, bins, 4)]


def near_kernel(keep, near, out):
    matrix = near[lax.axis_index("rg")]
    for index, group in enumerate(bin_groups(WINDOW)):
        out[index, :, : len(group) * FACTOR] = dot(matrix, long_rows(gather_lines(keep, WINDOW, group)))


def band_kernel(
    partial, keep, got, phase, weights, choice, far, there, back, last, twists, keep_out, give_out, spectra, band, picked
):
    side = lax.axis_index("rg")
    bins = WINDOW

    lane = lax.broadcasted_iota(jnp.int32, (REF_LINES, FACTOR), 1)
    lines = []
    for which in range(2):
        value = jnp.zeros((REF_LINES, FACTOR), jnp.float32)
        for option in range(2 * len(STEPS)):
            at = 2 * bins * 2 * PART + option % len(STEPS) * REF_LINES
            candidate = (keep if option < len(STEPS) else got)[at : at + REF_LINES, :]
            value = jnp.where(choice[which, option : option + 1, :] > 0.5, candidate, value)
        lines.append(value)
    for block in range(2):
        coarse = (lane >> 1) + block * HALF
        wide = [jnp.take_along_axis(lines[which], coarse, axis=1) for which in range(2)]
        ref_phase = jnp.where(lane < HALF, wide[1], wide[0])
        ref_cos, ref_sin = cos_sin_quarters(ref_phase * (2 / math.pi))
        picked[0, block * REF_LINES : (block + 1) * REF_LINES, :] = ref_cos
        picked[1, block * REF_LINES : (block + 1) * REF_LINES, :] = ref_sin

    far, last = far[side], (last[0, side], last[1, side])
    there, back = (there[0], there[1]), (back[0], back[1])
    twist_cos, twist_sin = twists[side, 0], twists[side, 1]
    for number, group in enumerate(bin_groups(bins)):
        passed = partial[number, :, : len(group) * FACTOR] + dot(far, long_rows(gather_lines(got, bins, group)))
        rows = []
        for index in range(len(group)):
            real = passed[:HALF, index * FACTOR : (index + 1) * FACTOR]
            imag = passed[HALF:, index * FACTOR : (index + 1) * FACTOR]
            rows.append(
                jnp.concatenate([real * twist_cos + imag * twist_sin, imag * twist_cos - real * twist_sin], axis=1)
            )
        passed = dot_split(split_bf16(jnp.concatenate(rows, axis=0)), there)
        for index, bin_num in enumerate(group):
            real = passed[index * HALF : (index + 1) * HALF, :FACTOR]
            imag = passed[index * HALF : (index + 1) * HALF, FACTOR:]
            model_cos, model_sin = phase[bin_num, 0], phase[bin_num, 1]
            row_cos, row_sin = picked[0, bin_num : bin_num + 1, :], picked[1, bin_num : bin_num + 1, :]
            cosine = model_cos * row_cos - model_sin * row_sin
            sine = model_sin * row_cos + model_cos * row_sin
            spectra[bin_num, 0] = real * cosine - imag * sine
            spectra[bin_num, 1] = real * sine + imag * cosine

    strip = 8
    for part in range(2):
        for at in range(0, HALF, strip):
            rows = slice(at, at + strip)
            sums = {}
            for bin_num in range(bins):
                value = spectra[bin_num, part, rows]
                for out in range(max(0, bin_num - TAPS + 1), min(OUT_BINS, bin_num + 1)):
                    weight = out * TAPS + bin_num - out
                    term = value * weights[weight : weight + 1, :]
                    sums[out] = sums[out] + term if out in sums else term
            for out in range(OUT_BINS):
                line = out * HALF + at
                band[line : line + strip, part * FACTOR : (part + 1) * FACTOR] = sums[out]

    scale = 1.0 / (FACTOR * FACTOR)
    cos_table, sin_table = twist_cos * scale, twist_sin * scale
    for at in range(0, OUT_BINS, 4):
        passed = dot_split(split_bf16(band[at * HALF : (at + 4) * HALF, :]), back)
        columns = []
        for index in range(4):
            real = passed[index * HALF : (index + 1) * HALF, :FACTOR]
            imag = passed[index * HALF : (index + 1) * HALF, FACTOR:]
            columns.append(
                jnp.concatenate([real * cos_table - imag * sin_table, imag * cos_table + real * sin_table], axis=0)
            )
        passed = dot_split(last, split_bf16(jnp.concatenate(columns, axis=1)))
        for index in range(4):
            lines = slice((at + index) * HALF, (at + index + 1) * HALF)
            keep_out[lines, :] = passed[:HALF, index * FACTOR : (index + 1) * FACTOR]
            give_out[lines, :] = passed[HALF:, index * FACTOR : (index + 1) * FACTOR]


def crossed(quarter):
    return ((quarter & 1) << 1) | (quarter >> 1)


def join_kernel(keep, got, *messages):
    place, side = lax.axis_index("az"), lax.axis_index("rg")
    quarter = lax.rem(place, PLACES // 2)
    sign = jnp.where(side == 0, 1.0, -1.0)
    for step, message in enumerate(messages):
        target = crossed(quarter) ^ step
        top, middle = target >> 1, target & 1
        keep_factor, got_factor = jnp.where(top == 0, 1.0, sign), jnp.where(top == 0, 1.0, -sign)
        for line in range(2 * OUT_BINS):
            read = pl.ds(pl.multiple_of(line * 2 * PART + middle * PART, 8), PART)
            message[line * PART : (line + 1) * PART, :] = keep[read, :] * keep_factor + got[read, :] * got_factor


def place_kernel(step, message, *refs):
    outs, (tiles, sems) = refs[-4:-2], refs[-2:]
    sender = crossed((lax.axis_index("az") >> 1) ^ step)
    rows = pl.ds(pl.multiple_of(sender * OUT_BINS, 8), OUT_BINS)
    copies = []
    for part, out in enumerate(outs):
        for row in range(PART):
            tiles[part, :, row * FACTOR : (row + 1) * FACTOR] = message[
                pl.ds(part * PART + row, OUT_BINS, stride=2 * PART), :
            ]
        copies.append(pltpu.make_async_copy(tiles.at[part], out.at[rows], sems.at[part]))
        copies[-1].start()
    for copy in copies:
        copy.wait()


VMEM = pl.BlockSpec(memory_space=pltpu.VMEM)
SMEM = pl.BlockSpec(memory_space=pltpu.SMEM)


def kernel_call(body, name, out_shape, operands, scratch=(), flops=0, count=10**6, limit=8):
    specs = [SMEM if operand.size <= 256 else VMEM for operand in operands]
    return pl.pallas_call(
        body,
        out_shape=out_shape,
        in_specs=specs,
        out_specs=jax.tree.map(lambda _: VMEM, out_shape),
        scratch_shapes=[pltpu.VMEM(shape, jnp.float32) for shape in scratch],
        compiler_params=pltpu.CompilerParams(vmem_limit_bytes=limit * 1024 * 1024),
        cost_estimate=pl.CostEstimate(flops=flops, bytes_accessed=count, transcendentals=0),
        name=name,
    )(*operands)


def transposed_shards(raw_re, raw_im, ref_blocks, owners, offsets, taps):
    bins, samples = raw_re.shape

    def array(*shape):
        return jax.ShapeDtypeStruct(shape, jnp.float32)

    matrices, twists = dft_constants()
    near_table, *tables = [jnp.asarray(table) for table in (*matrices, twists)]
    swap = functools.partial(lax.ppermute, axis_name="rg", perm=[(0, 1), (1, 0)])
    half = PLACES // 2
    ref_own = ref_blocks[0].T
    offsets_other = swap(offsets)
    ref_other, re_other, im_other, taps_other = swap(ref_own), swap(raw_re), swap(raw_im), swap(taps)

    lines = [raw_re.reshape(bins * PART, FACTOR), raw_im.reshape(bins * PART, FACTOR)]
    all_bins = 2 * bins + 2 * EDGE
    anywhere = pl.BlockSpec(memory_space=pl.ANY)
    messages = pl.pallas_call(
        pack_kernel,
        out_shape=[array(2 * WINDOW * PART + REF_LINES, FACTOR)] * half,
        in_specs=[VMEM] * 6 + [anywhere] * 2,
        out_specs=[VMEM] * half,
        scratch_shapes=[
            pltpu.VMEM((all_bins * PART, FACTOR), jnp.float32),
            pltpu.VMEM((all_bins * PART, FACTOR), jnp.float32),
            pltpu.VMEM((all_bins, FACTOR), jnp.float32),
            pltpu.SMEM(offsets.shape, jnp.int32),
            pltpu.SMEM(offsets.shape, jnp.int32),
            pltpu.SemaphoreType.DMA((2,)),
        ],
        compiler_params=pltpu.CompilerParams(vmem_limit_bytes=8 * 1024 * 1024),
        cost_estimate=pl.CostEstimate(flops=1, bytes_accessed=1, transcendentals=0),
        name="pack",
    )(*lines, re_other, im_other, ref_own, ref_other, offsets, offsets_other)
    prepared = kernel_call(
        functools.partial(phase_kernel, 2 * bins),
        "phase",
        [array(WINDOW, 2, HALF, FACTOR), array(OUT_BINS * TAPS, FACTOR), array(2, 2 * half, FACTOR)],
        [offsets, offsets_other, owners, taps, taps_other],
    )

    routes = [
        [
            (chip * 2 + core, (((chip >> 1) ^ step) * 2 + core) * 2 + (chip & 1))
            for chip in range(PLACES)
            for core in range(2)
        ]
        for step in range(half)
    ]
    routes_back = [
        [
            (chip * 2 + core, ((crossed(chip % half) ^ step) * 2 + core) * 2 + chip // half)
            for chip in range(PLACES)
            for core in range(2)
        ]
        for step in range(half)
    ]
    arrived = [lax.ppermute(messages[step], ("az", "rg"), routes[step]) for step in STEPS]
    *arrived, phases, weights, choice = lax.optimization_barrier((*arrived, *prepared))

    size = 2 * WINDOW * 2 * PART + half * REF_LINES
    keep, give = kernel_call(parity_kernel, "parity", [array(size, FACTOR)] * 2, arrived)
    got = swap(give)
    partial = kernel_call(
        near_kernel, "near", array(len(bin_groups(WINDOW)), FACTOR, 4 * FACTOR), [keep, near_table]
    )
    keep, give = kernel_call(
        band_kernel,
        "band",
        [array(OUT_BINS * HALF, FACTOR)] * 2,
        [partial, keep, got, phases, weights, choice, *tables],
        scratch=[(WINDOW, 2, HALF, FACTOR), (OUT_BINS * HALF, 2 * FACTOR), (2, 2 * REF_LINES, FACTOR)],
        limit=16,
    )
    sent = kernel_call(join_kernel, "join", [array(2 * OUT_BINS * PART, FACTOR)] * half, [keep, swap(give)])
    results = [lax.ppermute(message, ("az", "rg"), route) for message, route in zip(sent, routes_back)]
    images = []
    for step, message in enumerate(results):
        images = pl.pallas_call(
            functools.partial(place_kernel, step),
            out_shape=[array(bins, samples)] * 2,
            in_specs=[VMEM] + [anywhere] * len(images),
            out_specs=[anywhere] * 2,
            scratch_shapes=[pltpu.VMEM((2, OUT_BINS, samples), jnp.float32), pltpu.SemaphoreType.DMA((2,))],
            input_output_aliases={1: 0, 2: 1} if images else {},
            compiler_params=pltpu.CompilerParams(vmem_limit_bytes=8 * 1024 * 1024),
            cost_estimate=pl.CostEstimate(flops=1, bytes_accessed=1, transcendentals=0),
            name="place",
        )(message, *images)
    return images


def solution(mesh):
    sizes = mesh.shape

    def whole(raw_re, raw_im, ref_blocks, owners, offsets, taps):
        line = raw_re.shape[1] // sizes["scene"]
        fits = (
            sizes["rg"] == 2
            and sizes["az"] == PLACES
            and raw_re.shape[0] == OUT_BINS * PLACES
            and line == FACTOR * FACTOR
            and ref_blocks.shape[1] == HALF
        )
        return jax.shard_map(
            transposed_shards if fits else butterfly_shards,
            mesh=mesh,
            in_specs=(
                P("rg", ("scene", "az")),
                P("rg", ("scene", "az")),
                P(("scene", "az"), None, "rg"),
                P("scene"),
                P("rg"),
                P("rg", None),
            ),
            out_specs=(P("rg", ("scene", "az")), P("rg", ("scene", "az"))),
            check_vma=False,
        )(raw_re, raw_im, ref_blocks, owners, offsets, taps)

    return whole
```

```python
import functools
import math

import jax
import jax.numpy as jnp
import numpy as np
from jax import lax
from jax.experimental import pallas as pl
from jax.experimental.pallas import tpu as pltpu
from jax.sharding import PartitionSpec as P

SPLIT = 4
TAPS = 8
REACH = 8
BLOCK = 16


PRECISE = lax.Precision.HIGHEST
PHASE_GAIN = 50.0


def partner_2(value, axis, stride):
    return lax.ppermute(value, axis, [(i, i ^ 1 << stride) for i in range(lax.axis_size(axis))])


def from_root(block, axis, source):
    block = jnp.where(lax.axis_index(axis) == source, block, jnp.zeros_like(block))
    return lax.psum(block, axis)


def padded_2(value, sides, width):
    for axis, dim in sides:
        size, length = (lax.axis_size(axis), value.shape[dim])
        up = [(i, (i + 1) % size) for i in range(size - 1)]
        down = [(j, i) for i, j in up]
        last = lax.slice_in_dim(value, length - width, length, axis=dim)
        initial = lax.slice_in_dim(value, 0, width, axis=dim)
        before = lax.ppermute(last, axis, up)
        after = lax.ppermute(initial, axis, down)
        value = jnp.concatenate([before, value, after], axis=dim)
    return value


def angles(numerator, denominator, sign_value):
    return sign_value * 2.0 * math.pi * numerator.astype(jnp.float32) / denominator


def rotate(signal, cosine, sine_part):
    real_part = signal[0] * cosine - signal[1] * sine_part
    imag_part = signal[0] * sine_part + signal[1] * cosine
    return jnp.stack([real_part, imag_part])


def dft_table(length_n, sign_value):
    counter = jnp.arange(length_n, dtype=jnp.int32)
    turn_count = counter[:, None] * counter[None, :] % length_n
    angle_set = angles(turn_count, length_n, sign_value)
    return (jnp.cos(angle_set), jnp.sin(angle_set))


def complex_apply(einsum_form, cosine, sine_part, signal):
    real_part = jnp.einsum(einsum_form, cosine, signal[0], precision=PRECISE) - jnp.einsum(
        einsum_form, sine_part, signal[1], precision=PRECISE
    )
    imag_part = jnp.einsum(einsum_form, cosine, signal[1], precision=PRECISE) + jnp.einsum(
        einsum_form, sine_part, signal[0], precision=PRECISE
    )
    return jnp.stack([real_part, imag_part])


def local_dft(signal, sign_value):
    rg_cols = signal.shape[1]
    az_rows = signal.shape[2]
    inner_len = az_rows // SPLIT
    shaped = signal.reshape(2, rg_cols, SPLIT, inner_len)
    first_cos, first_sin = dft_table(SPLIT, sign_value)
    first_pass = complex_apply("aj,cjk->cak", first_cos, first_sin, shaped)
    outer_idx = jnp.arange(SPLIT, dtype=jnp.int32)
    inner_idx = jnp.arange(inner_len, dtype=jnp.int32)
    twist = angles(outer_idx[:, None] * inner_idx[None, :] % az_rows, az_rows, sign_value)
    first_pass = rotate(first_pass, jnp.cos(twist)[None, :, :], jnp.sin(twist)[None, :, :])
    second_cos, second_sin = dft_table(inner_len, sign_value)
    second_pass = complex_apply("bk,cak->cba", second_cos, second_sin, first_pass)
    return second_pass.reshape(2, rg_cols, az_rows)


def butterfly_down(signal, az_place, bit_count):
    for bit_num in reversed(range(bit_count)):
        half_span = 1 << bit_num
        partner = partner_2(signal, "az", bit_num)
        is_upper = az_place >> bit_num & 1 == 1
        angle_set = angles(az_place % half_span, 2 * half_span, -1.0)
        difference = rotate(partner - signal, jnp.cos(angle_set), jnp.sin(angle_set))
        signal = jnp.where(is_upper, difference, signal + partner)
    return signal


def butterfly_up(signal, az_place, bit_count):
    for bit_num in range(bit_count):
        half_span = 1 << bit_num
        partner = partner_2(signal, "az", bit_num)
        is_upper = az_place >> bit_num & 1 == 1
        angle_set = angles(az_place % half_span, 2 * half_span, 1.0)
        cosine = jnp.cos(angle_set)
        sine_part = jnp.sin(angle_set)
        lower_new = (signal + rotate(partner, cosine, sine_part)) * 0.5
        upper_new = (partner - rotate(signal, cosine, sine_part)) * 0.5
        signal = jnp.where(is_upper, upper_new, lower_new)
    return signal


def butterfly_shards(raw_re, raw_im, ref_blocks, owners, offsets, taps):
    rg_cols = raw_re.shape[0]
    az_rows = raw_re.shape[1]
    az_count = lax.axis_size("az")
    az_place = lax.axis_index("az")
    bit_count = az_count.bit_length() - 1
    az_total = az_rows * az_count
    rg_total = rg_cols * lax.axis_size("rg")
    own_block = ref_blocks[0]
    lower_ref = from_root(own_block, "az", owners[0])
    upper_ref = from_root(own_block, "az", owners[1])
    signal = jnp.stack([raw_re, raw_im])
    signal = butterfly_down(signal, az_place, bit_count)
    column = jnp.zeros((), jnp.int32)
    for bit_num in range(bit_count):
        column = column + ((az_place >> bit_num & 1) << bit_count - 1 - bit_num)
    row_index = jnp.arange(az_rows, dtype=jnp.int32)
    twist = angles(row_index * column % az_total, az_total, -1.0)
    signal = rotate(signal, jnp.cos(twist)[None, :], jnp.sin(twist)[None, :])
    signal = local_dft(signal, -1.0)
    frequency = column + az_count * row_index
    signed = (frequency + az_total // 2) % az_total - az_total // 2
    az_freq = signed.astype(jnp.float32) / az_total
    rg_index = lax.axis_index("rg") * rg_cols + jnp.arange(rg_cols, dtype=jnp.int32)
    rg_freq = (rg_index.astype(jnp.float32) + 0.5) / (2 * rg_total) - 0.25
    model_phase = PHASE_GAIN * jnp.sqrt((1.0 + rg_freq)[:, None] ** 2 - az_freq[None, :] ** 2)
    ref_rows = own_block.shape[0]
    coarse = frequency * ref_rows // az_total
    slot_index = jnp.where(signed >= 0, ref_rows + coarse, coarse)
    one_hot = (jnp.arange(2 * ref_rows, dtype=jnp.int32)[:, None] == slot_index[None, :]).astype(
        jnp.float32
    )
    both_refs = jnp.concatenate([lower_ref, upper_ref], axis=0)
    picked = jnp.dot(both_refs.T, one_hot, precision=PRECISE)
    phase_all = model_phase + picked
    signal = rotate(signal, jnp.cos(phase_all), jnp.sin(phase_all))
    rim_width = REACH + TAPS // 2
    padded = padded_2(signal, (("rg", 1),), rim_width)
    offset_cols = jnp.repeat(offsets, BLOCK)
    local_cols = jnp.arange(rg_cols, dtype=jnp.int32)
    tap_index = jnp.arange(TAPS, dtype=jnp.int32)
    target = local_cols[:, None] + rim_width + offset_cols[:, None] + tap_index[None, :] - TAPS // 2
    padded_index = jnp.arange(rg_cols + 2 * rim_width, dtype=jnp.int32)
    hits = (padded_index[:, None, None] == target[None, :, :]).astype(jnp.float32)
    band_matrix = jnp.sum(hits * taps[None, :, :], axis=2)
    signal = jnp.einsum("zma,mi->zia", padded, band_matrix, precision=PRECISE)
    signal = local_dft(signal, 1.0) / az_rows
    twist_back = angles(row_index * column % az_total, az_total, 1.0)
    signal = rotate(signal, jnp.cos(twist_back)[None, :], jnp.sin(twist_back)[None, :])
    signal = butterfly_up(signal, az_place, bit_count)
    return (signal[0], signal[1])


FACTOR = 128
PLACES = 8
PART = FACTOR // PLACES
HALF = FACTOR // 2
OUT_BINS = 8
WINDOW = OUT_BINS + TAPS - 1
REF_LINES = 8
EDGE = 16
STEPS = (3, 2, 1, 0)


def split_bf16(value):
    high = value.astype(jnp.bfloat16)
    low = (value - high.astype(jnp.float32)).astype(jnp.bfloat16)
    return high, low


def dot(left, right):
    return jnp.dot(left, right, preferred_element_type=jnp.float32)


def dot_split(left, right):
    return dot(left[0], right[0]) + (dot(left[0], right[1]) + dot(left[1], right[0]))


def both_bf16(matrix):
    high = matrix.astype(jnp.bfloat16)
    return np.stack([high, (matrix - high.astype(np.float64)).astype(jnp.bfloat16)])


def long_bf16(matrix):
    high, low = both_bf16(matrix)
    return np.concatenate([high, high, low], axis=-1)


def long_rows(value):
    high, low = split_bf16(value)
    return jnp.concatenate([high, low, high], axis=0)


def dft_constants():
    counter = np.arange(FACTOR)
    kappa = np.arange(HALF)
    near, far, last, twists = [], [], [], []
    for side in range(2):
        order = [(middle, low, line) for low in (side, 1 - side) for middle in range(2) for line in range(PART)]
        mine = np.array([(2 * middle + low) * PART + line for middle, low, line in order])
        angle = 2 * np.pi * (np.outer(2 * kappa + side, mine) % FACTOR) / FACTOR
        cosine, sine = np.cos(angle), np.sin(angle)
        whole = np.block([[cosine, sine], [-sine, cosine]])
        quarters = np.split(whole, 4, axis=1)
        near.append(np.concatenate(quarters[0::2], axis=1))
        far.append(np.concatenate(quarters[1::2], axis=1))
        back_re, back_im = np.block([cosine.T, -sine.T]), np.block([sine.T, cosine.T])
        own, other = slice(0, HALF // 2), slice(HALF // 2, HALF)
        last.append(np.concatenate([back_re[own], back_im[own], back_re[other], back_im[other]]))
        twist = 2 * np.pi * np.outer(2 * kappa + side, counter) / FACTOR**2
        twists.append(np.stack([np.cos(twist), np.sin(twist)]))
    angle = 2 * np.pi * (np.outer(counter, counter) % FACTOR) / FACTOR
    cosine, sine = np.cos(angle), np.sin(angle)
    there = np.block([[cosine, -sine], [sine, cosine]])
    back = np.block([[cosine, sine], [-sine, cosine]])
    matrices = [
        long_bf16(np.stack(near)),
        long_bf16(np.stack(far)),
        both_bf16(there),
        both_bf16(back),
        both_bf16(np.stack(last)),
    ]
    return matrices, np.stack(twists).astype(np.float32)


def cos_sin_quarters(quarters):
    whole = jnp.floor(quarters + 0.5)
    rest = (quarters - whole) * (math.pi / 2)
    square = rest * rest
    sine = rest + rest * square * (
        -1.6666654611e-1 + square * (8.3321608736e-3 + square * (-1.9515295891e-4))
    )
    cosine = 1.0 - 0.5 * square + square * square * (
        4.166664568298827e-2 + square * (-1.388731625493765e-3 + square * 2.443315711809948e-5)
    )
    number = whole.astype(jnp.int32)
    odd = (number & 1) == 1
    turned_cos = jnp.where(odd, sine, cosine)
    turned_sin = jnp.where(odd, cosine, sine)
    cos_sign = jnp.where(((number + 1) & 2) == 2, -1.0, 1.0)
    sin_sign = jnp.where((number & 2) == 2, -1.0, 1.0)
    return turned_cos * cos_sign, turned_sin * sin_sign


def window_start(chip, side, offsets_own, offsets_other):
    block = chip * OUT_BINS // BLOCK
    blocks = offsets_own.shape[0]
    local = lax.rem(block, blocks)
    shift = jnp.where(lax.div(block, blocks) == side, offsets_own[local], offsets_other[local])
    return chip * OUT_BINS + shift - TAPS // 2


def spread_lines(target, base, source):
    bins, samples = source.shape
    part_rows = samples // FACTOR
    for tile in range(0, bins, 8):
        for row in range(part_rows):
            target[pl.ds((base + tile) * part_rows + row, 8, stride=part_rows), :] = source[
                tile : tile + 8, row * FACTOR : (row + 1) * FACTOR
            ]


def pack_kernel(re_lines, im_lines, re_other, im_other, ref_own, ref_other, own_offsets, other_offsets, *refs):
    messages, (re_all, im_all, ref_all, off_own, off_other, sems) = refs[:-6], refs[-6:]
    copies = [
        pltpu.make_async_copy(source, target, sems.at[at])
        for at, (source, target) in enumerate(((own_offsets, off_own), (other_offsets, off_other)))
    ]
    for copy in copies:
        copy.start()
    bins, samples = re_other.shape
    part_rows = samples // FACTOR
    place, side = lax.axis_index("az"), lax.axis_index("rg")
    own_at, other_at = EDGE + side * bins, EDGE + (1 - side) * bins
    zeros = jnp.zeros((EDGE * part_rows, FACTOR), jnp.float32)
    for all_ref, own, other in ((re_all, re_lines, re_other), (im_all, im_lines, im_other)):
        all_ref[: EDGE * part_rows, :] = zeros
        all_ref[(EDGE + 2 * bins) * part_rows :, :] = zeros
        all_ref[pl.ds(pl.multiple_of(own_at * part_rows, 8), bins * part_rows), :] = own[...]
        spread_lines(all_ref, other_at, other)
    ref_all[:EDGE, :] = jnp.zeros((EDGE, FACTOR), jnp.float32)
    ref_all[EDGE + 2 * bins :, :] = jnp.zeros((EDGE, FACTOR), jnp.float32)
    for at, ref in ((own_at, ref_own), (other_at, ref_other)):
        ref_all[pl.ds(pl.multiple_of(at, 16), bins), :] = jnp.concatenate([ref[...], ref[...]], axis=1)
    for copy in copies:
        copy.wait()
    lane = lax.broadcasted_iota(jnp.int32, (1, FACTOR), 1)
    for at, message in enumerate(messages):
        body = WINDOW * part_rows
        start = window_start(((place >> 1) ^ at) * 2 + side, side, off_own, off_other) + EDGE
        rows = pl.ds(pl.multiple_of(start * part_rows, 8), body)
        message[:body, :] = re_all[rows, :]
        message[body : 2 * body, :] = im_all[rows, :]
        for bin_num in range(REF_LINES):
            low = ref_all[pl.ds(start + bin_num, 1), :]
            high = ref_all[pl.ds(start + REF_LINES + bin_num, 1), :]
            message[2 * body + bin_num : 2 * body + bin_num + 1, :] = jnp.where(lane < HALF, low, high)


def phase_kernel(bins_total, off_own, off_other, owners, taps_own, taps_other, out, weights, choice):
    place, side = lax.axis_index("az"), lax.axis_index("rg")
    bins_held = taps_own.shape[0]
    held = lax.div(place * OUT_BINS, bins_held) == side
    local = lax.rem(place * OUT_BINS, bins_held)
    for bin_num in range(OUT_BINS):
        for tap in range(TAPS):
            weight = jnp.where(held, taps_own[local + bin_num, tap], taps_other[local + bin_num, tap])
            line = bin_num * TAPS + tap
            weights[line : line + 1, :] = jnp.full((1, FACTOR), weight, jnp.float32)
    line = lax.broadcasted_iota(jnp.int32, (2 * len(STEPS), FACTOR), 0)
    for which in range(2):
        owner = owners[which]
        step = (owner >> 1) ^ (place >> 1)
        wanted = jnp.where((owner & 1) == side, step, step + len(STEPS))
        choice[which] = jnp.where(line == wanted, 1.0, 0.0)
    start = window_start(place, side, off_own, off_other)
    shape = (HALF, FACTOR)
    kappa = lax.broadcasted_iota(jnp.int32, shape, 0)
    frequency = 2 * kappa + side + FACTOR * lax.broadcasted_iota(jnp.int32, shape, 1)
    total = FACTOR * FACTOR
    signed = jnp.where(frequency >= total // 2, frequency - total, frequency)
    az_freq = signed.astype(jnp.float32) / total
    az_square = az_freq * az_freq
    for bin_num in range(WINDOW):
        rg_index = (start + bin_num).astype(jnp.float32)
        rg_freq = (rg_index + 0.5) / (2 * bins_total) - 0.25
        base = (1.0 + rg_freq) * (1.0 + rg_freq)
        root = jnp.sqrt(base - az_square)
        cosine, sine = cos_sin_quarters(root * (PHASE_GAIN * 2 / math.pi))
        out[bin_num, 0] = cosine
        out[bin_num, 1] = sine


def parity_kernel(*refs):
    chunks = dict(zip(STEPS, refs))
    keep, give = refs[len(STEPS) :]
    place, side = lax.axis_index("az"), lax.axis_index("rg")
    sign = jnp.where(place >= PLACES // 2, -1.0, 1.0)
    even = side == 0
    keep_near, keep_far = jnp.where(even, 1.0, sign), jnp.where(even, 1.0, -sign)
    give_near, give_far = jnp.where(even, sign, 1.0), jnp.where(even, -sign, 1.0)
    plain = ((place >> 1) & 1) == 0
    for line in range(2 * WINDOW):
        read = slice(line * PART, (line + 1) * PART)
        write = line * 2 * PART
        values = [chunks[step][read, :] for step in range(4)]
        for target, near_factor, far_factor in ((keep, keep_near, keep_far), (give, give_near, give_far)):
            pair = [values[step] * near_factor + values[step + 2] * far_factor for step in range(2)]
            target[write : write + PART, :] = jnp.where(plain, pair[0], pair[1])
            target[write + PART : write + 2 * PART, :] = jnp.where(plain, pair[1], pair[0])
    for step in range(len(STEPS)):
        value = chunks[step][2 * WINDOW * PART :, :]
        at = 2 * WINDOW * 2 * PART + step * REF_LINES
        keep[at : at + REF_LINES, :] = value
        give[at : at + REF_LINES, :] = value


def gather_lines(ref, bins, group):
    width = 2 * PART
    columns = [
        jnp.concatenate(
            [ref[(part * bins + bin_num) * width : (part * bins + bin_num + 1) * width, :] for part in range(2)], axis=0
        )
        for bin_num in group
    ]
    return jnp.concatenate(columns, axis=1)


def bin_groups(bins):
    return [range(at, min(at + 4, bins)) for at in range(0, bins, 4)]


def near_kernel(keep, near, out):
    matrix = near[lax.axis_index("rg")]
    for index, group in enumerate(bin_groups(WINDOW)):
        out[index, :, : len(group) * FACTOR] = dot(matrix, long_rows(gather_lines(keep, WINDOW, group)))


def band_kernel(
    partial, keep, got, phase, weights, choice, far, there, back, last, twists, keep_out, give_out, spectra, band, picked
):
    side = lax.axis_index("rg")
    bins = WINDOW

    lane = lax.broadcasted_iota(jnp.int32, (REF_LINES, FACTOR), 1)
    lines = []
    for which in range(2):
        value = jnp.zeros((REF_LINES, FACTOR), jnp.float32)
        for option in range(2 * len(STEPS)):
            at = 2 * bins * 2 * PART + option % len(STEPS) * REF_LINES
            candidate = (keep if option < len(STEPS) else got)[at : at + REF_LINES, :]
            value = jnp.where(choice[which, option : option + 1, :] > 0.5, candidate, value)
        lines.append(value)
    for block in range(2):
        coarse = (lane >> 1) + block * HALF
        wide = [jnp.take_along_axis(lines[which], coarse, axis=1) for which in range(2)]
        ref_phase = jnp.where(lane < HALF, wide[1], wide[0])
        ref_cos, ref_sin = cos_sin_quarters(ref_phase * (2 / math.pi))
        picked[0, block * REF_LINES : (block + 1) * REF_LINES, :] = ref_cos
        picked[1, block * REF_LINES : (block + 1) * REF_LINES, :] = ref_sin

    far, last = far[side], (last[0, side], last[1, side])
    there, back = (there[0], there[1]), (back[0], back[1])
    twist_cos, twist_sin = twists[side, 0], twists[side, 1]
    for number, group in enumerate(bin_groups(bins)):
        passed = partial[number, :, : len(group) * FACTOR] + dot(far, long_rows(gather_lines(got, bins, group)))
        rows = []
        for index in range(len(group)):
            real = passed[:HALF, index * FACTOR : (index + 1) * FACTOR]
            imag = passed[HALF:, index * FACTOR : (index + 1) * FACTOR]
            rows.append(
                jnp.concatenate([real * twist_cos + imag * twist_sin, imag * twist_cos - real * twist_sin], axis=1)
            )
        passed = dot_split(split_bf16(jnp.concatenate(rows, axis=0)), there)
        for index, bin_num in enumerate(group):
            real = passed[index * HALF : (index + 1) * HALF, :FACTOR]
            imag = passed[index * HALF : (index + 1) * HALF, FACTOR:]
            model_cos, model_sin = phase[bin_num, 0], phase[bin_num, 1]
            row_cos, row_sin = picked[0, bin_num : bin_num + 1, :], picked[1, bin_num : bin_num + 1, :]
            cosine = model_cos * row_cos - model_sin * row_sin
            sine = model_sin * row_cos + model_cos * row_sin
            spectra[bin_num, 0] = real * cosine - imag * sine
            spectra[bin_num, 1] = real * sine + imag * cosine

    strip = 8
    for part in range(2):
        for at in range(0, HALF, strip):
            rows = slice(at, at + strip)
            sums = {}
            for bin_num in range(bins):
                value = spectra[bin_num, part, rows]
                for out in range(max(0, bin_num - TAPS + 1), min(OUT_BINS, bin_num + 1)):
                    weight = out * TAPS + bin_num - out
                    term = value * weights[weight : weight + 1, :]
                    sums[out] = sums[out] + term if out in sums else term
            for out in range(OUT_BINS):
                line = out * HALF + at
                band[line : line + strip, part * FACTOR : (part + 1) * FACTOR] = sums[out]

    scale = 1.0 / (FACTOR * FACTOR)
    cos_table, sin_table = twist_cos * scale, twist_sin * scale
    for at in range(0, OUT_BINS, 4):
        passed = dot_split(split_bf16(band[at * HALF : (at + 4) * HALF, :]), back)
        columns = []
        for index in range(4):
            real = passed[index * HALF : (index + 1) * HALF, :FACTOR]
            imag = passed[index * HALF : (index + 1) * HALF, FACTOR:]
            columns.append(
                jnp.concatenate([real * cos_table - imag * sin_table, imag * cos_table + real * sin_table], axis=0)
            )
        passed = dot_split(last, split_bf16(jnp.concatenate(columns, axis=1)))
        for index in range(4):
            lines = slice((at + index) * HALF, (at + index + 1) * HALF)
            keep_out[lines, :] = passed[:HALF, index * FACTOR : (index + 1) * FACTOR]
            give_out[lines, :] = passed[HALF:, index * FACTOR : (index + 1) * FACTOR]


def crossed(quarter):
    return ((quarter & 1) << 1) | (quarter >> 1)


def join_kernel(keep, got, *messages):
    place, side = lax.axis_index("az"), lax.axis_index("rg")
    quarter = lax.rem(place, PLACES // 2)
    sign = jnp.where(side == 0, 1.0, -1.0)
    for step, message in enumerate(messages):
        target = crossed(quarter) ^ step
        top, middle = target >> 1, target & 1
        keep_factor, got_factor = jnp.where(top == 0, 1.0, sign), jnp.where(top == 0, 1.0, -sign)
        for line in range(2 * OUT_BINS):
            read = pl.ds(pl.multiple_of(line * 2 * PART + middle * PART, 8), PART)
            message[line * PART : (line + 1) * PART, :] = keep[read, :] * keep_factor + got[read, :] * got_factor


def place_kernel(step, message, *refs):
    outs, (tiles, sems) = refs[-4:-2], refs[-2:]
    sender = crossed((lax.axis_index("az") >> 1) ^ step)
    rows = pl.ds(pl.multiple_of(sender * OUT_BINS, 8), OUT_BINS)
    copies = []
    for part, out in enumerate(outs):
        for row in range(PART):
            tiles[part, :, row * FACTOR : (row + 1) * FACTOR] = message[
                pl.ds(part * PART + row, OUT_BINS, stride=2 * PART), :
            ]
        copies.append(pltpu.make_async_copy(tiles.at[part], out.at[rows], sems.at[part]))
        copies[-1].start()
    for copy in copies:
        copy.wait()


VMEM = pl.BlockSpec(memory_space=pltpu.VMEM)
SMEM = pl.BlockSpec(memory_space=pltpu.SMEM)


def kernel_call(body, name, out_shape, operands, scratch=(), flops=0, count=10**6, limit=8):
    specs = [SMEM if operand.size <= 256 else VMEM for operand in operands]
    return pl.pallas_call(
        body,
        out_shape=out_shape,
        in_specs=specs,
        out_specs=jax.tree.map(lambda _: VMEM, out_shape),
        scratch_shapes=[pltpu.VMEM(shape, jnp.float32) for shape in scratch],
        compiler_params=pltpu.CompilerParams(vmem_limit_bytes=limit * 1024 * 1024),
        cost_estimate=pl.CostEstimate(flops=flops, bytes_accessed=count, transcendentals=0),
        name=name,
    )(*operands)


def transposed_shards(raw_re, raw_im, ref_blocks, owners, offsets, taps):
    bins, samples = raw_re.shape

    def array(*shape):
        return jax.ShapeDtypeStruct(shape, jnp.float32)

    matrices, twists = dft_constants()
    near_table, *tables = [jnp.asarray(table) for table in (*matrices, twists)]
    swap = functools.partial(lax.ppermute, axis_name="rg", perm=[(0, 1), (1, 0)])
    half = PLACES // 2
    ref_own = ref_blocks[0].T
    offsets_other = swap(offsets)
    ref_other, re_other, im_other, taps_other = swap(ref_own), swap(raw_re), swap(raw_im), swap(taps)

    lines = [raw_re.reshape(bins * PART, FACTOR), raw_im.reshape(bins * PART, FACTOR)]
    all_bins = 2 * bins + 2 * EDGE
    anywhere = pl.BlockSpec(memory_space=pl.ANY)
    messages = pl.pallas_call(
        pack_kernel,
        out_shape=[array(2 * WINDOW * PART + REF_LINES, FACTOR)] * half,
        in_specs=[VMEM] * 6 + [anywhere] * 2,
        out_specs=[VMEM] * half,
        scratch_shapes=[
            pltpu.VMEM((all_bins * PART, FACTOR), jnp.float32),
            pltpu.VMEM((all_bins * PART, FACTOR), jnp.float32),
            pltpu.VMEM((all_bins, FACTOR), jnp.float32),
            pltpu.SMEM(offsets.shape, jnp.int32),
            pltpu.SMEM(offsets.shape, jnp.int32),
            pltpu.SemaphoreType.DMA((2,)),
        ],
        compiler_params=pltpu.CompilerParams(vmem_limit_bytes=8 * 1024 * 1024),
        cost_estimate=pl.CostEstimate(flops=1, bytes_accessed=1, transcendentals=0),
        name="pack",
    )(*lines, re_other, im_other, ref_own, ref_other, offsets, offsets_other)
    prepared = kernel_call(
        functools.partial(phase_kernel, 2 * bins),
        "phase",
        [array(WINDOW, 2, HALF, FACTOR), array(OUT_BINS * TAPS, FACTOR), array(2, 2 * half, FACTOR)],
        [offsets, offsets_other, owners, taps, taps_other],
    )

    routes = [
        [
            (chip * 2 + core, (((chip >> 1) ^ step) * 2 + core) * 2 + (chip & 1))
            for chip in range(PLACES)
            for core in range(2)
        ]
        for step in range(half)
    ]
    routes_back = [
        [
            (chip * 2 + core, ((crossed(chip % half) ^ step) * 2 + core) * 2 + chip // half)
            for chip in range(PLACES)
            for core in range(2)
        ]
        for step in range(half)
    ]
    arrived = [lax.ppermute(messages[step], ("az", "rg"), routes[step]) for step in STEPS]
    *arrived, phases, weights, choice = lax.optimization_barrier((*arrived, *prepared))

    size = 2 * WINDOW * 2 * PART + half * REF_LINES
    keep, give = kernel_call(parity_kernel, "parity", [array(size, FACTOR)] * 2, arrived)
    got = swap(give)
    partial = kernel_call(
        near_kernel, "near", array(len(bin_groups(WINDOW)), FACTOR, 4 * FACTOR), [keep, near_table]
    )
    keep, give = kernel_call(
        band_kernel,
        "band",
        [array(OUT_BINS * HALF, FACTOR)] * 2,
        [partial, keep, got, phases, weights, choice, *tables],
        scratch=[(WINDOW, 2, HALF, FACTOR), (OUT_BINS * HALF, 2 * FACTOR), (2, 2 * REF_LINES, FACTOR)],
        limit=16,
    )
    sent = kernel_call(join_kernel, "join", [array(2 * OUT_BINS * PART, FACTOR)] * half, [keep, swap(give)])
    results = [lax.ppermute(message, ("az", "rg"), route) for message, route in zip(sent, routes_back)]
    images = []
    for step, message in enumerate(results):
        images = pl.pallas_call(
            functools.partial(place_kernel, step),
            out_shape=[array(bins, samples)] * 2,
            in_specs=[VMEM] + [anywhere] * len(images),
            out_specs=[anywhere] * 2,
            scratch_shapes=[pltpu.VMEM((2, OUT_BINS, samples), jnp.float32), pltpu.SemaphoreType.DMA((2,))],
            input_output_aliases={1: 0, 2: 1} if images else {},
            compiler_params=pltpu.CompilerParams(vmem_limit_bytes=8 * 1024 * 1024),
            cost_estimate=pl.CostEstimate(flops=1, bytes_accessed=1, transcendentals=0),
            name="place",
        )(message, *images)
    return images


def solution(mesh):
    sizes = mesh.shape

    def whole(raw_re, raw_im, ref_blocks, owners, offsets, taps):
        line = raw_re.shape[1] // sizes["scene"]
        fits = (
            sizes["rg"] == 2
            and sizes["az"] == PLACES
            and raw_re.shape[0] == OUT_BINS * PLACES
            and line == FACTOR * FACTOR
            and ref_blocks.shape[1] == HALF
        )
        return jax.shard_map(
            transposed_shards if fits else butterfly_shards,
            mesh=mesh,
            in_specs=(
                P("rg", ("scene", "az")),
                P("rg", ("scene", "az")),
                P(("scene", "az"), None, "rg"),
                P("scene"),
                P("rg"),
                P("rg", None),
            ),
            out_specs=(P("rg", ("scene", "az")), P("rg", ("scene", "az"))),
            check_vma=False,
        )(raw_re, raw_im, ref_blocks, owners, offsets, taps)

    return whole
```

```python
import functools
import math

import jax
import jax.numpy as jnp
import numpy as np
from jax import lax
from jax.experimental import pallas as pl
from jax.experimental.pallas import tpu as pltpu
from jax.sharding import PartitionSpec as P

SPLIT = 4
TAPS = 8
REACH = 8
BLOCK = 16


PRECISE = lax.Precision.HIGHEST
PHASE_GAIN = 50.0


def partner_2(value, axis, stride):
    return lax.ppermute(value, axis, [(i, i ^ 1 << stride) for i in range(lax.axis_size(axis))])


def from_root(block, axis, source):
    block = jnp.where(lax.axis_index(axis) == source, block, jnp.zeros_like(block))
    return lax.psum(block, axis)


def padded_2(value, sides, width):
    for axis, dim in sides:
        size, length = (lax.axis_size(axis), value.shape[dim])
        up = [(i, (i + 1) % size) for i in range(size - 1)]
        down = [(j, i) for i, j in up]
        last = lax.slice_in_dim(value, length - width, length, axis=dim)
        initial = lax.slice_in_dim(value, 0, width, axis=dim)
        before = lax.ppermute(last, axis, up)
        after = lax.ppermute(initial, axis, down)
        value = jnp.concatenate([before, value, after], axis=dim)
    return value


def angles(numerator, denominator, sign_value):
    return sign_value * 2.0 * math.pi * numerator.astype(jnp.float32) / denominator


def rotate(signal, cosine, sine_part):
    real_part = signal[0] * cosine - signal[1] * sine_part
    imag_part = signal[0] * sine_part + signal[1] * cosine
    return jnp.stack([real_part, imag_part])


def dft_table(length_n, sign_value):
    counter = jnp.arange(length_n, dtype=jnp.int32)
    turn_count = counter[:, None] * counter[None, :] % length_n
    angle_set = angles(turn_count, length_n, sign_value)
    return (jnp.cos(angle_set), jnp.sin(angle_set))


def complex_apply(einsum_form, cosine, sine_part, signal):
    real_part = jnp.einsum(einsum_form, cosine, signal[0], precision=PRECISE) - jnp.einsum(
        einsum_form, sine_part, signal[1], precision=PRECISE
    )
    imag_part = jnp.einsum(einsum_form, cosine, signal[1], precision=PRECISE) + jnp.einsum(
        einsum_form, sine_part, signal[0], precision=PRECISE
    )
    return jnp.stack([real_part, imag_part])


def local_dft(signal, sign_value):
    rg_cols = signal.shape[1]
    az_rows = signal.shape[2]
    inner_len = az_rows // SPLIT
    shaped = signal.reshape(2, rg_cols, SPLIT, inner_len)
    first_cos, first_sin = dft_table(SPLIT, sign_value)
    first_pass = complex_apply("aj,cjk->cak", first_cos, first_sin, shaped)
    outer_idx = jnp.arange(SPLIT, dtype=jnp.int32)
    inner_idx = jnp.arange(inner_len, dtype=jnp.int32)
    twist = angles(outer_idx[:, None] * inner_idx[None, :] % az_rows, az_rows, sign_value)
    first_pass = rotate(first_pass, jnp.cos(twist)[None, :, :], jnp.sin(twist)[None, :, :])
    second_cos, second_sin = dft_table(inner_len, sign_value)
    second_pass = complex_apply("bk,cak->cba", second_cos, second_sin, first_pass)
    return second_pass.reshape(2, rg_cols, az_rows)


def butterfly_down(signal, az_place, bit_count):
    for bit_num in reversed(range(bit_count)):
        half_span = 1 << bit_num
        partner = partner_2(signal, "az", bit_num)
        is_upper = az_place >> bit_num & 1 == 1
        angle_set = angles(az_place % half_span, 2 * half_span, -1.0)
        difference = rotate(partner - signal, jnp.cos(angle_set), jnp.sin(angle_set))
        signal = jnp.where(is_upper, difference, signal + partner)
    return signal


def butterfly_up(signal, az_place, bit_count):
    for bit_num in range(bit_count):
        half_span = 1 << bit_num
        partner = partner_2(signal, "az", bit_num)
        is_upper = az_place >> bit_num & 1 == 1
        angle_set = angles(az_place % half_span, 2 * half_span, 1.0)
        cosine = jnp.cos(angle_set)
        sine_part = jnp.sin(angle_set)
        lower_new = (signal + rotate(partner, cosine, sine_part)) * 0.5
        upper_new = (partner - rotate(signal, cosine, sine_part)) * 0.5
        signal = jnp.where(is_upper, upper_new, lower_new)
    return signal


def butterfly_shards(raw_re, raw_im, ref_blocks, owners, offsets, taps):
    rg_cols = raw_re.shape[0]
    az_rows = raw_re.shape[1]
    az_count = lax.axis_size("az")
    az_place = lax.axis_index("az")
    bit_count = az_count.bit_length() - 1
    az_total = az_rows * az_count
    rg_total = rg_cols * lax.axis_size("rg")
    own_block = ref_blocks[0]
    lower_ref = from_root(own_block, "az", owners[0])
    upper_ref = from_root(own_block, "az", owners[1])
    signal = jnp.stack([raw_re, raw_im])
    signal = butterfly_down(signal, az_place, bit_count)
    column = jnp.zeros((), jnp.int32)
    for bit_num in range(bit_count):
        column = column + ((az_place >> bit_num & 1) << bit_count - 1 - bit_num)
    row_index = jnp.arange(az_rows, dtype=jnp.int32)
    twist = angles(row_index * column % az_total, az_total, -1.0)
    signal = rotate(signal, jnp.cos(twist)[None, :], jnp.sin(twist)[None, :])
    signal = local_dft(signal, -1.0)
    frequency = column + az_count * row_index
    signed = (frequency + az_total // 2) % az_total - az_total // 2
    az_freq = signed.astype(jnp.float32) / az_total
    rg_index = lax.axis_index("rg") * rg_cols + jnp.arange(rg_cols, dtype=jnp.int32)
    rg_freq = (rg_index.astype(jnp.float32) + 0.5) / (2 * rg_total) - 0.25
    model_phase = PHASE_GAIN * jnp.sqrt((1.0 + rg_freq)[:, None] ** 2 - az_freq[None, :] ** 2)
    ref_rows = own_block.shape[0]
    coarse = frequency * ref_rows // az_total
    slot_index = jnp.where(signed >= 0, ref_rows + coarse, coarse)
    one_hot = (jnp.arange(2 * ref_rows, dtype=jnp.int32)[:, None] == slot_index[None, :]).astype(
        jnp.float32
    )
    both_refs = jnp.concatenate([lower_ref, upper_ref], axis=0)
    picked = jnp.dot(both_refs.T, one_hot, precision=PRECISE)
    phase_all = model_phase + picked
    signal = rotate(signal, jnp.cos(phase_all), jnp.sin(phase_all))
    rim_width = REACH + TAPS // 2
    padded = padded_2(signal, (("rg", 1),), rim_width)
    offset_cols = jnp.repeat(offsets, BLOCK)
    local_cols = jnp.arange(rg_cols, dtype=jnp.int32)
    tap_index = jnp.arange(TAPS, dtype=jnp.int32)
    target = local_cols[:, None] + rim_width + offset_cols[:, None] + tap_index[None, :] - TAPS // 2
    padded_index = jnp.arange(rg_cols + 2 * rim_width, dtype=jnp.int32)
    hits = (padded_index[:, None, None] == target[None, :, :]).astype(jnp.float32)
    band_matrix = jnp.sum(hits * taps[None, :, :], axis=2)
    signal = jnp.einsum("zma,mi->zia", padded, band_matrix, precision=PRECISE)
    signal = local_dft(signal, 1.0) / az_rows
    twist_back = angles(row_index * column % az_total, az_total, 1.0)
    signal = rotate(signal, jnp.cos(twist_back)[None, :], jnp.sin(twist_back)[None, :])
    signal = butterfly_up(signal, az_place, bit_count)
    return (signal[0], signal[1])


FACTOR = 128
PLACES = 8
PART = FACTOR // PLACES
HALF = FACTOR // 2
OUT_BINS = 8
WINDOW = OUT_BINS + TAPS - 1
REF_LINES = 8
EDGE = 16
STEPS = (2, 3, 1, 0)
STEPS_BACK = (1, 0, 3, 2)


def split_bf16(value):
    high = value.astype(jnp.bfloat16)
    low = (value - high.astype(jnp.float32)).astype(jnp.bfloat16)
    return high, low


def dot(left, right):
    return jnp.dot(left, right, preferred_element_type=jnp.float32)


def dot_split(left, right):
    return dot(left[0], right[0]) + (dot(left[0], right[1]) + dot(left[1], right[0]))


def both_bf16(matrix):
    high = matrix.astype(jnp.bfloat16)
    return np.stack([high, (matrix - high.astype(np.float64)).astype(jnp.bfloat16)])


def long_bf16(matrix):
    high, low = both_bf16(matrix)
    return np.concatenate([high, high, low], axis=-1)


def long_rows(value):
    high, low = split_bf16(value)
    return jnp.concatenate([high, low, high], axis=0)


def dft_constants():
    counter = np.arange(FACTOR)
    kappa = np.arange(HALF)
    near, far, last, twists = [], [], [], []
    for side in range(2):
        order = [(middle, low, line) for low in (side, 1 - side) for middle in range(2) for line in range(PART)]
        mine = np.array([(2 * middle + low) * PART + line for middle, low, line in order])
        angle = 2 * np.pi * (np.outer(2 * kappa + side, mine) % FACTOR) / FACTOR
        cosine, sine = np.cos(angle), np.sin(angle)
        whole = np.block([[cosine, sine], [-sine, cosine]])
        quarters = np.split(whole, 4, axis=1)
        near.append(np.concatenate(quarters[0::2], axis=1))
        far.append(np.concatenate(quarters[1::2], axis=1))
        back_re, back_im = np.block([cosine.T, -sine.T]), np.block([sine.T, cosine.T])
        own, other = slice(0, HALF // 2), slice(HALF // 2, HALF)
        last.append(np.concatenate([back_re[own], back_im[own], back_re[other], back_im[other]]))
        twist = 2 * np.pi * np.outer(2 * kappa + side, counter) / FACTOR**2
        twists.append(np.stack([np.cos(twist), np.sin(twist)]))
    angle = 2 * np.pi * (np.outer(counter, counter) % FACTOR) / FACTOR
    cosine, sine = np.cos(angle), np.sin(angle)
    there = np.block([[cosine, -sine], [sine, cosine]])
    back = np.block([[cosine, sine], [-sine, cosine]])
    matrices = [
        long_bf16(np.stack(near)),
        long_bf16(np.stack(far)),
        both_bf16(there),
        both_bf16(back),
        both_bf16(np.stack(last)),
    ]
    return matrices, np.stack(twists).astype(np.float32)


def cos_sin_quarters(quarters):
    whole = jnp.floor(quarters + 0.5)
    rest = (quarters - whole) * (math.pi / 2)
    square = rest * rest
    sine = rest + rest * square * (
        -1.6666654611e-1 + square * (8.3321608736e-3 + square * (-1.9515295891e-4))
    )
    cosine = 1.0 - 0.5 * square + square * square * (
        4.166664568298827e-2 + square * (-1.388731625493765e-3 + square * 2.443315711809948e-5)
    )
    number = whole.astype(jnp.int32)
    odd = (number & 1) == 1
    turned_cos = jnp.where(odd, sine, cosine)
    turned_sin = jnp.where(odd, cosine, sine)
    cos_sign = jnp.where(((number + 1) & 2) == 2, -1.0, 1.0)
    sin_sign = jnp.where((number & 2) == 2, -1.0, 1.0)
    return turned_cos * cos_sign, turned_sin * sin_sign


def window_start(chip, side, offsets_own, offsets_other):
    block = chip * OUT_BINS // BLOCK
    blocks = offsets_own.shape[0]
    local = lax.rem(block, blocks)
    shift = jnp.where(lax.div(block, blocks) == side, offsets_own[local], offsets_other[local])
    return chip * OUT_BINS + shift - TAPS // 2


def spread_lines(target, base, source):
    bins, samples = source.shape
    part_rows = samples // FACTOR
    for tile in range(0, bins, 8):
        for row in range(part_rows):
            target[pl.ds((base + tile) * part_rows + row, 8, stride=part_rows), :] = source[
                tile : tile + 8, row * FACTOR : (row + 1) * FACTOR
            ]


def pack_kernel(re_lines, im_lines, re_other, im_other, ref_own, ref_other, own_offsets, other_offsets, *refs):
    messages, (re_all, im_all, ref_all, off_own, off_other, sems) = refs[:-6], refs[-6:]
    copies = [
        pltpu.make_async_copy(source, target, sems.at[at])
        for at, (source, target) in enumerate(((own_offsets, off_own), (other_offsets, off_other)))
    ]
    for copy in copies:
        copy.start()
    bins, samples = re_other.shape
    part_rows = samples // FACTOR
    place, side = lax.axis_index("az"), lax.axis_index("rg")
    own_at, other_at = EDGE + side * bins, EDGE + (1 - side) * bins
    zeros = jnp.zeros((EDGE * part_rows, FACTOR), jnp.float32)
    for all_ref, own, other in ((re_all, re_lines, re_other), (im_all, im_lines, im_other)):
        all_ref[: EDGE * part_rows, :] = zeros
        all_ref[(EDGE + 2 * bins) * part_rows :, :] = zeros
        all_ref[pl.ds(pl.multiple_of(own_at * part_rows, 8), bins * part_rows), :] = own[...]
        spread_lines(all_ref, other_at, other)
    ref_all[:EDGE, :] = jnp.zeros((EDGE, FACTOR), jnp.float32)
    ref_all[EDGE + 2 * bins :, :] = jnp.zeros((EDGE, FACTOR), jnp.float32)
    for at, ref in ((own_at, ref_own), (other_at, ref_other)):
        ref_all[pl.ds(pl.multiple_of(at, 16), bins), :] = jnp.concatenate([ref[...], ref[...]], axis=1)
    for copy in copies:
        copy.wait()
    lane = lax.broadcasted_iota(jnp.int32, (1, FACTOR), 1)
    for at, message in enumerate(messages):
        body = WINDOW * part_rows
        start = window_start(((place >> 1) ^ at) * 2 + side, side, off_own, off_other) + EDGE
        rows = pl.ds(pl.multiple_of(start * part_rows, 8), body)
        message[:body, :] = re_all[rows, :]
        message[body : 2 * body, :] = im_all[rows, :]
        for bin_num in range(REF_LINES):
            low = ref_all[pl.ds(start + bin_num, 1), :]
            high = ref_all[pl.ds(start + REF_LINES + bin_num, 1), :]
            message[2 * body + bin_num : 2 * body + bin_num + 1, :] = jnp.where(lane < HALF, low, high)


def phase_kernel(bins_total, off_own, off_other, owners, taps_own, taps_other, out, weights, choice):
    place, side = lax.axis_index("az"), lax.axis_index("rg")
    bins_held = taps_own.shape[0]
    held = lax.div(place * OUT_BINS, bins_held) == side
    local = lax.rem(place * OUT_BINS, bins_held)
    for bin_num in range(OUT_BINS):
        for tap in range(TAPS):
            weight = jnp.where(held, taps_own[local + bin_num, tap], taps_other[local + bin_num, tap])
            line = bin_num * TAPS + tap
            weights[line : line + 1, :] = jnp.full((1, FACTOR), weight, jnp.float32)
    line = lax.broadcasted_iota(jnp.int32, (2 * len(STEPS), FACTOR), 0)
    for which in range(2):
        owner = owners[which]
        step = (owner >> 1) ^ (place >> 1)
        wanted = jnp.where((owner & 1) == side, step, step + len(STEPS))
        choice[which] = jnp.where(line == wanted, 1.0, 0.0)
    start = window_start(place, side, off_own, off_other)
    shape = (HALF, FACTOR)
    kappa = lax.broadcasted_iota(jnp.int32, shape, 0)
    frequency = 2 * kappa + side + FACTOR * lax.broadcasted_iota(jnp.int32, shape, 1)
    total = FACTOR * FACTOR
    signed = jnp.where(frequency >= total // 2, frequency - total, frequency)
    az_freq = signed.astype(jnp.float32) / total
    az_square = az_freq * az_freq
    for bin_num in range(WINDOW):
        rg_index = (start + bin_num).astype(jnp.float32)
        rg_freq = (rg_index + 0.5) / (2 * bins_total) - 0.25
        base = (1.0 + rg_freq) * (1.0 + rg_freq)
        root = jnp.sqrt(base - az_square)
        cosine, sine = cos_sin_quarters(root * (PHASE_GAIN * 2 / math.pi))
        out[bin_num, 0] = cosine
        out[bin_num, 1] = sine


def parity_kernel(*refs):
    chunks = dict(zip(STEPS, refs))
    keep, give = refs[len(STEPS) :]
    place, side = lax.axis_index("az"), lax.axis_index("rg")
    sign = jnp.where(place >= PLACES // 2, -1.0, 1.0)
    even = side == 0
    keep_near, keep_far = jnp.where(even, 1.0, sign), jnp.where(even, 1.0, -sign)
    give_near, give_far = jnp.where(even, sign, 1.0), jnp.where(even, -sign, 1.0)
    plain = ((place >> 1) & 1) == 0
    for line in range(2 * WINDOW):
        read = slice(line * PART, (line + 1) * PART)
        write = line * 2 * PART
        values = [chunks[step][read, :] for step in range(4)]
        for target, near_factor, far_factor in ((keep, keep_near, keep_far), (give, give_near, give_far)):
            pair = [values[step] * near_factor + values[step + 2] * far_factor for step in range(2)]
            target[write : write + PART, :] = jnp.where(plain, pair[0], pair[1])
            target[write + PART : write + 2 * PART, :] = jnp.where(plain, pair[1], pair[0])
    for step in range(len(STEPS)):
        value = chunks[step][2 * WINDOW * PART :, :]
        at = 2 * WINDOW * 2 * PART + step * REF_LINES
        keep[at : at + REF_LINES, :] = value
        give[at : at + REF_LINES, :] = value


def gather_lines(ref, bins, group):
    width = 2 * PART
    columns = [
        jnp.concatenate(
            [ref[(part * bins + bin_num) * width : (part * bins + bin_num + 1) * width, :] for part in range(2)], axis=0
        )
        for bin_num in group
    ]
    return jnp.concatenate(columns, axis=1)


def bin_groups(bins):
    return [range(at, min(at + 4, bins)) for at in range(0, bins, 4)]


def near_kernel(keep, near, out):
    matrix = near[lax.axis_index("rg")]
    for index, group in enumerate(bin_groups(WINDOW)):
        out[index, :, : len(group) * FACTOR] = dot(matrix, long_rows(gather_lines(keep, WINDOW, group)))


def band_kernel(
    partial, keep, got, phase, weights, choice, far, there, back, last, twists, keep_out, give_out, spectra, band, picked
):
    side = lax.axis_index("rg")
    bins = WINDOW

    lane = lax.broadcasted_iota(jnp.int32, (REF_LINES, FACTOR), 1)
    lines = []
    for which in range(2):
        value = jnp.zeros((REF_LINES, FACTOR), jnp.float32)
        for option in range(2 * len(STEPS)):
            at = 2 * bins * 2 * PART + option % len(STEPS) * REF_LINES
            candidate = (keep if option < len(STEPS) else got)[at : at + REF_LINES, :]
            value = jnp.where(choice[which, option : option + 1, :] > 0.5, candidate, value)
        lines.append(value)
    for block in range(2):
        coarse = (lane >> 1) + block * HALF
        wide = [jnp.take_along_axis(lines[which], coarse, axis=1) for which in range(2)]
        ref_phase = jnp.where(lane < HALF, wide[1], wide[0])
        ref_cos, ref_sin = cos_sin_quarters(ref_phase * (2 / math.pi))
        picked[0, block * REF_LINES : (block + 1) * REF_LINES, :] = ref_cos
        picked[1, block * REF_LINES : (block + 1) * REF_LINES, :] = ref_sin

    far, last = far[side], (last[0, side], last[1, side])
    there, back = (there[0], there[1]), (back[0], back[1])
    twist_cos, twist_sin = twists[side, 0], twists[side, 1]
    for number, group in enumerate(bin_groups(bins)):
        passed = partial[number, :, : len(group) * FACTOR] + dot(far, long_rows(gather_lines(got, bins, group)))
        rows = []
        for index in range(len(group)):
            real = passed[:HALF, index * FACTOR : (index + 1) * FACTOR]
            imag = passed[HALF:, index * FACTOR : (index + 1) * FACTOR]
            rows.append(
                jnp.concatenate([real * twist_cos + imag * twist_sin, imag * twist_cos - real * twist_sin], axis=1)
            )
        passed = dot_split(split_bf16(jnp.concatenate(rows, axis=0)), there)
        for index, bin_num in enumerate(group):
            real = passed[index * HALF : (index + 1) * HALF, :FACTOR]
            imag = passed[index * HALF : (index + 1) * HALF, FACTOR:]
            model_cos, model_sin = phase[bin_num, 0], phase[bin_num, 1]
            row_cos, row_sin = picked[0, bin_num : bin_num + 1, :], picked[1, bin_num : bin_num + 1, :]
            cosine = model_cos * row_cos - model_sin * row_sin
            sine = model_sin * row_cos + model_cos * row_sin
            spectra[bin_num, 0] = real * cosine - imag * sine
            spectra[bin_num, 1] = real * sine + imag * cosine

    strip = 8
    for part in range(2):
        for at in range(0, HALF, strip):
            rows = slice(at, at + strip)
            sums = {}
            for bin_num in range(bins):
                value = spectra[bin_num, part, rows]
                for out in range(max(0, bin_num - TAPS + 1), min(OUT_BINS, bin_num + 1)):
                    weight = out * TAPS + bin_num - out
                    term = value * weights[weight : weight + 1, :]
                    sums[out] = sums[out] + term if out in sums else term
            for out in range(OUT_BINS):
                line = out * HALF + at
                band[line : line + strip, part * FACTOR : (part + 1) * FACTOR] = sums[out]

    scale = 1.0 / (FACTOR * FACTOR)
    cos_table, sin_table = twist_cos * scale, twist_sin * scale
    for at in range(0, OUT_BINS, 4):
        passed = dot_split(split_bf16(band[at * HALF : (at + 4) * HALF, :]), back)
        columns = []
        for index in range(4):
            real = passed[index * HALF : (index + 1) * HALF, :FACTOR]
            imag = passed[index * HALF : (index + 1) * HALF, FACTOR:]
            columns.append(
                jnp.concatenate([real * cos_table - imag * sin_table, imag * cos_table + real * sin_table], axis=0)
            )
        passed = dot_split(last, split_bf16(jnp.concatenate(columns, axis=1)))
        for index in range(4):
            lines = slice((at + index) * HALF, (at + index + 1) * HALF)
            keep_out[lines, :] = passed[:HALF, index * FACTOR : (index + 1) * FACTOR]
            give_out[lines, :] = passed[HALF:, index * FACTOR : (index + 1) * FACTOR]


def crossed(quarter):
    return ((quarter & 1) << 1) | (quarter >> 1)


def join_kernel(keep, got, *messages):
    place, side = lax.axis_index("az"), lax.axis_index("rg")
    quarter = lax.rem(place, PLACES // 2)
    sign = jnp.where(side == 0, 1.0, -1.0)
    for step, message in enumerate(messages):
        target = crossed(quarter) ^ step
        top, middle = target >> 1, target & 1
        keep_factor, got_factor = jnp.where(top == 0, 1.0, sign), jnp.where(top == 0, 1.0, -sign)
        for line in range(2 * OUT_BINS):
            read = pl.ds(pl.multiple_of(line * 2 * PART + middle * PART, 8), PART)
            message[line * PART : (line + 1) * PART, :] = keep[read, :] * keep_factor + got[read, :] * got_factor


def place_kernel(step, message, *refs):
    outs, (tiles, sems) = refs[-4:-2], refs[-2:]
    sender = crossed((lax.axis_index("az") >> 1) ^ step)
    rows = pl.ds(pl.multiple_of(sender * OUT_BINS, 8), OUT_BINS)
    copies = []
    for part, out in enumerate(outs):
        for row in range(PART):
            tiles[part, :, row * FACTOR : (row + 1) * FACTOR] = message[
                pl.ds(part * PART + row, OUT_BINS, stride=2 * PART), :
            ]
        copies.append(pltpu.make_async_copy(tiles.at[part], out.at[rows], sems.at[part]))
        copies[-1].start()
    for copy in copies:
        copy.wait()


VMEM = pl.BlockSpec(memory_space=pltpu.VMEM)
SMEM = pl.BlockSpec(memory_space=pltpu.SMEM)


def kernel_call(body, name, out_shape, operands, scratch=(), flops=0, count=10**6, limit=8):
    specs = [SMEM if operand.size <= 256 else VMEM for operand in operands]
    return pl.pallas_call(
        body,
        out_shape=out_shape,
        in_specs=specs,
        out_specs=jax.tree.map(lambda _: VMEM, out_shape),
        scratch_shapes=[pltpu.VMEM(shape, jnp.float32) for shape in scratch],
        compiler_params=pltpu.CompilerParams(vmem_limit_bytes=limit * 1024 * 1024),
        cost_estimate=pl.CostEstimate(flops=flops, bytes_accessed=count, transcendentals=0),
        name=name,
    )(*operands)


def transposed_shards(raw_re, raw_im, ref_blocks, owners, offsets, taps):
    bins, samples = raw_re.shape

    def array(*shape):
        return jax.ShapeDtypeStruct(shape, jnp.float32)

    matrices, twists = dft_constants()
    near_table, *tables = [jnp.asarray(table) for table in (*matrices, twists)]
    swap = functools.partial(lax.ppermute, axis_name="rg", perm=[(0, 1), (1, 0)])
    half = PLACES // 2
    ref_own = ref_blocks[0].T
    offsets_other = swap(offsets)
    ref_other, re_other, im_other, taps_other = swap(ref_own), swap(raw_re), swap(raw_im), swap(taps)

    lines = [raw_re.reshape(bins * PART, FACTOR), raw_im.reshape(bins * PART, FACTOR)]
    all_bins = 2 * bins + 2 * EDGE
    anywhere = pl.BlockSpec(memory_space=pl.ANY)
    messages = pl.pallas_call(
        pack_kernel,
        out_shape=[array(2 * WINDOW * PART + REF_LINES, FACTOR)] * half,
        in_specs=[VMEM] * 6 + [anywhere] * 2,
        out_specs=[VMEM] * half,
        scratch_shapes=[
            pltpu.VMEM((all_bins * PART, FACTOR), jnp.float32),
            pltpu.VMEM((all_bins * PART, FACTOR), jnp.float32),
            pltpu.VMEM((all_bins, FACTOR), jnp.float32),
            pltpu.SMEM(offsets.shape, jnp.int32),
            pltpu.SMEM(offsets.shape, jnp.int32),
            pltpu.SemaphoreType.DMA((2,)),
        ],
        compiler_params=pltpu.CompilerParams(vmem_limit_bytes=8 * 1024 * 1024),
        cost_estimate=pl.CostEstimate(flops=1, bytes_accessed=1, transcendentals=0),
        name="pack",
    )(*lines, re_other, im_other, ref_own, ref_other, offsets, offsets_other)
    prepared = kernel_call(
        functools.partial(phase_kernel, 2 * bins),
        "phase",
        [array(WINDOW, 2, HALF, FACTOR), array(OUT_BINS * TAPS, FACTOR), array(2, 2 * half, FACTOR)],
        [offsets, offsets_other, owners, taps, taps_other],
    )

    routes = [
        [
            (chip * 2 + core, (((chip >> 1) ^ step) * 2 + core) * 2 + (chip & 1))
            for chip in range(PLACES)
            for core in range(2)
        ]
        for step in range(half)
    ]
    routes_back = [
        [
            (chip * 2 + core, ((crossed(chip % half) ^ step) * 2 + core) * 2 + chip // half)
            for chip in range(PLACES)
            for core in range(2)
        ]
        for step in range(half)
    ]
    arrived = [lax.ppermute(messages[step], ("az", "rg"), routes[step]) for step in STEPS]
    *arrived, phases, weights, choice = lax.optimization_barrier((*arrived, *prepared))

    size = 2 * WINDOW * 2 * PART + half * REF_LINES
    keep, give = kernel_call(parity_kernel, "parity", [array(size, FACTOR)] * 2, arrived)
    got = swap(give)
    partial = kernel_call(
        near_kernel, "near", array(len(bin_groups(WINDOW)), FACTOR, 4 * FACTOR), [keep, near_table]
    )
    keep, give = kernel_call(
        band_kernel,
        "band",
        [array(OUT_BINS * HALF, FACTOR)] * 2,
        [partial, keep, got, phases, weights, choice, *tables],
        scratch=[(WINDOW, 2, HALF, FACTOR), (OUT_BINS * HALF, 2 * FACTOR), (2, 2 * REF_LINES, FACTOR)],
        limit=16,
    )
    sent = kernel_call(join_kernel, "join", [array(2 * OUT_BINS * PART, FACTOR)] * half, [keep, swap(give)])
    results = [lax.ppermute(message, ("az", "rg"), route) for message, route in zip(sent, routes_back)]
    images = []
    for step in STEPS_BACK:
        images = pl.pallas_call(
            functools.partial(place_kernel, step),
            out_shape=[array(bins, samples)] * 2,
            in_specs=[VMEM] + [anywhere] * len(images),
            out_specs=[anywhere] * 2,
            scratch_shapes=[pltpu.VMEM((2, OUT_BINS, samples), jnp.float32), pltpu.SemaphoreType.DMA((2,))],
            input_output_aliases={1: 0, 2: 1} if images else {},
            compiler_params=pltpu.CompilerParams(vmem_limit_bytes=8 * 1024 * 1024),
            cost_estimate=pl.CostEstimate(flops=1, bytes_accessed=1, transcendentals=0),
            name="place",
        )(results[step], *images)
    return images


def solution(mesh):
    sizes = mesh.shape

    def whole(raw_re, raw_im, ref_blocks, owners, offsets, taps):
        line = raw_re.shape[1] // sizes["scene"]
        fits = (
            sizes["rg"] == 2
            and sizes["az"] == PLACES
            and raw_re.shape[0] == OUT_BINS * PLACES
            and line == FACTOR * FACTOR
            and ref_blocks.shape[1] == HALF
        )
        return jax.shard_map(
            transposed_shards if fits else butterfly_shards,
            mesh=mesh,
            in_specs=(
                P("rg", ("scene", "az")),
                P("rg", ("scene", "az")),
                P(("scene", "az"), None, "rg"),
                P("scene"),
                P("rg"),
                P("rg", None),
            ),
            out_specs=(P("rg", ("scene", "az")), P("rg", ("scene", "az"))),
            check_vma=False,
        )(raw_re, raw_im, ref_blocks, owners, offsets, taps)

    return whole
```
